128 devices in a mesh: seq: 32 (over x, y, core), tensor: 4 (over z).
Axes of the slice: x: 4, y: 4, z: 4, core: 2. Of those that a mesh axis runs over, the one named last changes fastest.
Arguments:
- tokens: bfloat16 [12288, 2048], P('seq'), may hold values from -6 to 6
- cotangent: bfloat16 [12288, 2048], P('seq'), may hold values from -6 to 6
- w_query: bfloat16 [2048, 2048], P(None, 'tensor'), may hold values from -0.1875 to 0.1875
- w_key: bfloat16 [2048, 2048], P(None, 'tensor'), may hold values from -0.1875 to 0.1875
- w_value: bfloat16 [2048, 2048], P(None, 'tensor'), may hold values from -0.125 to 0.125
- w_output: bfloat16 [2048, 2048], P(None, 'tensor'), may hold values from -0.5 to 0.5
- w_gate: bfloat16 [2048, 8192], P(None, 'tensor'), may hold values from -0.125 to 0.125
- w_up: bfloat16 [2048, 8192], P(None, 'tensor'), may hold values from -0.125 to 0.125
- w_down: bfloat16 [2048, 8192], P(None, 'tensor'), may hold values from -0.0625 to 0.0625
- gain_attn: float32 [2048], replicated, may hold values from 0.5 to 1.5
- gain_mlp: float32 [2048], replicated, may hold values from 0.5 to 1.5
- gate_logit: float32 [16], P('tensor'), may hold values from -1.5 to 1.5
- valid_count: int32 [1], replicated, may hold values from 192 to 384
Outputs:
- layer_out: bfloat16 [12288, 2048], P('seq')
- grad_tokens: float32 [12288, 2048], P('seq')
- grad_w_query: float32 [2048, 2048], P('seq', 'tensor')
- grad_w_key: float32 [2048, 2048], P('seq', 'tensor')
- grad_w_value: float32 [2048, 2048], P('seq', 'tensor')
- grad_w_output: float32 [2048, 2048], P('seq', 'tensor')
- grad_w_gate: float32 [2048, 8192], P('seq', 'tensor')
- grad_w_up: float32 [2048, 8192], P('seq', 'tensor')
- grad_w_down: float32 [2048, 8192], P('seq', 'tensor')
- grad_gain_attn: float32 [2048], replicated
- grad_gain_mlp: float32 [2048], replicated
- grad_gate_logit: float32 [16], P('tensor')
- segment_memory: float32 [32, 16, 128, 128], P('seq', 'tensor')
- segment_normal: float32 [32, 16, 128], P('seq', 'tensor')
- grad_segment_normal: float32 [32, 16, 128], P('seq', 'tensor')
The draws below stay inside these ranges and needn't reach their ends.
All inputs are finite; a program needn't handle non-finite values.
Results may differ from the reference program's by a relative error of at most 0.014.
Values may be sent and summed in bfloat16 or wider, within the bound.
A program may use at most 384 MiB of HBM per device.

```python
import jax
import jax.numpy as jnp
from jax import lax

D = 2048
H = 16
HD = 128
FF = 8192
SEG = 384
SEQLEN = 12288
N_SEQ = 32


def shard_levels(stream_key, dims, shards, smallest, high):
    def one(dim, shards_of):
        draws = jax.random.uniform(jax.random.fold_in(jax.random.fold_in(stream_key, 6), dim), (shards_of,), jnp.float32, smallest / len(shards), high / len(shards))
        return jnp.repeat(jnp.exp(draws), dims[dim] // shards_of).reshape((-1,) + (1,) * (len(dims) - dim - 1))

    loudness = one(*shards[0])
    for cut in shards[1:]:
        loudness = loudness * one(*cut)
    return loudness


def normal_values(rng, extent, spread, limit, cuts=(), kind=jnp.bfloat16):
    array = spread * jax.random.normal(rng, extent, jnp.float32)
    if cuts:
        array = array * shard_levels(rng, extent, cuts, -0.22, 0.18)
    return jnp.clip(array, -limit, limit).astype(kind)


def setup_inputs(seed: int = 0) -> dict:
    seeds = jax.random.split(jax.random.key(seed), 14)
    return {
        "tokens": normal_values(seeds[0], (SEQLEN, D), 1.0, 6.0, ((0, 32),)),
        "cotangent": normal_values(seeds[1], (SEQLEN, D), 1.0, 6.0, ((0, 32),)),
        "w_query": normal_values(seeds[2], (D, H * HD), (D // 2) ** -0.5, 0.1875, ((1, 4),)),
        "w_key": normal_values(seeds[3], (D, H * HD), (D // 2) ** -0.5, 0.1875, ((1, 4),)),
        "w_value": normal_values(seeds[4], (D, H * HD), D ** -0.5, 0.125, ((1, 4),)),
        "w_output": normal_values(seeds[5], (D, H * HD), (H * HD // 16) ** -0.5, 0.5, ((1, 4),)),
        "w_gate": normal_values(seeds[6], (D, FF), D ** -0.5, 0.125, ((1, 4),)),
        "w_up": normal_values(seeds[7], (D, FF), D ** -0.5, 0.125, ((1, 4),)),
        "w_down": normal_values(seeds[8], (D, FF), FF ** -0.5, 0.0625, ((1, 4),)),
        "gain_attn": jnp.clip(1.0 + 0.1 * jax.random.normal(seeds[9], (D,), jnp.float32), 0.5, 1.5),
        "gain_mlp": jnp.clip(1.0 + 0.1 * jax.random.normal(seeds[10], (D,), jnp.float32), 0.5, 1.5),
        "gate_logit": jnp.clip(jax.random.uniform(seeds[11], (H,), jnp.float32, -1.5, 1.5) * shard_levels(seeds[11], (H,), ((0, 4),), -0.4, 0.0), -1.5, 1.5),
        "valid_count": jax.random.randint(seeds[12], (1,), SEG // 2, SEG + 1).astype(jnp.int32),
    }


epsilon = 1e-06
highest = lax.Precision.HIGHEST

@jax.custom_vjp
def low(v):
    return lax.optimization_barrier(v.astype(jnp.bfloat16)).astype(jnp.float32)

@jax.custom_vjp
def low_back(v):
    return v

def low_keep(v):
    return (low(v), None)

def low_pass(kept, grad):
    return (grad,)

def back_keep(v):
    return (v, None)

def back_low(kept, grad):
    return (low(grad),)
low.defvjp(low_keep, low_pass)
low_back.defvjp(back_keep, back_low)

def matmul(left_op, right_op):
    return jnp.dot(left_op, right_op, precision=highest)

def feature(values):
    return jax.nn.elu(values) + 1.0

def rms_norm(stream, gain_vec):
    inv_rms = lax.rsqrt(lax.optimization_barrier(jnp.mean(stream * stream, axis=1, keepdims=True)) + epsilon)
    return stream * inv_rms * gain_vec

def local_block(segment):
    queries, key_rows, values, keep_mask, probe = segment
    scores = low_back(jnp.einsum('qhd,khd->hqk', queries, key_rows, precision=highest) * HD ** (-0.5))
    position = jnp.arange(SEG, dtype=jnp.int32)
    allowed = (position[:, None] >= position[None, :]) & (keep_mask[None, :] > 0)
    masked = jnp.where(allowed[None], scores, -1e+30)
    row_top = lax.optimization_barrier(jnp.max(masked, axis=2, keepdims=True))
    exp_scores = jnp.exp(masked - row_top)
    attn_probs = low(exp_scores / lax.optimization_barrier(jnp.sum(exp_scores, axis=2, keepdims=True)))
    return jnp.einsum('hqk,khd->qhd', attn_probs, values, precision=highest)

def memory_step(state_pair, segment):
    memory, normal = state_pair
    queries, key_rows, values, keep_mask, probe = segment
    feat_query = feature(queries)
    feat_key = feature(key_rows)
    offset = normal + SEG
    den_query = jnp.einsum('shd,hd->sh', feat_query, offset, precision=highest)
    retrieved = jnp.einsum('shd,hde->she', feat_query, memory, precision=highest) / den_query[:, :, None]
    den_key = jnp.einsum('shd,hd->sh', feat_key, offset, precision=highest)
    recall = jnp.einsum('shd,hde->she', feat_key, memory, precision=highest) / den_key[:, :, None]
    kept_key = feat_key * keep_mask[:, None, None]
    memory = memory + jnp.einsum('shd,she->hde', kept_key, values - recall, precision=highest)
    normal = normal + lax.optimization_barrier(jnp.sum(kept_key, axis=0)) + probe
    return ((memory, normal), (retrieved, memory, normal))

def forward(tokens, w_query, w_key, w_value, w_output, w_gate, w_up, w_down, gain_attn, gain_mlp, gate_logit, normal_probe, keep_mask):
    normed = low(rms_norm(tokens, gain_attn))
    queries = low_back(low(matmul(normed, w_query)))
    key_rows = low_back(low(matmul(normed, w_key)))
    values = low_back(low(matmul(normed, w_value)))
    split_shape = (N_SEQ, SEG, H, HD)
    segments = (queries.reshape(split_shape), key_rows.reshape(split_shape), values.reshape(split_shape), keep_mask.reshape(N_SEQ, SEG), normal_probe)
    local_out = lax.map(jax.checkpoint(local_block), segments)
    init_state = (jnp.zeros((H, HD, HD), jnp.float32), jnp.zeros((H, HD), jnp.float32))
    last_state, (retrieved, memories, normals) = lax.scan(jax.checkpoint(memory_step), init_state, segments)
    gate_mix = jax.nn.sigmoid(gate_logit)[:, None]
    mixture = low(gate_mix * retrieved + (1.0 - gate_mix) * low_back(local_out)).reshape(SEQLEN, H * HD)
    middle = tokens + low_back(matmul(mixture, w_output.T))
    normed_two = low(rms_norm(middle, gain_mlp))
    gate_pre = low_back(matmul(normed_two, w_gate))
    up_pre = low_back(matmul(normed_two, w_up))
    hidden = low(jax.nn.silu(gate_pre) * up_pre)
    result = middle + matmul(hidden, w_down.T)
    return (result, (memories, normals))

def reference(tokens, cotangent, w_query, w_key, w_value, w_output, w_gate, w_up, w_down, gain_attn, gain_mlp, gate_logit, valid_count):
    position = jnp.arange(SEQLEN, dtype=jnp.int32)
    keep_mask = (position < SEQLEN - SEG + valid_count[0]).astype(jnp.float32)
    floats = [item.astype(jnp.float32) for item in (tokens, w_query, w_key, w_value, w_output, w_gate, w_up, w_down, gain_attn, gain_mlp, gate_logit)]
    floats.append(jnp.zeros((N_SEQ, H, HD), jnp.float32))

    def layer(*params):
        return forward(*params, keep_mask)
    result, pullback, memory_pair = jax.vjp(layer, *floats, has_aux=True)
    gradients = pullback(cotangent.astype(jnp.float32) * keep_mask[:, None])
    return (result.astype(jnp.bfloat16), gradients[0], gradients[1], gradients[2], gradients[3], gradients[4], gradients[5], gradients[6], gradients[7], gradients[8], gradients[9], gradients[10], memory_pair[0], memory_pair[1], gradients[11])
```

```python
import functools

import jax
import jax.numpy as jnp
from jax import lax
from jax.experimental import pallas as pl
from jax.experimental.pallas import tpu as pltpu
from jax.sharding import Mesh
from jax.sharding import PartitionSpec as P

SEQ = ("seq_0", "seq_1", "seq_2")
MESH_ID = pl.DeviceIdType.MESH
VMEM = pl.BlockSpec(memory_space=pltpu.VMEM)
BF = jnp.bfloat16
F32 = jnp.float32

epsilon = 1e-06


def remote(src, dst, send, recv, device):
    return pltpu.make_async_remote_copy(
        src_ref=src, dst_ref=dst, send_sem=send, recv_sem=recv, device_id=device, device_id_type=MESH_ID
    )


def meet(devices):
    barrier = pltpu.get_barrier_semaphore()
    for device in devices:
        pl.semaphore_signal(barrier, inc=1, device_id=device, device_id_type=MESH_ID)
    pl.semaphore_wait(barrier, len(devices))


def params(collective_id, mib):
    return pltpu.CompilerParams(
        collective_id=collective_id, has_side_effects=True, vmem_limit_bytes=mib << 20
    )


def row_sum_kernel(part, out, a1, b1, a2, b2, a_own, b_own, sum_a, sum_b, send, recv):
    z, n = lax.axis_index("tensor"), 4
    rows = part.shape[0] // n
    half = part.shape[1] // 2
    right, left, far = lax.rem(z + 1, n), lax.rem(z + 3, n), lax.rem(z + 2, n)
    to_right, to_left = {"tensor": right}, {"tensor": left}
    meet((to_left, to_right))

    def of(q):
        return pl.ds(pl.multiple_of(q * rows, 16), rows)

    a, b = pl.ds(0, half), pl.ds(half, half)
    c0 = remote(part.at[of(far), a], a1, send.at[0], recv.at[0], to_right)
    c1 = remote(part.at[of(far), b], b1, send.at[1], recv.at[1], to_left)
    c2 = remote(part.at[of(right), b], b_own, send.at[2], recv.at[2], to_right)
    c3 = remote(part.at[of(left), a], a_own, send.at[3], recv.at[3], to_left)
    for copy in (c0, c1, c2, c3):
        copy.start()
    c0.wait_recv()
    sum_a[...] = (a1[...].astype(F32) + part[of(right), a].astype(F32)).astype(BF)
    c4 = remote(sum_a, a2, send.at[4], recv.at[4], to_right)
    c4.start()
    c1.wait_recv()
    sum_b[...] = (b1[...].astype(F32) + part[of(left), b].astype(F32)).astype(BF)
    c5 = remote(sum_b, b2, send.at[5], recv.at[5], to_left)
    c5.start()
    c2.wait_recv()
    c3.wait_recv()
    c4.wait_recv()
    out[:, a] = part[of(z), a].astype(F32) + a2[...].astype(F32) + a_own[...].astype(F32)
    c5.wait_recv()
    out[:, b] = part[of(z), b].astype(F32) + b2[...].astype(F32) + b_own[...].astype(F32)
    for copy in (c0, c1, c2, c3, c4, c5):
        copy.wait_send()


def row_sum(part, collective_id):
    rows, cols = part.shape[0] // 4, part.shape[1]
    piece = pltpu.VMEM((rows, cols // 2), BF)
    return pl.pallas_call(
        row_sum_kernel,
        out_shape=jax.ShapeDtypeStruct((rows, cols), F32),
        in_specs=[VMEM],
        out_specs=VMEM,
        scratch_shapes=[piece] * 8 + [pltpu.SemaphoreType.DMA((6,)), pltpu.SemaphoreType.DMA((6,))],
        name=f"row_sum_{collective_id}",
        compiler_params=params(collective_id, 32),
    )(part)


def row_gather_kernel(own, out, landing, send, recv):
    z, n = lax.axis_index("tensor"), 4
    rows = own.shape[0]
    half = rows // 2
    right, left, far = lax.rem(z + 1, n), lax.rem(z + 3, n), lax.rem(z + 2, n)
    to_right, to_left = {"tensor": right}, {"tensor": left}
    meet((to_left, to_right))

    def of(q):
        return pl.ds(pl.multiple_of(q * rows, 16), rows)

    def part_of(q, h):
        return pl.ds(pl.multiple_of(q * rows + half * h, 16), half)

    def copy(h, slot, device):
        return remote(own.at[pl.ds(half * h, half)], landing.at[part_of(z, h)], send.at[slot], recv.at[slot], device)

    r0, l1, r1, l0 = copy(0, 0, to_right), copy(1, 1, to_left), copy(1, 2, to_right), copy(0, 3, to_left)
    for c in (r0, l1, r1, l0):
        c.start()
    r0.wait_recv()
    f0 = remote(landing.at[part_of(left, 0)], landing.at[part_of(left, 0)], send.at[4], recv.at[4], to_right)
    f0.start()
    l1.wait_recv()
    f1 = remote(landing.at[part_of(right, 1)], landing.at[part_of(right, 1)], send.at[5], recv.at[5], to_left)
    f1.start()
    out[of(z)] = own[...]
    r1.wait_recv()
    l0.wait_recv()
    out[of(left)] = landing[of(left)]
    out[of(right)] = landing[of(right)]
    f0.wait_recv()
    f1.wait_recv()
    out[of(far)] = landing[of(far)]
    for c in (r0, l1, r1, l0, f0, f1):
        c.wait_send()


def row_gather(own, collective_id):
    rows, cols = own.shape
    whole = (4 * rows, cols)
    return pl.pallas_call(
        row_gather_kernel,
        out_shape=jax.ShapeDtypeStruct(whole, BF),
        in_specs=[VMEM],
        out_specs=VMEM,
        scratch_shapes=[pltpu.VMEM(whole, BF), pltpu.SemaphoreType.DMA((6,)), pltpu.SemaphoreType.DMA((6,))],
        name=f"row_gather_{collective_id}",
        compiler_params=params(collective_id, 32),
    )(own)


def seq_place(index):
    return {"seq_0": index // 8, "seq_1": lax.rem(index // 2, 4), "seq_2": lax.rem(index, 2)}


def seq_index():
    return lax.axis_index("seq_0") * 8 + lax.axis_index("seq_1") * 2 + lax.axis_index("seq_2")


def spread_kernel(along, x, out, landing, send, recv):
    if along == "tensor":
        n, me = 4, lax.axis_index("tensor")
    else:
        n, me = 32, seq_index()

    def device(k):
        peer = lax.rem(me + k, n)
        return {"tensor": peer} if along == "tensor" else seq_place(peer)

    barrier = pltpu.get_barrier_semaphore()

    def greet(k, carry):
        pl.semaphore_signal(barrier, inc=1, device_id=device(k), device_id_type=MESH_ID)
        return carry

    lax.fori_loop(1, n, greet, 0)
    pl.semaphore_wait(barrier, n - 1)

    def push(k, carry):
        remote(x, landing.at[me], send, recv, device(k)).start()
        return carry

    lax.fori_loop(1, n, push, 0)
    others = landing.at[pl.ds(0, n - 1)]
    pltpu.make_async_copy(others, others, recv).wait()
    landing[me] = x[...]
    out[...] = landing[...]
    pltpu.make_async_copy(others, others, send).wait()


def spread(x, along, collective_id):
    n = 4 if along == "tensor" else 32
    return pl.pallas_call(
        functools.partial(spread_kernel, along),
        out_shape=jax.ShapeDtypeStruct((n, *x.shape), F32),
        in_specs=[VMEM],
        out_specs=VMEM,
        scratch_shapes=[pltpu.VMEM((n, *x.shape), F32), pltpu.SemaphoreType.DMA(()), pltpu.SemaphoreType.DMA(())],
        name=f"spread_{collective_id}",
        compiler_params=params(collective_id, 32),
    )(x)


def mul(a, b):
    return jnp.dot(a.astype(BF), b.astype(BF), preferred_element_type=F32)


def mul_t(a, b):
    return lax.dot_general(a.astype(BF), b.astype(BF), (((0,), (0,)), ((), ())), preferred_element_type=F32)


def ring_places():
    x, y, c = (lax.axis_index(a) for a in SEQ)
    return x, y, c


def ring_gather(buf, me, axis, send, recv, base):
    right, left = lax.rem(me + 1, 4), lax.rem(me + 3, 4)
    to_right, to_left = {axis: right}, {axis: left}

    def piece(q, h):
        return buf.at[q, pl.ds(h, 1)]

    def copy(q, h, slot, device):
        return remote(piece(q, h), piece(q, h), send.at[base + slot], recv.at[base + slot], device)

    r0, l1, r1, l0 = copy(me, 0, 0, to_right), copy(me, 1, 1, to_left), copy(me, 1, 2, to_right), copy(me, 0, 3, to_left)
    for c in (r0, l1, r1, l0):
        c.start()
    r0.wait_recv()
    f0 = copy(left, 0, 4, to_right)
    f0.start()
    l1.wait_recv()
    f1 = copy(right, 1, 5, to_left)
    f1.start()
    for c in (r1, l0, f0, f1):
        c.wait_recv()
    return (r0, l1, r1, l0, f0, f1)


def memory_kernel(eb, b_full, before, after, ys, xs, first_e, got, pair_m, got_m, send, recv):
    x, y, c = ring_places()
    hd = 128
    partner = {"seq_2": 1 - c}
    right_y, left_y = {"seq_1": lax.rem(y + 1, 4)}, {"seq_1": lax.rem(y + 3, 4)}
    right_x, left_x = {"seq_0": lax.rem(x + 1, 4)}, {"seq_0": lax.rem(x + 3, 4)}
    meet((partner, right_y, left_y, right_x, left_x))
    mine, theirs = 2 * c, 2 * (1 - c)
    c0 = remote(eb.at[pl.ds(theirs, 2)], got, send.at[12], recv.at[12], partner)
    c0.start()
    c0.wait_recv()
    firsts = []
    for h in (0, 1):
        here, there = eb[mine + h].astype(F32), got[h].astype(F32)
        first, second = jnp.where(c == 0, here, there), jnp.where(c == 0, there, here)
        firsts.append(first)
        first_e[0, h] = first[:, :hd].astype(BF)
        first_e[1, h] = second[:, :hd].astype(BF)
        ys[y, h] = (first + second - mul(second[:, :hd], first)).astype(BF)
    sent = ring_gather(ys, y, "seq_1", send, recv, 0)
    starts = []
    for h in (0, 1):
        so_far = ys[0, h].astype(F32)
        start = jnp.where(y > 0, so_far, 0.0)
        for k in (1, 2, 3):
            step = ys[k, h].astype(F32)
            so_far = so_far + step - mul(step[:, :hd], so_far)
            if k < 3:
                start = jnp.where(y > k, so_far, start)
        xs[x, h] = so_far.astype(BF)
        starts.append(start)
    sent += ring_gather(xs, x, "seq_0", send, recv, 6)
    for h in (0, 1):
        m = jnp.where(x > 0, xs[0, h][:, hd:].astype(F32), 0.0)
        for k in (1, 2):
            step = xs[k, h].astype(F32)
            m = jnp.where(x > k, m + step[:, hd:] - mul(step[:, :hd], m), m)
        m = m + starts[h][:, hd:] - mul(starts[h][:, :hd], m)
        second = m + firsts[h][:, hd:] - mul(firsts[h][:, :hd], m)
        before[mine + h] = jnp.where(c == 0, m, second)
        pair_m[h] = jnp.where(c == 0, second, m)
    c1 = remote(pair_m, got_m, send.at[13], recv.at[13], partner)
    c1.start()
    c1.wait_recv()
    for h in (0, 1):
        before[theirs + h] = got_m[h]
    for h in range(4):
        m = before[h]
        after[h] = m + b_full[h] - mul(eb[h][:, :hd], m)
    for copy in (c0, *sent, c1):
        copy.wait_send()


def memory_scan(eb, b_full, collective_id):
    square = jax.ShapeDtypeStruct((4, 128, 128), F32)
    slots = jax.ShapeDtypeStruct((4, 2, 128, 256), BF)
    pair = jax.ShapeDtypeStruct((2, 2, 128, 128), BF)
    return pl.pallas_call(
        memory_kernel,
        out_shape=(square, square, slots, slots, pair),
        in_specs=[VMEM] * 2,
        out_specs=(VMEM,) * 5,
        scratch_shapes=[
            pltpu.VMEM((2, 128, 256), BF),
            pltpu.VMEM((2, 128, 128), F32),
            pltpu.VMEM((2, 128, 128), F32),
            pltpu.SemaphoreType.DMA((14,)),
            pltpu.SemaphoreType.DMA((14,)),
        ],
        name="memory_scan",
        compiler_params=params(collective_id, 32),
    )(eb, b_full)


def adjoint_kernel(source, ys, xs, pair_e, adjoint, got, s_y, s_x, pair_l, got_l, send, recv):
    x, y, c = ring_places()
    hd = 128
    partner = {"seq_2": 1 - c}
    right_y, left_y = {"seq_1": lax.rem(y + 1, 4)}, {"seq_1": lax.rem(y + 3, 4)}
    right_x, left_x = {"seq_0": lax.rem(x + 1, 4)}, {"seq_0": lax.rem(x + 3, 4)}
    meet((partner, right_y, left_y, right_x, left_x))
    mine, theirs = 2 * c, 2 * (1 - c)
    c0 = remote(source.at[pl.ds(theirs, 2)], got, send.at[12], recv.at[12], partner)
    c0.start()
    c0.wait_recv()
    seconds = []
    for h in (0, 1):
        here, there = source[mine + h].astype(F32), got[h].astype(F32)
        first, second = jnp.where(c == 0, here, there), jnp.where(c == 0, there, here)
        seconds.append(second)
        s_y[y, h] = (first + second - mul_t(pair_e[0, h], second)).astype(BF)
    sent = ring_gather(s_y, y, "seq_1", send, recv, 0)
    for h in (0, 1):
        so_far = s_y[3, h].astype(F32)
        for k in (2, 1, 0):
            so_far = s_y[k, h].astype(F32) + so_far - mul_t(ys[k, h][:, :hd], so_far)
        s_x[x, h] = so_far.astype(BF)
    sent += ring_gather(s_x, x, "seq_0", send, recv, 6)
    for h in (0, 1):
        lam = jnp.where(x < 3, s_x[3, h].astype(F32), 0.0)
        for k in (2, 1):
            lam = jnp.where(x < k, s_x[k, h].astype(F32) + lam - mul_t(xs[k, h][:, :hd], lam), lam)
        for k in (3, 2, 1):
            lam = jnp.where(y < k, s_y[k, h].astype(F32) + lam - mul_t(ys[k, h][:, :hd], lam), lam)
        first = lam + seconds[h] - mul_t(pair_e[1, h], lam)
        adjoint[mine + h] = jnp.where(c == 0, first, lam)
        pair_l[h] = jnp.where(c == 0, lam, first)
    c1 = remote(pair_l, got_l, send.at[13], recv.at[13], partner)
    c1.start()
    c1.wait_recv()
    for h in (0, 1):
        adjoint[theirs + h] = got_l[h]
    for copy in (c0, *sent, c1):
        copy.wait_send()


def adjoint_scan(source, ys, xs, pair_e, collective_id):
    return pl.pallas_call(
        adjoint_kernel,
        out_shape=jax.ShapeDtypeStruct((4, 128, 128), F32),
        in_specs=[VMEM] * 4,
        out_specs=VMEM,
        scratch_shapes=[
            pltpu.VMEM((2, 128, 128), BF),
            pltpu.VMEM((4, 2, 128, 128), BF),
            pltpu.VMEM((4, 2, 128, 128), BF),
            pltpu.VMEM((2, 128, 128), F32),
            pltpu.VMEM((2, 128, 128), F32),
            pltpu.SemaphoreType.DMA((14,)),
            pltpu.SemaphoreType.DMA((14,)),
        ],
        name="adjoint_scan",
        compiler_params=params(collective_id, 32),
    )(source, ys, xs, pair_e)


def rows_by_rows(a, b):
    return lax.dot_general(a, b, (((1,), (1,)), ((), ())), preferred_element_type=F32)


def mlp_kernel(normed, grad_out, w_gate, w_up, w_down, back, forth, grads, normed_t, grad_out_t, back_sum, forth_sum):
    step = pl.program_id(0)

    @pl.when(step == 0)
    def _():
        normed_t[...] = normed[...].T
        grad_out_t[...] = grad_out[...].T
        back_sum[...] = jnp.zeros_like(back_sum)
        forth_sum[...] = jnp.zeros_like(forth_sum)

    gate_pre = jnp.dot(normed[...], w_gate[...], preferred_element_type=F32)
    up_pre = jnp.dot(normed[...], w_up[...], preferred_element_type=F32)
    grad_hidden = jnp.dot(grad_out[...], w_down[...], preferred_element_type=F32)
    sig = jax.nn.sigmoid(gate_pre)
    swish = gate_pre * sig
    hidden = (swish * up_pre).astype(BF)
    grad_up = (grad_hidden * swish).astype(BF)
    grad_gate = (grad_hidden * up_pre * sig * (1.0 + gate_pre * (1.0 - sig))).astype(BF)
    back_sum[...] += rows_by_rows(grad_gate, w_gate[...]) + rows_by_rows(grad_up, w_up[...])
    forth_sum[...] += rows_by_rows(hidden, w_down[...])
    tile = hidden.shape[1]
    grads[:, :tile] = jnp.dot(grad_out_t[...], hidden, preferred_element_type=F32).astype(BF)
    grads[:, tile : 2 * tile] = jnp.dot(normed_t[...], grad_gate, preferred_element_type=F32).astype(BF)
    grads[:, 2 * tile :] = jnp.dot(normed_t[...], grad_up, preferred_element_type=F32).astype(BF)

    @pl.when(step == pl.num_programs(0) - 1)
    def _():
        back[...] = back_sum[...].astype(BF)
        forth[...] = forth_sum[...].astype(BF)


MLP_TILE = 256


def mlp(normed, grad_out, w_gate, w_up, w_down):
    rows, width = normed.shape
    units = w_gate.shape[1]
    whole = pl.BlockSpec((rows, width), lambda f: (0, 0))
    weight = pl.BlockSpec((width, MLP_TILE), lambda f: (0, f))
    low = jax.ShapeDtypeStruct((rows, width), BF)
    return pl.pallas_call(
        mlp_kernel,
        grid=(units // MLP_TILE,),
        out_shape=(low, low, jax.ShapeDtypeStruct((width, 3 * units), BF)),
        in_specs=[whole, whole, weight, weight, weight],
        out_specs=(whole, whole, pl.BlockSpec((width, 3 * MLP_TILE), lambda f: (0, f))),
        scratch_shapes=[
            pltpu.VMEM((width, rows), BF),
            pltpu.VMEM((width, rows), BF),
            pltpu.VMEM((rows, width), F32),
            pltpu.VMEM((rows, width), F32),
        ],
        name="mlp",
        compiler_params=pltpu.CompilerParams(vmem_limit_bytes=56 << 20),
        cost_estimate=pl.CostEstimate(
            flops=18 * rows * width * units, bytes_accessed=12 * width * units, transcendentals=rows * units
        ),
    )(normed, grad_out, w_gate, w_up, w_down)


def feature(values):
    return jax.nn.elu(values) + 1.0


def feature_slope(values):
    return jnp.where(values > 0, 1.0, jnp.exp(jnp.minimum(values, 0.0)))


def norm_back(stream, inv_rms, gain_vec, grad_normed):
    weighted = grad_normed * gain_vec
    inner_sum = jnp.sum(weighted * stream, axis=1, keepdims=True)
    return inv_rms * weighted - stream * inv_rms**3 * inner_sum / stream.shape[1]


def heads_dot(spec, a, b):
    return jnp.einsum(spec, a.astype(BF), b.astype(BF), preferred_element_type=F32)


def on_device(
    tokens,
    cotangent,
    w_query,
    w_key,
    w_value,
    w_output,
    w_gate,
    w_up,
    w_down,
    gain_attn,
    gain_mlp,
    gate_logit,
    valid_count,
):
    seg_len = tokens.shape[0]
    head_count = gate_logit.shape[0]
    col_count = w_query.shape[1]
    head_dim = col_count // head_count
    scale_dot = head_dim ** (-0.5)
    here = seq_index()
    z = lax.axis_index("tensor")
    own_rows = seg_len // 4
    position = lax.iota(jnp.int32, seg_len)
    valid_len = jnp.where(here == 31, valid_count[0], seg_len)
    keep_mask = (position < valid_len).astype(F32)
    allowed = (position[:, None] >= position[None, :]) & (keep_mask[None, :] > 0)
    stream = tokens.astype(F32)
    inv_one = lax.rsqrt(jnp.mean(stream * stream, axis=1, keepdims=True) + epsilon)
    normed = (stream * inv_one * gain_attn).astype(BF)
    queries = jnp.dot(normed, w_query, preferred_element_type=F32).astype(BF)
    key_rows = jnp.dot(normed, w_key, preferred_element_type=F32).astype(BF)
    values = jnp.dot(normed, w_value, preferred_element_type=F32).astype(BF)
    heads_shape = (seg_len, head_count, head_dim)
    q_heads = queries.reshape(heads_shape)
    k_heads = key_rows.reshape(heads_shape)
    v_heads = values.reshape(heads_shape)
    q_float = q_heads.astype(F32)
    k_float = k_heads.astype(F32)
    v_float = v_heads.astype(F32)
    feat_query = feature(q_float)
    feat_key = feature(k_float)
    kept_key = feat_key * keep_mask[:, None, None]
    key_sum = jnp.sum(kept_key, axis=0)
    key_sums = spread(key_sum, "seq", 0)
    earlier = (jnp.arange(32) < here)[:, None, None]
    normal_prev = jnp.sum(jnp.where(earlier, key_sums, 0.0), axis=0)
    normal_next = normal_prev + key_sum
    scores = jnp.einsum("qhd,khd->hqk", q_heads, k_heads, preferred_element_type=F32) * scale_dot
    masked = jnp.where(allowed[None], scores, -1e30)
    row_top = jnp.max(masked, axis=2, keepdims=True)
    exp_scores = jnp.exp(masked - row_top)
    attn_again = exp_scores / jnp.sum(exp_scores, axis=2, keepdims=True)
    attn_low = attn_again.astype(BF)
    local_out = jnp.einsum("hqk,khd->qhd", attn_low, v_heads, preferred_element_type=F32)
    offset = normal_prev + seg_len
    den_key = jnp.sum(feat_key * offset, axis=2)
    den_query = jnp.sum(feat_query * offset, axis=2)
    taken = heads_dot("shd,she->hde", kept_key / den_key[:, :, None], feat_key)
    source = heads_dot("shd,she->hde", kept_key, v_heads)
    eb = jnp.concatenate((taken, source), axis=2).astype(BF)
    memory_prev, memory_next, ys, xs, pair_e = memory_scan(eb, source, 1)
    retrieved = heads_dot("shd,hde->she", feat_query, memory_prev) / den_query[:, :, None]
    gate_mix = jax.nn.sigmoid(gate_logit)[:, None]
    mixture = gate_mix * retrieved + (1.0 - gate_mix) * local_out
    mix_low = mixture.reshape(seg_len, col_count).astype(BF)
    attn_part = jnp.einsum("sc,dc->sd", mix_low, w_output, preferred_element_type=F32).astype(BF)
    own = lambda a: lax.dynamic_slice_in_dim(a, z * own_rows, own_rows, 0)
    middle = own(tokens).astype(F32) + row_sum(attn_part, 2)
    inv_two = lax.rsqrt(jnp.mean(middle * middle, axis=1, keepdims=True) + epsilon)
    normed_two = row_gather((middle * inv_two * gain_mlp).astype(BF), 3)
    grad_out = jnp.where(keep_mask[:, None] > 0, cotangent, jnp.zeros_like(cotangent))
    back_part, forth_part, mlp_grads = mlp(normed_two, grad_out, w_gate, w_up, w_down)
    mlp_grads = lax.psum_scatter(mlp_grads, SEQ, scatter_dimension=0, tiled=True)
    grad_normed_two = row_sum(back_part, 4)
    grad_middle = own(grad_out).astype(F32) + norm_back(middle, inv_two, gain_mlp, grad_normed_two)
    gain_mlp_grad = jnp.sum(grad_normed_two * middle * inv_two, axis=0)
    grad_branch = row_gather(grad_middle.astype(BF), 5)
    grad_mix = jnp.einsum("sd,dc->sc", grad_branch, w_output, preferred_element_type=F32).reshape(heads_shape)
    logit_grad = (
        jnp.sum(grad_mix * (retrieved - local_out), axis=(0, 2)) * gate_mix[:, 0] * (1.0 - gate_mix[:, 0])
    )
    grad_retrieved = gate_mix * grad_mix
    grad_point = grad_retrieved / den_query[:, :, None]
    mem_source = heads_dot("shd,she->hde", feat_query, grad_point)
    adjoint = adjoint_scan(mem_source.astype(BF), ys, xs, pair_e, 6)
    grad_local = ((1.0 - gate_mix) * grad_mix).astype(BF)
    grad_probs = jnp.einsum("qhd,khd->hqk", grad_local, v_heads, preferred_element_type=F32)
    grad_value = jnp.einsum("hqk,qhd->khd", attn_low, grad_local, preferred_element_type=F32)
    grad_scores = (
        attn_again * (grad_probs - jnp.sum(grad_probs * attn_again, axis=2, keepdims=True))
    ).astype(BF)
    grad_query = jnp.einsum("hqk,khd->qhd", grad_scores, k_heads, preferred_element_type=F32) * scale_dot
    grad_key = jnp.einsum("hqk,qhd->khd", grad_scores, q_heads, preferred_element_type=F32) * scale_dot
    recall = heads_dot("shd,hde->she", feat_key, memory_prev) / den_key[:, :, None]
    update = v_float - recall
    grad_update = heads_dot("shd,hde->she", kept_key, adjoint)
    grad_den_key = jnp.sum(grad_update * recall, axis=2) / den_key
    grad_den_query = -jnp.sum(grad_retrieved * retrieved, axis=2) / den_query
    grad_offset = jnp.sum(
        grad_den_key[:, :, None] * feat_key + grad_den_query[:, :, None] * feat_query, axis=0
    )
    grad_offsets = spread(grad_offset, "seq", 7)
    later = (jnp.arange(32) > here)[:, None, None]
    later_offset = jnp.sum(jnp.where(later, grad_offsets, 0.0), axis=0)
    grad_kept = heads_dot("she,hde->shd", update, adjoint)
    grad_feat_key = (
        -heads_dot("she,hde->shd", grad_update / den_key[:, :, None], memory_prev)
        + grad_den_key[:, :, None] * offset[None]
        + keep_mask[:, None, None] * (grad_kept + later_offset[None])
    )
    grad_feat_query = (
        heads_dot("she,hde->shd", grad_point, memory_prev) + grad_den_query[:, :, None] * offset[None]
    )
    flat = (seg_len, col_count)
    grad_q_low = (grad_query + grad_feat_query * feature_slope(q_float)).reshape(flat).astype(BF)
    grad_k_low = (grad_key + grad_feat_key * feature_slope(k_float)).reshape(flat).astype(BF)
    grad_v_low = (grad_value + grad_update).reshape(flat).astype(BF)
    grad_normed = (
        jnp.einsum("sc,dc->sd", grad_q_low, w_query, preferred_element_type=F32)
        + jnp.einsum("sc,dc->sd", grad_k_low, w_key, preferred_element_type=F32)
        + jnp.einsum("sc,dc->sd", grad_v_low, w_value, preferred_element_type=F32)
    ).astype(BF)
    rest_grads = jnp.concatenate(
        (
            jnp.einsum(
                "sd,sc->dc",
                normed,
                jnp.concatenate((grad_q_low, grad_k_low, grad_v_low), axis=1),
                preferred_element_type=F32,
            ).astype(BF),
            jnp.einsum("sd,sc->dc", grad_branch, mix_low, preferred_element_type=F32).astype(BF),
        ),
        axis=1,
    )
    rest_grads = lax.psum_scatter(rest_grads, SEQ, scatter_dimension=0, tiled=True).astype(F32)
    grad_normed = row_sum(grad_normed, 8)
    own_stream, own_inv = own(stream), own(inv_one)
    grad_tokens = grad_middle + norm_back(own_stream, own_inv, gain_attn, grad_normed)
    gain_attn_grad = jnp.sum(grad_normed * own_stream * own_inv, axis=0)
    grad_tokens = row_gather(grad_tokens.astype(BF), 9).astype(F32)
    layer_out = row_gather((middle + row_sum(forth_part, 10)).astype(BF), 11)
    logits = jnp.where(z == jnp.arange(4)[:, None], logit_grad[None, :], 0.0).reshape(-1)
    small = jnp.concatenate((gain_attn_grad, gain_mlp_grad, logits, jnp.zeros((1008,), F32))).reshape(40, 128)
    small = jnp.sum(spread(jnp.sum(spread(small, "seq", 12), axis=0), "tensor", 13), axis=0).reshape(-1)
    logit_grad = lax.dynamic_slice_in_dim(small, 4096 + 4 * z, 4)
    by_tile = mlp_grads.reshape(64, -1, 3, MLP_TILE).astype(F32)
    of_mlp = lambda k: by_tile[:, :, k].reshape(64, -1)
    return (
        layer_out,
        grad_tokens,
        rest_grads[:, :col_count],
        rest_grads[:, col_count : 2 * col_count],
        rest_grads[:, 2 * col_count : 3 * col_count],
        rest_grads[:, 3 * col_count :],
        of_mlp(1),
        of_mlp(2),
        of_mlp(0),
        small[:2048],
        small[2048:4096],
        logit_grad,
        memory_next[None],
        normal_next[None],
        later_offset[None],
    )


def solution(mesh):
    torus = Mesh(
        mesh.devices.reshape(4, 4, 2, mesh.shape["tensor"]), ("seq_0", "seq_1", "seq_2", "tensor")
    )
    weight = P(None, "tensor")
    grad = P(SEQ, "tensor")
    return jax.shard_map(
        on_device,
        mesh=torus,
        in_specs=(P(SEQ, None), P(SEQ, None)) + (weight,) * 7 + (P(), P(), P("tensor"), P()),
        out_specs=(P(SEQ, None), P(SEQ, None))
        + (grad,) * 7
        + (P(), P(), P("tensor"), P(SEQ, "tensor", None, None), P(SEQ, "tensor", None), P(SEQ, "tensor", None)),
        check_vma=False,
    )
```

```python
import functools

import jax
import jax.numpy as jnp
from jax import lax
from jax.experimental import pallas as pl
from jax.experimental.pallas import tpu as pltpu
from jax.sharding import Mesh
from jax.sharding import PartitionSpec as P

SEQ = ("seq_0", "seq_1", "seq_2")
MESH_ID = pl.DeviceIdType.MESH
VMEM = pl.BlockSpec(memory_space=pltpu.VMEM)
BF = jnp.bfloat16
F32 = jnp.float32

epsilon = 1e-06


def remote(src, dst, send, recv, device):
    return pltpu.make_async_remote_copy(
        src_ref=src, dst_ref=dst, send_sem=send, recv_sem=recv, device_id=device, device_id_type=MESH_ID
    )


def meet(devices):
    barrier = pltpu.get_barrier_semaphore()
    for device in devices:
        pl.semaphore_signal(barrier, inc=1, device_id=device, device_id_type=MESH_ID)
    pl.semaphore_wait(barrier, len(devices))


def params(collective_id, mib):
    return pltpu.CompilerParams(
        collective_id=collective_id, has_side_effects=True, vmem_limit_bytes=mib << 20
    )


def row_sum_kernel(part, out, a1, b1, a2, b2, a_own, b_own, sum_a, sum_b, send, recv):
    z, n = lax.axis_index("tensor"), 4
    rows = part.shape[0] // n
    half = part.shape[1] // 2
    right, left, far = lax.rem(z + 1, n), lax.rem(z + 3, n), lax.rem(z + 2, n)
    to_right, to_left = {"tensor": right}, {"tensor": left}
    meet((to_left, to_right))

    def of(q):
        return pl.ds(pl.multiple_of(q * rows, 16), rows)

    a, b = pl.ds(0, half), pl.ds(half, half)
    c0 = remote(part.at[of(far), a], a1, send.at[0], recv.at[0], to_right)
    c1 = remote(part.at[of(far), b], b1, send.at[1], recv.at[1], to_left)
    c2 = remote(part.at[of(right), b], b_own, send.at[2], recv.at[2], to_right)
    c3 = remote(part.at[of(left), a], a_own, send.at[3], recv.at[3], to_left)
    for copy in (c0, c1, c2, c3):
        copy.start()
    c0.wait_recv()
    sum_a[...] = (a1[...].astype(F32) + part[of(right), a].astype(F32)).astype(BF)
    c4 = remote(sum_a, a2, send.at[4], recv.at[4], to_right)
    c4.start()
    c1.wait_recv()
    sum_b[...] = (b1[...].astype(F32) + part[of(left), b].astype(F32)).astype(BF)
    c5 = remote(sum_b, b2, send.at[5], recv.at[5], to_left)
    c5.start()
    c2.wait_recv()
    c3.wait_recv()
    c4.wait_recv()
    out[:, a] = part[of(z), a].astype(F32) + a2[...].astype(F32) + a_own[...].astype(F32)
    c5.wait_recv()
    out[:, b] = part[of(z), b].astype(F32) + b2[...].astype(F32) + b_own[...].astype(F32)
    for copy in (c0, c1, c2, c3, c4, c5):
        copy.wait_send()


def row_sum(part, collective_id):
    rows, cols = part.shape[0] // 4, part.shape[1]
    piece = pltpu.VMEM((rows, cols // 2), BF)
    return pl.pallas_call(
        row_sum_kernel,
        out_shape=jax.ShapeDtypeStruct((rows, cols), F32),
        in_specs=[VMEM],
        out_specs=VMEM,
        scratch_shapes=[piece] * 8 + [pltpu.SemaphoreType.DMA((6,)), pltpu.SemaphoreType.DMA((6,))],
        name=f"row_sum_{collective_id}",
        compiler_params=params(collective_id, 32),
    )(part)


def row_gather_kernel(own, out, landing, send, recv):
    z, n = lax.axis_index("tensor"), 4
    rows = own.shape[0]
    half = rows // 2
    right, left, far = lax.rem(z + 1, n), lax.rem(z + 3, n), lax.rem(z + 2, n)
    to_right, to_left = {"tensor": right}, {"tensor": left}
    meet((to_left, to_right))

    def of(q):
        return pl.ds(pl.multiple_of(q * rows, 16), rows)

    def part_of(q, h):
        return pl.ds(pl.multiple_of(q * rows + half * h, 16), half)

    def copy(h, slot, device):
        return remote(own.at[pl.ds(half * h, half)], landing.at[part_of(z, h)], send.at[slot], recv.at[slot], device)

    r0, l1, r1, l0 = copy(0, 0, to_right), copy(1, 1, to_left), copy(1, 2, to_right), copy(0, 3, to_left)
    for c in (r0, l1, r1, l0):
        c.start()
    r0.wait_recv()
    f0 = remote(landing.at[part_of(left, 0)], landing.at[part_of(left, 0)], send.at[4], recv.at[4], to_right)
    f0.start()
    l1.wait_recv()
    f1 = remote(landing.at[part_of(right, 1)], landing.at[part_of(right, 1)], send.at[5], recv.at[5], to_left)
    f1.start()
    out[of(z)] = own[...]
    r1.wait_recv()
    l0.wait_recv()
    out[of(left)] = landing[of(left)]
    out[of(right)] = landing[of(right)]
    f0.wait_recv()
    f1.wait_recv()
    out[of(far)] = landing[of(far)]
    for c in (r0, l1, r1, l0, f0, f1):
        c.wait_send()


def row_gather(own, collective_id):
    rows, cols = own.shape
    whole = (4 * rows, cols)
    return pl.pallas_call(
        row_gather_kernel,
        out_shape=jax.ShapeDtypeStruct(whole, BF),
        in_specs=[VMEM],
        out_specs=VMEM,
        scratch_shapes=[pltpu.VMEM(whole, BF), pltpu.SemaphoreType.DMA((6,)), pltpu.SemaphoreType.DMA((6,))],
        name=f"row_gather_{collective_id}",
        compiler_params=params(collective_id, 32),
    )(own)


def seq_place(index):
    return {"seq_0": index // 8, "seq_1": lax.rem(index // 2, 4), "seq_2": lax.rem(index, 2)}


def seq_index():
    return lax.axis_index("seq_0") * 8 + lax.axis_index("seq_1") * 2 + lax.axis_index("seq_2")


def spread_kernel(along, x, out, landing, send, recv):
    if along == "tensor":
        n, me = 4, lax.axis_index("tensor")
    else:
        n, me = 32, seq_index()

    def device(k):
        peer = lax.rem(me + k, n)
        return {"tensor": peer} if along == "tensor" else seq_place(peer)

    barrier = pltpu.get_barrier_semaphore()

    def greet(k, carry):
        pl.semaphore_signal(barrier, inc=1, device_id=device(k), device_id_type=MESH_ID)
        return carry

    lax.fori_loop(1, n, greet, 0)
    pl.semaphore_wait(barrier, n - 1)

    def push(k, carry):
        remote(x, landing.at[me], send, recv, device(k)).start()
        return carry

    lax.fori_loop(1, n, push, 0)
    others = landing.at[pl.ds(0, n - 1)]
    pltpu.make_async_copy(others, others, recv).wait()
    landing[me] = x[...]
    out[...] = landing[...]
    pltpu.make_async_copy(others, others, send).wait()


def spread(x, along, collective_id):
    n = 4 if along == "tensor" else 32
    return pl.pallas_call(
        functools.partial(spread_kernel, along),
        out_shape=jax.ShapeDtypeStruct((n, *x.shape), F32),
        in_specs=[VMEM],
        out_specs=VMEM,
        scratch_shapes=[pltpu.VMEM((n, *x.shape), F32), pltpu.SemaphoreType.DMA(()), pltpu.SemaphoreType.DMA(())],
        name=f"spread_{collective_id}",
        compiler_params=params(collective_id, 32),
    )(x)


def mul(a, b):
    return jnp.dot(a.astype(BF), b.astype(BF), preferred_element_type=F32)


def mul_t(a, b):
    return lax.dot_general(a.astype(BF), b.astype(BF), (((0,), (0,)), ((), ())), preferred_element_type=F32)


def ring_places():
    x, y, c = (lax.axis_index(a) for a in SEQ)
    return x, y, c


def ring_gather(buf, me, axis, send, recv, base):
    right, left = lax.rem(me + 1, 4), lax.rem(me + 3, 4)
    to_right, to_left = {axis: right}, {axis: left}

    def piece(q, h):
        return buf.at[q, pl.ds(h, 1)]

    def copy(q, h, slot, device):
        return remote(piece(q, h), piece(q, h), send.at[base + slot], recv.at[base + slot], device)

    r0, l1, r1, l0 = copy(me, 0, 0, to_right), copy(me, 1, 1, to_left), copy(me, 1, 2, to_right), copy(me, 0, 3, to_left)
    for c in (r0, l1, r1, l0):
        c.start()
    r0.wait_recv()
    f0 = copy(left, 0, 4, to_right)
    f0.start()
    l1.wait_recv()
    f1 = copy(right, 1, 5, to_left)
    f1.start()
    for c in (r1, l0, f0, f1):
        c.wait_recv()
    return (r0, l1, r1, l0, f0, f1)


def memory_kernel(eb, b_full, before, after, ys, xs, first_e, got, pair_m, got_m, send, recv):
    x, y, c = ring_places()
    hd = 128
    partner = {"seq_2": 1 - c}
    right_y, left_y = {"seq_1": lax.rem(y + 1, 4)}, {"seq_1": lax.rem(y + 3, 4)}
    right_x, left_x = {"seq_0": lax.rem(x + 1, 4)}, {"seq_0": lax.rem(x + 3, 4)}
    meet((partner, right_y, left_y, right_x, left_x))
    mine, theirs = 2 * c, 2 * (1 - c)
    c0 = remote(eb.at[pl.ds(theirs, 2)], got, send.at[12], recv.at[12], partner)
    c0.start()
    c0.wait_recv()
    firsts = []
    for h in (0, 1):
        here, there = eb[mine + h].astype(F32), got[h].astype(F32)
        first, second = jnp.where(c == 0, here, there), jnp.where(c == 0, there, here)
        firsts.append(first)
        first_e[0, h] = first[:, :hd].astype(BF)
        first_e[1, h] = second[:, :hd].astype(BF)
        ys[y, h] = (first + second - mul(second[:, :hd], first)).astype(BF)
    sent = ring_gather(ys, y, "seq_1", send, recv, 0)
    starts = []
    for h in (0, 1):
        so_far = ys[0, h].astype(F32)
        start = jnp.where(y > 0, so_far, 0.0)
        for k in (1, 2, 3):
            step = ys[k, h].astype(F32)
            so_far = so_far + step - mul(step[:, :hd], so_far)
            if k < 3:
                start = jnp.where(y > k, so_far, start)
        xs[x, h] = so_far.astype(BF)
        starts.append(start)
    sent += ring_gather(xs, x, "seq_0", send, recv, 6)
    for h in (0, 1):
        m = jnp.where(x > 0, xs[0, h][:, hd:].astype(F32), 0.0)
        for k in (1, 2):
            step = xs[k, h].astype(F32)
            m = jnp.where(x > k, m + step[:, hd:] - mul(step[:, :hd], m), m)
        m = m + starts[h][:, hd:] - mul(starts[h][:, :hd], m)
        second = m + firsts[h][:, hd:] - mul(firsts[h][:, :hd], m)
        before[mine + h] = jnp.where(c == 0, m, second)
        pair_m[h] = jnp.where(c == 0, second, m)
    c1 = remote(pair_m, got_m, send.at[13], recv.at[13], partner)
    c1.start()
    c1.wait_recv()
    for h in (0, 1):
        before[theirs + h] = got_m[h]
    for h in range(4):
        m = before[h]
        after[h] = m + b_full[h] - mul(eb[h][:, :hd], m)
    for copy in (c0, *sent, c1):
        copy.wait_send()


def memory_scan(eb, b_full, collective_id):
    square = jax.ShapeDtypeStruct((4, 128, 128), F32)
    slots = jax.ShapeDtypeStruct((4, 2, 128, 256), BF)
    pair = jax.ShapeDtypeStruct((2, 2, 128, 128), BF)
    return pl.pallas_call(
        memory_kernel,
        out_shape=(square, square, slots, slots, pair),
        in_specs=[VMEM] * 2,
        out_specs=(VMEM,) * 5,
        scratch_shapes=[
            pltpu.VMEM((2, 128, 256), BF),
            pltpu.VMEM((2, 128, 128), F32),
            pltpu.VMEM((2, 128, 128), F32),
            pltpu.SemaphoreType.DMA((14,)),
            pltpu.SemaphoreType.DMA((14,)),
        ],
        name="memory_scan",
        compiler_params=params(collective_id, 32),
    )(eb, b_full)


def adjoint_kernel(source, ys, xs, pair_e, adjoint, got, s_y, s_x, pair_l, got_l, send, recv):
    x, y, c = ring_places()
    hd = 128
    partner = {"seq_2": 1 - c}
    right_y, left_y = {"seq_1": lax.rem(y + 1, 4)}, {"seq_1": lax.rem(y + 3, 4)}
    right_x, left_x = {"seq_0": lax.rem(x + 1, 4)}, {"seq_0": lax.rem(x + 3, 4)}
    meet((partner, right_y, left_y, right_x, left_x))
    mine, theirs = 2 * c, 2 * (1 - c)
    c0 = remote(source.at[pl.ds(theirs, 2)], got, send.at[12], recv.at[12], partner)
    c0.start()
    c0.wait_recv()
    seconds = []
    for h in (0, 1):
        here, there = source[mine + h].astype(F32), got[h].astype(F32)
        first, second = jnp.where(c == 0, here, there), jnp.where(c == 0, there, here)
        seconds.append(second)
        s_y[y, h] = (first + second - mul_t(pair_e[0, h], second)).astype(BF)
    sent = ring_gather(s_y, y, "seq_1", send, recv, 0)
    for h in (0, 1):
        so_far = s_y[3, h].astype(F32)
        for k in (2, 1, 0):
            so_far = s_y[k, h].astype(F32) + so_far - mul_t(ys[k, h][:, :hd], so_far)
        s_x[x, h] = so_far.astype(BF)
    sent += ring_gather(s_x, x, "seq_0", send, recv, 6)
    for h in (0, 1):
        lam = jnp.where(x < 3, s_x[3, h].astype(F32), 0.0)
        for k in (2, 1):
            lam = jnp.where(x < k, s_x[k, h].astype(F32) + lam - mul_t(xs[k, h][:, :hd], lam), lam)
        for k in (3, 2, 1):
            lam = jnp.where(y < k, s_y[k, h].astype(F32) + lam - mul_t(ys[k, h][:, :hd], lam), lam)
        first = lam + seconds[h] - mul_t(pair_e[1, h], lam)
        adjoint[mine + h] = jnp.where(c == 0, first, lam)
        pair_l[h] = jnp.where(c == 0, lam, first)
    c1 = remote(pair_l, got_l, send.at[13], recv.at[13], partner)
    c1.start()
    c1.wait_recv()
    for h in (0, 1):
        adjoint[theirs + h] = got_l[h]
    for copy in (c0, *sent, c1):
        copy.wait_send()


def adjoint_scan(source, ys, xs, pair_e, collective_id):
    return pl.pallas_call(
        adjoint_kernel,
        out_shape=jax.ShapeDtypeStruct((4, 128, 128), F32),
        in_specs=[VMEM] * 4,
        out_specs=VMEM,
        scratch_shapes=[
            pltpu.VMEM((2, 128, 128), BF),
            pltpu.VMEM((4, 2, 128, 128), BF),
            pltpu.VMEM((4, 2, 128, 128), BF),
            pltpu.VMEM((2, 128, 128), F32),
            pltpu.VMEM((2, 128, 128), F32),
            pltpu.SemaphoreType.DMA((14,)),
            pltpu.SemaphoreType.DMA((14,)),
        ],
        name="adjoint_scan",
        compiler_params=params(collective_id, 32),
    )(source, ys, xs, pair_e)


def rows_by_rows(a, b):
    return lax.dot_general(a, b, (((1,), (1,)), ((), ())), preferred_element_type=F32)


def mlp_kernel(
    normed, grad_out, w_gate, w_up, w_down, back, forth, grads, normed_t, grad_out_t, back_sum, forth_sum, grad_gate, grad_up
):
    step, kind = pl.program_id(0), pl.program_id(1)

    @pl.when((step == 0) & (kind == 0))
    def _():
        normed_t[...] = normed[...].T
        grad_out_t[...] = grad_out[...].T
        back_sum[...] = jnp.zeros_like(back_sum)
        forth_sum[...] = jnp.zeros_like(forth_sum)

    @pl.when(kind == 0)
    def _():
        gate_pre = jnp.dot(normed[...], w_gate[...], preferred_element_type=F32)
        up_pre = jnp.dot(normed[...], w_up[...], preferred_element_type=F32)
        grad_hidden = jnp.dot(grad_out[...], w_down[...], preferred_element_type=F32)
        sig = jax.nn.sigmoid(gate_pre)
        swish = gate_pre * sig
        hidden = (swish * up_pre).astype(BF)
        grad_up[...] = (grad_hidden * swish).astype(BF)
        grad_gate[...] = (grad_hidden * up_pre * sig * (1.0 + gate_pre * (1.0 - sig))).astype(BF)
        forth_sum[...] += rows_by_rows(hidden, w_down[...])
        grads[...] = jnp.dot(grad_out_t[...], hidden, preferred_element_type=F32).astype(BF)

    @pl.when(kind == 1)
    def _():
        back_sum[...] += rows_by_rows(grad_gate[...], w_gate[...])
        grads[...] = jnp.dot(normed_t[...], grad_gate[...], preferred_element_type=F32).astype(BF)

    @pl.when(kind == 2)
    def _():
        back_sum[...] += rows_by_rows(grad_up[...], w_up[...])
        grads[...] = jnp.dot(normed_t[...], grad_up[...], preferred_element_type=F32).astype(BF)

    @pl.when((step == pl.num_programs(0) - 1) & (kind == 2))
    def _():
        back[...] = back_sum[...].astype(BF)
        forth[...] = forth_sum[...].astype(BF)


MLP_TILE = 512


def mlp(normed, grad_out, w_gate, w_up, w_down):
    rows, width = normed.shape
    units = w_gate.shape[1]
    steps = units // MLP_TILE
    whole = pl.BlockSpec((rows, width), lambda f, k: (0, 0))
    weight = pl.BlockSpec((width, MLP_TILE), lambda f, k: (0, f))
    low = jax.ShapeDtypeStruct((rows, width), BF)
    return pl.pallas_call(
        mlp_kernel,
        grid=(steps, 3),
        out_shape=(low, low, jax.ShapeDtypeStruct((width, 3 * units), BF)),
        in_specs=[whole, whole, weight, weight, weight],
        out_specs=(whole, whole, pl.BlockSpec((width, MLP_TILE), lambda f, k: (0, k * steps + f))),
        scratch_shapes=[
            pltpu.VMEM((width, rows), BF),
            pltpu.VMEM((width, rows), BF),
            pltpu.VMEM((rows, width), F32),
            pltpu.VMEM((rows, width), F32),
            pltpu.VMEM((rows, MLP_TILE), BF),
            pltpu.VMEM((rows, MLP_TILE), BF),
        ],
        name="mlp",
        compiler_params=pltpu.CompilerParams(vmem_limit_bytes=56 << 20),
        cost_estimate=pl.CostEstimate(
            flops=18 * rows * width * units, bytes_accessed=12 * width * units, transcendentals=rows * units
        ),
    )(normed, grad_out, w_gate, w_up, w_down)


class RingSum:
    def __init__(self, src, bufs, send, recv, base, axis):
        self.src, self.bufs, self.me = src, bufs, lax.axis_index(axis)
        half = src.shape[2] // 2
        self.a, self.b = pl.ds(0, half), pl.ds(half, half)
        self.right, self.left = lax.rem(self.me + 1, 4), lax.rem(self.me + 3, 4)
        far = lax.rem(self.me + 2, 4)
        to_right, to_left = {axis: self.right}, {axis: self.left}

        def copy(piece, landing, slot, device):
            return remote(piece, bufs.at[landing], send.at[base + slot], recv.at[base + slot], device)

        rows = pl.ds(0, src.shape[1])
        self.c0 = copy(src.at[far, rows, self.a], 0, 0, to_right)
        self.c1 = copy(src.at[far, rows, self.b], 1, 1, to_left)
        self.c2 = copy(src.at[self.right, rows, self.b], 2, 2, to_right)
        self.c3 = copy(src.at[self.left, rows, self.a], 3, 3, to_left)
        self.c4 = copy(bufs.at[6], 4, 4, to_right)
        self.c5 = copy(bufs.at[7], 5, 5, to_left)

    def start_a(self):
        self.c0.start()
        self.c3.start()

    def start_b(self):
        self.c1.start()
        self.c2.start()

    def start(self):
        self.c0.start()
        self.c1.start()
        self.c3.start()
        self.c2.start()

    def middle(self):
        src, bufs = self.src, self.bufs
        self.c0.wait_recv()
        bufs[6] = (bufs[0].astype(F32) + src[self.right, :, self.a].astype(F32)).astype(BF)
        self.c4.start()
        self.c1.wait_recv()
        bufs[7] = (bufs[1].astype(F32) + src[self.left, :, self.b].astype(F32)).astype(BF)
        self.c5.start()

    def finish(self, put):
        src, bufs = self.src, self.bufs
        self.c3.wait_recv()
        self.c4.wait_recv()
        put(self.a, src[self.me, :, self.a].astype(F32) + bufs[4].astype(F32) + bufs[3].astype(F32))
        self.c2.wait_recv()
        self.c5.wait_recv()
        put(self.b, src[self.me, :, self.b].astype(F32) + bufs[5].astype(F32) + bufs[2].astype(F32))

    def drain(self):
        for copy in (self.c0, self.c1, self.c2, self.c3, self.c4, self.c5):
            copy.wait_send()


class RingGather:
    def __init__(self, buf, send, recv, base, axis):
        self.me = lax.axis_index(axis)
        half = buf.shape[1] // 2
        right, left = lax.rem(self.me + 1, 4), lax.rem(self.me + 3, 4)
        to_right, to_left = {axis: right}, {axis: left}

        def copy(q, h, slot, device):
            piece = buf.at[q, pl.ds(half * h, half)]
            return remote(piece, piece, send.at[base + slot], recv.at[base + slot], device)

        self.r0, self.l1 = copy(self.me, 0, 0, to_right), copy(self.me, 1, 1, to_left)
        self.r1, self.l0 = copy(self.me, 1, 2, to_right), copy(self.me, 0, 3, to_left)
        self.f0, self.f1 = copy(left, 0, 4, to_right), copy(right, 1, 5, to_left)

    def start(self):
        for copy in (self.r0, self.l1, self.r1, self.l0):
            copy.start()

    def middle(self):
        self.r0.wait_recv()
        self.f0.start()
        self.l1.wait_recv()
        self.f1.start()

    def finish(self):
        for copy in (self.r1, self.l0, self.f0, self.f1):
            copy.wait_recv()

    def drain(self):
        for copy in (self.r0, self.l1, self.r1, self.l0, self.f0, self.f1):
            copy.wait_send()


class SeqSum:
    def __init__(self, product, got, first, first_bufs, second, second_bufs, send, recv, base, x_first):
        self.product, self.got, self.first, self.second, self.x_first = product, got, first, second, x_first
        self.core = lax.axis_index("seq_2")
        self.swap = remote(
            product.at[pl.ds(0, 16), 1 - self.core], got, send.at[base], recv.at[base], {"seq_2": 1 - self.core}
        )
        axes = ("seq_0", "seq_1") if x_first else ("seq_1", "seq_0")
        self.one = RingSum(first, first_bufs, send, recv, base + 1, axes[0])
        self.two = RingSum(second, second_bufs, send, recv, base + 7, axes[1])

    def start(self):
        self.swap.start()

    def first_ring(self):
        self.swap.wait_recv()
        for x in range(4):
            for y in range(4):
                at = 4 * x + y
                q, r = (x, y) if self.x_first else (y, x)
                total = self.product[at, self.core].astype(F32) + self.got[at].astype(F32)
                self.first[q, pl.ds(64 * r, 64)] = total.astype(BF)
        self.one.start()

    def second_ring(self):
        def put(cols, value):
            for r in range(4):
                self.second[r, :, cols] = value[64 * r : 64 * (r + 1)].astype(BF)

        self.one.finish(put)
        self.two.start()

    def finish(self, out):
        def put(cols, value):
            out[:, cols] = value

        self.two.finish(put)

    def drain(self):
        self.swap.wait_send()
        self.one.drain()
        self.two.drain()


def greet_all():
    barrier = pltpu.get_barrier_semaphore()
    me, z = seq_index(), lax.axis_index("tensor")

    def greet_seq(k, carry):
        pl.semaphore_signal(barrier, inc=1, device_id=seq_place(lax.rem(me + k, 32)), device_id_type=MESH_ID)
        return carry

    lax.fori_loop(1, 32, greet_seq, 0)
    for k in (1, 2, 3):
        pl.semaphore_signal(barrier, inc=1, device_id={"tensor": lax.rem(z + k, 4)}, device_id_type=MESH_ID)


def all_greeted():
    pl.semaphore_wait(pltpu.get_barrier_semaphore(), 34)


class TotalOfAll:
    def __init__(self, mine, extra, by_z, line, by_seq, total, send, recv, base):
        self.mine, self.extra, self.by_z, self.line, self.by_seq, self.total = mine, extra, by_z, line, by_seq, total
        self.z, self.me = lax.axis_index("tensor"), seq_index()
        self.send, self.recv, self.base = send, recv, base
        peers = [lax.rem(self.z + k, 4) for k in (1, 2, 3)]
        self.split = [
            remote(mine.at[p], by_z.at[self.z], send.at[base + k], recv.at[base + k], {"tensor": p})
            for k, p in enumerate(peers)
        ]
        self.join = [
            remote(total.at[self.z], total.at[self.z], send.at[base + 3 + k], recv.at[base + 3 + k], {"tensor": p})
            for k, p in enumerate(peers)
        ]

    def start(self):
        for copy in self.split:
            copy.start()

    def over_seq(self):
        self.by_z[self.z] = self.mine[self.z]
        for copy in self.split:
            copy.wait_recv()
        self.line[0:8] = (self.by_z[0] + self.by_z[1]) + (self.by_z[2] + self.by_z[3])
        self.line[8:16] = self.extra[...]
        self.by_seq[self.me] = self.line[...]

        def push(k, carry):
            device = seq_place(lax.rem(self.me + k, 32))
            remote(self.line, self.by_seq.at[self.me], self.send.at[self.base + 6], self.recv.at[self.base + 6], device).start()
            return carry

        lax.fori_loop(1, 32, push, 0)

    def over_tensor(self, extra_out):
        others = self.by_seq.at[pl.ds(0, 31)]
        pltpu.make_async_copy(others, others, self.recv.at[self.base + 6]).wait()
        summed = jnp.sum(self.by_seq[...], axis=0)
        self.total[self.z] = summed[0:8]
        extra_out[...] = summed[8:16]
        for copy in self.join:
            copy.start()

    def finish(self):
        for copy in self.join:
            copy.wait_recv()

    def drain(self):
        for copy in (*self.split, *self.join):
            copy.wait_send()
        others = self.by_seq.at[pl.ds(0, 31)]
        pltpu.make_async_copy(others, others, self.send.at[self.base + 6]).wait()


def end_kernel(
    grads_in,
    normed,
    branch,
    mix,
    w_query,
    w_key,
    w_value,
    tokens_own,
    grad_middle,
    gain,
    gain_mlp_grad,
    logits,
    grad_tokens,
    out_query,
    out_key,
    out_value,
    out_output,
    gains,
    logits_out,
    weights,
    turned,
    part,
    part_bufs,
    grad_own,
    products,
    got,
    first,
    first_bufs,
    second,
    second_bufs,
    mine,
    by_z,
    line,
    by_seq,
    load,
    send,
    recv,
):
    loads = [
        pltpu.make_async_copy(w, weights.at[i], load.at[i]) for i, w in enumerate((w_query, w_key, w_value))
    ]
    for copy in loads:
        copy.start()
    greet_all()
    z = lax.axis_index("tensor")
    z_sum = RingSum(part, part_bufs, send, recv, 0, "tensor")
    z_gather = RingGather(grad_tokens, send, recv, 6, "tensor")
    sums = [
        SeqSum(
            products.at[i], got.at[i], first.at[i], first_bufs.at[i], second.at[i], second_bufs.at[i],
            send, recv, 12 + 13 * i, i % 2 == 0,
        )
        for i in range(4)
    ]
    total = TotalOfAll(mine, logits, by_z, line, by_seq, gains, send, recv, 64)

    def product(i, left, right):
        value = jnp.dot(left, right, preferred_element_type=F32).astype(BF)
        products[i] = value.reshape(16, 2, 64, 512)

    turned[...] = branch[...].T
    product(0, turned[...], mix[...])
    all_greeted()
    sums[0].start()
    for copy in loads:
        copy.wait()
    for half in (0, 1):
        rows = pl.ds(1024 * half, 1024)
        value = sum(rows_by_rows(grads_in[:, 512 * i : 512 * (i + 1)], weights[i, rows]) for i in range(3))
        part[:, :, rows] = value.astype(BF).reshape(4, 96, 1024)
        (z_sum.start_a, z_sum.start_b)[half]()
    turned[...] = normed[...].T
    product(1, turned[...], grads_in[:, 0:512])
    sums[1].start()
    sums[0].first_ring()
    product(2, turned[...], grads_in[:, 512:1024])
    sums[2].start()
    z_sum.middle()
    sums[1].first_ring()
    product(3, turned[...], grads_in[:, 1024:1536])
    sums[3].start()
    sums[2].first_ring()

    def keep(cols, value):
        grad_own[:, cols] = value

    sums[0].one.middle()
    z_sum.finish(keep)
    stream = tokens_own[...].astype(F32)
    inv = lax.rsqrt(jnp.mean(stream * stream, axis=1, keepdims=True) + epsilon)
    grad_normed = grad_own[...]
    weighted = grad_normed * gain[...]
    inner = jnp.sum(weighted * stream, axis=1, keepdims=True)
    scaled = stream * inv
    result = grad_middle[...] + inv * weighted - scaled * (inv * inv * inner * (1.0 / stream.shape[1]))
    grad_tokens[z] = result.astype(BF)
    z_gather.start()
    gain_grad = jnp.sum(grad_normed * scaled, axis=0, keepdims=True)
    for r in range(16):
        mine[r // 8, r % 8 : r % 8 + 1] = gain_grad[:, 128 * r : 128 * (r + 1)]
    mine[2:4] = gain_mlp_grad[...]
    total.start()
    sums[1].one.middle()
    sums[3].first_ring()
    sums[0].second_ring()
    total.over_seq()
    sums[2].one.middle()
    sums[1].second_ring()
    sums[0].two.middle()
    z_gather.middle()
    sums[3].one.middle()
    sums[2].second_ring()
    sums[1].two.middle()
    total.over_tensor(logits_out)
    sums[0].finish(out_output)
    sums[3].second_ring()
    sums[2].two.middle()
    sums[1].finish(out_query)
    sums[3].two.middle()
    sums[2].finish(out_key)
    sums[3].finish(out_value)
    total.finish()
    z_gather.finish()
    z_sum.drain()
    z_gather.drain()
    for s in sums:
        s.drain()
    total.drain()


def end(grads_in, normed, branch, mix, w_query, w_key, w_value, tokens_own, grad_middle, gain, gain_mlp_grad, logits, cid):
    shape = jax.ShapeDtypeStruct
    weight_grad = shape((64, 512), F32)
    low = lambda *dims: pltpu.VMEM(dims, BF)
    full = lambda *dims: pltpu.VMEM(dims, F32)
    anywhere = pl.BlockSpec(memory_space=pl.ANY)
    return pl.pallas_call(
        end_kernel,
        out_shape=(shape((4, 96, 2048), BF),) + (weight_grad,) * 4 + (shape((4, 8, 128), F32), shape((8, 128), F32)),
        in_specs=[VMEM] * 4 + [anywhere] * 3 + [VMEM] * 5,
        out_specs=(VMEM,) * 7,
        scratch_shapes=[
            low(3, 2048, 512),
            low(2048, 384),
            low(4, 96, 2048),
            low(8, 96, 1024),
            full(96, 2048),
            low(4, 16, 2, 64, 512),
            low(4, 16, 64, 512),
            low(4, 4, 256, 512),
            low(4, 8, 256, 256),
            low(4, 4, 64, 512),
            low(4, 8, 64, 256),
            full(4, 8, 128),
            full(4, 8, 128),
            full(16, 128),
            full(32, 16, 128),
            pltpu.SemaphoreType.DMA((3,)),
            pltpu.SemaphoreType.DMA((71,)),
            pltpu.SemaphoreType.DMA((71,)),
        ],
        name="end",
        compiler_params=params(cid, 56),
    )(grads_in, normed, branch, mix, w_query, w_key, w_value, tokens_own, grad_middle, gain, gain_mlp_grad, logits)


def feature(values):
    return jax.nn.elu(values) + 1.0


def feature_slope(values):
    return jnp.where(values > 0, 1.0, jnp.exp(jnp.minimum(values, 0.0)))


def norm_back(stream, inv_rms, gain_vec, grad_normed):
    weighted = grad_normed * gain_vec
    inner_sum = jnp.sum(weighted * stream, axis=1, keepdims=True)
    return inv_rms * weighted - stream * inv_rms**3 * inner_sum / stream.shape[1]


def heads_dot(spec, a, b):
    return jnp.einsum(spec, a.astype(BF), b.astype(BF), preferred_element_type=F32)


def on_device(
    tokens,
    cotangent,
    w_query,
    w_key,
    w_value,
    w_output,
    w_gate,
    w_up,
    w_down,
    gain_attn,
    gain_mlp,
    gate_logit,
    valid_count,
):
    seg_len = tokens.shape[0]
    head_count = gate_logit.shape[0]
    col_count = w_query.shape[1]
    head_dim = col_count // head_count
    scale_dot = head_dim ** (-0.5)
    here = seq_index()
    z = lax.axis_index("tensor")
    own_rows = seg_len // 4
    position = lax.iota(jnp.int32, seg_len)
    valid_len = jnp.where(here == 31, valid_count[0], seg_len)
    keep_mask = (position < valid_len).astype(F32)
    allowed = (position[:, None] >= position[None, :]) & (keep_mask[None, :] > 0)
    stream = tokens.astype(F32)
    inv_one = lax.rsqrt(jnp.mean(stream * stream, axis=1, keepdims=True) + epsilon)
    normed = (stream * inv_one * gain_attn).astype(BF)
    queries = jnp.dot(normed, w_query, preferred_element_type=F32).astype(BF)
    key_rows = jnp.dot(normed, w_key, preferred_element_type=F32).astype(BF)
    values = jnp.dot(normed, w_value, preferred_element_type=F32).astype(BF)
    heads_shape = (seg_len, head_count, head_dim)
    q_heads = queries.reshape(heads_shape)
    k_heads = key_rows.reshape(heads_shape)
    v_heads = values.reshape(heads_shape)
    q_float = q_heads.astype(F32)
    k_float = k_heads.astype(F32)
    v_float = v_heads.astype(F32)
    feat_query = feature(q_float)
    feat_key = feature(k_float)
    kept_key = feat_key * keep_mask[:, None, None]
    key_sum = jnp.sum(kept_key, axis=0)
    key_sums = spread(key_sum, "seq", 0)
    earlier = (jnp.arange(32) < here)[:, None, None]
    normal_prev = jnp.sum(jnp.where(earlier, key_sums, 0.0), axis=0)
    normal_next = normal_prev + key_sum
    scores = jnp.einsum("qhd,khd->hqk", q_heads, k_heads, preferred_element_type=F32) * scale_dot
    masked = jnp.where(allowed[None], scores, -1e30)
    row_top = jnp.max(masked, axis=2, keepdims=True)
    exp_scores = jnp.exp(masked - row_top)
    attn_again = exp_scores / jnp.sum(exp_scores, axis=2, keepdims=True)
    attn_low = attn_again.astype(BF)
    local_out = jnp.einsum("hqk,khd->qhd", attn_low, v_heads, preferred_element_type=F32)
    offset = normal_prev + seg_len
    den_key = jnp.sum(feat_key * offset, axis=2)
    den_query = jnp.sum(feat_query * offset, axis=2)
    taken = heads_dot("shd,she->hde", kept_key / den_key[:, :, None], feat_key)
    source = heads_dot("shd,she->hde", kept_key, v_heads)
    eb = jnp.concatenate((taken, source), axis=2).astype(BF)
    memory_prev, memory_next, ys, xs, pair_e = memory_scan(eb, source, 1)
    retrieved = heads_dot("shd,hde->she", feat_query, memory_prev) / den_query[:, :, None]
    gate_mix = jax.nn.sigmoid(gate_logit)[:, None]
    mixture = gate_mix * retrieved + (1.0 - gate_mix) * local_out
    mix_low = mixture.reshape(seg_len, col_count).astype(BF)
    attn_part = jnp.einsum("sc,dc->sd", mix_low, w_output, preferred_element_type=F32).astype(BF)
    own = lambda a: lax.dynamic_slice_in_dim(a, z * own_rows, own_rows, 0)
    middle = own(tokens).astype(F32) + row_sum(attn_part, 2)
    inv_two = lax.rsqrt(jnp.mean(middle * middle, axis=1, keepdims=True) + epsilon)
    normed_two = row_gather((middle * inv_two * gain_mlp).astype(BF), 3)
    grad_out = jnp.where(keep_mask[:, None] > 0, cotangent, jnp.zeros_like(cotangent))
    back_part, forth_part, mlp_grads = mlp(normed_two, grad_out, w_gate, w_up, w_down)
    mlp_grads = lax.psum_scatter(mlp_grads, SEQ, scatter_dimension=0, tiled=True)
    grad_normed_two = row_sum(back_part, 4)
    grad_middle = own(grad_out).astype(F32) + norm_back(middle, inv_two, gain_mlp, grad_normed_two)
    gain_mlp_grad = jnp.sum(grad_normed_two * middle * inv_two, axis=0)
    grad_branch = row_gather(grad_middle.astype(BF), 5)
    grad_mix = jnp.einsum("sd,dc->sc", grad_branch, w_output, preferred_element_type=F32).reshape(heads_shape)
    logit_grad = (
        jnp.sum(grad_mix * (retrieved - local_out), axis=(0, 2)) * gate_mix[:, 0] * (1.0 - gate_mix[:, 0])
    )
    grad_retrieved = gate_mix * grad_mix
    grad_point = grad_retrieved / den_query[:, :, None]
    mem_source = heads_dot("shd,she->hde", feat_query, grad_point)
    adjoint = adjoint_scan(mem_source.astype(BF), ys, xs, pair_e, 6)
    grad_local = ((1.0 - gate_mix) * grad_mix).astype(BF)
    grad_probs = jnp.einsum("qhd,khd->hqk", grad_local, v_heads, preferred_element_type=F32)
    grad_value = jnp.einsum("hqk,qhd->khd", attn_low, grad_local, preferred_element_type=F32)
    grad_scores = (
        attn_again * (grad_probs - jnp.sum(grad_probs * attn_again, axis=2, keepdims=True))
    ).astype(BF)
    grad_query = jnp.einsum("hqk,khd->qhd", grad_scores, k_heads, preferred_element_type=F32) * scale_dot
    grad_key = jnp.einsum("hqk,qhd->khd", grad_scores, q_heads, preferred_element_type=F32) * scale_dot
    recall = heads_dot("shd,hde->she", feat_key, memory_prev) / den_key[:, :, None]
    update = v_float - recall
    grad_update = heads_dot("shd,hde->she", kept_key, adjoint)
    grad_den_key = jnp.sum(grad_update * recall, axis=2) / den_key
    grad_den_query = -jnp.sum(grad_retrieved * retrieved, axis=2) / den_query
    grad_offset = jnp.sum(
        grad_den_key[:, :, None] * feat_key + grad_den_query[:, :, None] * feat_query, axis=0
    )
    grad_offsets = spread(grad_offset, "seq", 7)
    later = (jnp.arange(32) > here)[:, None, None]
    later_offset = jnp.sum(jnp.where(later, grad_offsets, 0.0), axis=0)
    grad_kept = heads_dot("she,hde->shd", update, adjoint)
    grad_feat_key = (
        -heads_dot("she,hde->shd", grad_update / den_key[:, :, None], memory_prev)
        + grad_den_key[:, :, None] * offset[None]
        + keep_mask[:, None, None] * (grad_kept + later_offset[None])
    )
    grad_feat_query = (
        heads_dot("she,hde->shd", grad_point, memory_prev) + grad_den_query[:, :, None] * offset[None]
    )
    flat = (seg_len, col_count)
    grad_q_low = (grad_query + grad_feat_query * feature_slope(q_float)).reshape(flat).astype(BF)
    grad_k_low = (grad_key + grad_feat_key * feature_slope(k_float)).reshape(flat).astype(BF)
    grad_v_low = (grad_value + grad_update).reshape(flat).astype(BF)
    layer_out = row_gather((middle + row_sum(forth_part, 10)).astype(BF), 11)
    grad_tokens, grad_query, grad_key, grad_value, grad_output, gains, logit_grad = end(
        jnp.concatenate((grad_q_low, grad_k_low, grad_v_low), axis=1),
        normed,
        grad_branch,
        mix_low,
        w_query,
        w_key,
        w_value,
        own(tokens),
        grad_middle,
        gain_attn[None],
        gain_mlp_grad.reshape(2, 8, 128),
        jnp.pad(logit_grad[None], ((0, 7), (0, 124))),
        8,
    )
    gains = gains.reshape(-1)
    units = w_gate.shape[1]
    of_mlp = lambda k: mlp_grads[:, units * k : units * (k + 1)].astype(F32)
    return (
        layer_out,
        grad_tokens.reshape(tokens.shape).astype(F32),
        grad_query,
        grad_key,
        grad_value,
        grad_output,
        of_mlp(1),
        of_mlp(2),
        of_mlp(0),
        gains[:2048],
        gains[2048:],
        logit_grad[0, :4],
        memory_next[None],
        normal_next[None],
        later_offset[None],
    )


def solution(mesh):
    torus = Mesh(
        mesh.devices.reshape(4, 4, 2, mesh.shape["tensor"]), ("seq_0", "seq_1", "seq_2", "tensor")
    )
    weight = P(None, "tensor")
    grad = P(SEQ, "tensor")
    return jax.shard_map(
        on_device,
        mesh=torus,
        in_specs=(P(SEQ, None), P(SEQ, None)) + (weight,) * 7 + (P(), P(), P("tensor"), P()),
        out_specs=(P(SEQ, None), P(SEQ, None))
        + (grad,) * 7
        + (P(), P(), P("tensor"), P(SEQ, "tensor", None, None), P(SEQ, "tensor", None), P(SEQ, "tensor", None)),
        check_vma=False,
    )
```

```python
import functools

import jax
import jax.numpy as jnp
from jax import lax
from jax.experimental import pallas as pl
from jax.experimental.pallas import tpu as pltpu
from jax.sharding import Mesh
from jax.sharding import PartitionSpec as P

SEQ = ("seq_0", "seq_1", "seq_2")
MESH_ID = pl.DeviceIdType.MESH
VMEM = pl.BlockSpec(memory_space=pltpu.VMEM)
BF = jnp.bfloat16
F32 = jnp.float32

epsilon = 1e-06


def remote(src, dst, send, recv, device):
    return pltpu.make_async_remote_copy(
        src_ref=src, dst_ref=dst, send_sem=send, recv_sem=recv, device_id=device, device_id_type=MESH_ID
    )


def meet(devices):
    barrier = pltpu.get_barrier_semaphore()
    for device in devices:
        pl.semaphore_signal(barrier, inc=1, device_id=device, device_id_type=MESH_ID)
    pl.semaphore_wait(barrier, len(devices))


def params(collective_id, mib):
    return pltpu.CompilerParams(
        collective_id=collective_id, has_side_effects=True, vmem_limit_bytes=mib << 20
    )


def row_sum_kernel(part, out, a1, b1, a2, b2, a_own, b_own, sum_a, sum_b, send, recv):
    z, n = lax.axis_index("tensor"), 4
    rows = part.shape[0] // n
    half = part.shape[1] // 2
    right, left, far = lax.rem(z + 1, n), lax.rem(z + 3, n), lax.rem(z + 2, n)
    to_right, to_left = {"tensor": right}, {"tensor": left}
    meet((to_left, to_right))

    def of(q):
        return pl.ds(pl.multiple_of(q * rows, 16), rows)

    a, b = pl.ds(0, half), pl.ds(half, half)
    c0 = remote(part.at[of(far), a], a1, send.at[0], recv.at[0], to_right)
    c1 = remote(part.at[of(far), b], b1, send.at[1], recv.at[1], to_left)
    c2 = remote(part.at[of(right), b], b_own, send.at[2], recv.at[2], to_right)
    c3 = remote(part.at[of(left), a], a_own, send.at[3], recv.at[3], to_left)
    for copy in (c0, c1, c2, c3):
        copy.start()
    c0.wait_recv()
    sum_a[...] = (a1[...].astype(F32) + part[of(right), a].astype(F32)).astype(BF)
    c4 = remote(sum_a, a2, send.at[4], recv.at[4], to_right)
    c4.start()
    c1.wait_recv()
    sum_b[...] = (b1[...].astype(F32) + part[of(left), b].astype(F32)).astype(BF)
    c5 = remote(sum_b, b2, send.at[5], recv.at[5], to_left)
    c5.start()
    c2.wait_recv()
    c3.wait_recv()
    c4.wait_recv()
    out[:, a] = part[of(z), a].astype(F32) + a2[...].astype(F32) + a_own[...].astype(F32)
    c5.wait_recv()
    out[:, b] = part[of(z), b].astype(F32) + b2[...].astype(F32) + b_own[...].astype(F32)
    for copy in (c0, c1, c2, c3, c4, c5):
        copy.wait_send()


def row_sum(part, collective_id):
    rows, cols = part.shape[0] // 4, part.shape[1]
    piece = pltpu.VMEM((rows, cols // 2), BF)
    return pl.pallas_call(
        row_sum_kernel,
        out_shape=jax.ShapeDtypeStruct((rows, cols), F32),
        in_specs=[VMEM],
        out_specs=VMEM,
        scratch_shapes=[piece] * 8 + [pltpu.SemaphoreType.DMA((6,)), pltpu.SemaphoreType.DMA((6,))],
        name=f"row_sum_{collective_id}",
        compiler_params=params(collective_id, 32),
    )(part)


def row_gather_kernel(own, out, landing, send, recv):
    z, n = lax.axis_index("tensor"), 4
    rows = own.shape[0]
    half = rows // 2
    right, left, far = lax.rem(z + 1, n), lax.rem(z + 3, n), lax.rem(z + 2, n)
    to_right, to_left = {"tensor": right}, {"tensor": left}
    meet((to_left, to_right))

    def of(q):
        return pl.ds(pl.multiple_of(q * rows, 16), rows)

    def part_of(q, h):
        return pl.ds(pl.multiple_of(q * rows + half * h, 16), half)

    def copy(h, slot, device):
        return remote(own.at[pl.ds(half * h, half)], landing.at[part_of(z, h)], send.at[slot], recv.at[slot], device)

    r0, l1, r1, l0 = copy(0, 0, to_right), copy(1, 1, to_left), copy(1, 2, to_right), copy(0, 3, to_left)
    for c in (r0, l1, r1, l0):
        c.start()
    r0.wait_recv()
    f0 = remote(landing.at[part_of(left, 0)], landing.at[part_of(left, 0)], send.at[4], recv.at[4], to_right)
    f0.start()
    l1.wait_recv()
    f1 = remote(landing.at[part_of(right, 1)], landing.at[part_of(right, 1)], send.at[5], recv.at[5], to_left)
    f1.start()
    out[of(z)] = own[...]
    r1.wait_recv()
    l0.wait_recv()
    out[of(left)] = landing[of(left)]
    out[of(right)] = landing[of(right)]
    f0.wait_recv()
    f1.wait_recv()
    out[of(far)] = landing[of(far)]
    for c in (r0, l1, r1, l0, f0, f1):
        c.wait_send()


def row_gather(own, collective_id):
    rows, cols = own.shape
    whole = (4 * rows, cols)
    return pl.pallas_call(
        row_gather_kernel,
        out_shape=jax.ShapeDtypeStruct(whole, BF),
        in_specs=[VMEM],
        out_specs=VMEM,
        scratch_shapes=[pltpu.VMEM(whole, BF), pltpu.SemaphoreType.DMA((6,)), pltpu.SemaphoreType.DMA((6,))],
        name=f"row_gather_{collective_id}",
        compiler_params=params(collective_id, 32),
    )(own)


def seq_place(index):
    return {"seq_0": index // 8, "seq_1": lax.rem(index // 2, 4), "seq_2": lax.rem(index, 2)}


def seq_index():
    return lax.axis_index("seq_0") * 8 + lax.axis_index("seq_1") * 2 + lax.axis_index("seq_2")


def spread_kernel(along, x, out, landing, send, recv):
    if along == "tensor":
        n, me = 4, lax.axis_index("tensor")
    else:
        n, me = 32, seq_index()

    def device(k):
        peer = lax.rem(me + k, n)
        return {"tensor": peer} if along == "tensor" else seq_place(peer)

    barrier = pltpu.get_barrier_semaphore()

    def greet(k, carry):
        pl.semaphore_signal(barrier, inc=1, device_id=device(k), device_id_type=MESH_ID)
        return carry

    lax.fori_loop(1, n, greet, 0)
    pl.semaphore_wait(barrier, n - 1)

    def push(k, carry):
        remote(x, landing.at[me], send, recv, device(k)).start()
        return carry

    lax.fori_loop(1, n, push, 0)
    others = landing.at[pl.ds(0, n - 1)]
    pltpu.make_async_copy(others, others, recv).wait()
    landing[me] = x[...]
    out[...] = landing[...]
    pltpu.make_async_copy(others, others, send).wait()


def spread(x, along, collective_id):
    n = 4 if along == "tensor" else 32
    return pl.pallas_call(
        functools.partial(spread_kernel, along),
        out_shape=jax.ShapeDtypeStruct((n, *x.shape), F32),
        in_specs=[VMEM],
        out_specs=VMEM,
        scratch_shapes=[pltpu.VMEM((n, *x.shape), F32), pltpu.SemaphoreType.DMA(()), pltpu.SemaphoreType.DMA(())],
        name=f"spread_{collective_id}",
        compiler_params=params(collective_id, 32),
    )(x)


def mul(a, b):
    return jnp.dot(a.astype(BF), b.astype(BF), preferred_element_type=F32)


def mul_t(a, b):
    return lax.dot_general(a.astype(BF), b.astype(BF), (((0,), (0,)), ((), ())), preferred_element_type=F32)


def ring_places():
    x, y, c = (lax.axis_index(a) for a in SEQ)
    return x, y, c


def ring_gather(buf, me, axis, send, recv, base):
    right, left = lax.rem(me + 1, 4), lax.rem(me + 3, 4)
    to_right, to_left = {axis: right}, {axis: left}

    def piece(q, h):
        return buf.at[q, pl.ds(h, 1)]

    def copy(q, h, slot, device):
        return remote(piece(q, h), piece(q, h), send.at[base + slot], recv.at[base + slot], device)

    r0, l1, r1, l0 = copy(me, 0, 0, to_right), copy(me, 1, 1, to_left), copy(me, 1, 2, to_right), copy(me, 0, 3, to_left)
    for c in (r0, l1, r1, l0):
        c.start()
    r0.wait_recv()
    f0 = copy(left, 0, 4, to_right)
    f0.start()
    l1.wait_recv()
    f1 = copy(right, 1, 5, to_left)
    f1.start()
    for c in (r1, l0, f0, f1):
        c.wait_recv()
    return (r0, l1, r1, l0, f0, f1)


def memory_kernel(eb, b_full, before, after, ys, xs, first_e, got, pair_m, got_m, send, recv):
    x, y, c = ring_places()
    hd = 128
    partner = {"seq_2": 1 - c}
    right_y, left_y = {"seq_1": lax.rem(y + 1, 4)}, {"seq_1": lax.rem(y + 3, 4)}
    right_x, left_x = {"seq_0": lax.rem(x + 1, 4)}, {"seq_0": lax.rem(x + 3, 4)}
    meet((partner, right_y, left_y, right_x, left_x))
    mine, theirs = 2 * c, 2 * (1 - c)
    c0 = remote(eb.at[pl.ds(theirs, 2)], got, send.at[12], recv.at[12], partner)
    c0.start()
    c0.wait_recv()
    firsts = []
    for h in (0, 1):
        here, there = eb[mine + h].astype(F32), got[h].astype(F32)
        first, second = jnp.where(c == 0, here, there), jnp.where(c == 0, there, here)
        firsts.append(first)
        first_e[0, h] = first[:, :hd].astype(BF)
        first_e[1, h] = second[:, :hd].astype(BF)
        ys[y, h] = (first + second - mul(second[:, :hd], first)).astype(BF)
    sent = ring_gather(ys, y, "seq_1", send, recv, 0)
    starts = []
    for h in (0, 1):
        so_far = ys[0, h].astype(F32)
        start = jnp.where(y > 0, so_far, 0.0)
        for k in (1, 2, 3):
            step = ys[k, h].astype(F32)
            so_far = so_far + step - mul(step[:, :hd], so_far)
            if k < 3:
                start = jnp.where(y > k, so_far, start)
        xs[x, h] = so_far.astype(BF)
        starts.append(start)
    sent += ring_gather(xs, x, "seq_0", send, recv, 6)
    for h in (0, 1):
        m = jnp.where(x > 0, xs[0, h][:, hd:].astype(F32), 0.0)
        for k in (1, 2):
            step = xs[k, h].astype(F32)
            m = jnp.where(x > k, m + step[:, hd:] - mul(step[:, :hd], m), m)
        m = m + starts[h][:, hd:] - mul(starts[h][:, :hd], m)
        second = m + firsts[h][:, hd:] - mul(firsts[h][:, :hd], m)
        before[mine + h] = jnp.where(c == 0, m, second)
        pair_m[h] = jnp.where(c == 0, second, m)
    c1 = remote(pair_m, got_m, send.at[13], recv.at[13], partner)
    c1.start()
    c1.wait_recv()
    for h in (0, 1):
        before[theirs + h] = got_m[h]
    for h in range(4):
        m = before[h]
        after[h] = m + b_full[h] - mul(eb[h][:, :hd], m)
    for copy in (c0, *sent, c1):
        copy.wait_send()


def memory_scan(eb, b_full, collective_id):
    square = jax.ShapeDtypeStruct((4, 128, 128), F32)
    slots = jax.ShapeDtypeStruct((4, 2, 128, 256), BF)
    pair = jax.ShapeDtypeStruct((2, 2, 128, 128), BF)
    return pl.pallas_call(
        memory_kernel,
        out_shape=(square, square, slots, slots, pair),
        in_specs=[VMEM] * 2,
        out_specs=(VMEM,) * 5,
        scratch_shapes=[
            pltpu.VMEM((2, 128, 256), BF),
            pltpu.VMEM((2, 128, 128), F32),
            pltpu.VMEM((2, 128, 128), F32),
            pltpu.SemaphoreType.DMA((14,)),
            pltpu.SemaphoreType.DMA((14,)),
        ],
        name="memory_scan",
        compiler_params=params(collective_id, 32),
    )(eb, b_full)


def rows_by_rows(a, b):
    return lax.dot_general(a, b, (((1,), (1,)), ((), ())), preferred_element_type=F32)


def mlp_kernel(
    normed, grad_out, w_gate, w_up, w_down, back, forth, grads, normed_t, grad_out_t, back_sum, forth_sum, grad_gate, grad_up
):
    step, kind = pl.program_id(0), pl.program_id(1)

    @pl.when((step == 0) & (kind == 0))
    def _():
        normed_t[...] = normed[...].T
        grad_out_t[...] = grad_out[...].T
        back_sum[...] = jnp.zeros_like(back_sum)
        forth_sum[...] = jnp.zeros_like(forth_sum)

    @pl.when(kind == 0)
    def _():
        gate_pre = jnp.dot(normed[...], w_gate[...], preferred_element_type=F32)
        up_pre = jnp.dot(normed[...], w_up[...], preferred_element_type=F32)
        grad_hidden = jnp.dot(grad_out[...], w_down[...], preferred_element_type=F32)
        sig = jax.nn.sigmoid(gate_pre)
        swish = gate_pre * sig
        hidden = (swish * up_pre).astype(BF)
        grad_up[...] = (grad_hidden * swish).astype(BF)
        grad_gate[...] = (grad_hidden * up_pre * sig * (1.0 + gate_pre * (1.0 - sig))).astype(BF)
        forth_sum[...] += rows_by_rows(hidden, w_down[...])
        grads[...] = jnp.dot(grad_out_t[...], hidden, preferred_element_type=F32).astype(BF)

    @pl.when(kind == 1)
    def _():
        back_sum[...] += rows_by_rows(grad_gate[...], w_gate[...])
        grads[...] = jnp.dot(normed_t[...], grad_gate[...], preferred_element_type=F32).astype(BF)

    @pl.when(kind == 2)
    def _():
        back_sum[...] += rows_by_rows(grad_up[...], w_up[...])
        grads[...] = jnp.dot(normed_t[...], grad_up[...], preferred_element_type=F32).astype(BF)

    @pl.when((step == pl.num_programs(0) - 1) & (kind == 2))
    def _():
        back[...] = back_sum[...].astype(BF)
        forth[...] = forth_sum[...].astype(BF)


MLP_TILE = 512


def mlp(normed, grad_out, w_gate, w_up, w_down):
    rows, width = normed.shape
    units = w_gate.shape[1]
    steps = units // MLP_TILE
    whole = pl.BlockSpec((rows, width), lambda f, k: (0, 0))
    weight = pl.BlockSpec((width, MLP_TILE), lambda f, k: (0, f))
    low = jax.ShapeDtypeStruct((rows, width), BF)
    return pl.pallas_call(
        mlp_kernel,
        grid=(steps, 3),
        out_shape=(low, low, jax.ShapeDtypeStruct((width, 3 * units), BF)),
        in_specs=[whole, whole, weight, weight, weight],
        out_specs=(whole, whole, pl.BlockSpec((width, MLP_TILE), lambda f, k: (0, k * steps + f))),
        scratch_shapes=[
            pltpu.VMEM((width, rows), BF),
            pltpu.VMEM((width, rows), BF),
            pltpu.VMEM((rows, width), F32),
            pltpu.VMEM((rows, width), F32),
            pltpu.VMEM((rows, MLP_TILE), BF),
            pltpu.VMEM((rows, MLP_TILE), BF),
        ],
        name="mlp",
        compiler_params=pltpu.CompilerParams(vmem_limit_bytes=56 << 20),
        cost_estimate=pl.CostEstimate(
            flops=18 * rows * width * units, bytes_accessed=12 * width * units, transcendentals=rows * units
        ),
    )(normed, grad_out, w_gate, w_up, w_down)


class RingSum:
    def __init__(self, src, bufs, send, recv, base, axis):
        self.src, self.bufs, self.me = src, bufs, lax.axis_index(axis)
        half = src.shape[2] // 2
        self.a, self.b = pl.ds(0, half), pl.ds(half, half)
        self.right, self.left = lax.rem(self.me + 1, 4), lax.rem(self.me + 3, 4)
        far = lax.rem(self.me + 2, 4)
        to_right, to_left = {axis: self.right}, {axis: self.left}

        def copy(piece, landing, slot, device):
            return remote(piece, bufs.at[landing], send.at[base + slot], recv.at[base + slot], device)

        rows = pl.ds(0, src.shape[1])
        self.c0 = copy(src.at[far, rows, self.a], 0, 0, to_right)
        self.c1 = copy(src.at[far, rows, self.b], 1, 1, to_left)
        self.c2 = copy(src.at[self.right, rows, self.b], 2, 2, to_right)
        self.c3 = copy(src.at[self.left, rows, self.a], 3, 3, to_left)
        self.c4 = copy(bufs.at[6], 4, 4, to_right)
        self.c5 = copy(bufs.at[7], 5, 5, to_left)

    def start_a(self):
        self.c0.start()
        self.c3.start()

    def start_b(self):
        self.c1.start()
        self.c2.start()

    def start(self):
        self.c0.start()
        self.c1.start()
        self.c3.start()
        self.c2.start()

    def middle(self):
        src, bufs = self.src, self.bufs
        self.c0.wait_recv()
        bufs[6] = (bufs[0].astype(F32) + src[self.right, :, self.a].astype(F32)).astype(BF)
        self.c4.start()
        self.c1.wait_recv()
        bufs[7] = (bufs[1].astype(F32) + src[self.left, :, self.b].astype(F32)).astype(BF)
        self.c5.start()

    def finish(self, put):
        src, bufs = self.src, self.bufs
        self.c3.wait_recv()
        self.c4.wait_recv()
        put(self.a, src[self.me, :, self.a].astype(F32) + bufs[4].astype(F32) + bufs[3].astype(F32))
        self.c2.wait_recv()
        self.c5.wait_recv()
        put(self.b, src[self.me, :, self.b].astype(F32) + bufs[5].astype(F32) + bufs[2].astype(F32))

    def drain(self):
        for copy in (self.c0, self.c1, self.c2, self.c3, self.c4, self.c5):
            copy.wait_send()


class RingGather:
    def __init__(self, buf, send, recv, base, axis):
        self.me = lax.axis_index(axis)
        half = buf.shape[1] // 2
        right, left = lax.rem(self.me + 1, 4), lax.rem(self.me + 3, 4)
        to_right, to_left = {axis: right}, {axis: left}

        def copy(q, h, slot, device):
            piece = buf.at[q, pl.ds(half * h, half)]
            return remote(piece, piece, send.at[base + slot], recv.at[base + slot], device)

        self.r0, self.l1 = copy(self.me, 0, 0, to_right), copy(self.me, 1, 1, to_left)
        self.r1, self.l0 = copy(self.me, 1, 2, to_right), copy(self.me, 0, 3, to_left)
        self.f0, self.f1 = copy(left, 0, 4, to_right), copy(right, 1, 5, to_left)

    def start(self):
        for copy in (self.r0, self.l1, self.r1, self.l0):
            copy.start()

    def middle(self):
        self.r0.wait_recv()
        self.f0.start()
        self.l1.wait_recv()
        self.f1.start()

    def finish(self):
        for copy in (self.r1, self.l0, self.f0, self.f1):
            copy.wait_recv()

    def drain(self):
        for copy in (self.r0, self.l1, self.r1, self.l0, self.f0, self.f1):
            copy.wait_send()


class SeqSum:
    def __init__(self, product, got, first, first_bufs, second, second_bufs, send, recv, base, x_first):
        self.product, self.got, self.first, self.second, self.x_first = product, got, first, second, x_first
        self.core = lax.axis_index("seq_2")
        self.swap = remote(
            product.at[pl.ds(0, 16), 1 - self.core], got, send.at[base], recv.at[base], {"seq_2": 1 - self.core}
        )
        axes = ("seq_0", "seq_1") if x_first else ("seq_1", "seq_0")
        self.one = RingSum(first, first_bufs, send, recv, base + 1, axes[0])
        self.two = RingSum(second, second_bufs, send, recv, base + 7, axes[1])

    def start(self):
        self.swap.start()

    def first_ring(self):
        self.swap.wait_recv()
        for x in range(4):
            for y in range(4):
                at = 4 * x + y
                q, r = (x, y) if self.x_first else (y, x)
                total = self.product[at, self.core].astype(F32) + self.got[at].astype(F32)
                self.first[q, pl.ds(64 * r, 64)] = total.astype(BF)
        self.one.start()

    def second_ring(self):
        def put(cols, value):
            for r in range(4):
                self.second[r, :, cols] = value[64 * r : 64 * (r + 1)].astype(BF)

        self.one.finish(put)
        self.two.start()

    def finish(self, out):
        def put(cols, value):
            out[:, cols] = value

        self.two.finish(put)

    def drain(self):
        self.swap.wait_send()
        self.one.drain()
        self.two.drain()


def greet_all():
    barrier = pltpu.get_barrier_semaphore()
    me, z = seq_index(), lax.axis_index("tensor")

    def greet_seq(k, carry):
        pl.semaphore_signal(barrier, inc=1, device_id=seq_place(lax.rem(me + k, 32)), device_id_type=MESH_ID)
        return carry

    lax.fori_loop(1, 32, greet_seq, 0)
    for k in (1, 2, 3):
        pl.semaphore_signal(barrier, inc=1, device_id={"tensor": lax.rem(z + k, 4)}, device_id_type=MESH_ID)


def all_greeted():
    pl.semaphore_wait(pltpu.get_barrier_semaphore(), 34)


class TotalOfAll:
    def __init__(self, mine, extra, by_z, line, by_seq, total, send, recv, base):
        self.mine, self.extra, self.by_z, self.line, self.by_seq, self.total = mine, extra, by_z, line, by_seq, total
        self.z, self.me = lax.axis_index("tensor"), seq_index()
        self.send, self.recv, self.base = send, recv, base
        peers = [lax.rem(self.z + k, 4) for k in (1, 2, 3)]
        self.split = [
            remote(mine.at[p], by_z.at[self.z], send.at[base + k], recv.at[base + k], {"tensor": p})
            for k, p in enumerate(peers)
        ]
        self.join = [
            remote(total.at[self.z], total.at[self.z], send.at[base + 3 + k], recv.at[base + 3 + k], {"tensor": p})
            for k, p in enumerate(peers)
        ]

    def start(self):
        for copy in self.split:
            copy.start()

    def over_seq(self):
        self.by_z[self.z] = self.mine[self.z]
        for copy in self.split:
            copy.wait_recv()
        self.line[0:8] = (self.by_z[0] + self.by_z[1]) + (self.by_z[2] + self.by_z[3])
        self.line[8:16] = self.extra[...]
        self.by_seq[self.me] = self.line[...]

        def push(k, carry):
            device = seq_place(lax.rem(self.me + k, 32))
            remote(self.line, self.by_seq.at[self.me], self.send.at[self.base + 6], self.recv.at[self.base + 6], device).start()
            return carry

        lax.fori_loop(1, 32, push, 0)

    def over_tensor(self, extra_out):
        others = self.by_seq.at[pl.ds(0, 31)]
        pltpu.make_async_copy(others, others, self.recv.at[self.base + 6]).wait()
        summed = jnp.sum(self.by_seq[...], axis=0)
        self.total[self.z] = summed[0:8]
        extra_out[...] = summed[8:16]
        for copy in self.join:
            copy.start()

    def finish(self):
        for copy in self.join:
            copy.wait_recv()

    def drain(self):
        for copy in (*self.split, *self.join):
            copy.wait_send()
        others = self.by_seq.at[pl.ds(0, 31)]
        pltpu.make_async_copy(others, others, self.send.at[self.base + 6]).wait()


def end_kernel(
    grads_in,
    normed,
    branch,
    mix,
    w_query,
    w_key,
    w_value,
    tokens_own,
    grad_middle,
    gain,
    gain_mlp_grad,
    logits,
    grad_tokens,
    out_query,
    out_key,
    out_value,
    out_output,
    gains,
    logits_out,
    weights,
    turned,
    part,
    part_bufs,
    grad_own,
    products,
    got,
    first,
    first_bufs,
    second,
    second_bufs,
    mine,
    by_z,
    line,
    by_seq,
    load,
    send,
    recv,
):
    loads = [
        pltpu.make_async_copy(w, weights.at[i], load.at[i]) for i, w in enumerate((w_query, w_key, w_value))
    ]
    for copy in loads:
        copy.start()
    greet_all()
    z = lax.axis_index("tensor")
    z_sum = RingSum(part, part_bufs, send, recv, 0, "tensor")
    z_gather = RingGather(grad_tokens, send, recv, 6, "tensor")
    sums = [
        SeqSum(
            products.at[i], got.at[i], first.at[i], first_bufs.at[i], second.at[i], second_bufs.at[i],
            send, recv, 12 + 13 * i, i % 2 == 0,
        )
        for i in range(4)
    ]
    total = TotalOfAll(mine, logits, by_z, line, by_seq, gains, send, recv, 64)

    def product(i, left, right):
        value = jnp.dot(left, right, preferred_element_type=F32).astype(BF)
        products[i] = value.reshape(16, 2, 64, 512)

    turned[...] = branch[...].T
    product(0, turned[...], mix[...])
    all_greeted()
    sums[0].start()
    for copy in loads:
        copy.wait()
    for half in (0, 1):
        rows = pl.ds(1024 * half, 1024)
        value = sum(rows_by_rows(grads_in[:, 512 * i : 512 * (i + 1)], weights[i, rows]) for i in range(3))
        part[:, :, rows] = value.astype(BF).reshape(4, 96, 1024)
        (z_sum.start_a, z_sum.start_b)[half]()
    turned[...] = normed[...].T
    product(1, turned[...], grads_in[:, 0:512])
    sums[1].start()
    sums[0].first_ring()
    product(2, turned[...], grads_in[:, 512:1024])
    sums[2].start()
    z_sum.middle()
    sums[1].first_ring()
    product(3, turned[...], grads_in[:, 1024:1536])
    sums[3].start()
    sums[2].first_ring()

    def keep(cols, value):
        grad_own[:, cols] = value

    sums[0].one.middle()
    z_sum.finish(keep)
    stream = tokens_own[...].astype(F32)
    inv = lax.rsqrt(jnp.mean(stream * stream, axis=1, keepdims=True) + epsilon)
    grad_normed = grad_own[...]
    weighted = grad_normed * gain[...]
    inner = jnp.sum(weighted * stream, axis=1, keepdims=True)
    scaled = stream * inv
    result = grad_middle[...] + inv * weighted - scaled * (inv * inv * inner * (1.0 / stream.shape[1]))
    grad_tokens[z] = result.astype(BF)
    z_gather.start()
    gain_grad = jnp.sum(grad_normed * scaled, axis=0, keepdims=True)
    for r in range(16):
        mine[r // 8, r % 8 : r % 8 + 1] = gain_grad[:, 128 * r : 128 * (r + 1)]
    mine[2:4] = gain_mlp_grad[...]
    total.start()
    sums[1].one.middle()
    sums[3].first_ring()
    sums[0].second_ring()
    total.over_seq()
    sums[2].one.middle()
    sums[1].second_ring()
    sums[0].two.middle()
    z_gather.middle()
    sums[3].one.middle()
    sums[2].second_ring()
    sums[1].two.middle()
    total.over_tensor(logits_out)
    sums[0].finish(out_output)
    sums[3].second_ring()
    sums[2].two.middle()
    sums[1].finish(out_query)
    sums[3].two.middle()
    sums[2].finish(out_key)
    sums[3].finish(out_value)
    total.finish()
    z_gather.finish()
    z_sum.drain()
    z_gather.drain()
    for s in sums:
        s.drain()
    total.drain()


def end(grads_in, normed, branch, mix, w_query, w_key, w_value, tokens_own, grad_middle, gain, gain_mlp_grad, logits, cid):
    shape = jax.ShapeDtypeStruct
    weight_grad = shape((64, 512), F32)
    low = lambda *dims: pltpu.VMEM(dims, BF)
    full = lambda *dims: pltpu.VMEM(dims, F32)
    anywhere = pl.BlockSpec(memory_space=pl.ANY)
    return pl.pallas_call(
        end_kernel,
        out_shape=(shape((4, 96, 2048), BF),) + (weight_grad,) * 4 + (shape((4, 8, 128), F32), shape((8, 128), F32)),
        in_specs=[VMEM] * 4 + [anywhere] * 3 + [VMEM] * 5,
        out_specs=(VMEM,) * 7,
        scratch_shapes=[
            low(3, 2048, 512),
            low(2048, 384),
            low(4, 96, 2048),
            low(8, 96, 1024),
            full(96, 2048),
            low(4, 16, 2, 64, 512),
            low(4, 16, 64, 512),
            low(4, 4, 256, 512),
            low(4, 8, 256, 256),
            low(4, 4, 64, 512),
            low(4, 8, 64, 256),
            full(4, 8, 128),
            full(4, 8, 128),
            full(16, 128),
            full(32, 16, 128),
            pltpu.SemaphoreType.DMA((3,)),
            pltpu.SemaphoreType.DMA((71,)),
            pltpu.SemaphoreType.DMA((71,)),
        ],
        name="end",
        compiler_params=params(cid, 56),
    )(grads_in, normed, branch, mix, w_query, w_key, w_value, tokens_own, grad_middle, gain, gain_mlp_grad, logits)


def feature_of(v):
    return jnp.where(v > 0, v + 1.0, jnp.exp(jnp.minimum(v, 0.0)))


def slope_of(v):
    return jnp.where(v > 0, 1.0, jnp.exp(jnp.minimum(v, 0.0)))


def back_kernel(
    back,
    forth,
    middle,
    gain,
    grad_out,
    w_output,
    query,
    key,
    value,
    probs,
    local_out,
    retrieved,
    keep,
    offset,
    gate,
    memory,
    ys,
    xs,
    pair_e,
    layer_out,
    branch,
    grad_middle,
    gain_grad,
    logits,
    grads,
    later,
    weight,
    back_bufs,
    forth_bufs,
    own,
    inverse,
    recall,
    grad_mix,
    grad_query,
    grad_key,
    grad_value,
    source,
    got,
    s_y,
    s_x,
    pair_l,
    got_l,
    adjoint,
    line,
    lines,
    load,
    send,
    recv,
):
    greet_all()
    fetch = pltpu.make_async_copy(w_output, weight, load)
    fetch.start()
    x, y, c = ring_places()
    z, me = lax.axis_index("tensor"), seq_index()
    partner = {"seq_2": 1 - c}
    mine, theirs = 2 * c, 2 * (1 - c)
    z_back = RingSum(back, back_bufs, send, recv, 0, "tensor")
    z_branch = RingGather(branch, send, recv, 6, "tensor")
    z_forth = RingSum(forth, forth_bufs, send, recv, 12, "tensor")
    z_layer = RingGather(layer_out, send, recv, 18, "tensor")
    y_ring = RingGather(s_y, send, recv, 24, "seq_1")
    x_ring = RingGather(s_x, send, recv, 30, "seq_0")
    swap = remote(source.at[pl.ds(theirs, 2)], got, send.at[36], recv.at[36], partner)
    give = remote(pair_l, got_l, send.at[37], recv.at[37], partner)
    cols = [slice(128 * h, 128 * (h + 1)) for h in range(4)]
    feat_q = lambda h: feature_of(query[:, cols[h]].astype(F32))
    feat_k = lambda h: feature_of(key[:, cols[h]].astype(F32))
    scale = 128 ** (-0.5)

    def recalled(h):
        fk, off = feat_k(h), offset[h : h + 1]
        inv_k = 1.0 / jnp.sum(fk * off, axis=1, keepdims=True)
        inverse[4 + h] = inv_k
        inverse[h] = 1.0 / jnp.sum(feat_q(h) * off, axis=1, keepdims=True)
        recall[:, cols[h]] = mul(fk, memory[h]) * inv_k

    all_greeted()
    z_back.start()
    recalled(0)
    recalled(1)
    z_back.middle()
    recalled(2)
    recalled(3)

    def put(at, total):
        own[:, at] = total

    z_back.finish(put)
    stream = middle[...]
    inv = lax.rsqrt(jnp.mean(stream * stream, axis=1, keepdims=True) + epsilon)
    grad_normed = own[...]
    weighted = grad_normed * gain[...]
    inner = jnp.sum(weighted * stream, axis=1, keepdims=True)
    scaled = stream * inv
    result = grad_out[...].astype(F32) + inv * weighted - scaled * (inv * inv * inner * (1.0 / stream.shape[1]))
    grad_middle[...] = result
    branch[z] = result.astype(BF)
    z_branch.start()
    total = jnp.sum(grad_normed * scaled, axis=0, keepdims=True)
    for r in range(16):
        gain_grad[r // 8, r % 8 : r % 8 + 1] = total[:, 128 * r : 128 * (r + 1)]
    z_branch.middle()
    fetch.wait()
    z_branch.finish()
    z_forth.start()
    grad_mix[...] = jnp.dot(branch[...].reshape(384, 2048), weight[...], preferred_element_type=F32)

    def point(h):
        return gate[h : h + 1] * grad_mix[:, cols[h]] * inverse[h]

    for h in range(4):
        source[h] = mul_t(feat_q(h), point(h)).astype(BF)
    swap.start()

    def attend(h):
        at = cols[h]
        grad_local = ((1.0 - gate[h : h + 1]) * grad_mix[:, at]).astype(BF)
        low = probs[h]
        p = low.astype(F32)
        grad_probs = rows_by_rows(grad_local, value[:, at])
        grad_value[:, at] = mul_t(low, grad_local)
        grad_scores = (p * (grad_probs - jnp.sum(grad_probs * p, axis=1, keepdims=True))).astype(BF)
        grad_query[:, at] = mul(grad_scores, key[:, at]) * scale
        grad_key[:, at] = mul_t(grad_scores, query[:, at]) * scale

    attend(0)
    swap.wait_recv()
    seconds = []
    for h in (0, 1):
        here, there = source[mine + h].astype(F32), got[h].astype(F32)
        first, second = jnp.where(c == 0, here, there), jnp.where(c == 0, there, here)
        seconds.append(second)
        s_y[y, pl.ds(128 * h, 128)] = (first + second - mul_t(pair_e[0, h], second)).astype(BF)
    y_ring.start()
    attend(1)
    y_ring.middle()
    attend(2)
    z_forth.middle()
    y_ring.finish()
    of = [pl.ds(0, 128), pl.ds(128, 128)]
    for h in (0, 1):
        so_far = s_y[3, of[h]].astype(F32)
        for k in (2, 1, 0):
            so_far = s_y[k, of[h]].astype(F32) + so_far - mul_t(ys[k, h][:, :128], so_far)
        s_x[x, of[h]] = so_far.astype(BF)
    x_ring.start()
    attend(3)
    x_ring.middle()
    logit_rows = []
    for h in range(4):
        at, gate_h, g = cols[h], gate[h : h + 1], grad_mix[:, cols[h]]
        ret = retrieved[:, at]
        moved = jnp.sum(g * (ret - local_out[:, at]), axis=0, keepdims=True) * gate_h * (1.0 - gate_h)
        logit_rows.append(jnp.sum(moved, axis=1, keepdims=True))
        grad_den = -jnp.sum(gate_h * g * ret, axis=1, keepdims=True) * inverse[h]
        q = query[:, at].astype(F32)
        grad_feat = rows_by_rows(point(h).astype(BF), memory[h].astype(BF)) + grad_den * offset[h : h + 1]
        grads[:, at] = (grad_query[:, at] + grad_feat * slope_of(q)).astype(BF)
        line[h : h + 1] = jnp.sum(grad_den * feature_of(q), axis=0, keepdims=True)
    lane = lax.broadcasted_iota(jnp.int32, (8, 128), 1)
    row = lax.broadcasted_iota(jnp.int32, (8, 128), 0)
    spot = jnp.zeros((8, 128), F32)
    for h in range(4):
        spot = jnp.where((lane == h) & (row == 0), logit_rows[h], spot)
    logits[...] = spot

    z_forth.finish(put)
    layer_out[z] = (middle[...] + own[...]).astype(BF)
    z_layer.start()
    x_ring.finish()
    for h in (0, 1):
        lam = jnp.where(x < 3, s_x[3, of[h]].astype(F32), 0.0)
        for k in (2, 1):
            lam = jnp.where(x < k, s_x[k, of[h]].astype(F32) + lam - mul_t(xs[k, h][:, :128], lam), lam)
        for k in (3, 2, 1):
            lam = jnp.where(y < k, s_y[k, of[h]].astype(F32) + lam - mul_t(ys[k, h][:, :128], lam), lam)
        first = lam + seconds[h] - mul_t(pair_e[1, h], lam)
        adjoint[mine + h] = jnp.where(c == 0, first, lam).astype(BF)
        pair_l[h] = jnp.where(c == 0, lam, first).astype(BF)
    give.start()
    give.wait_recv()
    for h in (0, 1):
        adjoint[theirs + h] = got_l[h]
    for h in range(4):
        at, fk = cols[h], feat_k(h)
        grad_update = mul(fk * keep[...], adjoint[h])
        grad_den = jnp.sum(grad_update * recall[:, at], axis=1, keepdims=True) * inverse[4 + h]
        line[h : h + 1] += jnp.sum(grad_den * fk, axis=0, keepdims=True)
        grads[:, 1024 + 128 * h : 1152 + 128 * h] = (grad_value[:, at] + grad_update).astype(BF)
        update = value[:, at].astype(F32) - recall[:, at]
        grad_feat = (
            grad_den * offset[h : h + 1]
            + keep[...] * rows_by_rows(update.astype(BF), adjoint[h])
            - rows_by_rows((grad_update * inverse[4 + h]).astype(BF), memory[h].astype(BF))
        )
        grad_key[:, at] += grad_feat * slope_of(key[:, at].astype(F32))
    line[4:8] = jnp.zeros((4, 128), F32)
    lines[me] = line[...]

    def push(k, carry):
        remote(line, lines.at[me], send.at[38], recv.at[38], seq_place(lax.rem(me + k, 32))).start()
        return carry

    lax.fori_loop(1, 32, push, 0)
    z_layer.middle()
    others = lines.at[pl.ds(0, 31)]
    pltpu.make_async_copy(others, others, recv.at[38]).wait()
    passed = lax.broadcasted_iota(jnp.int32, (32, 8, 128), 0) > me
    after = jnp.sum(jnp.where(passed, lines[...], 0.0), axis=0)
    later[...] = after
    for h in range(4):
        at = cols[h]
        rest = keep[...] * after[h : h + 1] * slope_of(key[:, at].astype(F32))
        grads[:, 512 + 128 * h : 640 + 128 * h] = (grad_key[:, at] + rest).astype(BF)
    z_layer.finish()
    for part in (z_back, z_branch, z_forth, z_layer, y_ring, x_ring):
        part.drain()
    swap.wait_send()
    give.wait_send()
    pltpu.make_async_copy(others, others, send.at[38]).wait()


def back_pass(cid, *args):
    shape = jax.ShapeDtypeStruct
    low = lambda *dims: pltpu.VMEM(dims, BF)
    full = lambda *dims: pltpu.VMEM(dims, F32)
    return pl.pallas_call(
        back_kernel,
        out_shape=(
            shape((4, 96, 2048), BF),
            shape((4, 96, 2048), BF),
            shape((96, 2048), F32),
            shape((2, 8, 128), F32),
            shape((8, 128), F32),
            shape((384, 1536), BF),
            shape((8, 128), F32),
        ),
        in_specs=[VMEM] * 5 + [pl.BlockSpec(memory_space=pl.ANY)] + [VMEM] * 13,
        out_specs=(VMEM,) * 7,
        scratch_shapes=[
            low(2048, 512),
            low(8, 96, 1024),
            low(8, 96, 1024),
            full(96, 2048),
            full(8, 384, 1),
            full(384, 512),
            full(384, 512),
            full(384, 512),
            full(384, 512),
            full(384, 512),
            low(4, 128, 128),
            low(2, 128, 128),
            low(4, 256, 128),
            low(4, 256, 128),
            low(2, 128, 128),
            low(2, 128, 128),
            low(4, 128, 128),
            full(8, 128),
            full(32, 8, 128),
            pltpu.SemaphoreType.DMA(()),
            pltpu.SemaphoreType.DMA((39,)),
            pltpu.SemaphoreType.DMA((39,)),
        ],
        name="back",
        compiler_params=params(cid, 56),
    )(*args)


def feature(values):
    return jax.nn.elu(values) + 1.0


def heads_dot(spec, a, b):
    return jnp.einsum(spec, a.astype(BF), b.astype(BF), preferred_element_type=F32)


def on_device(
    tokens,
    cotangent,
    w_query,
    w_key,
    w_value,
    w_output,
    w_gate,
    w_up,
    w_down,
    gain_attn,
    gain_mlp,
    gate_logit,
    valid_count,
):
    seg_len = tokens.shape[0]
    head_count = gate_logit.shape[0]
    col_count = w_query.shape[1]
    head_dim = col_count // head_count
    scale_dot = head_dim ** (-0.5)
    here = seq_index()
    z = lax.axis_index("tensor")
    own_rows = seg_len // 4
    position = lax.iota(jnp.int32, seg_len)
    valid_len = jnp.where(here == 31, valid_count[0], seg_len)
    keep_mask = (position < valid_len).astype(F32)
    allowed = (position[:, None] >= position[None, :]) & (keep_mask[None, :] > 0)
    stream = tokens.astype(F32)
    inv_one = lax.rsqrt(jnp.mean(stream * stream, axis=1, keepdims=True) + epsilon)
    normed = (stream * inv_one * gain_attn).astype(BF)
    queries = jnp.dot(normed, w_query, preferred_element_type=F32).astype(BF)
    key_rows = jnp.dot(normed, w_key, preferred_element_type=F32).astype(BF)
    values = jnp.dot(normed, w_value, preferred_element_type=F32).astype(BF)
    heads_shape = (seg_len, head_count, head_dim)
    q_heads = queries.reshape(heads_shape)
    k_heads = key_rows.reshape(heads_shape)
    v_heads = values.reshape(heads_shape)
    q_float = q_heads.astype(F32)
    k_float = k_heads.astype(F32)
    v_float = v_heads.astype(F32)
    feat_query = feature(q_float)
    feat_key = feature(k_float)
    kept_key = feat_key * keep_mask[:, None, None]
    key_sum = jnp.sum(kept_key, axis=0)
    key_sums = spread(key_sum, "seq", 0)
    earlier = (jnp.arange(32) < here)[:, None, None]
    normal_prev = jnp.sum(jnp.where(earlier, key_sums, 0.0), axis=0)
    normal_next = normal_prev + key_sum
    scores = jnp.einsum("qhd,khd->hqk", q_heads, k_heads, preferred_element_type=F32) * scale_dot
    masked = jnp.where(allowed[None], scores, -1e30)
    row_top = jnp.max(masked, axis=2, keepdims=True)
    exp_scores = jnp.exp(masked - row_top)
    attn_low = (exp_scores / jnp.sum(exp_scores, axis=2, keepdims=True)).astype(BF)
    local_out = jnp.einsum("hqk,khd->qhd", attn_low, v_heads, preferred_element_type=F32)
    offset = normal_prev + seg_len
    den_key = jnp.sum(feat_key * offset, axis=2)
    den_query = jnp.sum(feat_query * offset, axis=2)
    taken = heads_dot("shd,she->hde", kept_key / den_key[:, :, None], feat_key)
    source = heads_dot("shd,she->hde", kept_key, v_heads)
    eb = jnp.concatenate((taken, source), axis=2).astype(BF)
    memory_prev, memory_next, ys, xs, pair_e = memory_scan(eb, source, 1)
    retrieved = heads_dot("shd,hde->she", feat_query, memory_prev) / den_query[:, :, None]
    gate_mix = jax.nn.sigmoid(gate_logit)[:, None]
    mixture = gate_mix * retrieved + (1.0 - gate_mix) * local_out
    mix_low = mixture.reshape(seg_len, col_count).astype(BF)
    attn_part = jnp.einsum("sc,dc->sd", mix_low, w_output, preferred_element_type=F32).astype(BF)
    own = lambda a: lax.dynamic_slice_in_dim(a, z * own_rows, own_rows, 0)
    middle = own(tokens).astype(F32) + row_sum(attn_part, 2)
    inv_two = lax.rsqrt(jnp.mean(middle * middle, axis=1, keepdims=True) + epsilon)
    normed_two = row_gather((middle * inv_two * gain_mlp).astype(BF), 3)
    grad_out = jnp.where(keep_mask[:, None] > 0, cotangent, jnp.zeros_like(cotangent))
    back_part, forth_part, mlp_grads = mlp(normed_two, grad_out, w_gate, w_up, w_down)
    mlp_grads = lax.psum_scatter(mlp_grads, SEQ, scatter_dimension=0, tiled=True)
    flat = (seg_len, col_count)
    blocks = (4, own_rows, tokens.shape[1])
    layer_out, grad_branch, grad_middle, gain_mlp_grad, logit_grad, grads_in, later_offset = back_pass(
        4,
        back_part.reshape(blocks),
        forth_part.reshape(blocks),
        middle,
        gain_mlp[None],
        own(grad_out),
        w_output,
        queries,
        key_rows,
        values,
        attn_low,
        local_out.reshape(flat),
        retrieved.reshape(flat),
        keep_mask[:, None],
        offset,
        jnp.broadcast_to(gate_mix, (4, 128)),
        memory_prev,
        ys,
        xs,
        pair_e,
    )
    later_offset = later_offset[:4]
    grad_tokens, grad_query, grad_key, grad_value, grad_output, gains, logit_grad = end(
        grads_in,
        normed,
        grad_branch.reshape(tokens.shape),
        mix_low,
        w_query,
        w_key,
        w_value,
        own(tokens),
        grad_middle,
        gain_attn[None],
        gain_mlp_grad,
        logit_grad,
        8,
    )
    gains = gains.reshape(-1)
    units = w_gate.shape[1]
    of_mlp = lambda k: mlp_grads[:, units * k : units * (k + 1)].astype(F32)
    return (
        layer_out.reshape(tokens.shape),
        grad_tokens.reshape(tokens.shape).astype(F32),
        grad_query,
        grad_key,
        grad_value,
        grad_output,
        of_mlp(1),
        of_mlp(2),
        of_mlp(0),
        gains[:2048],
        gains[2048:],
        logit_grad[0, :4],
        memory_next[None],
        normal_next[None],
        later_offset[None],
    )


def solution(mesh):
    torus = Mesh(
        mesh.devices.reshape(4, 4, 2, mesh.shape["tensor"]), ("seq_0", "seq_1", "seq_2", "tensor")
    )
    weight = P(None, "tensor")
    grad = P(SEQ, "tensor")
    return jax.shard_map(
        on_device,
        mesh=torus,
        in_specs=(P(SEQ, None), P(SEQ, None)) + (weight,) * 7 + (P(), P(), P("tensor"), P()),
        out_specs=(P(SEQ, None), P(SEQ, None))
        + (grad,) * 7
        + (P(), P(), P("tensor"), P(SEQ, "tensor", None, None), P(SEQ, "tensor", None), P(SEQ, "tensor", None)),
        check_vma=False,
    )
```

```python
import functools

import jax
import jax.numpy as jnp
from jax import lax
from jax.experimental import pallas as pl
from jax.experimental.pallas import tpu as pltpu
from jax.sharding import Mesh
from jax.sharding import PartitionSpec as P

SEQ = ("seq_0", "seq_1", "seq_2")
MESH_ID = pl.DeviceIdType.MESH
VMEM = pl.BlockSpec(memory_space=pltpu.VMEM)
BF = jnp.bfloat16
F32 = jnp.float32

epsilon = 1e-06


def remote(src, dst, send, recv, device):
    return pltpu.make_async_remote_copy(
        src_ref=src, dst_ref=dst, send_sem=send, recv_sem=recv, device_id=device, device_id_type=MESH_ID
    )


def meet(devices):
    barrier = pltpu.get_barrier_semaphore()
    for device in devices:
        pl.semaphore_signal(barrier, inc=1, device_id=device, device_id_type=MESH_ID)
    pl.semaphore_wait(barrier, len(devices))


def params(collective_id, mib):
    return pltpu.CompilerParams(
        collective_id=collective_id, has_side_effects=True, vmem_limit_bytes=mib << 20
    )


def seq_place(index):
    return {"seq_0": index // 8, "seq_1": lax.rem(index // 2, 4), "seq_2": lax.rem(index, 2)}


def seq_index():
    return lax.axis_index("seq_0") * 8 + lax.axis_index("seq_1") * 2 + lax.axis_index("seq_2")


def mul(a, b):
    return jnp.dot(a.astype(BF), b.astype(BF), preferred_element_type=F32)


def mul_t(a, b):
    return lax.dot_general(a.astype(BF), b.astype(BF), (((0,), (0,)), ((), ())), preferred_element_type=F32)


def ring_places():
    x, y, c = (lax.axis_index(a) for a in SEQ)
    return x, y, c


def rows_by_rows(a, b):
    return lax.dot_general(a, b, (((1,), (1,)), ((), ())), preferred_element_type=F32)


def mlp_kernel(normed, grad_hidden, w_gate, w_up, back, hidden, grads, normed_t, back_sum, grad_up):
    step, kind = pl.program_id(0), pl.program_id(1)

    @pl.when((step == 0) & (kind == 0))
    def _():
        normed_t[...] = normed[...].T
        back_sum[...] = jnp.zeros_like(back_sum)

    @pl.when(kind == 0)
    def _():
        gate_pre = jnp.dot(normed[...], w_gate[...], preferred_element_type=F32)
        up_pre = jnp.dot(normed[...], w_up[...], preferred_element_type=F32)
        sig = jax.nn.sigmoid(gate_pre)
        swish = gate_pre * sig
        hidden[...] = (swish * up_pre).astype(BF)
        grad_up[...] = (grad_hidden[...] * swish).astype(BF)
        grad_gate = (grad_hidden[...] * up_pre * sig * (1.0 + gate_pre * (1.0 - sig))).astype(BF)
        back_sum[...] += rows_by_rows(grad_gate, w_gate[...])
        grads[...] = jnp.dot(normed_t[...], grad_gate, preferred_element_type=F32).astype(BF)

    @pl.when(kind == 1)
    def _():
        back_sum[...] += rows_by_rows(grad_up[...], w_up[...])
        grads[...] = jnp.dot(normed_t[...], grad_up[...], preferred_element_type=F32).astype(BF)

    @pl.when((step == pl.num_programs(0) - 1) & (kind == 1))
    def _():
        back[...] = back_sum[...].astype(BF)


MLP_TILE = 512


def mlp(normed, grad_hidden, w_gate, w_up):
    rows, width = normed.shape
    units = w_gate.shape[1]
    steps = units // MLP_TILE
    whole = pl.BlockSpec((rows, width), lambda f, k: (0, 0))
    weight = pl.BlockSpec((width, MLP_TILE), lambda f, k: (0, f))
    tile = pl.BlockSpec((rows, MLP_TILE), lambda f, k: (0, f))
    shape = jax.ShapeDtypeStruct
    return pl.pallas_call(
        mlp_kernel,
        grid=(steps, 2),
        out_shape=(shape((rows, width), BF), shape((rows, units), BF), shape((width, 2 * units), BF)),
        in_specs=[whole, tile, weight, weight],
        out_specs=(whole, tile, pl.BlockSpec((width, MLP_TILE), lambda f, k: (0, k * steps + f))),
        scratch_shapes=[
            pltpu.VMEM((width, rows), BF),
            pltpu.VMEM((rows, width), F32),
            pltpu.VMEM((rows, MLP_TILE), BF),
        ],
        name="mlp",
        compiler_params=pltpu.CompilerParams(vmem_limit_bytes=48 << 20),
        cost_estimate=pl.CostEstimate(
            flops=12 * rows * width * units, bytes_accessed=8 * width * units, transcendentals=rows * units
        ),
    )(normed, grad_hidden, w_gate, w_up)


class RingSum:
    def __init__(self, src, bufs, send, recv, base, axis):
        self.src, self.bufs, self.me = src, bufs, lax.axis_index(axis)
        half = src.shape[2] // 2
        self.a, self.b = pl.ds(0, half), pl.ds(half, half)
        self.right, self.left = lax.rem(self.me + 1, 4), lax.rem(self.me + 3, 4)
        far = lax.rem(self.me + 2, 4)
        to_right, to_left = {axis: self.right}, {axis: self.left}

        def copy(piece, landing, slot, device):
            return remote(piece, bufs.at[landing], send.at[base + slot], recv.at[base + slot], device)

        rows = pl.ds(0, src.shape[1])
        self.c0 = copy(src.at[far, rows, self.a], 0, 0, to_right)
        self.c1 = copy(src.at[far, rows, self.b], 1, 1, to_left)
        self.c2 = copy(src.at[self.right, rows, self.b], 2, 2, to_right)
        self.c3 = copy(src.at[self.left, rows, self.a], 3, 3, to_left)
        self.c4 = copy(bufs.at[6], 4, 4, to_right)
        self.c5 = copy(bufs.at[7], 5, 5, to_left)

    def start_a(self):
        self.c0.start()
        self.c3.start()

    def start_b(self):
        self.c1.start()
        self.c2.start()

    def start(self):
        self.c0.start()
        self.c1.start()
        self.c3.start()
        self.c2.start()

    def middle(self):
        src, bufs = self.src, self.bufs
        self.c0.wait_recv()
        bufs[6] = (bufs[0].astype(F32) + src[self.right, :, self.a].astype(F32)).astype(BF)
        self.c4.start()
        self.c1.wait_recv()
        bufs[7] = (bufs[1].astype(F32) + src[self.left, :, self.b].astype(F32)).astype(BF)
        self.c5.start()

    def finish(self, put):
        src, bufs = self.src, self.bufs
        self.c3.wait_recv()
        self.c4.wait_recv()
        put(self.a, src[self.me, :, self.a].astype(F32) + bufs[4].astype(F32) + bufs[3].astype(F32))
        self.c2.wait_recv()
        self.c5.wait_recv()
        put(self.b, src[self.me, :, self.b].astype(F32) + bufs[5].astype(F32) + bufs[2].astype(F32))

    def drain(self):
        for copy in (self.c0, self.c1, self.c2, self.c3, self.c4, self.c5):
            copy.wait_send()


class RingGather:
    def __init__(self, buf, send, recv, base, axis):
        self.me = lax.axis_index(axis)
        half = buf.shape[1] // 2
        right, left = lax.rem(self.me + 1, 4), lax.rem(self.me + 3, 4)
        to_right, to_left = {axis: right}, {axis: left}

        def copy(q, h, slot, device):
            piece = buf.at[q, pl.ds(half * h, half)]
            return remote(piece, piece, send.at[base + slot], recv.at[base + slot], device)

        self.r0, self.l1 = copy(self.me, 0, 0, to_right), copy(self.me, 1, 1, to_left)
        self.r1, self.l0 = copy(self.me, 1, 2, to_right), copy(self.me, 0, 3, to_left)
        self.f0, self.f1 = copy(left, 0, 4, to_right), copy(right, 1, 5, to_left)

    def start(self):
        for copy in (self.r0, self.l1, self.r1, self.l0):
            copy.start()

    def middle(self):
        self.r0.wait_recv()
        self.f0.start()
        self.l1.wait_recv()
        self.f1.start()

    def finish(self):
        for copy in (self.r1, self.l0, self.f0, self.f1):
            copy.wait_recv()

    def drain(self):
        for copy in (self.r0, self.l1, self.r1, self.l0, self.f0, self.f1):
            copy.wait_send()


class SeqSum:
    def __init__(self, product, got, first, first_bufs, second, second_bufs, send, recv, base, x_first):
        self.product, self.got, self.first, self.second, self.x_first = product, got, first, second, x_first
        self.core = lax.axis_index("seq_2")
        self.swap = remote(
            product.at[pl.ds(0, 16), 1 - self.core], got, send.at[base], recv.at[base], {"seq_2": 1 - self.core}
        )
        axes = ("seq_0", "seq_1") if x_first else ("seq_1", "seq_0")
        self.one = RingSum(first, first_bufs, send, recv, base + 1, axes[0])
        self.two = RingSum(second, second_bufs, send, recv, base + 7, axes[1])

    def start(self):
        self.swap.start()

    def first_ring(self):
        self.swap.wait_recv()
        for x in range(4):
            for y in range(4):
                at = 4 * x + y
                q, r = (x, y) if self.x_first else (y, x)
                total = self.product[at, self.core].astype(F32) + self.got[at].astype(F32)
                self.first[q, pl.ds(64 * r, 64)] = total.astype(BF)
        self.one.start()

    def second_ring(self):
        def put(cols, value):
            for r in range(4):
                self.second[r, :, cols] = value[64 * r : 64 * (r + 1)].astype(BF)

        self.one.finish(put)
        self.two.start()

    def finish(self, out):
        def put(cols, value):
            out[:, cols] = value

        self.two.finish(put)

    def drain(self):
        self.swap.wait_send()
        self.one.drain()
        self.two.drain()


def greet_all():
    barrier = pltpu.get_barrier_semaphore()
    me, z = seq_index(), lax.axis_index("tensor")

    def greet_seq(k, carry):
        pl.semaphore_signal(barrier, inc=1, device_id=seq_place(lax.rem(me + k, 32)), device_id_type=MESH_ID)
        return carry

    lax.fori_loop(1, 32, greet_seq, 0)
    for k in (1, 2, 3):
        pl.semaphore_signal(barrier, inc=1, device_id={"tensor": lax.rem(z + k, 4)}, device_id_type=MESH_ID)


def all_greeted():
    pl.semaphore_wait(pltpu.get_barrier_semaphore(), 34)


class TotalOfAll:
    def __init__(self, mine, extra, by_z, line, by_seq, total, send, recv, base):
        self.mine, self.extra, self.by_z, self.line, self.by_seq, self.total = mine, extra, by_z, line, by_seq, total
        self.z, self.me = lax.axis_index("tensor"), seq_index()
        self.send, self.recv, self.base = send, recv, base
        peers = [lax.rem(self.z + k, 4) for k in (1, 2, 3)]
        self.split = [
            remote(mine.at[p], by_z.at[self.z], send.at[base + k], recv.at[base + k], {"tensor": p})
            for k, p in enumerate(peers)
        ]
        self.join = [
            remote(total.at[self.z], total.at[self.z], send.at[base + 3 + k], recv.at[base + 3 + k], {"tensor": p})
            for k, p in enumerate(peers)
        ]

    def start(self):
        for copy in self.split:
            copy.start()

    def over_seq(self):
        self.by_z[self.z] = self.mine[self.z]
        for copy in self.split:
            copy.wait_recv()
        self.line[0:8] = (self.by_z[0] + self.by_z[1]) + (self.by_z[2] + self.by_z[3])
        self.line[8:16] = self.extra[...]
        self.by_seq[self.me] = self.line[...]

        def push(k, carry):
            device = seq_place(lax.rem(self.me + k, 32))
            remote(self.line, self.by_seq.at[self.me], self.send.at[self.base + 6], self.recv.at[self.base + 6], device).start()
            return carry

        lax.fori_loop(1, 32, push, 0)

    def over_tensor(self, extra_out):
        others = self.by_seq.at[pl.ds(0, 31)]
        pltpu.make_async_copy(others, others, self.recv.at[self.base + 6]).wait()
        summed = jnp.sum(self.by_seq[...], axis=0)
        self.total[self.z] = summed[0:8]
        extra_out[...] = summed[8:16]
        for copy in self.join:
            copy.start()

    def finish(self):
        for copy in self.join:
            copy.wait_recv()

    def drain(self):
        for copy in (*self.split, *self.join):
            copy.wait_send()
        others = self.by_seq.at[pl.ds(0, 31)]
        pltpu.make_async_copy(others, others, self.send.at[self.base + 6]).wait()


def end_kernel(
    grads_in,
    branch,
    grad_middle,
    gain,
    gain_mlp_grad,
    logits,
    i_mix,
    i_normed_t,
    w_query,
    w_key,
    w_value,
    tokens,
    grad_tokens,
    out_query,
    out_key,
    out_value,
    out_output,
    gains,
    logits_out,
    weights,
    mix,
    normed_t,
    tokens_own,
    turned,
    part,
    part_bufs,
    grad_own,
    products,
    got,
    first,
    first_bufs,
    second,
    second_bufs,
    mine,
    by_z,
    line,
    by_seq,
    moves,
    send,
    recv,
):
    z = lax.axis_index("tensor")
    move = Moves(moves)
    load_mix = move.start(i_mix, mix)
    loads = [move.start(w, weights.at[i]) for i, w in enumerate((w_query, w_key, w_value))]
    load_t = move.start(i_normed_t, normed_t)
    load_own = move.start(tokens.at[pl.ds(pl.multiple_of(96 * z, 96), 96)], tokens_own)
    greet_all()
    z_sum = RingSum(part, part_bufs, send, recv, 0, "tensor")
    z_gather = RingGather(grad_tokens, send, recv, 6, "tensor")
    sums = [
        SeqSum(
            products.at[i], got.at[i], first.at[i], first_bufs.at[i], second.at[i], second_bufs.at[i],
            send, recv, 12 + 13 * i, i % 2 == 0,
        )
        for i in range(4)
    ]
    total = TotalOfAll(mine, logits, by_z, line, by_seq, gains, send, recv, 64)

    def product(i, left, right):
        value = jnp.dot(left, right, preferred_element_type=F32).astype(BF)
        products[i] = value.reshape(16, 2, 64, 512)

    turned[...] = branch[...].reshape(384, 2048).T
    load_mix.wait()
    product(0, turned[...], mix[...])
    all_greeted()
    sums[0].start()
    for copy in loads:
        copy.wait()
    for half in (0, 1):
        rows = pl.ds(1024 * half, 1024)
        value = sum(rows_by_rows(grads_in[:, 512 * i : 512 * (i + 1)], weights[i, rows]) for i in range(3))
        part[:, :, rows] = value.astype(BF).reshape(4, 96, 1024)
        (z_sum.start_a, z_sum.start_b)[half]()
    load_t.wait()
    product(1, normed_t[...], grads_in[:, 0:512])
    sums[1].start()
    sums[0].first_ring()
    product(2, normed_t[...], grads_in[:, 512:1024])
    sums[2].start()
    z_sum.middle()
    sums[1].first_ring()
    product(3, normed_t[...], grads_in[:, 1024:1536])
    sums[3].start()
    sums[2].first_ring()

    def keep(cols, value):
        grad_own[:, cols] = value

    sums[0].one.middle()
    z_sum.finish(keep)
    load_own.wait()
    stream = tokens_own[...].astype(F32)
    inv = lax.rsqrt(jnp.mean(stream * stream, axis=1, keepdims=True) + epsilon)
    grad_normed = grad_own[...]
    weighted = grad_normed * gain[...]
    inner = jnp.sum(weighted * stream, axis=1, keepdims=True)
    scaled = stream * inv
    result = grad_middle[...] + inv * weighted - scaled * (inv * inv * inner * (1.0 / stream.shape[1]))
    grad_tokens[z] = result.astype(BF)
    z_gather.start()
    gain_grad = jnp.sum(grad_normed * scaled, axis=0, keepdims=True)
    for r in range(16):
        mine[r // 8, r % 8 : r % 8 + 1] = gain_grad[:, 128 * r : 128 * (r + 1)]
    mine[2:4] = gain_mlp_grad[...]
    total.start()
    sums[1].one.middle()
    sums[3].first_ring()
    sums[0].second_ring()
    total.over_seq()
    sums[2].one.middle()
    sums[1].second_ring()
    sums[0].two.middle()
    z_gather.middle()
    sums[3].one.middle()
    sums[2].second_ring()
    sums[1].two.middle()
    total.over_tensor(logits_out)
    sums[0].finish(out_output)
    sums[3].second_ring()
    sums[2].two.middle()
    sums[1].finish(out_query)
    sums[3].two.middle()
    sums[2].finish(out_key)
    sums[3].finish(out_value)
    total.finish()
    z_gather.finish()
    z_sum.drain()
    z_gather.drain()
    for s in sums:
        s.drain()
    total.drain()


def end(cid, *args):
    shape = jax.ShapeDtypeStruct
    weight_grad = shape((64, 512), F32)
    low = lambda *dims: pltpu.VMEM(dims, BF)
    full = lambda *dims: pltpu.VMEM(dims, F32)
    return pl.pallas_call(
        end_kernel,
        out_shape=(shape((4, 96, 2048), BF),) + (weight_grad,) * 4 + (shape((4, 8, 128), F32), shape((8, 128), F32)),
        in_specs=[VMEM] * 6 + [ANYWHERE] * 6,
        out_specs=(VMEM,) * 7,
        scratch_shapes=[
            low(3, 2048, 512),
            low(384, 512),
            low(2048, 384),
            low(96, 2048),
            low(2048, 384),
            low(4, 96, 2048),
            low(8, 96, 1024),
            full(96, 2048),
            low(4, 16, 2, 64, 512),
            low(4, 16, 64, 512),
            low(4, 4, 256, 512),
            low(4, 8, 256, 256),
            low(4, 4, 64, 512),
            low(4, 8, 64, 256),
            full(4, 8, 128),
            full(4, 8, 128),
            full(16, 128),
            full(32, 16, 128),
            pltpu.SemaphoreType.DMA((6,)),
            pltpu.SemaphoreType.DMA((71,)),
            pltpu.SemaphoreType.DMA((71,)),
        ],
        name="end",
        compiler_params=params(cid, 56),
    )(*args)


def feature_of(v):
    return jnp.where(v > 0, v + 1.0, jnp.exp(jnp.minimum(v, 0.0)))


def slope_of(v):
    return jnp.where(v > 0, 1.0, jnp.exp(jnp.minimum(v, 0.0)))


ANYWHERE = pl.BlockSpec(memory_space=pl.ANY)


class Moves:
    def __init__(self, sems):
        self.sems, self.count = sems, 0

    def start(self, src, dst):
        copy = pltpu.make_async_copy(src, dst, self.sems.at[self.count])
        self.count += 1
        copy.start()
        return copy


def front_kernel(
    tokens,
    cotangent,
    gain_attn,
    gain_mlp,
    keep,
    gate,
    w_query,
    w_key,
    w_value,
    w_output,
    w_down,
    o_normed_t,
    o_grad_out_t,
    o_grad_hidden,
    o_query,
    o_key,
    o_value,
    o_probs,
    o_local_out,
    o_retrieved,
    o_mix,
    grad_out_own,
    offset,
    normal_next,
    memory_prev,
    memory_next,
    ys,
    xs,
    pair_e,
    middle,
    normed_two,
    weights,
    weight_o,
    weight_d,
    normed,
    turned,
    grad_out,
    grad_out_t,
    grad_hidden,
    query,
    key,
    value,
    probs,
    local_out,
    retrieved,
    mix,
    line,
    lines,
    eb,
    source,
    got,
    pair_m,
    got_m,
    part,
    part_bufs,
    moves,
    send,
    recv,
):
    move = Moves(moves)
    loads = [move.start(w, weights.at[i]) for i, w in enumerate((w_key, w_query, w_value))]
    load_o = move.start(w_output, weight_o)
    load_d = [move.start(w_down.at[pl.ds(512 * i, 512)], weight_d.at[pl.ds(512 * i, 512)]) for i in range(4)]
    greet_all()
    x, y, c = ring_places()
    z, me = lax.axis_index("tensor"), seq_index()
    partner = {"seq_2": 1 - c}
    mine, theirs = 2 * c, 2 * (1 - c)
    z_sum = RingSum(part, part_bufs, send, recv, 0, "tensor")
    z_gather = RingGather(normed_two, send, recv, 6, "tensor")
    y_ring = RingGather(ys, send, recv, 12, "seq_1")
    x_ring = RingGather(xs, send, recv, 18, "seq_0")
    swap = remote(eb.at[pl.ds(theirs, 2)], got, send.at[24], recv.at[24], partner)
    give = remote(pair_m, got_m, send.at[25], recv.at[25], partner)
    cols = [slice(128 * h, 128 * (h + 1)) for h in range(4)]
    stores = []

    for q in range(4):
        rows = pl.ds(96 * q, 96)
        stream = tokens[rows].astype(F32)
        inv = lax.rsqrt(jnp.mean(stream * stream, axis=1, keepdims=True) + epsilon)
        normed[rows] = (stream * inv * gain_attn[...]).astype(BF)
    loads[0].wait()
    key[...] = jnp.dot(normed[...], weights[0], preferred_element_type=F32).astype(BF)
    feat_q = lambda h: feature_of(query[:, cols[h]].astype(F32))
    feat_k = lambda h: feature_of(key[:, cols[h]].astype(F32))
    line[...] = jnp.zeros_like(line)
    for h in range(4):
        line[h : h + 1] = jnp.sum(feat_k(h) * keep[...], axis=0, keepdims=True)
    lines[me] = line[...]
    all_greeted()

    def push(k, carry):
        remote(line, lines.at[me], send.at[26], recv.at[26], seq_place(lax.rem(me + k, 32))).start()
        return carry

    lax.fori_loop(1, 32, push, 0)
    stores.append(move.start(key, o_key))
    loads[1].wait()
    query[...] = jnp.dot(normed[...], weights[1], preferred_element_type=F32).astype(BF)
    stores.append(move.start(query, o_query))
    loads[2].wait()
    value[...] = jnp.dot(normed[...], weights[2], preferred_element_type=F32).astype(BF)
    stores.append(move.start(value, o_value))
    at_row = lax.broadcasted_iota(jnp.int32, (384, 384), 0)
    at_col = lax.broadcasted_iota(jnp.int32, (384, 384), 1)
    valid = jnp.sum(keep[...], axis=0, keepdims=True)
    allowed = (at_row >= at_col) & (at_col.astype(F32) < valid)

    def attend(h):
        at = cols[h]
        scores = rows_by_rows(query[:, at], key[:, at]) * 128 ** (-0.5)
        masked = jnp.where(allowed, scores, -1e30)
        raised = jnp.exp(masked - jnp.max(masked, axis=1, keepdims=True))
        low = (raised * (1.0 / jnp.sum(raised, axis=1, keepdims=True))).astype(BF)
        probs[h] = low
        local_out[:, at] = jnp.dot(low, value[:, at], preferred_element_type=F32)
        total = mul_t(feat_k(h) * keep[...], value[:, at])
        source[h] = total
        eb[h, :, 128:256] = total.astype(BF)

    for h in range(4):
        attend(h)
    stores.append(move.start(probs, o_probs))
    stores.append(move.start(local_out, o_local_out))
    others = lines.at[pl.ds(0, 31)]
    pltpu.make_async_copy(others, others, recv.at[26]).wait()
    passed = lax.broadcasted_iota(jnp.int32, (32, 8, 128), 0) < me
    before = jnp.sum(jnp.where(passed, lines[...], 0.0), axis=0)
    normal_next[...] = before + line[...]
    offset[...] = before + 384.0
    for h in range(4):
        fk = feat_k(h)
        kept = fk * keep[...] * (1.0 / jnp.sum(fk * offset[h : h + 1], axis=1, keepdims=True))
        eb[h, :, 0:128] = mul_t(kept, fk).astype(BF)
    swap.start()
    grad_out[...] = cotangent[...] * keep[...].astype(BF)
    grad_out_own[...] = grad_out[pl.ds(pl.multiple_of(96 * z, 96), 96)]
    swap.wait_recv()
    of = [pl.ds(0, 128), pl.ds(128, 128)]
    firsts = []
    for h in (0, 1):
        here, there = eb[mine + h].astype(F32), got[h].astype(F32)
        first, second = jnp.where(c == 0, here, there), jnp.where(c == 0, there, here)
        firsts.append(first)
        pair_e[0, h] = first[:, :128].astype(BF)
        pair_e[1, h] = second[:, :128].astype(BF)
        ys[y, of[h]] = (first + second - mul(second[:, :128], first)).astype(BF)
    y_ring.start()

    def hidden_part(i):
        load_d[i].wait()
        rows = pl.ds(512 * i, 512)
        product = jnp.dot(grad_out[:, 512 * i : 512 * (i + 1)], weight_d[rows], preferred_element_type=F32)
        if i == 0:
            grad_hidden[...] = product
        else:
            grad_hidden[...] += product

    hidden_part(0)
    y_ring.middle()
    hidden_part(1)
    y_ring.finish()
    starts = []
    for h in (0, 1):
        so_far = ys[0, of[h]].astype(F32)
        start = jnp.where(y > 0, so_far, 0.0)
        for k in (1, 2, 3):
            step = ys[k, of[h]].astype(F32)
            so_far = so_far + step - mul(step[:, :128], so_far)
            if k < 3:
                start = jnp.where(y > k, so_far, start)
        xs[x, of[h]] = so_far.astype(BF)
        starts.append(start)
    x_ring.start()
    hidden_part(2)
    x_ring.middle()
    hidden_part(3)
    stores.append(move.start(grad_hidden, o_grad_hidden))
    load_o.wait()
    x_ring.finish()
    for h in (0, 1):
        m = jnp.where(x > 0, xs[0, of[h]][:, 128:].astype(F32), 0.0)
        for k in (1, 2):
            step = xs[k, of[h]].astype(F32)
            m = jnp.where(x > k, m + step[:, 128:] - mul(step[:, :128], m), m)
        m = m + starts[h][:, 128:] - mul(starts[h][:, :128], m)
        second = m + firsts[h][:, 128:] - mul(firsts[h][:, :128], m)
        memory_prev[mine + h] = jnp.where(c == 0, m, second)
        pair_m[h] = jnp.where(c == 0, second, m)
    give.start()
    give.wait_recv()
    for h in (0, 1):
        memory_prev[theirs + h] = got_m[h]
    for h in range(4):
        at, fq, sig = cols[h], feat_q(h), gate[h : h + 1]
        inv_q = 1.0 / jnp.sum(fq * offset[h : h + 1], axis=1, keepdims=True)
        found = mul(fq, memory_prev[h]) * inv_q
        retrieved[:, at] = found
        mix[:, at] = (sig * found + (1.0 - sig) * local_out[:, at]).astype(BF)
    for half in (0, 1):
        rows = pl.ds(1024 * half, 1024)
        part[:, :, rows] = rows_by_rows(mix[...], weight_o[rows]).astype(BF).reshape(4, 96, 1024)
        (z_sum.start_a, z_sum.start_b)[half]()
    stores.append(move.start(retrieved, o_retrieved))
    stores.append(move.start(mix, o_mix))
    for h in range(4):
        m = memory_prev[h]
        memory_next[h] = m + source[h] - mul(eb[h][:, :128], m)
    turned[...] = normed[...].T
    stores.append(move.start(turned, o_normed_t))
    z_sum.middle()
    grad_out_t[...] = grad_out[...].T
    stores.append(move.start(grad_out_t, o_grad_out_t))
    own_tokens = tokens[pl.ds(pl.multiple_of(96 * z, 96), 96)].astype(F32)

    def put(at, total):
        lanes = slice(0, 1024) if at is z_sum.a else slice(1024, 2048)
        middle[:, at] = own_tokens[:, lanes] + total

    z_sum.finish(put)
    stream = middle[...]
    inv = lax.rsqrt(jnp.mean(stream * stream, axis=1, keepdims=True) + epsilon)
    normed_two[z] = (stream * inv * gain_mlp[...]).astype(BF)
    z_gather.start()
    z_gather.middle()
    for store in stores:
        store.wait()
    z_gather.finish()
    for ring in (z_sum, z_gather, y_ring, x_ring):
        ring.drain()
    swap.wait_send()
    give.wait_send()
    pltpu.make_async_copy(others, others, send.at[26]).wait()


def front(cid, *args):
    shape = jax.ShapeDtypeStruct
    low = lambda *dims: pltpu.VMEM(dims, BF)
    full = lambda *dims: pltpu.VMEM(dims, F32)
    return pl.pallas_call(
        front_kernel,
        out_shape=(
            shape((2048, 384), BF),
            shape((2048, 384), BF),
            shape((384, 2048), F32),
            shape((384, 512), BF),
            shape((384, 512), BF),
            shape((384, 512), BF),
            shape((4, 384, 384), BF),
            shape((384, 512), F32),
            shape((384, 512), F32),
            shape((384, 512), BF),
            shape((96, 2048), BF),
            shape((8, 128), F32),
            shape((8, 128), F32),
            shape((4, 128, 128), F32),
            shape((4, 128, 128), F32),
            shape((4, 256, 256), BF),
            shape((4, 256, 256), BF),
            shape((2, 2, 128, 128), BF),
            shape((96, 2048), F32),
            shape((4, 96, 2048), BF),
        ),
        in_specs=[VMEM] * 6 + [ANYWHERE] * 5,
        out_specs=(ANYWHERE,) * 10 + (VMEM,) * 10,
        scratch_shapes=[
            low(3, 2048, 512),
            low(2048, 512),
            low(2048, 2048),
            low(384, 2048),
            low(2048, 384),
            low(384, 2048),
            low(2048, 384),
            full(384, 2048),
            low(384, 512),
            low(384, 512),
            low(384, 512),
            low(4, 384, 384),
            full(384, 512),
            full(384, 512),
            low(384, 512),
            full(8, 128),
            full(32, 8, 128),
            low(4, 128, 256),
            full(4, 128, 128),
            low(2, 128, 256),
            full(2, 128, 128),
            full(2, 128, 128),
            low(4, 96, 2048),
            low(8, 96, 1024),
            pltpu.SemaphoreType.DMA((18,)),
            pltpu.SemaphoreType.DMA((27,)),
            pltpu.SemaphoreType.DMA((27,)),
        ],
        name="front",
        compiler_params=params(cid, 58),
    )(*args)


def back_kernel(
    back,
    middle,
    gain,
    grad_out,
    keep,
    offset,
    gate,
    memory,
    ys,
    xs,
    pair_e,
    i_grad_out_t,
    i_hidden,
    i_query,
    i_key,
    i_value,
    i_probs,
    i_local_out,
    i_retrieved,
    w_output,
    w_down,
    layer_out,
    branch,
    grad_middle,
    gain_grad,
    logits,
    grads,
    later,
    out_down,
    grad_out_t,
    hidden,
    query,
    key,
    value,
    probs,
    local_out,
    retrieved,
    weight,
    weight_d,
    products,
    got_rows,
    first_rows,
    first_bufs,
    second_rows,
    second_bufs,
    forth,
    back_bufs,
    forth_bufs,
    own,
    inverse,
    recall,
    grad_mix,
    grad_query,
    grad_key,
    grad_value,
    source,
    got,
    s_y,
    s_x,
    pair_l,
    got_l,
    adjoint,
    line,
    lines,
    moves,
    send,
    recv,
):
    move = Moves(moves)
    pairs = (
        (i_grad_out_t, grad_out_t),
        (i_hidden, hidden),
        (i_query, query),
        (i_key, key),
        (i_value, value),
        (w_down, weight_d),
        (w_output, weight),
        (i_probs, probs),
        (i_local_out, local_out),
        (i_retrieved, retrieved),
    )
    loads = [move.start(src, dst) for src, dst in pairs]
    greet_all()
    x, y, c = ring_places()
    z, me = lax.axis_index("tensor"), seq_index()
    partner = {"seq_2": 1 - c}
    mine, theirs = 2 * c, 2 * (1 - c)
    z_back = RingSum(back, back_bufs, send, recv, 0, "tensor")
    z_branch = RingGather(branch, send, recv, 6, "tensor")
    z_forth = RingSum(forth, forth_bufs, send, recv, 12, "tensor")
    z_layer = RingGather(layer_out, send, recv, 18, "tensor")
    y_ring = RingGather(s_y, send, recv, 24, "seq_1")
    x_ring = RingGather(s_x, send, recv, 30, "seq_0")
    swap = remote(source.at[pl.ds(theirs, 2)], got, send.at[36], recv.at[36], partner)
    give = remote(pair_l, got_l, send.at[37], recv.at[37], partner)
    cols = [slice(128 * h, 128 * (h + 1)) for h in range(4)]
    feat_q = lambda h: feature_of(query[:, cols[h]].astype(F32))
    feat_k = lambda h: feature_of(key[:, cols[h]].astype(F32))
    scale = 128 ** (-0.5)

    def recalled(h):
        fk, off = feat_k(h), offset[h : h + 1]
        inv_k = 1.0 / jnp.sum(fk * off, axis=1, keepdims=True)
        inverse[4 + h] = inv_k
        inverse[h] = 1.0 / jnp.sum(feat_q(h) * off, axis=1, keepdims=True)
        recall[:, cols[h]] = mul(fk, memory[h]) * inv_k

    sums = [
        SeqSum(
            products.at[i], got_rows.at[i], first_rows.at[i], first_bufs.at[i], second_rows.at[i], second_bufs.at[i],
            send, recv, 39 + 13 * i, i % 2 == 0,
        )
        for i in range(4)
    ]

    def product(i):
        lanes = slice(512 * i, 512 * (i + 1))
        result = jnp.dot(grad_out_t[...], hidden[:, lanes], preferred_element_type=F32).astype(BF)
        products[i] = result.reshape(16, 2, 64, 512)
        sums[i].start()

    all_greeted()
    z_back.start()
    for load in loads[:2]:
        load.wait()
    product(0)
    product(1)
    z_back.middle()
    sums[0].first_ring()
    product(2)
    sums[1].first_ring()
    for load in loads[2:5]:
        load.wait()
    recalled(0)
    recalled(1)

    def put(at, total):
        own[:, at] = total

    z_back.finish(put)
    stream = middle[...]
    inv = lax.rsqrt(jnp.mean(stream * stream, axis=1, keepdims=True) + epsilon)
    grad_normed = own[...]
    weighted = grad_normed * gain[...]
    inner = jnp.sum(weighted * stream, axis=1, keepdims=True)
    scaled = stream * inv
    result = grad_out[...].astype(F32) + inv * weighted - scaled * (inv * inv * inner * (1.0 / stream.shape[1]))
    grad_middle[...] = result
    branch[z] = result.astype(BF)
    z_branch.start()
    total = jnp.sum(grad_normed * scaled, axis=0, keepdims=True)
    for r in range(16):
        gain_grad[r // 8, r % 8 : r % 8 + 1] = total[:, 128 * r : 128 * (r + 1)]
    product(3)
    sums[0].one.middle()
    sums[2].first_ring()
    z_branch.middle()
    recalled(2)
    recalled(3)
    sums[1].one.middle()
    loads[5].wait()
    for half in (0, 1):
        rows = pl.ds(1024 * half, 1024)
        forth[:, :, rows] = rows_by_rows(hidden[...], weight_d[rows]).astype(BF).reshape(4, 96, 1024)
    sums[3].first_ring()
    sums[0].second_ring()
    for load in loads[6:]:
        load.wait()
    z_branch.finish()
    z_forth.start()
    grad_mix[...] = jnp.dot(branch[...].reshape(384, 2048), weight[...], preferred_element_type=F32)

    def point(h):
        return gate[h : h + 1] * grad_mix[:, cols[h]] * inverse[h]

    for h in range(4):
        source[h] = mul_t(feat_q(h), point(h)).astype(BF)
    swap.start()

    def attend(h):
        at = cols[h]
        grad_local = ((1.0 - gate[h : h + 1]) * grad_mix[:, at]).astype(BF)
        low = probs[h]
        p = low.astype(F32)
        grad_probs = rows_by_rows(grad_local, value[:, at])
        grad_value[:, at] = mul_t(low, grad_local)
        grad_scores = (p * (grad_probs - jnp.sum(grad_probs * p, axis=1, keepdims=True))).astype(BF)
        grad_query[:, at] = mul(grad_scores, key[:, at]) * scale
        grad_key[:, at] = mul_t(grad_scores, query[:, at]) * scale

    attend(0)
    swap.wait_recv()
    seconds = []
    for h in (0, 1):
        here, there = source[mine + h].astype(F32), got[h].astype(F32)
        first, second = jnp.where(c == 0, here, there), jnp.where(c == 0, there, here)
        seconds.append(second)
        s_y[y, pl.ds(128 * h, 128)] = (first + second - mul_t(pair_e[0, h], second)).astype(BF)
    y_ring.start()
    attend(1)
    y_ring.middle()
    attend(2)
    sums[2].one.middle()
    sums[1].second_ring()
    z_forth.middle()
    y_ring.finish()
    of = [pl.ds(0, 128), pl.ds(128, 128)]
    for h in (0, 1):
        so_far = s_y[3, of[h]].astype(F32)
        for k in (2, 1, 0):
            so_far = s_y[k, of[h]].astype(F32) + so_far - mul_t(ys[k, of[h]][:, :128], so_far)
        s_x[x, of[h]] = so_far.astype(BF)
    x_ring.start()
    attend(3)
    sums[3].one.middle()
    x_ring.middle()
    logit_rows = []
    for h in range(4):
        at, gate_h, g = cols[h], gate[h : h + 1], grad_mix[:, cols[h]]
        ret = retrieved[:, at]
        moved = jnp.sum(g * (ret - local_out[:, at]), axis=0, keepdims=True) * gate_h * (1.0 - gate_h)
        logit_rows.append(jnp.sum(moved, axis=1, keepdims=True))
        grad_den = -jnp.sum(gate_h * g * ret, axis=1, keepdims=True) * inverse[h]
        q = query[:, at].astype(F32)
        grad_feat = rows_by_rows(point(h).astype(BF), memory[h].astype(BF)) + grad_den * offset[h : h + 1]
        grads[:, at] = (grad_query[:, at] + grad_feat * slope_of(q)).astype(BF)
        line[h : h + 1] = jnp.sum(grad_den * feature_of(q), axis=0, keepdims=True)
    lane = lax.broadcasted_iota(jnp.int32, (8, 128), 1)
    row = lax.broadcasted_iota(jnp.int32, (8, 128), 0)
    spot = jnp.zeros((8, 128), F32)
    for h in range(4):
        spot = jnp.where((lane == h) & (row == 0), logit_rows[h], spot)
    logits[...] = spot

    z_forth.finish(put)
    layer_out[z] = (middle[...] + own[...]).astype(BF)
    z_layer.start()
    x_ring.finish()
    for h in (0, 1):
        lam = jnp.where(x < 3, s_x[3, of[h]].astype(F32), 0.0)
        for k in (2, 1):
            lam = jnp.where(x < k, s_x[k, of[h]].astype(F32) + lam - mul_t(xs[k, of[h]][:, :128], lam), lam)
        for k in (3, 2, 1):
            lam = jnp.where(y < k, s_y[k, of[h]].astype(F32) + lam - mul_t(ys[k, of[h]][:, :128], lam), lam)
        first = lam + seconds[h] - mul_t(pair_e[1, h], lam)
        adjoint[mine + h] = jnp.where(c == 0, first, lam).astype(BF)
        pair_l[h] = jnp.where(c == 0, lam, first).astype(BF)
    give.start()
    give.wait_recv()
    for h in (0, 1):
        adjoint[theirs + h] = got_l[h]
    for h in range(4):
        at, fk = cols[h], feat_k(h)
        grad_update = mul(fk * keep[...], adjoint[h])
        grad_den = jnp.sum(grad_update * recall[:, at], axis=1, keepdims=True) * inverse[4 + h]
        line[h : h + 1] += jnp.sum(grad_den * fk, axis=0, keepdims=True)
        grads[:, 1024 + 128 * h : 1152 + 128 * h] = (grad_value[:, at] + grad_update).astype(BF)
        update = value[:, at].astype(F32) - recall[:, at]
        grad_feat = (
            grad_den * offset[h : h + 1]
            + keep[...] * rows_by_rows(update.astype(BF), adjoint[h])
            - rows_by_rows((grad_update * inverse[4 + h]).astype(BF), memory[h].astype(BF))
        )
        grad_key[:, at] += grad_feat * slope_of(key[:, at].astype(F32))
    line[4:8] = jnp.zeros((4, 128), F32)
    lines[me] = line[...]

    def push(k, carry):
        remote(line, lines.at[me], send.at[38], recv.at[38], seq_place(lax.rem(me + k, 32))).start()
        return carry

    lax.fori_loop(1, 32, push, 0)
    z_layer.middle()
    sums[2].second_ring()
    sums[0].two.middle()
    sums[3].second_ring()
    sums[1].two.middle()
    others = lines.at[pl.ds(0, 31)]
    pltpu.make_async_copy(others, others, recv.at[38]).wait()
    passed = lax.broadcasted_iota(jnp.int32, (32, 8, 128), 0) > me
    after = jnp.sum(jnp.where(passed, lines[...], 0.0), axis=0)
    later[...] = after
    for h in range(4):
        at = cols[h]
        rest = keep[...] * after[h : h + 1] * slope_of(key[:, at].astype(F32))
        grads[:, 512 + 128 * h : 640 + 128 * h] = (grad_key[:, at] + rest).astype(BF)
    for i in (2, 3, 0, 1):
        if i > 1:
            sums[i].two.middle()
        sums[i].finish(out_down.at[:, pl.ds(512 * i, 512)])
    z_layer.finish()
    for part in (*sums, z_back, z_branch, z_forth, z_layer, y_ring, x_ring):
        part.drain()
    swap.wait_send()
    give.wait_send()
    pltpu.make_async_copy(others, others, send.at[38]).wait()


def back_pass(cid, *args):
    shape = jax.ShapeDtypeStruct
    low = lambda *dims: pltpu.VMEM(dims, BF)
    full = lambda *dims: pltpu.VMEM(dims, F32)
    return pl.pallas_call(
        back_kernel,
        out_shape=(
            shape((4, 96, 2048), BF),
            shape((4, 96, 2048), BF),
            shape((96, 2048), F32),
            shape((2, 8, 128), F32),
            shape((8, 128), F32),
            shape((384, 1536), BF),
            shape((8, 128), F32),
            shape((64, 2048), F32),
        ),
        in_specs=[VMEM] * 11 + [ANYWHERE] * 10,
        out_specs=(VMEM,) * 8,
        scratch_shapes=[
            low(2048, 384),
            low(384, 2048),
            low(384, 512),
            low(384, 512),
            low(384, 512),
            low(4, 384, 384),
            full(384, 512),
            full(384, 512),
            low(2048, 512),
            low(2048, 2048),
            low(4, 16, 2, 64, 512),
            low(4, 16, 64, 512),
            low(4, 4, 256, 512),
            low(4, 8, 256, 256),
            low(4, 4, 64, 512),
            low(4, 8, 64, 256),
            low(4, 96, 2048),
            low(8, 96, 1024),
            low(8, 96, 1024),
            full(96, 2048),
            full(8, 384, 1),
            full(384, 512),
            full(384, 512),
            full(384, 512),
            full(384, 512),
            full(384, 512),
            low(4, 128, 128),
            low(2, 128, 128),
            low(4, 256, 128),
            low(4, 256, 128),
            low(2, 128, 128),
            low(2, 128, 128),
            low(4, 128, 128),
            full(8, 128),
            full(32, 8, 128),
            pltpu.SemaphoreType.DMA((10,)),
            pltpu.SemaphoreType.DMA((91,)),
            pltpu.SemaphoreType.DMA((91,)),
        ],
        name="back",
        compiler_params=params(cid, 62),
    )(*args)


def on_device(
    tokens,
    cotangent,
    w_query,
    w_key,
    w_value,
    w_output,
    w_gate,
    w_up,
    w_down,
    gain_attn,
    gain_mlp,
    gate_logit,
    valid_count,
):
    seg_len = tokens.shape[0]
    valid_len = jnp.where(seq_index() == 31, valid_count[0], seg_len)
    keep = (lax.iota(jnp.int32, seg_len) < valid_len).astype(F32)[:, None]
    gate = jnp.broadcast_to(jax.nn.sigmoid(gate_logit)[:, None], (4, 128))
    (
        normed_t, grad_out_t, grad_hidden, query, key, value, probs, local_out, retrieved, mix,
        grad_out_own, offset, normal_next, memory_prev, memory_next, ys, xs, pair_e, middle, normed_two,
    ) = front(
        0, tokens, cotangent, gain_attn[None], gain_mlp[None], keep, gate, w_query, w_key, w_value, w_output, w_down
    )
    back, hidden, mlp_grads = mlp(normed_two.reshape(tokens.shape), grad_hidden, w_gate, w_up)
    mlp_grads = lax.psum_scatter(mlp_grads, SEQ, scatter_dimension=0, tiled=True)
    layer_out, branch, grad_middle, gain_mlp_grad, logit_grad, grads_in, later_offset, grad_down = back_pass(
        1, back.reshape(4, 96, 2048), middle, gain_mlp[None], grad_out_own, keep, offset, gate, memory_prev, ys, xs,
        pair_e, grad_out_t, hidden, query, key, value, probs, local_out, retrieved, w_output, w_down,
    )
    grad_tokens, grad_query, grad_key, grad_value, grad_output, gains, logit_grad = end(
        2, grads_in, branch, grad_middle, gain_attn[None], gain_mlp_grad, logit_grad,
        mix, normed_t, w_query, w_key, w_value, tokens,
    )
    gains = gains.reshape(-1)
    units = w_gate.shape[1]
    return (
        layer_out.reshape(tokens.shape),
        grad_tokens.reshape(tokens.shape).astype(F32),
        grad_query,
        grad_key,
        grad_value,
        grad_output,
        mlp_grads[:, :units].astype(F32),
        mlp_grads[:, units:].astype(F32),
        grad_down,
        gains[:2048],
        gains[2048:],
        logit_grad[0, :4],
        memory_next[None],
        normal_next[None, :4],
        later_offset[None, :4],
    )


def solution(mesh):
    torus = Mesh(
        mesh.devices.reshape(4, 4, 2, mesh.shape["tensor"]), ("seq_0", "seq_1", "seq_2", "tensor")
    )
    weight = P(None, "tensor")
    grad = P(SEQ, "tensor")
    return jax.shard_map(
        on_device,
        mesh=torus,
        in_specs=(P(SEQ, None), P(SEQ, None)) + (weight,) * 7 + (P(), P(), P("tensor"), P()),
        out_specs=(P(SEQ, None), P(SEQ, None))
        + (grad,) * 7
        + (P(), P(), P("tensor"), P(SEQ, "tensor", None, None), P(SEQ, "tensor", None), P(SEQ, "tensor", None)),
        check_vma=False,
    )
```

```python
import functools

import jax
import jax.numpy as jnp
from jax import lax
from jax.experimental import pallas as pl
from jax.experimental.pallas import tpu as pltpu
from jax.sharding import Mesh
from jax.sharding import PartitionSpec as P

SEQ = ("seq_0", "seq_1", "seq_2")
MESH_ID = pl.DeviceIdType.MESH
VMEM = pl.BlockSpec(memory_space=pltpu.VMEM)
BF = jnp.bfloat16
F32 = jnp.float32

epsilon = 1e-06


def remote(src, dst, send, recv, device):
    return pltpu.make_async_remote_copy(
        src_ref=src, dst_ref=dst, send_sem=send, recv_sem=recv, device_id=device, device_id_type=MESH_ID
    )


def meet(devices):
    barrier = pltpu.get_barrier_semaphore()
    for device in devices:
        pl.semaphore_signal(barrier, inc=1, device_id=device, device_id_type=MESH_ID)
    pl.semaphore_wait(barrier, len(devices))


def params(collective_id, mib):
    return pltpu.CompilerParams(
        collective_id=collective_id, has_side_effects=True, vmem_limit_bytes=mib << 20
    )


def seq_place(index):
    return {"seq_0": index // 8, "seq_1": lax.rem(index // 2, 4), "seq_2": lax.rem(index, 2)}


def seq_index():
    return lax.axis_index("seq_0") * 8 + lax.axis_index("seq_1") * 2 + lax.axis_index("seq_2")


def mul(a, b):
    return jnp.dot(a.astype(BF), b.astype(BF), preferred_element_type=F32)


def mul_t(a, b):
    return lax.dot_general(a.astype(BF), b.astype(BF), (((0,), (0,)), ((), ())), preferred_element_type=F32)


def ring_places():
    x, y, c = (lax.axis_index(a) for a in SEQ)
    return x, y, c


def rows_by_rows(a, b):
    return lax.dot_general(a, b, (((1,), (1,)), ((), ())), preferred_element_type=F32)


class RingSum:
    def __init__(self, src, bufs, send, recv, base, axis):
        self.src, self.bufs, self.me = src, bufs, lax.axis_index(axis)
        half = src.shape[2] // 2
        self.a, self.b = pl.ds(0, half), pl.ds(half, half)
        self.right, self.left = lax.rem(self.me + 1, 4), lax.rem(self.me + 3, 4)
        far = lax.rem(self.me + 2, 4)
        to_right, to_left = {axis: self.right}, {axis: self.left}

        def copy(piece, landing, slot, device):
            return remote(piece, bufs.at[landing], send.at[base + slot], recv.at[base + slot], device)

        rows = pl.ds(0, src.shape[1])
        self.c0 = copy(src.at[far, rows, self.a], 0, 0, to_right)
        self.c1 = copy(src.at[far, rows, self.b], 1, 1, to_left)
        self.c2 = copy(src.at[self.right, rows, self.b], 2, 2, to_right)
        self.c3 = copy(src.at[self.left, rows, self.a], 3, 3, to_left)
        self.c4 = copy(bufs.at[6], 4, 4, to_right)
        self.c5 = copy(bufs.at[7], 5, 5, to_left)

    def start_a(self):
        self.c0.start()
        self.c3.start()

    def start_b(self):
        self.c1.start()
        self.c2.start()

    def start(self):
        self.c0.start()
        self.c1.start()
        self.c3.start()
        self.c2.start()

    def middle(self):
        src, bufs = self.src, self.bufs
        self.c0.wait_recv()
        bufs[6] = (bufs[0].astype(F32) + src[self.right, :, self.a].astype(F32)).astype(BF)
        self.c4.start()
        self.c1.wait_recv()
        bufs[7] = (bufs[1].astype(F32) + src[self.left, :, self.b].astype(F32)).astype(BF)
        self.c5.start()

    def finish(self, put):
        src, bufs = self.src, self.bufs
        self.c3.wait_recv()
        self.c4.wait_recv()
        put(self.a, src[self.me, :, self.a].astype(F32) + bufs[4].astype(F32) + bufs[3].astype(F32))
        self.c2.wait_recv()
        self.c5.wait_recv()
        put(self.b, src[self.me, :, self.b].astype(F32) + bufs[5].astype(F32) + bufs[2].astype(F32))

    def drain(self):
        for copy in (self.c0, self.c1, self.c2, self.c3, self.c4, self.c5):
            copy.wait_send()


class RingGather:
    def __init__(self, buf, send, recv, base, axis):
        self.me = lax.axis_index(axis)
        half = buf.shape[1] // 2
        right, left = lax.rem(self.me + 1, 4), lax.rem(self.me + 3, 4)
        to_right, to_left = {axis: right}, {axis: left}

        def copy(q, h, slot, device):
            piece = buf.at[q, pl.ds(half * h, half)]
            return remote(piece, piece, send.at[base + slot], recv.at[base + slot], device)

        self.r0, self.l1 = copy(self.me, 0, 0, to_right), copy(self.me, 1, 1, to_left)
        self.r1, self.l0 = copy(self.me, 1, 2, to_right), copy(self.me, 0, 3, to_left)
        self.f0, self.f1 = copy(left, 0, 4, to_right), copy(right, 1, 5, to_left)

    def start(self):
        for copy in (self.r0, self.l1, self.r1, self.l0):
            copy.start()

    def middle(self):
        self.r0.wait_recv()
        self.f0.start()
        self.l1.wait_recv()
        self.f1.start()

    def finish(self):
        for copy in (self.r1, self.l0, self.f0, self.f1):
            copy.wait_recv()

    def drain(self):
        for copy in (self.r0, self.l1, self.r1, self.l0, self.f0, self.f1):
            copy.wait_send()


class SeqSum:
    def __init__(self, product, got, first, first_bufs, second, second_bufs, send, recv, base, x_first):
        self.product, self.got, self.first, self.second, self.x_first = product, got, first, second, x_first
        self.core = lax.axis_index("seq_2")
        self.swap = remote(
            product.at[pl.ds(0, 16), 1 - self.core], got, send.at[base], recv.at[base], {"seq_2": 1 - self.core}
        )
        axes = ("seq_0", "seq_1") if x_first else ("seq_1", "seq_0")
        self.one = RingSum(first, first_bufs, send, recv, base + 1, axes[0])
        self.two = RingSum(second, second_bufs, send, recv, base + 7, axes[1])

    def start(self):
        self.swap.start()

    def first_ring(self):
        self.swap.wait_recv()
        for x in range(4):
            for y in range(4):
                at = 4 * x + y
                q, r = (x, y) if self.x_first else (y, x)
                total = self.product[at, self.core].astype(F32) + self.got[at].astype(F32)
                self.first[q, pl.ds(64 * r, 64)] = total.astype(BF)
        self.one.start()

    def second_ring(self):
        def put(cols, value):
            for r in range(4):
                self.second[r, :, cols] = value[64 * r : 64 * (r + 1)].astype(BF)

        self.one.finish(put)
        self.two.start()

    def finish(self, out):
        def put(cols, value):
            out[:, cols] = value

        self.two.finish(put)

    def drain(self):
        self.swap.wait_send()
        self.one.drain()
        self.two.drain()


def greet_all():
    barrier = pltpu.get_barrier_semaphore()
    me, z = seq_index(), lax.axis_index("tensor")

    def greet_seq(k, carry):
        pl.semaphore_signal(barrier, inc=1, device_id=seq_place(lax.rem(me + k, 32)), device_id_type=MESH_ID)
        return carry

    lax.fori_loop(1, 32, greet_seq, 0)
    for k in (1, 2, 3):
        pl.semaphore_signal(barrier, inc=1, device_id={"tensor": lax.rem(z + k, 4)}, device_id_type=MESH_ID)


def all_greeted():
    pl.semaphore_wait(pltpu.get_barrier_semaphore(), 34)


class TotalOfAll:
    def __init__(self, mine, extra, by_z, line, by_seq, total, send, recv, base):
        self.mine, self.extra, self.by_z, self.line, self.by_seq, self.total = mine, extra, by_z, line, by_seq, total
        self.z, self.me = lax.axis_index("tensor"), seq_index()
        self.send, self.recv, self.base = send, recv, base
        peers = [lax.rem(self.z + k, 4) for k in (1, 2, 3)]
        self.split = [
            remote(mine.at[p], by_z.at[self.z], send.at[base + k], recv.at[base + k], {"tensor": p})
            for k, p in enumerate(peers)
        ]
        self.join = [
            remote(total.at[self.z], total.at[self.z], send.at[base + 3 + k], recv.at[base + 3 + k], {"tensor": p})
            for k, p in enumerate(peers)
        ]

    def start(self):
        for copy in self.split:
            copy.start()

    def over_seq(self):
        self.by_z[self.z] = self.mine[self.z]
        for copy in self.split:
            copy.wait_recv()
        self.line[0:8] = (self.by_z[0] + self.by_z[1]) + (self.by_z[2] + self.by_z[3])
        self.line[8:16] = self.extra[...]
        self.by_seq[self.me] = self.line[...]

        def push(k, carry):
            device = seq_place(lax.rem(self.me + k, 32))
            remote(self.line, self.by_seq.at[self.me], self.send.at[self.base + 6], self.recv.at[self.base + 6], device).start()
            return carry

        lax.fori_loop(1, 32, push, 0)

    def over_tensor(self, extra_out):
        others = self.by_seq.at[pl.ds(0, 31)]
        pltpu.make_async_copy(others, others, self.recv.at[self.base + 6]).wait()
        summed = jnp.sum(self.by_seq[...], axis=0)
        self.total[self.z] = summed[0:8]
        extra_out[...] = summed[8:16]
        for copy in self.join:
            copy.start()

    def finish(self):
        for copy in self.join:
            copy.wait_recv()

    def drain(self):
        for copy in (*self.split, *self.join):
            copy.wait_send()
        others = self.by_seq.at[pl.ds(0, 31)]
        pltpu.make_async_copy(others, others, self.send.at[self.base + 6]).wait()


def end_kernel(
    grads_in,
    branch,
    grad_middle,
    gain,
    gain_mlp_grad,
    logits,
    i_mix,
    i_normed_t,
    w_query,
    w_key,
    w_value,
    tokens,
    grad_tokens,
    out_query,
    out_key,
    out_value,
    out_output,
    gains,
    logits_out,
    weights,
    mix,
    normed_t,
    tokens_own,
    turned,
    part,
    part_bufs,
    grad_own,
    products,
    got,
    first,
    first_bufs,
    second,
    second_bufs,
    mine,
    by_z,
    line,
    by_seq,
    moves,
    send,
    recv,
):
    z = lax.axis_index("tensor")
    move = Moves(moves)
    load_mix = move.start(i_mix, mix)
    loads = [move.start(w, weights.at[i]) for i, w in enumerate((w_query, w_key, w_value))]
    load_t = move.start(i_normed_t, normed_t)
    load_own = move.start(tokens.at[pl.ds(pl.multiple_of(96 * z, 96), 96)], tokens_own)
    greet_all()
    z_sum = RingSum(part, part_bufs, send, recv, 0, "tensor")
    z_gather = RingGather(grad_tokens, send, recv, 6, "tensor")
    sums = [
        SeqSum(
            products.at[i], got.at[i], first.at[i], first_bufs.at[i], second.at[i], second_bufs.at[i],
            send, recv, 12 + 13 * i, i % 2 == 0,
        )
        for i in range(4)
    ]
    total = TotalOfAll(mine, logits, by_z, line, by_seq, gains, send, recv, 64)

    def product(i, left, right):
        value = jnp.dot(left, right, preferred_element_type=F32).astype(BF)
        products[i] = value.reshape(16, 2, 64, 512)

    turned[...] = branch[...].reshape(384, 2048).T
    load_mix.wait()
    product(0, turned[...], mix[...])
    all_greeted()
    sums[0].start()
    for copy in loads:
        copy.wait()
    for half in (0, 1):
        rows = pl.ds(1024 * half, 1024)
        value = sum(rows_by_rows(grads_in[:, 512 * i : 512 * (i + 1)], weights[i, rows]) for i in range(3))
        part[:, :, rows] = value.astype(BF).reshape(4, 96, 1024)
        (z_sum.start_a, z_sum.start_b)[half]()
    load_t.wait()
    product(1, normed_t[...], grads_in[:, 0:512])
    sums[1].start()
    sums[0].first_ring()
    product(2, normed_t[...], grads_in[:, 512:1024])
    sums[2].start()
    z_sum.middle()
    sums[1].first_ring()
    product(3, normed_t[...], grads_in[:, 1024:1536])
    sums[3].start()
    sums[2].first_ring()

    def keep(cols, value):
        grad_own[:, cols] = value

    sums[0].one.middle()
    z_sum.finish(keep)
    load_own.wait()
    stream = tokens_own[...].astype(F32)
    inv = lax.rsqrt(jnp.mean(stream * stream, axis=1, keepdims=True) + epsilon)
    grad_normed = grad_own[...]
    weighted = grad_normed * gain[...]
    inner = jnp.sum(weighted * stream, axis=1, keepdims=True)
    scaled = stream * inv
    result = grad_middle[...] + inv * weighted - scaled * (inv * inv * inner * (1.0 / stream.shape[1]))
    grad_tokens[z] = result.astype(BF)
    z_gather.start()
    gain_grad = jnp.sum(grad_normed * scaled, axis=0, keepdims=True)
    for r in range(16):
        mine[r // 8, r % 8 : r % 8 + 1] = gain_grad[:, 128 * r : 128 * (r + 1)]
    mine[2:4] = gain_mlp_grad[...]
    total.start()
    sums[1].one.middle()
    sums[3].first_ring()
    sums[0].second_ring()
    total.over_seq()
    sums[2].one.middle()
    sums[1].second_ring()
    sums[0].two.middle()
    z_gather.middle()
    sums[3].one.middle()
    sums[2].second_ring()
    sums[1].two.middle()
    total.over_tensor(logits_out)
    sums[0].finish(out_output)
    sums[3].second_ring()
    sums[2].two.middle()
    sums[1].finish(out_query)
    sums[3].two.middle()
    sums[2].finish(out_key)
    sums[3].finish(out_value)
    total.finish()
    z_gather.finish()
    z_sum.drain()
    z_gather.drain()
    for s in sums:
        s.drain()
    total.drain()


def end(cid, *args):
    shape = jax.ShapeDtypeStruct
    weight_grad = shape((64, 512), F32)
    low = lambda *dims: pltpu.VMEM(dims, BF)
    full = lambda *dims: pltpu.VMEM(dims, F32)
    return pl.pallas_call(
        end_kernel,
        out_shape=(shape((4, 96, 2048), BF),) + (weight_grad,) * 4 + (shape((4, 8, 128), F32), shape((8, 128), F32)),
        in_specs=[VMEM] * 6 + [ANYWHERE] * 6,
        out_specs=(VMEM,) * 7,
        scratch_shapes=[
            low(3, 2048, 512),
            low(384, 512),
            low(2048, 384),
            low(96, 2048),
            low(2048, 384),
            low(4, 96, 2048),
            low(8, 96, 1024),
            full(96, 2048),
            low(4, 16, 2, 64, 512),
            low(4, 16, 64, 512),
            low(4, 4, 256, 512),
            low(4, 8, 256, 256),
            low(4, 4, 64, 512),
            low(4, 8, 64, 256),
            full(4, 8, 128),
            full(4, 8, 128),
            full(16, 128),
            full(32, 16, 128),
            pltpu.SemaphoreType.DMA((6,)),
            pltpu.SemaphoreType.DMA((71,)),
            pltpu.SemaphoreType.DMA((71,)),
        ],
        name="end",
        compiler_params=params(cid, 56),
    )(*args)


def feature_of(v):
    return jnp.where(v > 0, v + 1.0, jnp.exp(jnp.minimum(v, 0.0)))


def slope_of(v):
    return jnp.where(v > 0, 1.0, jnp.exp(jnp.minimum(v, 0.0)))


ANYWHERE = pl.BlockSpec(memory_space=pl.ANY)


def keep_of(valid):
    length = jnp.where(seq_index() == 31, valid[...], 384)
    return (lax.broadcasted_iota(jnp.int32, (384, 1), 0) < length).astype(F32)


class Moves:
    def __init__(self, sems):
        self.sems, self.count = sems, 0

    def start(self, src, dst):
        copy = pltpu.make_async_copy(src, dst, self.sems.at[self.count])
        self.count += 1
        copy.start()
        return copy


def front_kernel(
    tokens,
    cotangent,
    gain_attn,
    gain_mlp,
    valid,
    gate_logit,
    w_query,
    w_key,
    w_value,
    w_output,
    w_down,
    w_gate,
    w_up,
    o_normed_t,
    o_grad_out_t,
    o_query,
    o_key,
    o_value,
    o_probs,
    o_local_out,
    o_retrieved,
    o_mix,
    o_hidden,
    o_grads,
    grad_out_own,
    offset,
    normal_next,
    memory_prev,
    memory_next,
    ys,
    xs,
    pair_e,
    middle,
    back,
    keep,
    gate,
    weights,
    weight_o,
    weight_d,
    weight_g,
    hidden,
    normed_two,
    normed,
    turned,
    grad_out,
    grad_out_t,
    grad_hidden,
    query,
    key,
    value,
    probs,
    local_out,
    retrieved,
    mix,
    line,
    lines,
    eb,
    source,
    got,
    pair_m,
    got_m,
    part,
    part_bufs,
    moves,
    send,
    recv,
):
    move = Moves(moves)
    loads = [move.start(w, weights.at[i]) for i, w in enumerate((w_key, w_query, w_value))]
    load_o = move.start(w_output, weight_o)
    load_d = [move.start(w_down.at[pl.ds(512 * i, 512)], weight_d.at[pl.ds(512 * i, 512)]) for i in range(4)]
    greet_all()
    keep[...] = keep_of(valid)
    gate[...] = jnp.broadcast_to(jax.nn.sigmoid(gate_logit[...]), (4, 128))
    x, y, c = ring_places()
    z, me = lax.axis_index("tensor"), seq_index()
    partner = {"seq_2": 1 - c}
    mine, theirs = 2 * c, 2 * (1 - c)
    z_sum = RingSum(part, part_bufs, send, recv, 0, "tensor")
    z_gather = RingGather(normed_two, send, recv, 6, "tensor")
    y_ring = RingGather(ys, send, recv, 12, "seq_1")
    x_ring = RingGather(xs, send, recv, 18, "seq_0")
    swap = remote(eb.at[pl.ds(theirs, 2)], got, send.at[24], recv.at[24], partner)
    give = remote(pair_m, got_m, send.at[25], recv.at[25], partner)
    cols = [slice(128 * h, 128 * (h + 1)) for h in range(4)]
    stores = []

    for q in range(4):
        rows = pl.ds(96 * q, 96)
        stream = tokens[rows].astype(F32)
        inv = lax.rsqrt(jnp.mean(stream * stream, axis=1, keepdims=True) + epsilon)
        normed[rows] = (stream * inv * gain_attn[...]).astype(BF)
    loads[0].wait()
    key[...] = jnp.dot(normed[...], weights[0], preferred_element_type=F32).astype(BF)
    feat_q = lambda h: feature_of(query[:, cols[h]].astype(F32))
    feat_k = lambda h: feature_of(key[:, cols[h]].astype(F32))
    line[...] = jnp.zeros_like(line)
    for h in range(4):
        line[h : h + 1] = jnp.sum(feat_k(h) * keep[...], axis=0, keepdims=True)
    lines[me] = line[...]
    all_greeted()

    def push(k, carry):
        remote(line, lines.at[me], send.at[26], recv.at[26], seq_place(lax.rem(me + k, 32))).start()
        return carry

    lax.fori_loop(1, 32, push, 0)
    stores.append(move.start(key, o_key))
    loads[1].wait()
    query[...] = jnp.dot(normed[...], weights[1], preferred_element_type=F32).astype(BF)
    stores.append(move.start(query, o_query))
    loads[2].wait()
    value[...] = jnp.dot(normed[...], weights[2], preferred_element_type=F32).astype(BF)
    stores.append(move.start(value, o_value))
    load_g = move.start(w_gate, weight_g)
    at_row = lax.broadcasted_iota(jnp.int32, (384, 384), 0)
    at_col = lax.broadcasted_iota(jnp.int32, (384, 384), 1)
    valid = jnp.sum(keep[...], axis=0, keepdims=True)
    allowed = (at_row >= at_col) & (at_col.astype(F32) < valid)

    def attend(h):
        at = cols[h]
        scores = rows_by_rows(query[:, at], key[:, at]) * 128 ** (-0.5)
        masked = jnp.where(allowed, scores, -1e30)
        raised = jnp.exp(masked - jnp.max(masked, axis=1, keepdims=True))
        low = (raised * (1.0 / jnp.sum(raised, axis=1, keepdims=True))).astype(BF)
        probs[h] = low
        local_out[:, at] = jnp.dot(low, value[:, at], preferred_element_type=F32)
        total = mul_t(feat_k(h) * keep[...], value[:, at])
        source[h] = total
        eb[h, :, 128:256] = total.astype(BF)

    for h in range(4):
        attend(h)
    stores.append(move.start(probs, o_probs))
    stores.append(move.start(local_out, o_local_out))
    others = lines.at[pl.ds(0, 31)]
    pltpu.make_async_copy(others, others, recv.at[26]).wait()
    passed = lax.broadcasted_iota(jnp.int32, (32, 8, 128), 0) < me
    before = jnp.sum(jnp.where(passed, lines[...], 0.0), axis=0)
    normal_next[...] = before + line[...]
    offset[...] = before + 384.0
    for h in range(4):
        fk = feat_k(h)
        kept = fk * keep[...] * (1.0 / jnp.sum(fk * offset[h : h + 1], axis=1, keepdims=True))
        eb[h, :, 0:128] = mul_t(kept, fk).astype(BF)
    swap.start()
    grad_out[...] = cotangent[...] * keep[...].astype(BF)
    grad_out_own[...] = grad_out[pl.ds(pl.multiple_of(96 * z, 96), 96)]
    swap.wait_recv()
    of = [pl.ds(0, 128), pl.ds(128, 128)]
    firsts = []
    for h in (0, 1):
        here, there = eb[mine + h].astype(F32), got[h].astype(F32)
        first, second = jnp.where(c == 0, here, there), jnp.where(c == 0, there, here)
        firsts.append(first)
        pair_e[0, h] = first[:, :128].astype(BF)
        pair_e[1, h] = second[:, :128].astype(BF)
        ys[y, of[h]] = (first + second - mul(second[:, :128], first)).astype(BF)
    y_ring.start()

    def hidden_part(i):
        load_d[i].wait()
        rows = pl.ds(512 * i, 512)
        product = jnp.dot(grad_out[:, 512 * i : 512 * (i + 1)], weight_d[rows], preferred_element_type=F32)
        if i == 0:
            grad_hidden[...] = product
        else:
            grad_hidden[...] += product

    hidden_part(0)
    y_ring.middle()
    hidden_part(1)
    y_ring.finish()
    starts = []
    for h in (0, 1):
        so_far = ys[0, of[h]].astype(F32)
        start = jnp.where(y > 0, so_far, 0.0)
        for k in (1, 2, 3):
            step = ys[k, of[h]].astype(F32)
            so_far = so_far + step - mul(step[:, :128], so_far)
            if k < 3:
                start = jnp.where(y > k, so_far, start)
        xs[x, of[h]] = so_far.astype(BF)
        starts.append(start)
    x_ring.start()
    hidden_part(2)
    x_ring.middle()
    hidden_part(3)
    load_u = move.start(w_up, weight_d)
    load_o.wait()
    x_ring.finish()
    for h in (0, 1):
        m = jnp.where(x > 0, xs[0, of[h]][:, 128:].astype(F32), 0.0)
        for k in (1, 2):
            step = xs[k, of[h]].astype(F32)
            m = jnp.where(x > k, m + step[:, 128:] - mul(step[:, :128], m), m)
        m = m + starts[h][:, 128:] - mul(starts[h][:, :128], m)
        second = m + firsts[h][:, 128:] - mul(firsts[h][:, :128], m)
        memory_prev[mine + h] = jnp.where(c == 0, m, second)
        pair_m[h] = jnp.where(c == 0, second, m)
    give.start()
    give.wait_recv()
    for h in (0, 1):
        memory_prev[theirs + h] = got_m[h]
    for h in range(4):
        at, fq, sig = cols[h], feat_q(h), gate[h : h + 1]
        inv_q = 1.0 / jnp.sum(fq * offset[h : h + 1], axis=1, keepdims=True)
        found = mul(fq, memory_prev[h]) * inv_q
        retrieved[:, at] = found
        mix[:, at] = (sig * found + (1.0 - sig) * local_out[:, at]).astype(BF)
    for half in (0, 1):
        rows = pl.ds(1024 * half, 1024)
        part[:, :, rows] = rows_by_rows(mix[...], weight_o[rows]).astype(BF).reshape(4, 96, 1024)
        (z_sum.start_a, z_sum.start_b)[half]()
    stores.append(move.start(retrieved, o_retrieved))
    stores.append(move.start(mix, o_mix))
    for h in range(4):
        m = memory_prev[h]
        memory_next[h] = m + source[h] - mul(eb[h][:, :128], m)
    turned[...] = normed[...].T
    stores.append(move.start(turned, o_normed_t))
    z_sum.middle()
    grad_out_t[...] = grad_out[...].T
    stores.append(move.start(grad_out_t, o_grad_out_t))
    own_tokens = tokens[pl.ds(pl.multiple_of(96 * z, 96), 96)].astype(F32)

    def put(at, total):
        lanes = slice(0, 1024) if at is z_sum.a else slice(1024, 2048)
        middle[:, at] = own_tokens[:, lanes] + total

    z_sum.finish(put)
    stream = middle[...]
    inv = lax.rsqrt(jnp.mean(stream * stream, axis=1, keepdims=True) + epsilon)
    normed_two[z] = (stream * inv * gain_mlp[...]).astype(BF)
    z_gather.start()
    z_gather.middle()
    for store in stores:
        store.wait()
    load_g.wait()
    load_u.wait()
    z_gather.finish()
    turned[...] = normed_two[...].reshape(384, 2048).T

    def tile(i, carry):
        lanes = pl.ds(pl.multiple_of(512 * i, 512), 512)
        rows = normed_two[...].reshape(384, 2048)
        gate_pre = jnp.dot(rows, weight_g[:, lanes], preferred_element_type=F32)
        up_pre = jnp.dot(rows, weight_d[:, lanes], preferred_element_type=F32)
        back_hidden = grad_hidden[:, lanes]
        sig = jax.nn.sigmoid(gate_pre)
        swish = gate_pre * sig
        hidden[:, lanes] = (swish * up_pre).astype(BF)
        grad_out[:, lanes] = (back_hidden * swish).astype(BF)
        normed[:, lanes] = (back_hidden * up_pre * sig * (1.0 + gate_pre * (1.0 - sig))).astype(BF)
        return carry

    lax.fori_loop(0, 4, tile, 0)
    stores = [move.start(hidden, o_hidden)]
    slots = []
    for i in range(8):
        if i >= 3:
            slots[i - 3].wait()
        lanes = slice(512 * (i % 4), 512 * (i % 4 + 1))
        side = (normed, grad_out)[i // 4]
        weights[i % 3] = jnp.dot(turned[...], side[:, lanes], preferred_element_type=F32).astype(BF)
        slots.append(move.start(weights.at[i % 3], o_grads.at[:, pl.ds(512 * i, 512)]))
    for i in range(4):
        rows = pl.ds(512 * i, 512)
        value = rows_by_rows(normed[...], weight_g[rows]) + rows_by_rows(grad_out[...], weight_d[rows])
        back[:, :, rows] = value.astype(BF).reshape(4, 96, 512)
    for copy in (*stores, *slots[5:]):
        copy.wait()
    for ring in (z_sum, z_gather, y_ring, x_ring):
        ring.drain()
    swap.wait_send()
    give.wait_send()
    pltpu.make_async_copy(others, others, send.at[26]).wait()


def front(cid, *args):
    shape = jax.ShapeDtypeStruct
    low = lambda *dims: pltpu.VMEM(dims, BF)
    full = lambda *dims: pltpu.VMEM(dims, F32)
    return pl.pallas_call(
        front_kernel,
        out_shape=(
            shape((2048, 384), BF),
            shape((2048, 384), BF),
            shape((384, 512), BF),
            shape((384, 512), BF),
            shape((384, 512), BF),
            shape((4, 384, 384), BF),
            shape((384, 512), F32),
            shape((384, 512), F32),
            shape((384, 512), BF),
            shape((384, 2048), BF),
            shape((2048, 4096), BF),
            shape((96, 2048), BF),
            shape((8, 128), F32),
            shape((8, 128), F32),
            shape((4, 128, 128), F32),
            shape((4, 128, 128), F32),
            shape((4, 256, 256), BF),
            shape((4, 256, 256), BF),
            shape((2, 2, 128, 128), BF),
            shape((96, 2048), F32),
            shape((4, 96, 2048), BF),
        ),
        in_specs=[VMEM] * 6 + [ANYWHERE] * 7,
        out_specs=(ANYWHERE,) * 11 + (VMEM,) * 10,
        scratch_shapes=[
            full(384, 1),
            full(4, 128),
            low(3, 2048, 512),
            low(2048, 512),
            low(2048, 2048),
            low(2048, 2048),
            low(384, 2048),
            low(4, 96, 2048),
            low(384, 2048),
            low(2048, 384),
            low(384, 2048),
            low(2048, 384),
            full(384, 2048),
            low(384, 512),
            low(384, 512),
            low(384, 512),
            low(4, 384, 384),
            full(384, 512),
            full(384, 512),
            low(384, 512),
            full(8, 128),
            full(32, 8, 128),
            low(4, 128, 256),
            full(4, 128, 128),
            low(2, 128, 256),
            full(2, 128, 128),
            full(2, 128, 128),
            low(4, 96, 2048),
            low(8, 96, 1024),
            pltpu.SemaphoreType.DMA((28,)),
            pltpu.SemaphoreType.DMA((27,)),
            pltpu.SemaphoreType.DMA((27,)),
        ],
        name="front",
        compiler_params=params(cid, 62),
    )(*args)


def back_kernel(
    back,
    middle,
    gain,
    grad_out,
    valid,
    offset,
    gate_logit,
    memory,
    ys,
    xs,
    pair_e,
    i_grad_out_t,
    i_hidden,
    i_query,
    i_key,
    i_value,
    i_probs,
    i_local_out,
    i_retrieved,
    w_output,
    w_down,
    layer_out,
    branch,
    grad_middle,
    gain_grad,
    logits,
    grads,
    later,
    out_down,
    keep,
    gate,
    grad_out_t,
    hidden,
    query,
    key,
    value,
    probs,
    local_out,
    retrieved,
    weight,
    weight_d,
    products,
    got_rows,
    first_rows,
    first_bufs,
    second_rows,
    second_bufs,
    forth,
    back_bufs,
    forth_bufs,
    own,
    inverse,
    recall,
    grad_mix,
    grad_query,
    grad_key,
    grad_value,
    source,
    got,
    s_y,
    s_x,
    pair_l,
    got_l,
    adjoint,
    line,
    lines,
    moves,
    send,
    recv,
):
    move = Moves(moves)
    pairs = (
        (i_grad_out_t, grad_out_t),
        (i_hidden, hidden),
        (i_query, query),
        (i_key, key),
        (i_value, value),
        (w_down, weight_d),
        (w_output, weight),
        (i_probs, probs),
        (i_local_out, local_out),
        (i_retrieved, retrieved),
    )
    loads = [move.start(src, dst) for src, dst in pairs]
    greet_all()
    keep[...] = keep_of(valid)
    gate[...] = jnp.broadcast_to(jax.nn.sigmoid(gate_logit[...]), (4, 128))
    x, y, c = ring_places()
    z, me = lax.axis_index("tensor"), seq_index()
    partner = {"seq_2": 1 - c}
    mine, theirs = 2 * c, 2 * (1 - c)
    z_back = RingSum(back, back_bufs, send, recv, 0, "tensor")
    z_branch = RingGather(branch, send, recv, 6, "tensor")
    z_forth = RingSum(forth, forth_bufs, send, recv, 12, "tensor")
    z_layer = RingGather(layer_out, send, recv, 18, "tensor")
    y_ring = RingGather(s_y, send, recv, 24, "seq_1")
    x_ring = RingGather(s_x, send, recv, 30, "seq_0")
    swap = remote(source.at[pl.ds(theirs, 2)], got, send.at[36], recv.at[36], partner)
    give = remote(pair_l, got_l, send.at[37], recv.at[37], partner)
    cols = [slice(128 * h, 128 * (h + 1)) for h in range(4)]
    feat_q = lambda h: feature_of(query[:, cols[h]].astype(F32))
    feat_k = lambda h: feature_of(key[:, cols[h]].astype(F32))
    scale = 128 ** (-0.5)

    def recalled(h):
        fk, off = feat_k(h), offset[h : h + 1]
        inv_k = 1.0 / jnp.sum(fk * off, axis=1, keepdims=True)
        inverse[4 + h] = inv_k
        inverse[h] = 1.0 / jnp.sum(feat_q(h) * off, axis=1, keepdims=True)
        recall[:, cols[h]] = mul(fk, memory[h]) * inv_k

    sums = [
        SeqSum(
            products.at[i], got_rows.at[i], first_rows.at[i], first_bufs.at[i], second_rows.at[i], second_bufs.at[i],
            send, recv, 39 + 13 * i, i % 2 == 0,
        )
        for i in range(4)
    ]

    def product(i):
        lanes = slice(512 * i, 512 * (i + 1))
        result = jnp.dot(grad_out_t[...], hidden[:, lanes], preferred_element_type=F32).astype(BF)
        products[i] = result.reshape(16, 2, 64, 512)
        sums[i].start()

    all_greeted()
    z_back.start()
    for load in loads[:2]:
        load.wait()
    product(0)
    product(1)
    z_back.middle()
    sums[0].first_ring()
    product(2)
    sums[1].first_ring()
    for load in loads[2:5]:
        load.wait()
    recalled(0)
    recalled(1)

    def put(at, total):
        own[:, at] = total

    z_back.finish(put)
    stream = middle[...]
    inv = lax.rsqrt(jnp.mean(stream * stream, axis=1, keepdims=True) + epsilon)
    grad_normed = own[...]
    weighted = grad_normed * gain[...]
    inner = jnp.sum(weighted * stream, axis=1, keepdims=True)
    scaled = stream * inv
    result = grad_out[...].astype(F32) + inv * weighted - scaled * (inv * inv * inner * (1.0 / stream.shape[1]))
    grad_middle[...] = result
    branch[z] = result.astype(BF)
    z_branch.start()
    total = jnp.sum(grad_normed * scaled, axis=0, keepdims=True)
    for r in range(16):
        gain_grad[r // 8, r % 8 : r % 8 + 1] = total[:, 128 * r : 128 * (r + 1)]
    product(3)
    sums[0].one.middle()
    sums[2].first_ring()
    z_branch.middle()
    recalled(2)
    recalled(3)
    sums[1].one.middle()
    loads[5].wait()
    for half in (0, 1):
        rows = pl.ds(1024 * half, 1024)
        forth[:, :, rows] = rows_by_rows(hidden[...], weight_d[rows]).astype(BF).reshape(4, 96, 1024)
    sums[3].first_ring()
    sums[0].second_ring()
    for load in loads[6:]:
        load.wait()
    z_branch.finish()
    z_forth.start()
    grad_mix[...] = jnp.dot(branch[...].reshape(384, 2048), weight[...], preferred_element_type=F32)

    def point(h):
        return gate[h : h + 1] * grad_mix[:, cols[h]] * inverse[h]

    for h in range(4):
        source[h] = mul_t(feat_q(h), point(h)).astype(BF)
    swap.start()

    def attend(h):
        at = cols[h]
        grad_local = ((1.0 - gate[h : h + 1]) * grad_mix[:, at]).astype(BF)
        low = probs[h]
        p = low.astype(F32)
        grad_probs = rows_by_rows(grad_local, value[:, at])
        grad_value[:, at] = mul_t(low, grad_local)
        grad_scores = (p * (grad_probs - jnp.sum(grad_probs * p, axis=1, keepdims=True))).astype(BF)
        grad_query[:, at] = mul(grad_scores, key[:, at]) * scale
        grad_key[:, at] = mul_t(grad_scores, query[:, at]) * scale

    attend(0)
    swap.wait_recv()
    seconds = []
    for h in (0, 1):
        here, there = source[mine + h].astype(F32), got[h].astype(F32)
        first, second = jnp.where(c == 0, here, there), jnp.where(c == 0, there, here)
        seconds.append(second)
        s_y[y, pl.ds(128 * h, 128)] = (first + second - mul_t(pair_e[0, h], second)).astype(BF)
    y_ring.start()
    attend(1)
    y_ring.middle()
    attend(2)
    sums[2].one.middle()
    sums[1].second_ring()
    z_forth.middle()
    y_ring.finish()
    of = [pl.ds(0, 128), pl.ds(128, 128)]
    for h in (0, 1):
        so_far = s_y[3, of[h]].astype(F32)
        for k in (2, 1, 0):
            so_far = s_y[k, of[h]].astype(F32) + so_far - mul_t(ys[k, of[h]][:, :128], so_far)
        s_x[x, of[h]] = so_far.astype(BF)
    x_ring.start()
    attend(3)
    sums[3].one.middle()
    x_ring.middle()
    logit_rows = []
    for h in range(4):
        at, gate_h, g = cols[h], gate[h : h + 1], grad_mix[:, cols[h]]
        ret = retrieved[:, at]
        moved = jnp.sum(g * (ret - local_out[:, at]), axis=0, keepdims=True) * gate_h * (1.0 - gate_h)
        logit_rows.append(jnp.sum(moved, axis=1, keepdims=True))
        grad_den = -jnp.sum(gate_h * g * ret, axis=1, keepdims=True) * inverse[h]
        q = query[:, at].astype(F32)
        grad_feat = rows_by_rows(point(h).astype(BF), memory[h].astype(BF)) + grad_den * offset[h : h + 1]
        grads[:, at] = (grad_query[:, at] + grad_feat * slope_of(q)).astype(BF)
        line[h : h + 1] = jnp.sum(grad_den * feature_of(q), axis=0, keepdims=True)
    lane = lax.broadcasted_iota(jnp.int32, (8, 128), 1)
    row = lax.broadcasted_iota(jnp.int32, (8, 128), 0)
    spot = jnp.zeros((8, 128), F32)
    for h in range(4):
        spot = jnp.where((lane == h) & (row == 0), logit_rows[h], spot)
    logits[...] = spot

    z_forth.finish(put)
    layer_out[z] = (middle[...] + own[...]).astype(BF)
    z_layer.start()
    x_ring.finish()
    for h in (0, 1):
        lam = jnp.where(x < 3, s_x[3, of[h]].astype(F32), 0.0)
        for k in (2, 1):
            lam = jnp.where(x < k, s_x[k, of[h]].astype(F32) + lam - mul_t(xs[k, of[h]][:, :128], lam), lam)
        for k in (3, 2, 1):
            lam = jnp.where(y < k, s_y[k, of[h]].astype(F32) + lam - mul_t(ys[k, of[h]][:, :128], lam), lam)
        first = lam + seconds[h] - mul_t(pair_e[1, h], lam)
        adjoint[mine + h] = jnp.where(c == 0, first, lam).astype(BF)
        pair_l[h] = jnp.where(c == 0, lam, first).astype(BF)
    give.start()
    give.wait_recv()
    for h in (0, 1):
        adjoint[theirs + h] = got_l[h]
    for h in range(4):
        at, fk = cols[h], feat_k(h)
        grad_update = mul(fk * keep[...], adjoint[h])
        grad_den = jnp.sum(grad_update * recall[:, at], axis=1, keepdims=True) * inverse[4 + h]
        line[h : h + 1] += jnp.sum(grad_den * fk, axis=0, keepdims=True)
        grads[:, 1024 + 128 * h : 1152 + 128 * h] = (grad_value[:, at] + grad_update).astype(BF)
        update = value[:, at].astype(F32) - recall[:, at]
        grad_feat = (
            grad_den * offset[h : h + 1]
            + keep[...] * rows_by_rows(update.astype(BF), adjoint[h])
            - rows_by_rows((grad_update * inverse[4 + h]).astype(BF), memory[h].astype(BF))
        )
        grad_key[:, at] += grad_feat * slope_of(key[:, at].astype(F32))
    line[4:8] = jnp.zeros((4, 128), F32)
    lines[me] = line[...]

    def push(k, carry):
        remote(line, lines.at[me], send.at[38], recv.at[38], seq_place(lax.rem(me + k, 32))).start()
        return carry

    lax.fori_loop(1, 32, push, 0)
    z_layer.middle()
    sums[2].second_ring()
    sums[0].two.middle()
    sums[3].second_ring()
    sums[1].two.middle()
    others = lines.at[pl.ds(0, 31)]
    pltpu.make_async_copy(others, others, recv.at[38]).wait()
    passed = lax.broadcasted_iota(jnp.int32, (32, 8, 128), 0) > me
    after = jnp.sum(jnp.where(passed, lines[...], 0.0), axis=0)
    later[...] = after
    for h in range(4):
        at = cols[h]
        rest = keep[...] * after[h : h + 1] * slope_of(key[:, at].astype(F32))
        grads[:, 512 + 128 * h : 640 + 128 * h] = (grad_key[:, at] + rest).astype(BF)
    for i in (2, 3, 0, 1):
        if i > 1:
            sums[i].two.middle()
        sums[i].finish(out_down.at[:, pl.ds(512 * i, 512)])
    z_layer.finish()
    for part in (*sums, z_back, z_branch, z_forth, z_layer, y_ring, x_ring):
        part.drain()
    swap.wait_send()
    give.wait_send()
    pltpu.make_async_copy(others, others, send.at[38]).wait()


def back_pass(cid, *args):
    shape = jax.ShapeDtypeStruct
    low = lambda *dims: pltpu.VMEM(dims, BF)
    full = lambda *dims: pltpu.VMEM(dims, F32)
    return pl.pallas_call(
        back_kernel,
        out_shape=(
            shape((4, 96, 2048), BF),
            shape((4, 96, 2048), BF),
            shape((96, 2048), F32),
            shape((2, 8, 128), F32),
            shape((8, 128), F32),
            shape((384, 1536), BF),
            shape((8, 128), F32),
            shape((64, 2048), F32),
        ),
        in_specs=[VMEM] * 11 + [ANYWHERE] * 10,
        out_specs=(VMEM,) * 8,
        scratch_shapes=[
            full(384, 1),
            full(4, 128),
            low(2048, 384),
            low(384, 2048),
            low(384, 512),
            low(384, 512),
            low(384, 512),
            low(4, 384, 384),
            full(384, 512),
            full(384, 512),
            low(2048, 512),
            low(2048, 2048),
            low(4, 16, 2, 64, 512),
            low(4, 16, 64, 512),
            low(4, 4, 256, 512),
            low(4, 8, 256, 256),
            low(4, 4, 64, 512),
            low(4, 8, 64, 256),
            low(4, 96, 2048),
            low(8, 96, 1024),
            low(8, 96, 1024),
            full(96, 2048),
            full(8, 384, 1),
            full(384, 512),
            full(384, 512),
            full(384, 512),
            full(384, 512),
            full(384, 512),
            low(4, 128, 128),
            low(2, 128, 128),
            low(4, 256, 128),
            low(4, 256, 128),
            low(2, 128, 128),
            low(2, 128, 128),
            low(4, 128, 128),
            full(8, 128),
            full(32, 8, 128),
            pltpu.SemaphoreType.DMA((10,)),
            pltpu.SemaphoreType.DMA((91,)),
            pltpu.SemaphoreType.DMA((91,)),
        ],
        name="back",
        compiler_params=params(cid, 62),
    )(*args)


def last_kernel(*refs):
    ins, outs = refs[:13], refs[13:28]
    wide, gate, up, sems = refs[28:]
    move = Moves(sems)
    copies = []
    grad_tokens, mlp_grads, gains, *same = ins
    o_tokens, o_gate, o_up, o_attn, o_mlp, *o_same = outs
    for src, dst in zip(same, o_same):
        copies.append(move.start(src, dst))
    copies.append(move.start(gains.at[pl.ds(0, 2)], o_attn))
    copies.append(move.start(gains.at[pl.ds(2, 2)], o_mlp))
    for q in range(4):
        wide[q] = grad_tokens[q].astype(F32)
        copies.append(move.start(wide.at[q], o_tokens.at[q]))
    units = gate.shape[1]
    gate[...] = mlp_grads[:, :units].astype(F32)
    copies.append(move.start(gate, o_gate))
    up[...] = mlp_grads[:, units:].astype(F32)
    copies.append(move.start(up, o_up))
    for copy in copies:
        copy.wait()


def last(grad_tokens, mlp_grads, gains, *same):
    shape = jax.ShapeDtypeStruct
    wide = shape((64, mlp_grads.shape[1] // 2), F32)
    gain = shape((2, 8, 128), F32)
    outs = (shape(grad_tokens.shape, F32), wide, wide, gain, gain, *(shape(a.shape, a.dtype) for a in same))
    return pl.pallas_call(
        last_kernel,
        out_shape=outs,
        in_specs=[VMEM] * 13,
        out_specs=(ANYWHERE,) * len(outs),
        scratch_shapes=[
            pltpu.VMEM(grad_tokens.shape, F32),
            pltpu.VMEM(wide.shape, F32),
            pltpu.VMEM(wide.shape, F32),
            pltpu.SemaphoreType.DMA((18,)),
        ],
        name="last",
        compiler_params=pltpu.CompilerParams(vmem_limit_bytes=24 << 20),
    )(grad_tokens, mlp_grads, gains, *same)


def on_device(
    tokens,
    cotangent,
    w_query,
    w_key,
    w_value,
    w_output,
    w_gate,
    w_up,
    w_down,
    gain_attn,
    gain_mlp,
    gate_logit,
    valid_count,
):
    valid, logit = valid_count[None], gate_logit[:, None]
    (
        normed_t, grad_out_t, query, key, value, probs, local_out, retrieved, mix, hidden, mlp_grads,
        grad_out_own, offset, normal_next, memory_prev, memory_next, ys, xs, pair_e, middle, back,
    ) = front(
        0, tokens, cotangent, gain_attn[None], gain_mlp[None], valid, logit, w_query, w_key, w_value, w_output, w_down,
        w_gate, w_up,
    )
    mlp_grads = lax.psum_scatter(mlp_grads, SEQ, scatter_dimension=0, tiled=True)
    layer_out, branch, grad_middle, gain_mlp_grad, logit_grad, grads_in, later_offset, grad_down = back_pass(
        1, back, middle, gain_mlp[None], grad_out_own, valid, offset, logit, memory_prev, ys, xs,
        pair_e, grad_out_t, hidden, query, key, value, probs, local_out, retrieved, w_output, w_down,
    )
    grad_tokens, grad_query, grad_key, grad_value, grad_output, gains, logit_grad = end(
        2, grads_in, branch, grad_middle, gain_attn[None], gain_mlp_grad, logit_grad,
        mix, normed_t, w_query, w_key, w_value, tokens,
    )
    (
        grad_tokens, grad_gate, grad_up, gain_attn_grad, gain_mlp_grad, layer_out, grad_query, grad_key, grad_value,
        grad_output, grad_down, logit_grad, memory_next, normal_next, later_offset,
    ) = last(
        grad_tokens, mlp_grads, gains, layer_out, grad_query, grad_key, grad_value, grad_output, grad_down, logit_grad,
        memory_next, normal_next, later_offset,
    )
    return (
        layer_out.reshape(tokens.shape),
        grad_tokens.reshape(tokens.shape),
        grad_query,
        grad_key,
        grad_value,
        grad_output,
        grad_gate,
        grad_up,
        grad_down,
        gain_attn_grad.reshape(-1),
        gain_mlp_grad.reshape(-1),
        logit_grad[0, :4],
        memory_next[None],
        normal_next[None, :4],
        later_offset[None, :4],
    )


def solution(mesh):
    torus = Mesh(
        mesh.devices.reshape(4, 4, 2, mesh.shape["tensor"]), ("seq_0", "seq_1", "seq_2", "tensor")
    )
    weight = P(None, "tensor")
    grad = P(SEQ, "tensor")
    return jax.shard_map(
        on_device,
        mesh=torus,
        in_specs=(P(SEQ, None), P(SEQ, None)) + (weight,) * 7 + (P(), P(), P("tensor"), P()),
        out_specs=(P(SEQ, None), P(SEQ, None))
        + (grad,) * 7
        + (P(), P(), P("tensor"), P(SEQ, "tensor", None, None), P(SEQ, "tensor", None), P(SEQ, "tensor", None)),
        check_vma=False,
    )
```

```python
import functools

import jax
import jax.numpy as jnp
from jax import lax
from jax.experimental import pallas as pl
from jax.experimental.pallas import tpu as pltpu
from jax.sharding import Mesh
from jax.sharding import PartitionSpec as P

SEQ = ("seq_0", "seq_1", "seq_2")
MESH_ID = pl.DeviceIdType.MESH
VMEM = pl.BlockSpec(memory_space=pltpu.VMEM)
BF = jnp.bfloat16
F32 = jnp.float32

epsilon = 1e-06


def remote(src, dst, send, recv, device):
    return pltpu.make_async_remote_copy(
        src_ref=src, dst_ref=dst, send_sem=send, recv_sem=recv, device_id=device, device_id_type=MESH_ID
    )


def meet(devices):
    barrier = pltpu.get_barrier_semaphore()
    for device in devices:
        pl.semaphore_signal(barrier, inc=1, device_id=device, device_id_type=MESH_ID)
    pl.semaphore_wait(barrier, len(devices))


def params(collective_id, mib):
    return pltpu.CompilerParams(
        collective_id=collective_id, has_side_effects=True, vmem_limit_bytes=mib << 20
    )


def seq_place(index):
    return {"seq_0": index // 8, "seq_1": lax.rem(index // 2, 4), "seq_2": lax.rem(index, 2)}


def seq_index():
    return lax.axis_index("seq_0") * 8 + lax.axis_index("seq_1") * 2 + lax.axis_index("seq_2")


def mul(a, b):
    return jnp.dot(a.astype(BF), b.astype(BF), preferred_element_type=F32)


def mul_t(a, b):
    return lax.dot_general(a.astype(BF), b.astype(BF), (((0,), (0,)), ((), ())), preferred_element_type=F32)


def ring_places():
    x, y, c = (lax.axis_index(a) for a in SEQ)
    return x, y, c


def rows_by_rows(a, b):
    return lax.dot_general(a, b, (((1,), (1,)), ((), ())), preferred_element_type=F32)


class RingSum:
    def __init__(self, src, bufs, send, recv, base, axis):
        self.src, self.bufs, self.me = src, bufs, lax.axis_index(axis)
        half = src.shape[2] // 2
        self.a, self.b = pl.ds(0, half), pl.ds(half, half)
        self.right, self.left = lax.rem(self.me + 1, 4), lax.rem(self.me + 3, 4)
        far = lax.rem(self.me + 2, 4)
        to_right, to_left = {axis: self.right}, {axis: self.left}

        def copy(piece, landing, slot, device):
            return remote(piece, bufs.at[landing], send.at[base + slot], recv.at[base + slot], device)

        rows = pl.ds(0, src.shape[1])
        self.c0 = copy(src.at[far, rows, self.a], 0, 0, to_right)
        self.c1 = copy(src.at[far, rows, self.b], 1, 1, to_left)
        self.c2 = copy(src.at[self.right, rows, self.b], 2, 2, to_right)
        self.c3 = copy(src.at[self.left, rows, self.a], 3, 3, to_left)
        self.c4 = copy(bufs.at[6], 4, 4, to_right)
        self.c5 = copy(bufs.at[7], 5, 5, to_left)

    def start_a(self):
        self.c0.start()
        self.c3.start()

    def start_b(self):
        self.c1.start()
        self.c2.start()

    def start(self):
        self.c0.start()
        self.c1.start()
        self.c3.start()
        self.c2.start()

    def middle(self):
        src, bufs = self.src, self.bufs
        self.c0.wait_recv()
        bufs[6] = (bufs[0].astype(F32) + src[self.right, :, self.a].astype(F32)).astype(BF)
        self.c4.start()
        self.c1.wait_recv()
        bufs[7] = (bufs[1].astype(F32) + src[self.left, :, self.b].astype(F32)).astype(BF)
        self.c5.start()

    def finish(self, put):
        src, bufs = self.src, self.bufs
        self.c3.wait_recv()
        self.c4.wait_recv()
        put(self.a, src[self.me, :, self.a].astype(F32) + bufs[4].astype(F32) + bufs[3].astype(F32))
        self.c2.wait_recv()
        self.c5.wait_recv()
        put(self.b, src[self.me, :, self.b].astype(F32) + bufs[5].astype(F32) + bufs[2].astype(F32))

    def drain(self):
        for copy in (self.c0, self.c1, self.c2, self.c3, self.c4, self.c5):
            copy.wait_send()


class RingGather:
    def __init__(self, buf, send, recv, base, axis):
        self.me = lax.axis_index(axis)
        half = buf.shape[1] // 2
        right, left = lax.rem(self.me + 1, 4), lax.rem(self.me + 3, 4)
        to_right, to_left = {axis: right}, {axis: left}

        def copy(q, h, slot, device):
            piece = buf.at[q, pl.ds(half * h, half)]
            return remote(piece, piece, send.at[base + slot], recv.at[base + slot], device)

        self.r0, self.l1 = copy(self.me, 0, 0, to_right), copy(self.me, 1, 1, to_left)
        self.r1, self.l0 = copy(self.me, 1, 2, to_right), copy(self.me, 0, 3, to_left)
        self.f0, self.f1 = copy(left, 0, 4, to_right), copy(right, 1, 5, to_left)

    def start(self):
        for copy in (self.r0, self.l1, self.r1, self.l0):
            copy.start()

    def middle(self):
        self.r0.wait_recv()
        self.f0.start()
        self.l1.wait_recv()
        self.f1.start()

    def finish(self):
        for copy in (self.r1, self.l0, self.f0, self.f1):
            copy.wait_recv()

    def drain(self):
        for copy in (self.r0, self.l1, self.r1, self.l0, self.f0, self.f1):
            copy.wait_send()


class SeqSum:
    def __init__(self, product, got, first, first_bufs, second, second_bufs, send, recv, base, x_first):
        self.product, self.got, self.first, self.second, self.x_first = product, got, first, second, x_first
        self.core = lax.axis_index("seq_2")
        self.swap = remote(
            product.at[pl.ds(0, 16), 1 - self.core], got, send.at[base], recv.at[base], {"seq_2": 1 - self.core}
        )
        axes = ("seq_0", "seq_1") if x_first else ("seq_1", "seq_0")
        self.one = RingSum(first, first_bufs, send, recv, base + 1, axes[0])
        self.two = RingSum(second, second_bufs, send, recv, base + 7, axes[1])

    def start(self):
        self.swap.start()

    def first_ring(self):
        self.swap.wait_recv()
        for x in range(4):
            for y in range(4):
                at = 4 * x + y
                q, r = (x, y) if self.x_first else (y, x)
                total = self.product[at, self.core].astype(F32) + self.got[at].astype(F32)
                self.first[q, pl.ds(64 * r, 64)] = total.astype(BF)
        self.one.start()

    def second_ring(self):
        def put(cols, value):
            for r in range(4):
                self.second[r, :, cols] = value[64 * r : 64 * (r + 1)].astype(BF)

        self.one.finish(put)
        self.two.start()

    def finish(self, out):
        def put(cols, value):
            out[:, cols] = value

        self.two.finish(put)

    def drain(self):
        self.swap.wait_send()
        self.one.drain()
        self.two.drain()


def greet_all():
    barrier = pltpu.get_barrier_semaphore()
    me, z = seq_index(), lax.axis_index("tensor")

    def greet_seq(k, carry):
        pl.semaphore_signal(barrier, inc=1, device_id=seq_place(lax.rem(me + k, 32)), device_id_type=MESH_ID)
        return carry

    lax.fori_loop(1, 32, greet_seq, 0)
    for k in (1, 2, 3):
        pl.semaphore_signal(barrier, inc=1, device_id={"tensor": lax.rem(z + k, 4)}, device_id_type=MESH_ID)


def all_greeted():
    pl.semaphore_wait(pltpu.get_barrier_semaphore(), 34)


class TotalOfAll:
    def __init__(self, mine, extra, by_z, line, by_seq, total, send, recv, base):
        self.mine, self.extra, self.by_z, self.line, self.by_seq, self.total = mine, extra, by_z, line, by_seq, total
        self.z, self.me = lax.axis_index("tensor"), seq_index()
        self.send, self.recv, self.base = send, recv, base
        peers = [lax.rem(self.z + k, 4) for k in (1, 2, 3)]
        self.split = [
            remote(mine.at[p], by_z.at[self.z], send.at[base + k], recv.at[base + k], {"tensor": p})
            for k, p in enumerate(peers)
        ]
        self.join = [
            remote(total.at[self.z], total.at[self.z], send.at[base + 3 + k], recv.at[base + 3 + k], {"tensor": p})
            for k, p in enumerate(peers)
        ]

    def start(self):
        for copy in self.split:
            copy.start()

    def over_seq(self):
        self.by_z[self.z] = self.mine[self.z]
        for copy in self.split:
            copy.wait_recv()
        self.line[0:8] = (self.by_z[0] + self.by_z[1]) + (self.by_z[2] + self.by_z[3])
        self.line[8:16] = self.extra[...]
        self.by_seq[self.me] = self.line[...]

        def push(k, carry):
            device = seq_place(lax.rem(self.me + k, 32))
            remote(self.line, self.by_seq.at[self.me], self.send.at[self.base + 6], self.recv.at[self.base + 6], device).start()
            return carry

        lax.fori_loop(1, 32, push, 0)

    def over_tensor(self, extra_out):
        others = self.by_seq.at[pl.ds(0, 31)]
        pltpu.make_async_copy(others, others, self.recv.at[self.base + 6]).wait()
        summed = jnp.sum(self.by_seq[...], axis=0)
        self.total[self.z] = summed[0:8]
        extra_out[...] = summed[8:16]
        for copy in self.join:
            copy.start()

    def finish(self):
        for copy in self.join:
            copy.wait_recv()

    def drain(self):
        for copy in (*self.split, *self.join):
            copy.wait_send()
        others = self.by_seq.at[pl.ds(0, 31)]
        pltpu.make_async_copy(others, others, self.send.at[self.base + 6]).wait()


def feature_of(v):
    return jnp.where(v > 0, v + 1.0, jnp.exp(jnp.minimum(v, 0.0)))


def slope_of(v):
    return jnp.where(v > 0, 1.0, jnp.exp(jnp.minimum(v, 0.0)))


ANYWHERE = pl.BlockSpec(memory_space=pl.ANY)


def keep_of(valid):
    length = jnp.where(seq_index() == 31, valid[...], 384)
    return (lax.broadcasted_iota(jnp.int32, (384, 1), 0) < length).astype(F32)


class Moves:
    def __init__(self, sems):
        self.sems, self.count = sems, 0

    def start(self, src, dst):
        copy = pltpu.make_async_copy(src, dst, self.sems.at[self.count])
        self.count += 1
        copy.start()
        return copy


def front_kernel(
    tokens,
    cotangent,
    gain_attn,
    gain_mlp,
    valid,
    gate_logit,
    w_query,
    w_key,
    w_value,
    w_output,
    w_down,
    w_gate,
    w_up,
    o_normed_t,
    o_grad_out_t,
    o_query,
    o_key,
    o_value,
    o_probs,
    o_local_out,
    o_retrieved,
    o_mix,
    o_hidden,
    o_grads,
    grad_out_own,
    offset,
    normal_next,
    memory_prev,
    memory_next,
    ys,
    xs,
    pair_e,
    middle,
    back,
    keep,
    gate,
    weights,
    weight_o,
    weight_d,
    weight_g,
    hidden,
    normed_two,
    normed,
    turned,
    grad_out,
    grad_out_t,
    grad_hidden,
    query,
    key,
    value,
    probs,
    local_out,
    retrieved,
    mix,
    line,
    lines,
    eb,
    source,
    got,
    pair_m,
    got_m,
    part,
    part_bufs,
    moves,
    send,
    recv,
):
    move = Moves(moves)
    loads = [move.start(w, weights.at[i]) for i, w in enumerate((w_key, w_query, w_value))]
    load_o = move.start(w_output, weight_o)
    load_d = [move.start(w_down.at[pl.ds(512 * i, 512)], weight_d.at[pl.ds(512 * i, 512)]) for i in range(4)]
    greet_all()
    keep[...] = keep_of(valid)
    gate[...] = jnp.broadcast_to(jax.nn.sigmoid(gate_logit[...]), (4, 128))
    x, y, c = ring_places()
    z, me = lax.axis_index("tensor"), seq_index()
    partner = {"seq_2": 1 - c}
    mine, theirs = 2 * c, 2 * (1 - c)
    z_sum = RingSum(part, part_bufs, send, recv, 0, "tensor")
    z_gather = RingGather(normed_two, send, recv, 6, "tensor")
    y_ring = RingGather(ys, send, recv, 12, "seq_1")
    x_ring = RingGather(xs, send, recv, 18, "seq_0")
    swap = remote(eb.at[pl.ds(theirs, 2)], got, send.at[24], recv.at[24], partner)
    give = remote(pair_m, got_m, send.at[25], recv.at[25], partner)
    cols = [slice(128 * h, 128 * (h + 1)) for h in range(4)]
    stores = []

    for q in range(4):
        rows = pl.ds(96 * q, 96)
        stream = tokens[rows].astype(F32)
        inv = lax.rsqrt(jnp.mean(stream * stream, axis=1, keepdims=True) + epsilon)
        normed[rows] = (stream * inv * gain_attn[...]).astype(BF)
    loads[0].wait()
    key[...] = jnp.dot(normed[...], weights[0], preferred_element_type=F32).astype(BF)
    feat_q = lambda h: feature_of(query[:, cols[h]].astype(F32))
    feat_k = lambda h: feature_of(key[:, cols[h]].astype(F32))
    line[...] = jnp.zeros_like(line)
    for h in range(4):
        line[h : h + 1] = jnp.sum(feat_k(h) * keep[...], axis=0, keepdims=True)
    lines[me] = line[...]
    all_greeted()

    def push(k, carry):
        remote(line, lines.at[me], send.at[26], recv.at[26], seq_place(lax.rem(me + k, 32))).start()
        return carry

    lax.fori_loop(1, 32, push, 0)
    stores.append(move.start(key, o_key))
    loads[1].wait()
    query[...] = jnp.dot(normed[...], weights[1], preferred_element_type=F32).astype(BF)
    stores.append(move.start(query, o_query))
    loads[2].wait()
    value[...] = jnp.dot(normed[...], weights[2], preferred_element_type=F32).astype(BF)
    stores.append(move.start(value, o_value))
    load_g = move.start(w_gate, weight_g)
    at_row = lax.broadcasted_iota(jnp.int32, (384, 384), 0)
    at_col = lax.broadcasted_iota(jnp.int32, (384, 384), 1)
    valid = jnp.sum(keep[...], axis=0, keepdims=True)
    allowed = (at_row >= at_col) & (at_col.astype(F32) < valid)

    def attend(h):
        at = cols[h]
        scores = rows_by_rows(query[:, at], key[:, at]) * 128 ** (-0.5)
        masked = jnp.where(allowed, scores, -1e30)
        raised = jnp.exp(masked - jnp.max(masked, axis=1, keepdims=True))
        low = (raised * (1.0 / jnp.sum(raised, axis=1, keepdims=True))).astype(BF)
        probs[h] = low
        local_out[:, at] = jnp.dot(low, value[:, at], preferred_element_type=F32)
        total = mul_t(feat_k(h) * keep[...], value[:, at])
        source[h] = total
        eb[h, :, 128:256] = total.astype(BF)

    for h in range(4):
        attend(h)
    stores.append(move.start(probs, o_probs))
    stores.append(move.start(local_out, o_local_out))
    others = lines.at[pl.ds(0, 31)]
    pltpu.make_async_copy(others, others, recv.at[26]).wait()
    passed = lax.broadcasted_iota(jnp.int32, (32, 8, 128), 0) < me
    before = jnp.sum(jnp.where(passed, lines[...], 0.0), axis=0)
    normal_next[...] = before + line[...]
    offset[...] = before + 384.0
    for h in range(4):
        fk = feat_k(h)
        kept = fk * keep[...] * (1.0 / jnp.sum(fk * offset[h : h + 1], axis=1, keepdims=True))
        eb[h, :, 0:128] = mul_t(kept, fk).astype(BF)
    swap.start()
    grad_out[...] = cotangent[...] * keep[...].astype(BF)
    grad_out_own[...] = grad_out[pl.ds(pl.multiple_of(96 * z, 96), 96)]
    swap.wait_recv()
    of = [pl.ds(0, 128), pl.ds(128, 128)]
    firsts = []
    for h in (0, 1):
        here, there = eb[mine + h].astype(F32), got[h].astype(F32)
        first, second = jnp.where(c == 0, here, there), jnp.where(c == 0, there, here)
        firsts.append(first)
        pair_e[0, h] = first[:, :128].astype(BF)
        pair_e[1, h] = second[:, :128].astype(BF)
        ys[y, of[h]] = (first + second - mul(second[:, :128], first)).astype(BF)
    y_ring.start()

    def hidden_part(i):
        load_d[i].wait()
        rows = pl.ds(512 * i, 512)
        product = jnp.dot(grad_out[:, 512 * i : 512 * (i + 1)], weight_d[rows], preferred_element_type=F32)
        if i == 0:
            grad_hidden[...] = product
        else:
            grad_hidden[...] += product

    hidden_part(0)
    y_ring.middle()
    hidden_part(1)
    y_ring.finish()
    starts = []
    for h in (0, 1):
        so_far = ys[0, of[h]].astype(F32)
        start = jnp.where(y > 0, so_far, 0.0)
        for k in (1, 2, 3):
            step = ys[k, of[h]].astype(F32)
            so_far = so_far + step - mul(step[:, :128], so_far)
            if k < 3:
                start = jnp.where(y > k, so_far, start)
        xs[x, of[h]] = so_far.astype(BF)
        starts.append(start)
    x_ring.start()
    hidden_part(2)
    x_ring.middle()
    hidden_part(3)
    load_u = move.start(w_up, weight_d)
    load_o.wait()
    x_ring.finish()
    for h in (0, 1):
        m = jnp.where(x > 0, xs[0, of[h]][:, 128:].astype(F32), 0.0)
        for k in (1, 2):
            step = xs[k, of[h]].astype(F32)
            m = jnp.where(x > k, m + step[:, 128:] - mul(step[:, :128], m), m)
        m = m + starts[h][:, 128:] - mul(starts[h][:, :128], m)
        second = m + firsts[h][:, 128:] - mul(firsts[h][:, :128], m)
        memory_prev[mine + h] = jnp.where(c == 0, m, second)
        pair_m[h] = jnp.where(c == 0, second, m)
    give.start()
    give.wait_recv()
    for h in (0, 1):
        memory_prev[theirs + h] = got_m[h]
    for h in range(4):
        at, fq, sig = cols[h], feat_q(h), gate[h : h + 1]
        inv_q = 1.0 / jnp.sum(fq * offset[h : h + 1], axis=1, keepdims=True)
        found = mul(fq, memory_prev[h]) * inv_q
        retrieved[:, at] = found
        mix[:, at] = (sig * found + (1.0 - sig) * local_out[:, at]).astype(BF)
    for half in (0, 1):
        rows = pl.ds(1024 * half, 1024)
        part[:, :, rows] = rows_by_rows(mix[...], weight_o[rows]).astype(BF).reshape(4, 96, 1024)
        (z_sum.start_a, z_sum.start_b)[half]()
    stores.append(move.start(retrieved, o_retrieved))
    stores.append(move.start(mix, o_mix))
    for h in range(4):
        m = memory_prev[h]
        memory_next[h] = m + source[h] - mul(eb[h][:, :128], m)
    turned[...] = normed[...].T
    stores.append(move.start(turned, o_normed_t))
    z_sum.middle()
    grad_out_t[...] = grad_out[...].T
    stores.append(move.start(grad_out_t, o_grad_out_t))
    own_tokens = tokens[pl.ds(pl.multiple_of(96 * z, 96), 96)].astype(F32)

    def put(at, total):
        lanes = slice(0, 1024) if at is z_sum.a else slice(1024, 2048)
        middle[:, at] = own_tokens[:, lanes] + total

    z_sum.finish(put)
    stream = middle[...]
    inv = lax.rsqrt(jnp.mean(stream * stream, axis=1, keepdims=True) + epsilon)
    normed_two[z] = (stream * inv * gain_mlp[...]).astype(BF)
    z_gather.start()
    z_gather.middle()
    for store in stores:
        store.wait()
    load_g.wait()
    load_u.wait()
    z_gather.finish()
    turned[...] = normed_two[...].reshape(384, 2048).T

    def tile(i, carry):
        lanes = pl.ds(pl.multiple_of(512 * i, 512), 512)
        rows = normed_two[...].reshape(384, 2048)
        gate_pre = jnp.dot(rows, weight_g[:, lanes], preferred_element_type=F32)
        up_pre = jnp.dot(rows, weight_d[:, lanes], preferred_element_type=F32)
        back_hidden = grad_hidden[:, lanes]
        sig = jax.nn.sigmoid(gate_pre)
        swish = gate_pre * sig
        hidden[:, lanes] = (swish * up_pre).astype(BF)
        grad_out[:, lanes] = (back_hidden * swish).astype(BF)
        normed[:, lanes] = (back_hidden * up_pre * sig * (1.0 + gate_pre * (1.0 - sig))).astype(BF)
        return carry

    lax.fori_loop(0, 4, tile, 0)
    stores = [move.start(hidden, o_hidden)]
    slots = []
    for i in range(8):
        if i >= 3:
            slots[i - 3].wait()
        lanes = slice(512 * (i % 4), 512 * (i % 4 + 1))
        side = (normed, grad_out)[i // 4]
        weights[i % 3] = jnp.dot(turned[...], side[:, lanes], preferred_element_type=F32).astype(BF)
        slots.append(move.start(weights.at[i % 3], o_grads.at[:, pl.ds(512 * i, 512)]))
    for i in range(4):
        rows = pl.ds(512 * i, 512)
        value = rows_by_rows(normed[...], weight_g[rows]) + rows_by_rows(grad_out[...], weight_d[rows])
        back[:, :, rows] = value.astype(BF).reshape(4, 96, 512)
    for copy in (*stores, *slots[5:]):
        copy.wait()
    for ring in (z_sum, z_gather, y_ring, x_ring):
        ring.drain()
    swap.wait_send()
    give.wait_send()
    pltpu.make_async_copy(others, others, send.at[26]).wait()


def front(cid, *args):
    shape = jax.ShapeDtypeStruct
    low = lambda *dims: pltpu.VMEM(dims, BF)
    full = lambda *dims: pltpu.VMEM(dims, F32)
    return pl.pallas_call(
        front_kernel,
        out_shape=(
            shape((2048, 384), BF),
            shape((2048, 384), BF),
            shape((384, 512), BF),
            shape((384, 512), BF),
            shape((384, 512), BF),
            shape((4, 384, 384), BF),
            shape((384, 512), F32),
            shape((384, 512), F32),
            shape((384, 512), BF),
            shape((384, 2048), BF),
            shape((2048, 4096), BF),
            shape((96, 2048), BF),
            shape((8, 128), F32),
            shape((8, 128), F32),
            shape((4, 128, 128), F32),
            shape((4, 128, 128), F32),
            shape((4, 256, 256), BF),
            shape((4, 256, 256), BF),
            shape((2, 2, 128, 128), BF),
            shape((96, 2048), F32),
            shape((4, 96, 2048), BF),
        ),
        in_specs=[VMEM] * 6 + [ANYWHERE] * 7,
        out_specs=(ANYWHERE,) * 11 + (VMEM,) * 10,
        scratch_shapes=[
            full(384, 1),
            full(4, 128),
            low(3, 2048, 512),
            low(2048, 512),
            low(2048, 2048),
            low(2048, 2048),
            low(384, 2048),
            low(4, 96, 2048),
            low(384, 2048),
            low(2048, 384),
            low(384, 2048),
            low(2048, 384),
            full(384, 2048),
            low(384, 512),
            low(384, 512),
            low(384, 512),
            low(4, 384, 384),
            full(384, 512),
            full(384, 512),
            low(384, 512),
            full(8, 128),
            full(32, 8, 128),
            low(4, 128, 256),
            full(4, 128, 128),
            low(2, 128, 256),
            full(2, 128, 128),
            full(2, 128, 128),
            low(4, 96, 2048),
            low(8, 96, 1024),
            pltpu.SemaphoreType.DMA((28,)),
            pltpu.SemaphoreType.DMA((27,)),
            pltpu.SemaphoreType.DMA((27,)),
        ],
        name="front",
        compiler_params=params(cid, 62),
    )(*args)


def neighbours():
    x, y, c = ring_places()
    z = lax.axis_index("tensor")
    near = [{"seq_2": 1 - c}]
    for axis, at in (("seq_0", x), ("seq_1", y), ("tensor", z)):
        near += [{axis: lax.rem(at + 1, 4)}, {axis: lax.rem(at + 3, 4)}]
    return near


def rest_kernel(
    back,
    middle,
    gain_attn,
    gain_mlp,
    grad_out,
    valid,
    offset,
    gate_logit,
    memory,
    ys,
    xs,
    pair_e,
    i_grad_out_t,
    i_hidden,
    i_query,
    i_key,
    i_value,
    i_probs,
    i_local_out,
    i_retrieved,
    i_mix,
    i_normed_t,
    w_query,
    w_key,
    w_value,
    w_output,
    w_down,
    tokens,
    layer_out,
    grad_tokens,
    later,
    out_down,
    out_query,
    out_key,
    out_value,
    out_output,
    gains,
    logits_out,
    keep,
    gate,
    branch,
    grad_middle,
    grads,
    left,
    hidden,
    query,
    key,
    value,
    probs,
    local_out,
    retrieved,
    mix,
    tokens_own,
    weight_o,
    weight_d,
    products,
    got_rows,
    first_rows,
    first_bufs,
    second_rows,
    second_bufs,
    forth,
    z_bufs,
    own,
    inverse,
    recall,
    grad_mix,
    grad_query,
    grad_key,
    grad_value,
    source,
    got,
    s_y,
    s_x,
    pair_l,
    got_l,
    adjoint,
    line,
    lines,
    mine_gains,
    logits,
    by_z,
    total_line,
    by_seq,
    moves,
    send,
    recv,
):
    x, y, c = ring_places()
    z, me = lax.axis_index("tensor"), seq_index()
    move = Moves(moves)
    pairs = (
        (i_grad_out_t, left),
        (i_hidden, hidden),
        (i_query, query),
        (i_key, key),
        (i_value, value),
        (w_down, weight_d),
        (w_output, weight_o),
        (i_probs, probs),
        (i_local_out, local_out),
        (i_retrieved, retrieved),
        (i_mix, mix),
        (tokens.at[pl.ds(pl.multiple_of(96 * z, 96), 96)], tokens_own),
    )
    barrier = pltpu.get_barrier_semaphore()
    for device in neighbours():
        pl.semaphore_signal(barrier, inc=1, device_id=device, device_id_type=MESH_ID)
    loads = [move.start(src, dst) for src, dst in pairs]
    keep[...] = keep_of(valid)
    gate[...] = jnp.broadcast_to(jax.nn.sigmoid(gate_logit[...]), (4, 128))
    partner = {"seq_2": 1 - c}
    mine, theirs = 2 * c, 2 * (1 - c)
    z_back = RingSum(back, z_bufs, send, recv, 0, "tensor")
    z_branch = RingGather(branch, send, recv, 6, "tensor")
    z_forth = RingSum(forth, z_bufs, send, recv, 12, "tensor")
    z_layer = RingGather(layer_out, send, recv, 18, "tensor")
    y_ring = RingGather(s_y, send, recv, 24, "seq_1")
    x_ring = RingGather(s_x, send, recv, 30, "seq_0")
    swap = remote(source.at[pl.ds(theirs, 2)], got, send.at[36], recv.at[36], partner)
    give = remote(pair_l, got_l, send.at[37], recv.at[37], partner)
    z_end = RingSum(forth, z_bufs, send, recv, 143, "tensor")
    z_tokens = RingGather(grad_tokens, send, recv, 149, "tensor")
    total = TotalOfAll(mine_gains, logits, by_z, total_line, by_seq, gains, send, recv, 155)

    def seq_sums(base):
        return [
            SeqSum(
                products.at[i], got_rows.at[i], first_rows.at[i], first_bufs.at[i], second_rows.at[i],
                second_bufs.at[i], send, recv, base + 13 * i, i % 2 == 0,
            )
            for i in range(4)
        ]

    sums, ends = seq_sums(39), seq_sums(91)
    cols = [slice(128 * h, 128 * (h + 1)) for h in range(4)]
    of = [pl.ds(0, 128), pl.ds(128, 128)]
    feat_q = lambda h: feature_of(query[:, cols[h]].astype(F32))
    feat_k = lambda h: feature_of(key[:, cols[h]].astype(F32))
    scale = 128 ** (-0.5)

    def recalled(h):
        fk, off = feat_k(h), offset[h : h + 1]
        inv_k = 1.0 / jnp.sum(fk * off, axis=1, keepdims=True)
        inverse[:, 4 + h : 5 + h] = inv_k
        inverse[:, h : h + 1] = 1.0 / jnp.sum(feat_q(h) * off, axis=1, keepdims=True)
        recall[:, cols[h]] = mul(fk, memory[h]) * inv_k

    def product(group, i, right):
        result = jnp.dot(left[...], right, preferred_element_type=F32).astype(BF)
        products[i] = result.reshape(16, 2, 64, 512)
        group[i].start()

    def down(i):
        product(sums, i, hidden[:, 512 * i : 512 * (i + 1)])

    def put(at, result):
        own[:, at] = result

    def norm_back(stream, gain, first_row):
        inv = lax.rsqrt(jnp.mean(stream * stream, axis=1, keepdims=True) + epsilon)
        grad_normed = own[...]
        weighted = grad_normed * gain[...]
        inner = jnp.sum(weighted * stream, axis=1, keepdims=True)
        scaled = stream * inv
        line_of = jnp.sum(grad_normed * scaled, axis=0, keepdims=True)
        for r in range(16):
            mine_gains[first_row + r // 8, r % 8 : r % 8 + 1] = line_of[:, 128 * r : 128 * (r + 1)]
        return inv * weighted - scaled * (inv * inv * inner * (1.0 / stream.shape[1]))

    pl.semaphore_wait(barrier, 7)
    z_back.start()
    loads[0].wait()
    loads[1].wait()
    down(0)
    down(1)
    z_back.middle()
    sums[0].first_ring()
    down(2)
    sums[1].first_ring()
    down(3)
    z_back.finish(put)
    result = grad_out[...].astype(F32) + norm_back(middle[...], gain_mlp, 2)
    grad_middle[...] = result
    branch[z] = result.astype(BF)
    z_branch.start()
    sums[2].first_ring()
    sums[0].one.middle()
    for load in loads[2:6]:
        load.wait()
    recalled(0)
    recalled(1)
    sums[3].first_ring()
    z_branch.middle()
    sums[1].one.middle()
    recalled(2)
    recalled(3)
    sums[0].second_ring()
    for half in (0, 1):
        rows = pl.ds(1024 * half, 1024)
        forth[:, :, rows] = rows_by_rows(hidden[...], weight_d[rows]).astype(BF).reshape(4, 96, 1024)
    sums[2].one.middle()
    sums[1].second_ring()
    loads += [
        move.start(w, weight_d.at[:, pl.ds(512 * i, 512)]) for i, w in enumerate((w_query, w_key, w_value))
    ]
    for load in loads[6:12]:
        load.wait()
    z_branch.finish()
    z_back.drain()
    z_forth.start()
    grad_mix[...] = jnp.dot(branch[...].reshape(384, 2048), weight_o[...], preferred_element_type=F32)

    def point(h):
        return gate[h : h + 1] * grad_mix[:, cols[h]] * inverse[:, h : h + 1]

    for h in range(4):
        source[h] = mul_t(feat_q(h), point(h)).astype(BF)
    swap.start()

    def attend(h):
        at = cols[h]
        grad_local = ((1.0 - gate[h : h + 1]) * grad_mix[:, at]).astype(BF)
        low = probs[h]
        p = low.astype(F32)
        grad_probs = rows_by_rows(grad_local, value[:, at])
        grad_value[:, at] = mul_t(low, grad_local)
        grad_scores = (p * (grad_probs - jnp.sum(grad_probs * p, axis=1, keepdims=True))).astype(BF)
        grad_query[:, at] = mul(grad_scores, key[:, at]) * scale
        grad_key[:, at] = mul_t(grad_scores, query[:, at]) * scale

    sums[0].two.middle()
    sums[3].one.middle()
    attend(0)
    sums[2].second_ring()
    sums[1].two.middle()
    swap.wait_recv()
    seconds = []
    for h in (0, 1):
        here, there = source[mine + h].astype(F32), got[h].astype(F32)
        first, second = jnp.where(c == 0, here, there), jnp.where(c == 0, there, here)
        seconds.append(second)
        s_y[y, of[h]] = (first + second - mul_t(pair_e[0, h], second)).astype(BF)
    sums[3].second_ring()
    y_ring.start()
    attend(1)
    y_ring.middle()
    attend(2)
    z_forth.middle()
    for s in sums:
        s.swap.wait_send()
        s.one.drain()
    left[...] = branch[...].reshape(384, 2048).T
    y_ring.finish()
    for h in (0, 1):
        so_far = s_y[3, of[h]].astype(F32)
        for k in (2, 1, 0):
            so_far = s_y[k, of[h]].astype(F32) + so_far - mul_t(ys[k, of[h]][:, :128], so_far)
        s_x[x, of[h]] = so_far.astype(BF)
    x_ring.start()
    product(ends, 0, mix[...])
    x_ring.middle()
    load_t = move.start(i_normed_t, left)
    attend(3)
    logit_rows = []
    for h in range(4):
        at, gate_h, g = cols[h], gate[h : h + 1], grad_mix[:, cols[h]]
        ret = retrieved[:, at]
        moved = jnp.sum(g * (ret - local_out[:, at]), axis=0, keepdims=True) * gate_h * (1.0 - gate_h)
        logit_rows.append(jnp.sum(moved, axis=1, keepdims=True))
        grad_den = -jnp.sum(gate_h * g * ret, axis=1, keepdims=True) * inverse[:, h : h + 1]
        q = query[:, at].astype(F32)
        grad_feat = rows_by_rows(point(h).astype(BF), memory[h].astype(BF)) + grad_den * offset[h : h + 1]
        grads[:, at] = (grad_query[:, at] + grad_feat * slope_of(q)).astype(BF)
        line[h : h + 1] = jnp.sum(grad_den * feature_of(q), axis=0, keepdims=True)
    lane = lax.broadcasted_iota(jnp.int32, (8, 128), 1)
    row = lax.broadcasted_iota(jnp.int32, (8, 128), 0)
    spot = jnp.zeros((8, 128), F32)
    for h in range(4):
        spot = jnp.where((lane == h) & (row == 0), logit_rows[h], spot)
    logits[...] = spot
    z_forth.finish(put)
    layer_out[z] = (middle[...] + own[...]).astype(BF)
    z_layer.start()
    sums[2].two.middle()
    sums[3].two.middle()
    x_ring.finish()
    for h in (0, 1):
        lam = jnp.where(x < 3, s_x[3, of[h]].astype(F32), 0.0)
        for k in (2, 1):
            lam = jnp.where(x < k, s_x[k, of[h]].astype(F32) + lam - mul_t(xs[k, of[h]][:, :128], lam), lam)
        for k in (3, 2, 1):
            lam = jnp.where(y < k, s_y[k, of[h]].astype(F32) + lam - mul_t(ys[k, of[h]][:, :128], lam), lam)
        first = lam + seconds[h] - mul_t(pair_e[1, h], lam)
        adjoint[mine + h] = jnp.where(c == 0, first, lam).astype(BF)
        pair_l[h] = jnp.where(c == 0, lam, first).astype(BF)
    give.start()
    for i in range(4):
        sums[i].finish(out_down.at[:, pl.ds(512 * i, 512)])
    give.wait_recv()
    for h in (0, 1):
        adjoint[theirs + h] = got_l[h]
    for h in range(4):
        at, fk = cols[h], feat_k(h)
        grad_update = mul(fk * keep[...], adjoint[h])
        grad_value[:, at] += grad_update
        grad_den = jnp.sum(grad_update * recall[:, at], axis=1, keepdims=True) * inverse[:, 4 + h : 5 + h]
        line[h : h + 1] += jnp.sum(grad_den * fk, axis=0, keepdims=True)
        grad_key[:, at] += slope_of(key[:, at].astype(F32)) * (
            grad_den * offset[h : h + 1]
            - rows_by_rows((grad_update * inverse[:, 4 + h : 5 + h]).astype(BF), memory[h].astype(BF))
        )
    line[4:8] = jnp.zeros((4, 128), F32)
    lines[me] = line[...]

    def push(k, carry):
        remote(line, lines.at[me], send.at[38], recv.at[38], seq_place(lax.rem(me + k, 32))).start()
        return carry

    lax.fori_loop(1, 32, push, 0)
    for h in range(4):
        at = cols[h]
        grads[:, 1024 + 128 * h : 1152 + 128 * h] = grad_value[:, at].astype(BF)
        update = value[:, at].astype(F32) - recall[:, at]
        grad_key[:, at] += (
            keep[...] * slope_of(key[:, at].astype(F32)) * rows_by_rows(update.astype(BF), adjoint[h])
        )
    ends[0].first_ring()
    load_t.wait()
    product(ends, 1, grads[:, 0:512])
    z_layer.middle()
    product(ends, 3, grads[:, 1024:1536])
    for s in sums:
        s.two.drain()
    z_forth.drain()
    for load in loads[12:]:
        load.wait()
    others = lines.at[pl.ds(0, 31)]
    pltpu.make_async_copy(others, others, recv.at[38]).wait()
    passed = lax.broadcasted_iota(jnp.int32, (32, 8, 128), 0) > me
    after = jnp.sum(jnp.where(passed, lines[...], 0.0), axis=0)
    later[...] = after
    for h in range(4):
        at = cols[h]
        late = keep[...] * after[h : h + 1] * slope_of(key[:, at].astype(F32))
        grads[:, 512 + 128 * h : 640 + 128 * h] = (grad_key[:, at] + late).astype(BF)
    z_layer.finish()
    for half in (0, 1):
        rows = pl.ds(1024 * half, 1024)
        forth[:, :, rows] = rows_by_rows(grads[...], weight_d[rows, 0:1536]).astype(BF).reshape(4, 96, 1024)
        (z_end.start_a, z_end.start_b)[half]()
    ends[1].first_ring()
    product(ends, 2, grads[:, 512:1024])
    ends[0].one.middle()
    z_end.middle()
    ends[3].first_ring()
    ends[1].one.middle()
    ends[2].first_ring()
    ends[0].second_ring()
    z_end.finish(put)
    result = grad_middle[...] + norm_back(tokens_own[...].astype(F32), gain_attn, 0)
    grad_tokens[z] = result.astype(BF)
    z_tokens.start()
    total.start()
    ends[3].one.middle()
    ends[1].second_ring()
    total.over_seq()
    ends[2].one.middle()
    ends[0].two.middle()
    z_tokens.middle()
    ends[3].second_ring()
    ends[1].two.middle()
    total.over_tensor(logits_out)
    ends[2].second_ring()
    ends[0].finish(out_output)
    ends[3].two.middle()
    ends[1].finish(out_query)
    ends[2].two.middle()
    ends[3].finish(out_value)
    ends[2].finish(out_key)
    total.finish()
    z_tokens.finish()
    for part in (z_branch, z_layer, y_ring, x_ring, z_end, z_tokens, total, *ends):
        part.drain()
    swap.wait_send()
    give.wait_send()
    pltpu.make_async_copy(others, others, send.at[38]).wait()


def rest(cid, *args):
    shape = jax.ShapeDtypeStruct
    low = lambda *dims: pltpu.VMEM(dims, BF)
    full = lambda *dims: pltpu.VMEM(dims, F32)
    weight_grad = shape((64, 512), F32)
    return pl.pallas_call(
        rest_kernel,
        out_shape=(
            shape((4, 96, 2048), BF),
            shape((4, 96, 2048), BF),
            shape((8, 128), F32),
            shape((64, 2048), F32),
            weight_grad,
            weight_grad,
            weight_grad,
            weight_grad,
            shape((4, 8, 128), F32),
            shape((8, 128), F32),
        ),
        in_specs=[VMEM] * 12 + [ANYWHERE] * 16,
        out_specs=(VMEM,) * 10,
        scratch_shapes=[
            full(384, 1),
            full(4, 128),
            low(4, 96, 2048),
            full(96, 2048),
            low(384, 1536),
            low(2048, 384),
            low(384, 2048),
            low(384, 512),
            low(384, 512),
            low(384, 512),
            low(4, 384, 384),
            full(384, 512),
            full(384, 512),
            low(384, 512),
            low(96, 2048),
            low(2048, 512),
            low(2048, 2048),
            low(4, 16, 2, 64, 512),
            low(4, 16, 64, 512),
            low(4, 4, 256, 512),
            low(4, 8, 256, 256),
            low(4, 4, 64, 512),
            low(4, 8, 64, 256),
            low(4, 96, 2048),
            low(8, 96, 1024),
            full(96, 2048),
            full(384, 128),
            full(384, 512),
            full(384, 512),
            full(384, 512),
            full(384, 512),
            full(384, 512),
            low(4, 128, 128),
            low(2, 128, 128),
            low(4, 256, 128),
            low(4, 256, 128),
            low(2, 128, 128),
            low(2, 128, 128),
            low(4, 128, 128),
            full(8, 128),
            full(32, 8, 128),
            full(4, 8, 128),
            full(8, 128),
            full(4, 8, 128),
            full(16, 128),
            full(32, 16, 128),
            pltpu.SemaphoreType.DMA((16,)),
            pltpu.SemaphoreType.DMA((162,)),
            pltpu.SemaphoreType.DMA((162,)),
        ],
        name="rest",
        compiler_params=params(cid, 63),
    )(*args)


def last_kernel(*refs):
    ins, outs = refs[:13], refs[13:28]
    wide, gate, up, sems = refs[28:]
    move = Moves(sems)
    copies = []
    grad_tokens, mlp_grads, gains, *same = ins
    o_tokens, o_gate, o_up, o_attn, o_mlp, *o_same = outs
    for src, dst in zip(same, o_same):
        copies.append(move.start(src, dst))
    copies.append(move.start(gains.at[pl.ds(0, 2)], o_attn))
    copies.append(move.start(gains.at[pl.ds(2, 2)], o_mlp))
    for q in range(4):
        wide[q] = grad_tokens[q].astype(F32)
        copies.append(move.start(wide.at[q], o_tokens.at[q]))
    units = gate.shape[1]
    gate[...] = mlp_grads[:, :units].astype(F32)
    copies.append(move.start(gate, o_gate))
    up[...] = mlp_grads[:, units:].astype(F32)
    copies.append(move.start(up, o_up))
    for copy in copies:
        copy.wait()


def last(grad_tokens, mlp_grads, gains, *same):
    shape = jax.ShapeDtypeStruct
    wide = shape((64, mlp_grads.shape[1] // 2), F32)
    gain = shape((2, 8, 128), F32)
    outs = (shape(grad_tokens.shape, F32), wide, wide, gain, gain, *(shape(a.shape, a.dtype) for a in same))
    return pl.pallas_call(
        last_kernel,
        out_shape=outs,
        in_specs=[VMEM] * 13,
        out_specs=(ANYWHERE,) * len(outs),
        scratch_shapes=[
            pltpu.VMEM(grad_tokens.shape, F32),
            pltpu.VMEM(wide.shape, F32),
            pltpu.VMEM(wide.shape, F32),
            pltpu.SemaphoreType.DMA((18,)),
        ],
        name="last",
        compiler_params=pltpu.CompilerParams(vmem_limit_bytes=24 << 20),
    )(grad_tokens, mlp_grads, gains, *same)


def on_device(
    tokens,
    cotangent,
    w_query,
    w_key,
    w_value,
    w_output,
    w_gate,
    w_up,
    w_down,
    gain_attn,
    gain_mlp,
    gate_logit,
    valid_count,
):
    valid, logit = valid_count[None], gate_logit[:, None]
    (
        normed_t, grad_out_t, query, key, value, probs, local_out, retrieved, mix, hidden, mlp_grads,
        grad_out_own, offset, normal_next, memory_prev, memory_next, ys, xs, pair_e, middle, back,
    ) = front(
        0, tokens, cotangent, gain_attn[None], gain_mlp[None], valid, logit, w_query, w_key, w_value, w_output, w_down,
        w_gate, w_up,
    )
    mlp_grads = lax.psum_scatter(mlp_grads, SEQ, scatter_dimension=0, tiled=True)
    (
        layer_out, grad_tokens, later_offset, grad_down, grad_query, grad_key, grad_value, grad_output, gains, logit_grad,
    ) = rest(
        1, back, middle, gain_attn[None], gain_mlp[None], grad_out_own, valid, offset, logit, memory_prev, ys, xs, pair_e,
        grad_out_t, hidden, query, key, value, probs, local_out, retrieved, mix, normed_t,
        w_query, w_key, w_value, w_output, w_down, tokens,
    )
    (
        grad_tokens, grad_gate, grad_up, gain_attn_grad, gain_mlp_grad, layer_out, grad_query, grad_key, grad_value,
        grad_output, grad_down, logit_grad, memory_next, normal_next, later_offset,
    ) = last(
        grad_tokens, mlp_grads, gains, layer_out, grad_query, grad_key, grad_value, grad_output, grad_down, logit_grad,
        memory_next, normal_next, later_offset,
    )
    return (
        layer_out.reshape(tokens.shape),
        grad_tokens.reshape(tokens.shape),
        grad_query,
        grad_key,
        grad_value,
        grad_output,
        grad_gate,
        grad_up,
        grad_down,
        gain_attn_grad.reshape(-1),
        gain_mlp_grad.reshape(-1),
        logit_grad[0, :4],
        memory_next[None],
        normal_next[None, :4],
        later_offset[None, :4],
    )


def solution(mesh):
    torus = Mesh(
        mesh.devices.reshape(4, 4, 2, mesh.shape["tensor"]), ("seq_0", "seq_1", "seq_2", "tensor")
    )
    weight = P(None, "tensor")
    grad = P(SEQ, "tensor")
    return jax.shard_map(
        on_device,
        mesh=torus,
        in_specs=(P(SEQ, None), P(SEQ, None)) + (weight,) * 7 + (P(), P(), P("tensor"), P()),
        out_specs=(P(SEQ, None), P(SEQ, None))
        + (grad,) * 7
        + (P(), P(), P("tensor"), P(SEQ, "tensor", None, None), P(SEQ, "tensor", None), P(SEQ, "tensor", None)),
        check_vma=False,
    )
```

```python
import functools

import jax
import jax.numpy as jnp
from jax import lax
from jax.experimental import pallas as pl
from jax.experimental.pallas import tpu as pltpu
from jax.sharding import Mesh
from jax.sharding import PartitionSpec as P

SEQ = ("seq_0", "seq_1", "seq_2")
MESH_ID = pl.DeviceIdType.MESH
VMEM = pl.BlockSpec(memory_space=pltpu.VMEM)
BF = jnp.bfloat16
F32 = jnp.float32

epsilon = 1e-06


def remote(src, dst, send, recv, device):
    return pltpu.make_async_remote_copy(
        src_ref=src, dst_ref=dst, send_sem=send, recv_sem=recv, device_id=device, device_id_type=MESH_ID
    )


def meet(devices):
    barrier = pltpu.get_barrier_semaphore()
    for device in devices:
        pl.semaphore_signal(barrier, inc=1, device_id=device, device_id_type=MESH_ID)
    pl.semaphore_wait(barrier, len(devices))


def params(collective_id, mib):
    return pltpu.CompilerParams(
        collective_id=collective_id, has_side_effects=True, vmem_limit_bytes=mib << 20
    )


def seq_place(index):
    return {"seq_0": index // 8, "seq_1": lax.rem(index // 2, 4), "seq_2": lax.rem(index, 2)}


def seq_index():
    return lax.axis_index("seq_0") * 8 + lax.axis_index("seq_1") * 2 + lax.axis_index("seq_2")


def mul(a, b):
    return jnp.dot(a.astype(BF), b.astype(BF), preferred_element_type=F32)


def mul_t(a, b):
    return lax.dot_general(a.astype(BF), b.astype(BF), (((0,), (0,)), ((), ())), preferred_element_type=F32)


def ring_places():
    x, y, c = (lax.axis_index(a) for a in SEQ)
    return x, y, c


def rows_by_rows(a, b):
    return lax.dot_general(a, b, (((1,), (1,)), ((), ())), preferred_element_type=F32)


class RingSum:
    def __init__(self, src, bufs, send, recv, base, axis):
        self.src, self.bufs, self.me = src, bufs, lax.axis_index(axis)
        half = src.shape[2] // 2
        self.a, self.b = pl.ds(0, half), pl.ds(half, half)
        self.right, self.left = lax.rem(self.me + 1, 4), lax.rem(self.me + 3, 4)
        far = lax.rem(self.me + 2, 4)
        to_right, to_left = {axis: self.right}, {axis: self.left}

        def copy(piece, landing, slot, device):
            return remote(piece, bufs.at[landing], send.at[base + slot], recv.at[base + slot], device)

        rows = pl.ds(0, src.shape[1])
        self.c0 = copy(src.at[far, rows, self.a], 0, 0, to_right)
        self.c1 = copy(src.at[far, rows, self.b], 1, 1, to_left)
        self.c2 = copy(src.at[self.right, rows, self.b], 2, 2, to_right)
        self.c3 = copy(src.at[self.left, rows, self.a], 3, 3, to_left)
        self.c4 = copy(bufs.at[6], 4, 4, to_right)
        self.c5 = copy(bufs.at[7], 5, 5, to_left)

    def start_a(self):
        self.c0.start()
        self.c3.start()

    def start_b(self):
        self.c1.start()
        self.c2.start()

    def start(self):
        self.c0.start()
        self.c1.start()
        self.c3.start()
        self.c2.start()

    def middle(self):
        src, bufs = self.src, self.bufs
        self.c0.wait_recv()
        bufs[6] = (bufs[0].astype(F32) + src[self.right, :, self.a].astype(F32)).astype(BF)
        self.c4.start()
        self.c1.wait_recv()
        bufs[7] = (bufs[1].astype(F32) + src[self.left, :, self.b].astype(F32)).astype(BF)
        self.c5.start()

    def finish(self, put):
        src, bufs = self.src, self.bufs
        self.c3.wait_recv()
        self.c4.wait_recv()
        put(self.a, src[self.me, :, self.a].astype(F32) + bufs[4].astype(F32) + bufs[3].astype(F32))
        self.c2.wait_recv()
        self.c5.wait_recv()
        put(self.b, src[self.me, :, self.b].astype(F32) + bufs[5].astype(F32) + bufs[2].astype(F32))

    def drain(self):
        for copy in (self.c0, self.c1, self.c2, self.c3, self.c4, self.c5):
            copy.wait_send()


class RingGather:
    def __init__(self, buf, send, recv, base, axis):
        self.me = lax.axis_index(axis)
        half = buf.shape[1] // 2
        right, left = lax.rem(self.me + 1, 4), lax.rem(self.me + 3, 4)
        to_right, to_left = {axis: right}, {axis: left}

        def copy(q, h, slot, device):
            piece = buf.at[q, pl.ds(half * h, half)]
            return remote(piece, piece, send.at[base + slot], recv.at[base + slot], device)

        self.r0, self.l1 = copy(self.me, 0, 0, to_right), copy(self.me, 1, 1, to_left)
        self.r1, self.l0 = copy(self.me, 1, 2, to_right), copy(self.me, 0, 3, to_left)
        self.f0, self.f1 = copy(left, 0, 4, to_right), copy(right, 1, 5, to_left)

    def start(self):
        for copy in (self.r0, self.l1, self.r1, self.l0):
            copy.start()

    def middle(self):
        self.r0.wait_recv()
        self.f0.start()
        self.l1.wait_recv()
        self.f1.start()

    def finish(self):
        for copy in (self.r1, self.l0, self.f0, self.f1):
            copy.wait_recv()

    def drain(self):
        for copy in (self.r0, self.l1, self.r1, self.l0, self.f0, self.f1):
            copy.wait_send()


class SeqSum:
    def __init__(self, product, got, first, first_bufs, second, second_bufs, send, recv, base, x_first):
        self.product, self.got, self.first, self.second, self.x_first = product, got, first, second, x_first
        self.core = lax.axis_index("seq_2")
        self.swap = remote(
            product.at[pl.ds(0, 16), 1 - self.core], got, send.at[base], recv.at[base], {"seq_2": 1 - self.core}
        )
        axes = ("seq_0", "seq_1") if x_first else ("seq_1", "seq_0")
        self.one = RingSum(first, first_bufs, send, recv, base + 1, axes[0])
        self.two = RingSum(second, second_bufs, send, recv, base + 7, axes[1])

    def start(self):
        self.swap.start()

    def first_ring(self):
        self.swap.wait_recv()
        for x in range(4):
            for y in range(4):
                at = 4 * x + y
                q, r = (x, y) if self.x_first else (y, x)
                total = self.product[at, self.core].astype(F32) + self.got[at].astype(F32)
                self.first[q, pl.ds(64 * r, 64)] = total.astype(BF)
        self.one.start()

    def second_ring(self):
        def put(cols, value):
            for r in range(4):
                self.second[r, :, cols] = value[64 * r : 64 * (r + 1)].astype(BF)

        self.one.finish(put)
        self.two.start()

    def finish(self, out):
        def put(cols, value):
            out[:, cols] = value

        self.two.finish(put)

    def drain(self):
        self.swap.wait_send()
        self.one.drain()
        self.two.drain()


def greet_all():
    barrier = pltpu.get_barrier_semaphore()
    me, z = seq_index(), lax.axis_index("tensor")

    def greet_seq(k, carry):
        pl.semaphore_signal(barrier, inc=1, device_id=seq_place(lax.rem(me + k, 32)), device_id_type=MESH_ID)
        return carry

    lax.fori_loop(1, 32, greet_seq, 0)
    for k in (1, 2, 3):
        pl.semaphore_signal(barrier, inc=1, device_id={"tensor": lax.rem(z + k, 4)}, device_id_type=MESH_ID)


def all_greeted():
    pl.semaphore_wait(pltpu.get_barrier_semaphore(), 34)


class TotalOfAll:
    def __init__(self, mine, extra, by_z, line, by_seq, total, send, recv, base):
        self.mine, self.extra, self.by_z, self.line, self.by_seq, self.total = mine, extra, by_z, line, by_seq, total
        self.z, self.me = lax.axis_index("tensor"), seq_index()
        self.send, self.recv, self.base = send, recv, base
        peers = [lax.rem(self.z + k, 4) for k in (1, 2, 3)]
        self.split = [
            remote(mine.at[p], by_z.at[self.z], send.at[base + k], recv.at[base + k], {"tensor": p})
            for k, p in enumerate(peers)
        ]
        self.join = [
            remote(total.at[self.z], total.at[self.z], send.at[base + 3 + k], recv.at[base + 3 + k], {"tensor": p})
            for k, p in enumerate(peers)
        ]

    def start(self):
        for copy in self.split:
            copy.start()

    def over_seq(self):
        self.by_z[self.z] = self.mine[self.z]
        for copy in self.split:
            copy.wait_recv()
        self.line[0:8] = (self.by_z[0] + self.by_z[1]) + (self.by_z[2] + self.by_z[3])
        self.line[8:16] = self.extra[...]
        self.by_seq[self.me] = self.line[...]

        def push(k, carry):
            device = seq_place(lax.rem(self.me + k, 32))
            remote(self.line, self.by_seq.at[self.me], self.send.at[self.base + 6], self.recv.at[self.base + 6], device).start()
            return carry

        lax.fori_loop(1, 32, push, 0)

    def over_tensor(self, extra_out):
        others = self.by_seq.at[pl.ds(0, 31)]
        pltpu.make_async_copy(others, others, self.recv.at[self.base + 6]).wait()
        summed = jnp.sum(self.by_seq[...], axis=0)
        self.total[self.z] = summed[0:8]
        extra_out[...] = summed[8:16]
        for copy in self.join:
            copy.start()

    def finish(self):
        for copy in self.join:
            copy.wait_recv()

    def drain(self):
        for copy in (*self.split, *self.join):
            copy.wait_send()
        others = self.by_seq.at[pl.ds(0, 31)]
        pltpu.make_async_copy(others, others, self.send.at[self.base + 6]).wait()


def feature_of(v):
    return jnp.where(v > 0, v + 1.0, jnp.exp(jnp.minimum(v, 0.0)))


def slope_of(v):
    return jnp.where(v > 0, 1.0, jnp.exp(jnp.minimum(v, 0.0)))


ANYWHERE = pl.BlockSpec(memory_space=pl.ANY)


def keep_of(valid):
    length = jnp.where(seq_index() == 31, valid[...], 384)
    return (lax.broadcasted_iota(jnp.int32, (384, 1), 0) < length).astype(F32)


SMEM = pl.BlockSpec(memory_space=pltpu.SMEM)


def gate_rows(gate, logit):
    for h in range(4):
        gate[h : h + 1] = jax.nn.sigmoid(jnp.full((1, 128), logit[h], F32))


def flat(weight):
    return weight.reshape(-1, 512)


class Moves:
    def __init__(self, sems):
        self.sems, self.count = sems, 0

    def start(self, src, dst):
        copy = pltpu.make_async_copy(src, dst, self.sems.at[self.count])
        self.count += 1
        copy.start()
        return copy


def front_kernel(
    gain_attn,
    gain_mlp,
    valid,
    gate_logit,
    i_tokens,
    cotangent,
    w_query,
    w_key,
    w_value,
    w_output,
    w_down,
    w_gate,
    w_up,
    o_normed_t,
    o_grad_out_t,
    o_query,
    o_key,
    o_value,
    o_probs,
    o_local_out,
    o_retrieved,
    o_mix,
    o_hidden,
    o_grads,
    grad_out_own,
    offset,
    normal_next,
    memory_prev,
    memory_next,
    ys,
    xs,
    pair_e,
    middle,
    back,
    out_gate,
    keep,
    gate,
    weights,
    weight_o,
    weight_d,
    weight_g,
    hidden,
    normed_two,
    normed,
    turned,
    grad_out,
    got_rows,
    first_rows,
    first_bufs,
    second_rows,
    second_bufs,
    grad_hidden,
    query,
    key,
    value,
    probs,
    local_out,
    retrieved,
    mix,
    line,
    lines,
    eb,
    source,
    got,
    pair_m,
    got_m,
    part,
    part_bufs,
    moves,
    send,
    recv,
):
    move = Moves(moves)
    tokens = hidden
    load_tokens = move.start(i_tokens, tokens)
    loads = [move.start(w, weights.at[i]) for i, w in enumerate((w_key, w_query, w_value))]
    load_cotangent = move.start(cotangent, grad_out)
    load_o = move.start(w_output, weight_o)
    load_d = [move.start(w_down.at[pl.ds(512 * i, 512)], weight_d.at[pl.ds(512 * i, 512)]) for i in range(4)]
    greet_all()
    keep[...] = keep_of(valid)
    gate_rows(gate, gate_logit)
    x, y, c = ring_places()
    z, me = lax.axis_index("tensor"), seq_index()
    partner = {"seq_2": 1 - c}
    mine, theirs = 2 * c, 2 * (1 - c)
    sums = [
        SeqSum(
            rows, got_rows.at[i], first_rows.at[i], first_bufs.at[i], second_rows.at[i], second_bufs.at[i],
            send, recv, 27 + 13 * i, i % 2 == 0,
        )
        for i, rows in enumerate((weight_o, weights.at[2]))
    ]
    z_sum = RingSum(part, part_bufs, send, recv, 0, "tensor")
    z_gather = RingGather(normed_two, send, recv, 6, "tensor")
    y_ring = RingGather(ys, send, recv, 12, "seq_1")
    x_ring = RingGather(xs, send, recv, 18, "seq_0")
    swap = remote(eb.at[pl.ds(theirs, 2)], got, send.at[24], recv.at[24], partner)
    give = remote(pair_m, got_m, send.at[25], recv.at[25], partner)
    cols = [slice(128 * h, 128 * (h + 1)) for h in range(4)]
    stores = []

    load_tokens.wait()
    for q in range(4):
        rows = pl.ds(96 * q, 96)
        stream = tokens[rows].astype(F32)
        inv = lax.rsqrt(jnp.mean(stream * stream, axis=1, keepdims=True) + epsilon)
        normed[rows] = (stream * inv * gain_attn[...]).astype(BF)
    loads[0].wait()
    key[...] = jnp.dot(normed[...], flat(weights[0]), preferred_element_type=F32).astype(BF)
    feat_q = lambda h: feature_of(query[:, cols[h]].astype(F32))
    feat_k = lambda h: feature_of(key[:, cols[h]].astype(F32))
    line[...] = jnp.zeros_like(line)
    for h in range(4):
        line[h : h + 1] = jnp.sum(feat_k(h) * keep[...], axis=0, keepdims=True)
    lines[me] = line[...]
    all_greeted()

    def push(k, carry):
        remote(line, lines.at[me], send.at[26], recv.at[26], seq_place(lax.rem(me + k, 32))).start()
        return carry

    lax.fori_loop(1, 32, push, 0)
    stores.append(move.start(key, o_key))
    loads[1].wait()
    query[...] = jnp.dot(normed[...], flat(weights[1]), preferred_element_type=F32).astype(BF)
    stores.append(move.start(query, o_query))
    loads[2].wait()
    value[...] = jnp.dot(normed[...], flat(weights[2]), preferred_element_type=F32).astype(BF)
    stores.append(move.start(value, o_value))
    load_g = move.start(w_gate, weight_g)
    at_row = lax.broadcasted_iota(jnp.int32, (384, 384), 0)
    at_col = lax.broadcasted_iota(jnp.int32, (384, 384), 1)
    valid = jnp.sum(keep[...], axis=0, keepdims=True)
    allowed = (at_row >= at_col) & (at_col.astype(F32) < valid)

    def attend(h):
        at = cols[h]
        scores = rows_by_rows(query[:, at], key[:, at]) * 128 ** (-0.5)
        masked = jnp.where(allowed, scores, -1e30)
        raised = jnp.exp(masked - jnp.max(masked, axis=1, keepdims=True))
        low = (raised * (1.0 / jnp.sum(raised, axis=1, keepdims=True))).astype(BF)
        probs[h] = low
        local_out[:, at] = jnp.dot(low, value[:, at], preferred_element_type=F32)
        total = mul_t(feat_k(h) * keep[...], value[:, at])
        source[h] = total
        eb[h, :, 128:256] = total.astype(BF)

    for h in range(4):
        attend(h)
    stores.append(move.start(probs, o_probs))
    stores.append(move.start(local_out, o_local_out))
    others = lines.at[pl.ds(0, 31)]
    pltpu.make_async_copy(others, others, recv.at[26]).wait()
    passed = lax.broadcasted_iota(jnp.int32, (32, 8, 128), 0) < me
    before = jnp.sum(jnp.where(passed, lines[...], 0.0), axis=0)
    normal_next[...] = before + line[...]
    offset[...] = before + 384.0
    for h in range(4):
        fk = feat_k(h)
        kept = fk * keep[...] * (1.0 / jnp.sum(fk * offset[h : h + 1], axis=1, keepdims=True))
        eb[h, :, 0:128] = mul_t(kept, fk).astype(BF)
    swap.start()
    load_cotangent.wait()
    grad_out[...] = grad_out[...] * keep[...].astype(BF)
    grad_out_own[...] = grad_out[pl.ds(pl.multiple_of(96 * z, 96), 96)]
    swap.wait_recv()
    of = [pl.ds(0, 128), pl.ds(128, 128)]
    firsts = []
    for h in (0, 1):
        here, there = eb[mine + h].astype(F32), got[h].astype(F32)
        first, second = jnp.where(c == 0, here, there), jnp.where(c == 0, there, here)
        firsts.append(first)
        pair_e[0, h] = first[:, :128].astype(BF)
        pair_e[1, h] = second[:, :128].astype(BF)
        ys[y, of[h]] = (first + second - mul(second[:, :128], first)).astype(BF)
    y_ring.start()

    def hidden_part(i):
        load_d[i].wait()
        rows = pl.ds(512 * i, 512)
        product = jnp.dot(grad_out[:, 512 * i : 512 * (i + 1)], weight_d[rows], preferred_element_type=F32)
        if i == 0:
            grad_hidden[...] = product
        else:
            grad_hidden[...] += product

    hidden_part(0)
    y_ring.middle()
    hidden_part(1)
    y_ring.finish()
    starts = []
    for h in (0, 1):
        so_far = ys[0, of[h]].astype(F32)
        start = jnp.where(y > 0, so_far, 0.0)
        for k in (1, 2, 3):
            step = ys[k, of[h]].astype(F32)
            so_far = so_far + step - mul(step[:, :128], so_far)
            if k < 3:
                start = jnp.where(y > k, so_far, start)
        xs[x, of[h]] = so_far.astype(BF)
        starts.append(start)
    x_ring.start()
    hidden_part(2)
    x_ring.middle()
    hidden_part(3)
    load_u = move.start(w_up, weight_d)
    load_o.wait()
    x_ring.finish()
    for h in (0, 1):
        m = jnp.where(x > 0, xs[0, of[h]][:, 128:].astype(F32), 0.0)
        for k in (1, 2):
            step = xs[k, of[h]].astype(F32)
            m = jnp.where(x > k, m + step[:, 128:] - mul(step[:, :128], m), m)
        m = m + starts[h][:, 128:] - mul(starts[h][:, :128], m)
        second = m + firsts[h][:, 128:] - mul(firsts[h][:, :128], m)
        memory_prev[mine + h] = jnp.where(c == 0, m, second)
        pair_m[h] = jnp.where(c == 0, second, m)
    give.start()
    give.wait_recv()
    for h in (0, 1):
        memory_prev[theirs + h] = got_m[h]
    for h in range(4):
        at, fq, sig = cols[h], feat_q(h), gate[h : h + 1]
        inv_q = 1.0 / jnp.sum(fq * offset[h : h + 1], axis=1, keepdims=True)
        found = mul(fq, memory_prev[h]) * inv_q
        retrieved[:, at] = found
        mix[:, at] = (sig * found + (1.0 - sig) * local_out[:, at]).astype(BF)
    for half in (0, 1):
        rows = pl.ds(1024 * half, 1024)
        part[:, :, rows] = rows_by_rows(mix[...], flat(weight_o[8 * half : 8 * half + 8])).astype(BF).reshape(4, 96, 1024)
        (z_sum.start_a, z_sum.start_b)[half]()
    stores.append(move.start(retrieved, o_retrieved))
    stores.append(move.start(mix, o_mix))
    for h in range(4):
        m = memory_prev[h]
        memory_next[h] = m + source[h] - mul(eb[h][:, :128], m)
    turned[...] = normed[...].T
    store_t = move.start(turned, o_normed_t)
    z_sum.middle()
    store_t.wait()
    turned[...] = grad_out[...].T
    stores.append(move.start(turned, o_grad_out_t))
    own_tokens = tokens[pl.ds(pl.multiple_of(96 * z, 96), 96)].astype(F32)

    def put(at, total):
        lanes = slice(0, 1024) if at is z_sum.a else slice(1024, 2048)
        middle[:, at] = own_tokens[:, lanes] + total

    z_sum.finish(put)
    stream = middle[...]
    inv = lax.rsqrt(jnp.mean(stream * stream, axis=1, keepdims=True) + epsilon)
    normed_two[z] = (stream * inv * gain_mlp[...]).astype(BF)
    z_gather.start()
    z_gather.middle()
    for store in stores:
        store.wait()
    load_g.wait()
    load_u.wait()
    z_gather.finish()
    turned[...] = normed_two[...].reshape(384, 2048).T

    def tile(i):
        lanes = slice(512 * i, 512 * (i + 1))
        rows = normed_two[...].reshape(384, 2048)
        gate_pre = jnp.dot(rows, weight_g[:, lanes], preferred_element_type=F32)
        up_pre = jnp.dot(rows, weight_d[:, lanes], preferred_element_type=F32)
        back_hidden = grad_hidden[:, lanes]
        sig = jax.nn.sigmoid(gate_pre)
        swish = gate_pre * sig
        hidden[:, lanes] = (swish * up_pre).astype(BF)
        grad_out[:, lanes] = (back_hidden * swish).astype(BF)
        normed[:, lanes] = (back_hidden * up_pre * sig * (1.0 + gate_pre * (1.0 - sig))).astype(BF)

    def gradient(side, i):
        result = jnp.dot(turned[...], side[:, 512 * i : 512 * (i + 1)], preferred_element_type=F32)
        return result.astype(BF).reshape(16, 2, 64, 512)

    slots = []

    def leave(side, i):
        n = len(slots)
        if n >= 2:
            slots[n - 2].wait()
        weights[n % 2] = gradient(side, i)
        slots.append(move.start(weights.at[n % 2], o_grads.at[:, :, :, pl.ds(512 * n, 512)]))

    def return_part(i):
        rows = pl.ds(512 * i, 512)
        value = rows_by_rows(normed[...], weight_g[rows]) + rows_by_rows(grad_out[...], weight_d[rows])
        back[:, :, rows] = value.astype(BF).reshape(4, 96, 512)

    tile(0)
    weight_o[...] = gradient(normed, 0)
    sums[0].start()
    tile(1)
    weights[2] = gradient(normed, 1)
    sums[1].start()
    sums[0].first_ring()
    tile(2)
    leave(normed, 2)
    sums[1].first_ring()
    tile(3)
    stores = [move.start(hidden, o_hidden)]
    sums[0].one.middle()
    leave(normed, 3)
    leave(grad_out, 0)
    sums[1].one.middle()
    leave(grad_out, 1)
    sums[0].second_ring()
    leave(grad_out, 2)
    sums[1].second_ring()
    leave(grad_out, 3)
    sums[0].two.middle()
    return_part(0)
    sums[1].two.middle()
    return_part(1)
    for i in (0, 1):
        sums[i].finish(out_gate.at[:, pl.ds(512 * i, 512)])
    return_part(2)
    return_part(3)
    for copy in (*stores, *slots[4:]):
        copy.wait()
    for ring in (*sums, z_sum, z_gather, y_ring, x_ring):
        ring.drain()
    swap.wait_send()
    give.wait_send()
    pltpu.make_async_copy(others, others, send.at[26]).wait()


def front(cid, *args):
    shape = jax.ShapeDtypeStruct
    low = lambda *dims: pltpu.VMEM(dims, BF)
    full = lambda *dims: pltpu.VMEM(dims, F32)
    return pl.pallas_call(
        front_kernel,
        out_shape=(
            shape((2048, 384), BF),
            shape((2048, 384), BF),
            shape((384, 512), BF),
            shape((384, 512), BF),
            shape((384, 512), BF),
            shape((4, 384, 384), BF),
            shape((384, 512), F32),
            shape((384, 512), F32),
            shape((384, 512), BF),
            shape((384, 2048), BF),
            shape((16, 2, 64, 3072), BF),
            shape((96, 2048), BF),
            shape((8, 128), F32),
            shape((8, 128), F32),
            shape((4, 128, 128), F32),
            shape((4, 128, 128), F32),
            shape((4, 256, 256), BF),
            shape((4, 256, 256), BF),
            shape((2, 2, 128, 128), BF),
            shape((96, 2048), F32),
            shape((4, 96, 2048), BF),
            shape((64, 1024), F32),
        ),
        in_specs=[VMEM] * 3 + [SMEM] + [ANYWHERE] * 9,
        out_specs=(ANYWHERE,) * 11 + (VMEM,) * 11,
        scratch_shapes=[
            full(384, 1),
            full(4, 128),
            low(3, 16, 2, 64, 512),
            low(16, 2, 64, 512),
            low(2048, 2048),
            low(2048, 2048),
            low(384, 2048),
            low(4, 96, 2048),
            low(384, 2048),
            low(2048, 384),
            low(384, 2048),
            low(2, 16, 64, 512),
            low(2, 4, 256, 512),
            low(2, 8, 256, 256),
            low(2, 4, 64, 512),
            low(2, 8, 64, 256),
            full(384, 2048),
            low(384, 512),
            low(384, 512),
            low(384, 512),
            low(4, 384, 384),
            full(384, 512),
            full(384, 512),
            low(384, 512),
            full(8, 128),
            full(32, 8, 128),
            low(4, 128, 256),
            full(4, 128, 128),
            low(2, 128, 256),
            full(2, 128, 128),
            full(2, 128, 128),
            low(4, 96, 2048),
            low(8, 96, 1024),
            pltpu.SemaphoreType.DMA((28,)),
            pltpu.SemaphoreType.DMA((53,)),
            pltpu.SemaphoreType.DMA((53,)),
        ],
        name="front",
        compiler_params=params(cid, 63),
    )(*args)


def neighbours():
    x, y, c = ring_places()
    z = lax.axis_index("tensor")
    near = [{"seq_2": 1 - c}]
    for axis, at in (("seq_0", x), ("seq_1", y), ("tensor", z)):
        near += [{axis: lax.rem(at + 1, 4)}, {axis: lax.rem(at + 3, 4)}]
    return near


def rest_kernel(
    back,
    middle,
    gain_attn,
    gain_mlp,
    grad_out,
    valid,
    offset,
    gate_logit,
    memory,
    ys,
    xs,
    pair_e,
    i_grad_out_t,
    i_hidden,
    i_query,
    i_key,
    i_value,
    i_probs,
    i_local_out,
    i_retrieved,
    i_mix,
    i_normed_t,
    w_query,
    w_key,
    w_value,
    w_output,
    w_down,
    tokens,
    o_layer_out,
    o_grad_tokens,
    o_later,
    o_out_down,
    o_out_query,
    o_out_key,
    o_out_value,
    o_out_output,
    o_gains,
    o_logits_out,
    layer_out,
    grad_tokens,
    later,
    out_down,
    out_query,
    out_key,
    out_value,
    out_output,
    gains,
    logits_out,
    keep,
    gate,
    branch,
    grad_middle,
    grads,
    left,
    hidden,
    query,
    key,
    value,
    probs,
    local_out,
    retrieved,
    mix,
    tokens_own,
    weight_o,
    weight_d,
    products,
    got_rows,
    first_rows,
    first_bufs,
    second_rows,
    second_bufs,
    forth,
    z_bufs,
    own,
    inverse,
    recall,
    grad_mix,
    grad_query,
    grad_key,
    grad_value,
    source,
    got,
    s_y,
    s_x,
    pair_l,
    got_l,
    adjoint,
    line,
    lines,
    mine_gains,
    logits,
    by_z,
    total_line,
    by_seq,
    moves,
    send,
    recv,
):
    x, y, c = ring_places()
    z, me = lax.axis_index("tensor"), seq_index()
    move = Moves(moves)
    pairs = (
        (i_grad_out_t, left),
        (i_hidden, hidden),
        (i_query, query),
        (i_key, key),
        (i_value, value),
        (w_down, weight_d),
        (w_output, weight_o),
        (i_probs, probs),
        (i_local_out, local_out),
        (i_retrieved, retrieved),
        (i_mix, mix),
        (tokens.at[pl.ds(pl.multiple_of(96 * z, 96), 96)], tokens_own),
    )
    barrier = pltpu.get_barrier_semaphore()
    for device in neighbours():
        pl.semaphore_signal(barrier, inc=1, device_id=device, device_id_type=MESH_ID)
    loads = [move.start(src, dst) for src, dst in pairs]
    keep[...] = keep_of(valid)
    gate_rows(gate, gate_logit)
    partner = {"seq_2": 1 - c}
    mine, theirs = 2 * c, 2 * (1 - c)
    z_back = RingSum(back, z_bufs, send, recv, 0, "tensor")
    z_branch = RingGather(branch, send, recv, 6, "tensor")
    z_forth = RingSum(forth, z_bufs, send, recv, 12, "tensor")
    z_layer = RingGather(layer_out, send, recv, 18, "tensor")
    y_ring = RingGather(s_y, send, recv, 24, "seq_1")
    x_ring = RingGather(s_x, send, recv, 30, "seq_0")
    swap = remote(source.at[pl.ds(theirs, 2)], got, send.at[36], recv.at[36], partner)
    give = remote(pair_l, got_l, send.at[37], recv.at[37], partner)
    z_end = RingSum(forth, z_bufs, send, recv, 143, "tensor")
    z_tokens = RingGather(grad_tokens, send, recv, 149, "tensor")
    total = TotalOfAll(mine_gains, logits, by_z, total_line, by_seq, gains, send, recv, 155)

    def seq_sums(base):
        return [
            SeqSum(
                products.at[i], got_rows.at[i], first_rows.at[i], first_bufs.at[i], second_rows.at[i],
                second_bufs.at[i], send, recv, base + 13 * i, i % 2 == 0,
            )
            for i in range(4)
        ]

    sums, ends = seq_sums(39), seq_sums(91)
    cols = [slice(128 * h, 128 * (h + 1)) for h in range(4)]
    of = [pl.ds(0, 128), pl.ds(128, 128)]
    feat_q = lambda h: feature_of(query[:, cols[h]].astype(F32))
    feat_k = lambda h: feature_of(key[:, cols[h]].astype(F32))
    scale = 128 ** (-0.5)

    def recalled(h):
        fk, off = feat_k(h), offset[h : h + 1]
        inv_k = 1.0 / jnp.sum(fk * off, axis=1, keepdims=True)
        inverse[:, 4 + h : 5 + h] = inv_k
        inverse[:, h : h + 1] = 1.0 / jnp.sum(feat_q(h) * off, axis=1, keepdims=True)
        recall[:, cols[h]] = mul(fk, memory[h]) * inv_k

    def product(group, i, right):
        result = jnp.dot(left[...], right, preferred_element_type=F32).astype(BF)
        products[i] = result.reshape(16, 2, 64, 512)
        group[i].start()

    def down(i):
        product(sums, i, hidden[:, 512 * i : 512 * (i + 1)])

    def put(at, result):
        own[:, at] = result

    def norm_back(stream, gain, first_row):
        inv = lax.rsqrt(jnp.mean(stream * stream, axis=1, keepdims=True) + epsilon)
        grad_normed = own[...]
        weighted = grad_normed * gain[...]
        inner = jnp.sum(weighted * stream, axis=1, keepdims=True)
        scaled = stream * inv
        line_of = jnp.sum(grad_normed * scaled, axis=0, keepdims=True)
        for r in range(16):
            mine_gains[first_row + r // 8, r % 8 : r % 8 + 1] = line_of[:, 128 * r : 128 * (r + 1)]
        return inv * weighted - scaled * (inv * inv * inner * (1.0 / stream.shape[1]))

    pl.semaphore_wait(barrier, 7)
    z_back.start()
    loads[0].wait()
    loads[1].wait()
    down(0)
    down(1)
    z_back.middle()
    sums[0].first_ring()
    down(2)
    sums[1].first_ring()
    down(3)
    z_back.finish(put)
    result = grad_out[...].astype(F32) + norm_back(middle[...], gain_mlp, 2)
    grad_middle[...] = result
    branch[z] = result.astype(BF)
    z_branch.start()
    sums[2].first_ring()
    sums[0].one.middle()
    for load in loads[2:6]:
        load.wait()
    recalled(0)
    recalled(1)
    sums[3].first_ring()
    z_branch.middle()
    sums[1].one.middle()
    recalled(2)
    recalled(3)
    sums[0].second_ring()
    for half in (0, 1):
        rows = pl.ds(1024 * half, 1024)
        forth[:, :, rows] = rows_by_rows(hidden[...], weight_d[rows]).astype(BF).reshape(4, 96, 1024)
    sums[2].one.middle()
    sums[1].second_ring()
    loads += [
        move.start(w, weight_d.at[:, pl.ds(512 * i, 512)]) for i, w in enumerate((w_query, w_key, w_value))
    ]
    for load in loads[6:12]:
        load.wait()
    z_branch.finish()
    z_back.drain()
    z_forth.start()
    grad_mix[...] = jnp.dot(branch[...].reshape(384, 2048), weight_o[...], preferred_element_type=F32)

    def point(h):
        return gate[h : h + 1] * grad_mix[:, cols[h]] * inverse[:, h : h + 1]

    for h in range(4):
        source[h] = mul_t(feat_q(h), point(h)).astype(BF)
    swap.start()

    def attend(h):
        at = cols[h]
        grad_local = ((1.0 - gate[h : h + 1]) * grad_mix[:, at]).astype(BF)
        low = probs[h]
        p = low.astype(F32)
        grad_probs = rows_by_rows(grad_local, value[:, at])
        grad_value[:, at] = mul_t(low, grad_local)
        grad_scores = (p * (grad_probs - jnp.sum(grad_probs * p, axis=1, keepdims=True))).astype(BF)
        grad_query[:, at] = mul(grad_scores, key[:, at]) * scale
        grad_key[:, at] = mul_t(grad_scores, query[:, at]) * scale

    sums[0].two.middle()
    sums[3].one.middle()
    attend(0)
    sums[2].second_ring()
    sums[1].two.middle()
    swap.wait_recv()
    seconds = []
    for h in (0, 1):
        here, there = source[mine + h].astype(F32), got[h].astype(F32)
        first, second = jnp.where(c == 0, here, there), jnp.where(c == 0, there, here)
        seconds.append(second)
        s_y[y, of[h]] = (first + second - mul_t(pair_e[0, h], second)).astype(BF)
    sums[3].second_ring()
    y_ring.start()
    attend(1)
    y_ring.middle()
    attend(2)
    z_forth.middle()
    for s in sums:
        s.swap.wait_send()
        s.one.drain()
    left[...] = branch[...].reshape(384, 2048).T
    y_ring.finish()
    for h in (0, 1):
        so_far = s_y[3, of[h]].astype(F32)
        for k in (2, 1, 0):
            so_far = s_y[k, of[h]].astype(F32) + so_far - mul_t(ys[k, of[h]][:, :128], so_far)
        s_x[x, of[h]] = so_far.astype(BF)
    x_ring.start()
    product(ends, 0, mix[...])
    x_ring.middle()
    load_t = move.start(i_normed_t, left)
    attend(3)
    logit_rows = []
    for h in range(4):
        at, gate_h, g = cols[h], gate[h : h + 1], grad_mix[:, cols[h]]
        ret = retrieved[:, at]
        moved = jnp.sum(g * (ret - local_out[:, at]), axis=0, keepdims=True) * gate_h * (1.0 - gate_h)
        logit_rows.append(jnp.sum(moved, axis=1, keepdims=True))
        grad_den = -jnp.sum(gate_h * g * ret, axis=1, keepdims=True) * inverse[:, h : h + 1]
        q = query[:, at].astype(F32)
        grad_feat = rows_by_rows(point(h).astype(BF), memory[h].astype(BF)) + grad_den * offset[h : h + 1]
        grads[:, at] = (grad_query[:, at] + grad_feat * slope_of(q)).astype(BF)
        line[h : h + 1] = jnp.sum(grad_den * feature_of(q), axis=0, keepdims=True)
    lane = lax.broadcasted_iota(jnp.int32, (8, 128), 1)
    row = lax.broadcasted_iota(jnp.int32, (8, 128), 0)
    spot = jnp.zeros((8, 128), F32)
    for h in range(4):
        spot = jnp.where((lane == h) & (row == 0), logit_rows[h], spot)
    logits[...] = spot
    z_forth.finish(put)
    layer_out[z] = (middle[...] + own[...]).astype(BF)
    z_layer.start()
    sums[2].two.middle()
    sums[3].two.middle()
    x_ring.finish()
    for h in (0, 1):
        lam = jnp.where(x < 3, s_x[3, of[h]].astype(F32), 0.0)
        for k in (2, 1):
            lam = jnp.where(x < k, s_x[k, of[h]].astype(F32) + lam - mul_t(xs[k, of[h]][:, :128], lam), lam)
        for k in (3, 2, 1):
            lam = jnp.where(y < k, s_y[k, of[h]].astype(F32) + lam - mul_t(ys[k, of[h]][:, :128], lam), lam)
        first = lam + seconds[h] - mul_t(pair_e[1, h], lam)
        adjoint[mine + h] = jnp.where(c == 0, first, lam).astype(BF)
        pair_l[h] = jnp.where(c == 0, lam, first).astype(BF)
    give.start()
    for i in range(4):
        sums[i].finish(out_down.at[:, pl.ds(512 * i, 512)])
    store_down = move.start(out_down, o_out_down)
    give.wait_recv()
    for h in (0, 1):
        adjoint[theirs + h] = got_l[h]
    for h in range(4):
        at, fk = cols[h], feat_k(h)
        grad_update = mul(fk * keep[...], adjoint[h])
        grad_value[:, at] += grad_update
        grad_den = jnp.sum(grad_update * recall[:, at], axis=1, keepdims=True) * inverse[:, 4 + h : 5 + h]
        line[h : h + 1] += jnp.sum(grad_den * fk, axis=0, keepdims=True)
        grad_key[:, at] += slope_of(key[:, at].astype(F32)) * (
            grad_den * offset[h : h + 1]
            - rows_by_rows((grad_update * inverse[:, 4 + h : 5 + h]).astype(BF), memory[h].astype(BF))
        )
    line[4:8] = jnp.zeros((4, 128), F32)
    lines[me] = line[...]

    def push(k, carry):
        remote(line, lines.at[me], send.at[38], recv.at[38], seq_place(lax.rem(me + k, 32))).start()
        return carry

    lax.fori_loop(1, 32, push, 0)
    for h in range(4):
        at = cols[h]
        grads[:, 1024 + 128 * h : 1152 + 128 * h] = grad_value[:, at].astype(BF)
        update = value[:, at].astype(F32) - recall[:, at]
        grad_key[:, at] += (
            keep[...] * slope_of(key[:, at].astype(F32)) * rows_by_rows(update.astype(BF), adjoint[h])
        )
    ends[0].first_ring()
    load_t.wait()
    product(ends, 1, grads[:, 0:512])
    z_layer.middle()
    product(ends, 3, grads[:, 1024:1536])
    for s in sums:
        s.two.drain()
    z_forth.drain()
    for load in loads[12:]:
        load.wait()
    others = lines.at[pl.ds(0, 31)]
    pltpu.make_async_copy(others, others, recv.at[38]).wait()
    passed = lax.broadcasted_iota(jnp.int32, (32, 8, 128), 0) > me
    after = jnp.sum(jnp.where(passed, lines[...], 0.0), axis=0)
    later[...] = after
    stores = [move.start(later, o_later)]
    for h in range(4):
        at = cols[h]
        late = keep[...] * after[h : h + 1] * slope_of(key[:, at].astype(F32))
        grads[:, 512 + 128 * h : 640 + 128 * h] = (grad_key[:, at] + late).astype(BF)
    z_layer.finish()
    stores += [store_down, move.start(layer_out, o_layer_out)]
    for half in (0, 1):
        rows = pl.ds(1024 * half, 1024)
        forth[:, :, rows] = rows_by_rows(grads[...], weight_d[rows, 0:1536]).astype(BF).reshape(4, 96, 1024)
        (z_end.start_a, z_end.start_b)[half]()
    ends[1].first_ring()
    product(ends, 2, grads[:, 512:1024])
    ends[0].one.middle()
    z_end.middle()
    ends[3].first_ring()
    ends[1].one.middle()
    ends[2].first_ring()
    ends[0].second_ring()
    z_end.finish(put)
    result = grad_middle[...] + norm_back(tokens_own[...].astype(F32), gain_attn, 0)
    grad_tokens[z] = result.astype(BF)
    z_tokens.start()
    total.start()
    ends[3].one.middle()
    ends[1].second_ring()
    total.over_seq()
    ends[2].one.middle()
    ends[0].two.middle()
    z_tokens.middle()
    ends[3].second_ring()
    ends[1].two.middle()
    total.over_tensor(logits_out)
    stores.append(move.start(logits_out, o_logits_out))
    ends[2].second_ring()
    ends[0].finish(out_output)
    stores.append(move.start(out_output, o_out_output))
    ends[3].two.middle()
    ends[1].finish(out_query)
    stores.append(move.start(out_query, o_out_query))
    ends[2].two.middle()
    ends[3].finish(out_value)
    stores.append(move.start(out_value, o_out_value))
    ends[2].finish(out_key)
    stores.append(move.start(out_key, o_out_key))
    total.finish()
    stores.append(move.start(gains, o_gains))
    z_tokens.finish()
    stores.append(move.start(grad_tokens, o_grad_tokens))
    for part in (z_branch, z_layer, y_ring, x_ring, z_end, z_tokens, total, *ends):
        part.drain()
    swap.wait_send()
    give.wait_send()
    for store in stores:
        store.wait()
    pltpu.make_async_copy(others, others, send.at[38]).wait()


def rest(cid, *args):
    shape = jax.ShapeDtypeStruct
    low = lambda *dims: pltpu.VMEM(dims, BF)
    full = lambda *dims: pltpu.VMEM(dims, F32)
    weight_grad = shape((64, 512), F32)
    return pl.pallas_call(
        rest_kernel,
        out_shape=(
            shape((4, 96, 2048), BF),
            shape((4, 96, 2048), BF),
            shape((8, 128), F32),
            shape((64, 2048), F32),
            weight_grad,
            weight_grad,
            weight_grad,
            weight_grad,
            shape((4, 8, 128), F32),
            shape((8, 128), F32),
        ),
        in_specs=[VMEM] * 7 + [SMEM] + [VMEM] * 4 + [ANYWHERE] * 16,
        out_specs=(ANYWHERE,) * 10,
        scratch_shapes=[
            low(4, 96, 2048),
            low(4, 96, 2048),
            full(8, 128),
            full(64, 2048),
            full(64, 512),
            full(64, 512),
            full(64, 512),
            full(64, 512),
            full(4, 8, 128),
            full(8, 128),
            full(384, 1),
            full(4, 128),
            low(4, 96, 2048),
            full(96, 2048),
            low(384, 1536),
            low(2048, 384),
            low(384, 2048),
            low(384, 512),
            low(384, 512),
            low(384, 512),
            low(4, 384, 384),
            full(384, 512),
            full(384, 512),
            low(384, 512),
            low(96, 2048),
            low(2048, 512),
            low(2048, 2048),
            low(4, 16, 2, 64, 512),
            low(4, 16, 64, 512),
            low(4, 4, 256, 512),
            low(4, 8, 256, 256),
            low(4, 4, 64, 512),
            low(4, 8, 64, 256),
            low(4, 96, 2048),
            low(8, 96, 1024),
            full(96, 2048),
            full(384, 128),
            full(384, 512),
            full(384, 512),
            full(384, 512),
            full(384, 512),
            full(384, 512),
            low(4, 128, 128),
            low(2, 128, 128),
            low(4, 256, 128),
            low(4, 256, 128),
            low(2, 128, 128),
            low(2, 128, 128),
            low(4, 128, 128),
            full(8, 128),
            full(32, 8, 128),
            full(4, 8, 128),
            full(8, 128),
            full(4, 8, 128),
            full(16, 128),
            full(32, 16, 128),
            pltpu.SemaphoreType.DMA((26,)),
            pltpu.SemaphoreType.DMA((162,)),
            pltpu.SemaphoreType.DMA((162,)),
        ],
        name="rest",
        compiler_params=params(cid, 63),
    )(*args)


def last_kernel(*refs):
    ins, outs = refs[:14], refs[14:29]
    narrow, wide, rows, gate, up, sems = refs[29:]
    move = Moves(sems)
    grad_tokens, mlp_grads, grad_gate, gains, *same = ins
    o_tokens, o_gate, o_up, o_attn, o_mlp, *o_same = outs
    fetch_rows = move.start(mlp_grads, rows)
    fetch = [move.start(grad_tokens.at[q], narrow.at[q]) for q in range(4)]
    known = grad_gate.shape[1]
    copies = [move.start(src, dst) for src, dst in zip(same, o_same)]
    copies.append(move.start(grad_gate, o_gate.at[:, pl.ds(0, known)]))
    copies.append(move.start(gains.at[pl.ds(0, 2)], o_attn))
    copies.append(move.start(gains.at[pl.ds(2, 2)], o_mlp))
    fetch_rows.wait()
    split = gate.shape[1]
    gate[...] = rows[:, :split].astype(F32)
    copies.append(move.start(gate, o_gate.at[:, pl.ds(known, split)]))
    up[...] = rows[:, split:].astype(F32)
    copies.append(move.start(up, o_up))
    for q in range(4):
        fetch[q].wait()
        wide[q] = narrow[q].astype(F32)
        copies.append(move.start(wide.at[q], o_tokens.at[q]))
    for copy in copies:
        copy.wait()


def last(grad_tokens, mlp_grads, grad_gate, gains, *same):
    shape = jax.ShapeDtypeStruct
    units = mlp_grads.shape[1] - grad_gate.shape[1]
    wide = shape((64, units), F32)
    gain = shape((2, 8, 128), F32)
    outs = (shape(grad_tokens.shape, F32), wide, wide, gain, gain, *(shape(a.shape, a.dtype) for a in same))
    return pl.pallas_call(
        last_kernel,
        out_shape=outs,
        in_specs=[ANYWHERE] * 14,
        out_specs=(ANYWHERE,) * len(outs),
        scratch_shapes=[
            pltpu.VMEM(grad_tokens.shape, BF),
            pltpu.VMEM(grad_tokens.shape, F32),
            pltpu.VMEM(mlp_grads.shape, BF),
            pltpu.VMEM((64, units - grad_gate.shape[1]), F32),
            pltpu.VMEM(wide.shape, F32),
            pltpu.SemaphoreType.DMA((24,)),
        ],
        name="last",
        compiler_params=pltpu.CompilerParams(vmem_limit_bytes=24 << 20),
    )(grad_tokens, mlp_grads, grad_gate, gains, *same)


def on_device(
    tokens,
    cotangent,
    w_query,
    w_key,
    w_value,
    w_output,
    w_gate,
    w_up,
    w_down,
    gain_attn,
    gain_mlp,
    gate_logit,
    valid_count,
):
    valid = valid_count[None]
    rows = (16, 2, 64, 512)
    (
        normed_t, grad_out_t, query, key, value, probs, local_out, retrieved, mix, hidden, mlp_grads,
        grad_out_own, offset, normal_next, memory_prev, memory_next, ys, xs, pair_e, middle, back, grad_gate,
    ) = front(
        0, gain_attn[None], gain_mlp[None], valid, gate_logit, tokens, cotangent,
        *(w.reshape(rows) for w in (w_query, w_key, w_value, w_output)), w_down, w_gate, w_up,
    )
    mlp_grads = lax.psum_scatter(mlp_grads.reshape(2048, -1), SEQ, scatter_dimension=0, tiled=True)
    (
        layer_out, grad_tokens, later_offset, grad_down, grad_query, grad_key, grad_value, grad_output, gains, logit_grad,
    ) = rest(
        1, back, middle, gain_attn[None], gain_mlp[None], grad_out_own, valid, offset, gate_logit, memory_prev, ys, xs, pair_e,
        grad_out_t, hidden, query, key, value, probs, local_out, retrieved, mix, normed_t,
        w_query, w_key, w_value, w_output, w_down, tokens,
    )
    (
        grad_tokens, grad_gate, grad_up, gain_attn_grad, gain_mlp_grad, layer_out, grad_query, grad_key, grad_value,
        grad_output, grad_down, logit_grad, memory_next, normal_next, later_offset,
    ) = last(
        grad_tokens, mlp_grads, grad_gate, gains, layer_out, grad_query, grad_key, grad_value, grad_output, grad_down, logit_grad,
        memory_next, normal_next, later_offset,
    )
    return (
        layer_out.reshape(tokens.shape),
        grad_tokens.reshape(tokens.shape),
        grad_query,
        grad_key,
        grad_value,
        grad_output,
        grad_gate,
        grad_up,
        grad_down,
        gain_attn_grad.reshape(-1),
        gain_mlp_grad.reshape(-1),
        logit_grad[0, :4],
        memory_next[None],
        normal_next[None, :4],
        later_offset[None, :4],
    )


def solution(mesh):
    torus = Mesh(
        mesh.devices.reshape(4, 4, 2, mesh.shape["tensor"]), ("seq_0", "seq_1", "seq_2", "tensor")
    )
    weight = P(None, "tensor")
    grad = P(SEQ, "tensor")
    return jax.shard_map(
        on_device,
        mesh=torus,
        in_specs=(P(SEQ, None), P(SEQ, None)) + (weight,) * 7 + (P(), P(), P("tensor"), P()),
        out_specs=(P(SEQ, None), P(SEQ, None))
        + (grad,) * 7
        + (P(), P(), P("tensor"), P(SEQ, "tensor", None, None), P(SEQ, "tensor", None), P(SEQ, "tensor", None)),
        check_vma=False,
    )
```

```python
import functools

import jax
import jax.numpy as jnp
from jax import lax
from jax.experimental import pallas as pl
from jax.experimental.pallas import tpu as pltpu
from jax.sharding import Mesh
from jax.sharding import PartitionSpec as P

SEQ = ("seq_0", "seq_1", "seq_2")
MESH_ID = pl.DeviceIdType.MESH
VMEM = pl.BlockSpec(memory_space=pltpu.VMEM)
BF = jnp.bfloat16
F32 = jnp.float32

epsilon = 1e-06


def remote(src, dst, send, recv, device):
    return pltpu.make_async_remote_copy(
        src_ref=src, dst_ref=dst, send_sem=send, recv_sem=recv, device_id=device, device_id_type=MESH_ID
    )


def meet(devices):
    barrier = pltpu.get_barrier_semaphore()
    for device in devices:
        pl.semaphore_signal(barrier, inc=1, device_id=device, device_id_type=MESH_ID)
    pl.semaphore_wait(barrier, len(devices))


def params(collective_id, mib):
    return pltpu.CompilerParams(
        collective_id=collective_id, has_side_effects=True, vmem_limit_bytes=mib << 20
    )


def seq_place(index):
    return {"seq_0": index // 8, "seq_1": lax.rem(index // 2, 4), "seq_2": lax.rem(index, 2)}


def seq_index():
    return lax.axis_index("seq_0") * 8 + lax.axis_index("seq_1") * 2 + lax.axis_index("seq_2")


def mul(a, b):
    return jnp.dot(a.astype(BF), b.astype(BF), preferred_element_type=F32)


def mul_t(a, b):
    return lax.dot_general(a.astype(BF), b.astype(BF), (((0,), (0,)), ((), ())), preferred_element_type=F32)


def ring_places():
    x, y, c = (lax.axis_index(a) for a in SEQ)
    return x, y, c


def rows_by_rows(a, b):
    return lax.dot_general(a, b, (((1,), (1,)), ((), ())), preferred_element_type=F32)


class RingSum:
    def __init__(self, src, bufs, send, recv, base, axis, rows=None):
        self.src, self.bufs, self.me = src, bufs, lax.axis_index(axis)
        rows = pl.ds(0, src.shape[1]) if rows is None else rows
        self.rows = rows
        half = src.shape[2] // 2
        self.a, self.b = pl.ds(0, half), pl.ds(half, half)
        self.right, self.left = lax.rem(self.me + 1, 4), lax.rem(self.me + 3, 4)
        far = lax.rem(self.me + 2, 4)
        to_right, to_left = {axis: self.right}, {axis: self.left}

        def copy(piece, landing, slot, device):
            return remote(piece, bufs.at[landing], send.at[base + slot], recv.at[base + slot], device)

        self.c0 = copy(src.at[far, rows, self.a], 0, 0, to_right)
        self.c1 = copy(src.at[far, rows, self.b], 1, 1, to_left)
        self.c2 = copy(src.at[self.right, rows, self.b], 2, 2, to_right)
        self.c3 = copy(src.at[self.left, rows, self.a], 3, 3, to_left)
        self.c4 = copy(bufs.at[6], 4, 4, to_right)
        self.c5 = copy(bufs.at[7], 5, 5, to_left)

    def start_a(self):
        self.c0.start()
        self.c3.start()

    def start_b(self):
        self.c1.start()
        self.c2.start()

    def start(self):
        self.c0.start()
        self.c1.start()
        self.c3.start()
        self.c2.start()

    def middle(self):
        src, bufs = self.src, self.bufs
        self.c0.wait_recv()
        bufs[6] = (bufs[0].astype(F32) + src[self.right, self.rows, self.a].astype(F32)).astype(BF)
        self.c4.start()
        self.c1.wait_recv()
        bufs[7] = (bufs[1].astype(F32) + src[self.left, self.rows, self.b].astype(F32)).astype(BF)
        self.c5.start()

    def finish(self, put):
        src, bufs = self.src, self.bufs
        self.c3.wait_recv()
        self.c4.wait_recv()
        put(self.a, src[self.me, self.rows, self.a].astype(F32) + bufs[4].astype(F32) + bufs[3].astype(F32))
        self.c2.wait_recv()
        self.c5.wait_recv()
        put(self.b, src[self.me, self.rows, self.b].astype(F32) + bufs[5].astype(F32) + bufs[2].astype(F32))

    def drain(self):
        for copy in (self.c0, self.c1, self.c2, self.c3, self.c4, self.c5):
            copy.wait_send()


class RingGather:
    def __init__(self, buf, send, recv, base, axis, rows=None):
        self.me = lax.axis_index(axis)
        half = buf.shape[1 if rows is None else 2] // 2
        right, left = lax.rem(self.me + 1, 4), lax.rem(self.me + 3, 4)
        to_right, to_left = {axis: right}, {axis: left}

        def copy(q, h, slot, device):
            part = pl.ds(half * h, half)
            piece = buf.at[q, part] if rows is None else buf.at[q, rows, part]
            return remote(piece, piece, send.at[base + slot], recv.at[base + slot], device)

        self.r0, self.l1 = copy(self.me, 0, 0, to_right), copy(self.me, 1, 1, to_left)
        self.r1, self.l0 = copy(self.me, 1, 2, to_right), copy(self.me, 0, 3, to_left)
        self.f0, self.f1 = copy(left, 0, 4, to_right), copy(right, 1, 5, to_left)

    def start(self):
        for copy in (self.r0, self.l1, self.r1, self.l0):
            copy.start()

    def middle(self):
        self.r0.wait_recv()
        self.f0.start()
        self.l1.wait_recv()
        self.f1.start()

    def finish(self):
        for copy in (self.r1, self.l0, self.f0, self.f1):
            copy.wait_recv()

    def drain(self):
        for copy in (self.r0, self.l1, self.r1, self.l0, self.f0, self.f1):
            copy.wait_send()


class SeqSum:
    def __init__(self, product, got, first, first_bufs, second, second_bufs, send, recv, base, x_first):
        self.product, self.got, self.first, self.second, self.x_first = product, got, first, second, x_first
        self.core = lax.axis_index("seq_2")
        self.swap = remote(
            product.at[pl.ds(0, 16), 1 - self.core], got, send.at[base], recv.at[base], {"seq_2": 1 - self.core}
        )
        axes = ("seq_0", "seq_1") if x_first else ("seq_1", "seq_0")
        self.one = RingSum(first, first_bufs, send, recv, base + 1, axes[0])
        self.two = RingSum(second, second_bufs, send, recv, base + 7, axes[1])

    def start(self):
        self.swap.start()

    def first_ring(self):
        self.add()
        self.one.start()

    def add(self):
        self.swap.wait_recv()
        for x in range(4):
            for y in range(4):
                at = 4 * x + y
                q, r = (x, y) if self.x_first else (y, x)
                total = self.product[at, self.core].astype(F32) + self.got[at].astype(F32)
                self.first[q, pl.ds(64 * r, 64)] = total.astype(BF)

    def second_ring(self):
        def put(cols, value):
            for r in range(4):
                self.second[r, :, cols] = value[64 * r : 64 * (r + 1)].astype(BF)

        self.one.finish(put)
        self.two.start()

    def finish(self, out):
        def put(cols, value):
            out[:, cols] = value

        self.two.finish(put)

    def drain(self):
        self.swap.wait_send()
        self.one.drain()
        self.two.drain()


def greet_all():
    barrier = pltpu.get_barrier_semaphore()
    me, z = seq_index(), lax.axis_index("tensor")

    def greet_seq(k, carry):
        pl.semaphore_signal(barrier, inc=1, device_id=seq_place(lax.rem(me + k, 32)), device_id_type=MESH_ID)
        return carry

    lax.fori_loop(1, 32, greet_seq, 0)
    for k in (1, 2, 3):
        pl.semaphore_signal(barrier, inc=1, device_id={"tensor": lax.rem(z + k, 4)}, device_id_type=MESH_ID)


def all_greeted():
    pl.semaphore_wait(pltpu.get_barrier_semaphore(), 34)


class TotalOfAll:
    def __init__(self, mine, extra, by_z, line, by_seq, total, send, recv, base):
        self.mine, self.extra, self.by_z, self.line, self.by_seq, self.total = mine, extra, by_z, line, by_seq, total
        self.z, self.me = lax.axis_index("tensor"), seq_index()
        self.send, self.recv, self.base = send, recv, base
        peers = [lax.rem(self.z + k, 4) for k in (1, 2, 3)]
        self.split = [
            remote(mine.at[p], by_z.at[self.z], send.at[base + k], recv.at[base + k], {"tensor": p})
            for k, p in enumerate(peers)
        ]
        self.join = [
            remote(total.at[self.z], total.at[self.z], send.at[base + 3 + k], recv.at[base + 3 + k], {"tensor": p})
            for k, p in enumerate(peers)
        ]

    def start(self):
        for copy in self.split:
            copy.start()

    def over_seq(self):
        self.by_z[self.z] = self.mine[self.z]
        for copy in self.split:
            copy.wait_recv()
        self.line[0:8] = (self.by_z[0] + self.by_z[1]) + (self.by_z[2] + self.by_z[3])
        self.line[8:16] = self.extra[...]
        self.by_seq[self.me] = self.line[...]

        def push(k, carry):
            device = seq_place(lax.rem(self.me + k, 32))
            remote(self.line, self.by_seq.at[self.me], self.send.at[self.base + 6], self.recv.at[self.base + 6], device).start()
            return carry

        lax.fori_loop(1, 32, push, 0)

    def over_tensor(self, extra_out):
        others = self.by_seq.at[pl.ds(0, 31)]
        pltpu.make_async_copy(others, others, self.recv.at[self.base + 6]).wait()
        summed = jnp.sum(self.by_seq[...], axis=0)
        self.total[self.z] = summed[0:8]
        extra_out[...] = summed[8:16]
        for copy in self.join:
            copy.start()

    def finish(self):
        for copy in self.join:
            copy.wait_recv()

    def drain(self):
        for copy in (*self.split, *self.join):
            copy.wait_send()
        others = self.by_seq.at[pl.ds(0, 31)]
        pltpu.make_async_copy(others, others, self.send.at[self.base + 6]).wait()


def feature_of(v):
    return jnp.where(v > 0, v + 1.0, jnp.exp(jnp.minimum(v, 0.0)))


def slope_of(v):
    return jnp.where(v > 0, 1.0, jnp.exp(jnp.minimum(v, 0.0)))


ANYWHERE = pl.BlockSpec(memory_space=pl.ANY)


def keep_of(valid):
    length = jnp.where(seq_index() == 31, valid[...], 384)
    return (lax.broadcasted_iota(jnp.int32, (384, 1), 0) < length).astype(F32)


SMEM = pl.BlockSpec(memory_space=pltpu.SMEM)


def gate_rows(gate, logit):
    for h in range(4):
        gate[h : h + 1] = jax.nn.sigmoid(jnp.full((1, 128), logit[h], F32))


def flat(weight):
    return weight.reshape(-1, 512)


class Moves:
    def __init__(self, sems):
        self.sems, self.count = sems, 0

    def start(self, src, dst):
        copy = pltpu.make_async_copy(src, dst, self.sems.at[self.count])
        self.count += 1
        copy.start()
        return copy


def front_kernel(
    gain_attn,
    gain_mlp,
    valid,
    gate_logit,
    i_tokens,
    cotangent,
    w_query,
    w_key,
    w_value,
    w_output,
    w_down,
    w_gate,
    w_up,
    o_normed_t,
    o_grad_out_t,
    o_query,
    o_key,
    o_value,
    o_probs,
    o_local_out,
    o_retrieved,
    o_mix,
    o_hidden,
    o_grads,
    o_recall,
    o_inverse,
    o_forth,
    grad_out_own,
    offset,
    normal_next,
    memory_prev,
    memory_next,
    ys,
    xs,
    pair_e,
    middle,
    grad_two,
    out_gate,
    keep,
    gate,
    weights,
    weight_o,
    weight_d,
    weight_g,
    hidden,
    normed_two,
    normed,
    turned,
    grad_out,
    got_rows,
    first_rows,
    first_bufs,
    second_rows,
    second_bufs,
    inverse,
    grad_hidden,
    query,
    key,
    value,
    probs,
    local_out,
    retrieved,
    mix,
    line,
    lines,
    eb,
    source,
    got,
    pair_m,
    got_m,
    part,
    part_bufs,
    moves,
    send,
    recv,
):
    move = Moves(moves)
    tokens = hidden
    load_tokens = move.start(i_tokens, tokens)
    loads = [move.start(w, weights.at[i]) for i, w in enumerate((w_key, w_query, w_value))]
    load_cotangent = move.start(cotangent, grad_out)
    load_o = move.start(w_output, weight_o)
    load_d = [move.start(w_down.at[pl.ds(512 * i, 512)], weight_d.at[pl.ds(512 * i, 512)]) for i in range(4)]
    greet_all()
    keep[...] = keep_of(valid)
    gate_rows(gate, gate_logit)
    x, y, c = ring_places()
    z, me = lax.axis_index("tensor"), seq_index()
    partner = {"seq_2": 1 - c}
    mine, theirs = 2 * c, 2 * (1 - c)
    sums = [
        SeqSum(
            rows, got_rows.at[i], first_rows.at[i], first_bufs.at[i], second_rows.at[i], second_bufs.at[i],
            send, recv, 27 + 13 * i, i % 2 == 0,
        )
        for i, rows in enumerate((weight_o, weights.at[2], weights.at[0], weights.at[1]))
    ]
    parts = [pl.ds(0, 48), pl.ds(48, 48)]
    z_sums = [RingSum(part, part_bufs.at[i], send, recv, 79 + 6 * i, "tensor", parts[i]) for i in (0, 1)]
    z_gathers = [RingGather(normed_two, send, recv, 91 + 6 * i, "tensor", parts[i]) for i in (0, 1)]
    z_backs = [RingSum(part, part_bufs.at[i], send, recv, 6 * i, "tensor", parts[i]) for i in (0, 1)]
    y_ring = RingGather(ys, send, recv, 12, "seq_1")
    x_ring = RingGather(xs, send, recv, 18, "seq_0")
    swap = remote(eb.at[pl.ds(theirs, 2)], got, send.at[24], recv.at[24], partner)
    give = remote(pair_m, got_m, send.at[25], recv.at[25], partner)
    cols = [slice(128 * h, 128 * (h + 1)) for h in range(4)]
    stores = []

    load_tokens.wait()
    for q in range(4):
        rows = pl.ds(96 * q, 96)
        stream = tokens[rows].astype(F32)
        inv = lax.rsqrt(jnp.mean(stream * stream, axis=1, keepdims=True) + epsilon)
        normed[rows] = (stream * inv * gain_attn[...]).astype(BF)
    loads[0].wait()
    key[...] = jnp.dot(normed[...], flat(weights[0]), preferred_element_type=F32).astype(BF)
    feat_q = lambda h: feature_of(query[:, cols[h]].astype(F32))
    feat_k = lambda h: feature_of(key[:, cols[h]].astype(F32))
    line[...] = jnp.zeros_like(line)
    for h in range(4):
        line[h : h + 1] = jnp.sum(feat_k(h) * keep[...], axis=0, keepdims=True)
    lines[me] = line[...]
    all_greeted()

    def push(k, carry):
        remote(line, lines.at[me], send.at[26], recv.at[26], seq_place(lax.rem(me + k, 32))).start()
        return carry

    lax.fori_loop(1, 32, push, 0)
    stores.append(move.start(key, o_key))
    loads[1].wait()
    query[...] = jnp.dot(normed[...], flat(weights[1]), preferred_element_type=F32).astype(BF)
    stores.append(move.start(query, o_query))
    loads[2].wait()
    value[...] = jnp.dot(normed[...], flat(weights[2]), preferred_element_type=F32).astype(BF)
    stores.append(move.start(value, o_value))
    load_g = move.start(w_gate, weight_g)
    at_row = lax.broadcasted_iota(jnp.int32, (384, 384), 0)
    at_col = lax.broadcasted_iota(jnp.int32, (384, 384), 1)
    valid = jnp.sum(keep[...], axis=0, keepdims=True)
    allowed = (at_row >= at_col) & (at_col.astype(F32) < valid)

    def attend(h):
        at = cols[h]
        scores = rows_by_rows(query[:, at], key[:, at]) * 128 ** (-0.5)
        masked = jnp.where(allowed, scores, -1e30)
        raised = jnp.exp(masked - jnp.max(masked, axis=1, keepdims=True))
        low = (raised * (1.0 / jnp.sum(raised, axis=1, keepdims=True))).astype(BF)
        probs[h] = low
        local_out[:, at] = jnp.dot(low, value[:, at], preferred_element_type=F32)
        total = mul_t(feat_k(h) * keep[...], value[:, at])
        source[h] = total
        eb[h, :, 128:256] = total.astype(BF)

    for h in range(4):
        attend(h)
    stores.append(move.start(probs, o_probs))
    stores.append(move.start(local_out, o_local_out))
    others = lines.at[pl.ds(0, 31)]
    pltpu.make_async_copy(others, others, recv.at[26]).wait()
    passed = lax.broadcasted_iota(jnp.int32, (32, 8, 128), 0) < me
    before = jnp.sum(jnp.where(passed, lines[...], 0.0), axis=0)
    normal_next[...] = before + line[...]
    offset[...] = before + 384.0
    for h in range(4):
        fk = feat_k(h)
        kept = fk * keep[...] * (1.0 / jnp.sum(fk * offset[h : h + 1], axis=1, keepdims=True))
        eb[h, :, 0:128] = mul_t(kept, fk).astype(BF)
    swap.start()
    load_cotangent.wait()
    grad_out[...] = grad_out[...] * keep[...].astype(BF)
    grad_out_own[...] = grad_out[pl.ds(pl.multiple_of(96 * z, 96), 96)]
    swap.wait_recv()
    of = [pl.ds(0, 128), pl.ds(128, 128)]
    firsts = []
    for h in (0, 1):
        here, there = eb[mine + h].astype(F32), got[h].astype(F32)
        first, second = jnp.where(c == 0, here, there), jnp.where(c == 0, there, here)
        firsts.append(first)
        pair_e[0, h] = first[:, :128].astype(BF)
        pair_e[1, h] = second[:, :128].astype(BF)
        ys[y, of[h]] = (first + second - mul(second[:, :128], first)).astype(BF)
    y_ring.start()

    def hidden_part(i):
        load_d[i].wait()
        rows = pl.ds(512 * i, 512)
        product = jnp.dot(grad_out[:, 512 * i : 512 * (i + 1)], weight_d[rows], preferred_element_type=F32)
        if i == 0:
            grad_hidden[...] = product
        else:
            grad_hidden[...] += product

    hidden_part(0)
    y_ring.middle()
    hidden_part(1)
    y_ring.finish()
    starts = []
    for h in (0, 1):
        so_far = ys[0, of[h]].astype(F32)
        start = jnp.where(y > 0, so_far, 0.0)
        for k in (1, 2, 3):
            step = ys[k, of[h]].astype(F32)
            so_far = so_far + step - mul(step[:, :128], so_far)
            if k < 3:
                start = jnp.where(y > k, so_far, start)
        xs[x, of[h]] = so_far.astype(BF)
        starts.append(start)
    x_ring.start()
    hidden_part(2)
    x_ring.middle()
    hidden_part(3)
    load_u = move.start(w_up, weight_d)
    load_o.wait()
    x_ring.finish()
    for h in (0, 1):
        m = jnp.where(x > 0, xs[0, of[h]][:, 128:].astype(F32), 0.0)
        for k in (1, 2):
            step = xs[k, of[h]].astype(F32)
            m = jnp.where(x > k, m + step[:, 128:] - mul(step[:, :128], m), m)
        m = m + starts[h][:, 128:] - mul(starts[h][:, :128], m)
        second = m + firsts[h][:, 128:] - mul(firsts[h][:, :128], m)
        memory_prev[mine + h] = jnp.where(c == 0, m, second)
        pair_m[h] = jnp.where(c == 0, second, m)
    give.start()
    give.wait_recv()
    inverse[...] = jnp.zeros_like(inverse)
    inverse[:, 8:9] = keep[...]
    for h in (0, 1):
        memory_prev[theirs + h] = got_m[h]
    for h in range(4):
        at, fq, sig = cols[h], feat_q(h), gate[h : h + 1]
        inv_q = 1.0 / jnp.sum(fq * offset[h : h + 1], axis=1, keepdims=True)
        inverse[:, h : h + 1] = inv_q
        found = mul(fq, memory_prev[h]) * inv_q
        retrieved[:, at] = found
        mix[:, at] = (sig * found + (1.0 - sig) * local_out[:, at]).astype(BF)
    for half in (0, 1):
        rows = pl.ds(1024 * half, 1024)
        part[:, :, rows] = rows_by_rows(mix[...], flat(weight_o[8 * half : 8 * half + 8])).astype(BF).reshape(4, 96, 1024)
        for z_sum in z_sums:
            (z_sum.start_a, z_sum.start_b)[half]()
    store_found = move.start(retrieved, o_retrieved)
    stores.append(move.start(mix, o_mix))
    for h in range(4):
        m = memory_prev[h]
        memory_next[h] = m + source[h] - mul(eb[h][:, :128], m)
    turned[...] = normed[...].T
    store_t = move.start(turned, o_normed_t)
    z_sums[0].middle()
    z_sums[1].middle()
    store_found.wait()
    recall = retrieved
    for h in range(4):
        fk, off = feat_k(h), offset[h : h + 1]
        inv_k = 1.0 / jnp.sum(fk * off, axis=1, keepdims=True)
        inverse[:, 4 + h : 5 + h] = inv_k
        recall[:, cols[h]] = mul(fk, memory_prev[h]) * inv_k
    stores.append(move.start(recall, o_recall))
    stores.append(move.start(inverse, o_inverse))

    def second_norm(i):
        own_tokens = tokens[pl.ds(pl.multiple_of(96 * z + 48 * i, 16), 48)].astype(F32)

        def put(at, total):
            lanes = slice(0, 1024) if at is z_sums[i].a else slice(1024, 2048)
            middle[parts[i], at] = own_tokens[:, lanes] + total

        z_sums[i].finish(put)
        stream = middle[parts[i]]
        inv = lax.rsqrt(jnp.mean(stream * stream, axis=1, keepdims=True) + epsilon)
        normed_two[z, parts[i]] = (stream * inv * gain_mlp[...]).astype(BF)
        z_gathers[i].start()

    second_norm(0)
    second_norm(1)
    z_gathers[0].middle()
    z_gathers[1].middle()
    store_t.wait()
    turned[...] = grad_out[...].T
    store_t = move.start(turned, o_grad_out_t)
    for store in stores:
        store.wait()
    store_t.wait()
    for z_sum in z_sums:
        z_sum.drain()
    load_g.wait()
    load_u.wait()
    for z_gather in z_gathers:
        z_gather.finish()
    for z_gather in z_gathers:
        z_gather.drain()
    turned[...] = normed_two[...].reshape(384, 2048).T

    def tile(i):
        for half in (2 * i, 2 * i + 1):
            narrow_tile(half)

    def narrow_tile(i):
        lanes = slice(256 * i, 256 * (i + 1))
        rows = normed_two[...].reshape(384, 2048)
        gate_pre = jnp.dot(rows, weight_g[:, lanes], preferred_element_type=F32)
        up_pre = jnp.dot(rows, weight_d[:, lanes], preferred_element_type=F32)
        back_hidden = grad_hidden[:, lanes]
        sig = jax.nn.sigmoid(gate_pre)
        swish = gate_pre * sig
        hidden[:, lanes] = (swish * up_pre).astype(BF)
        grad_out[:, lanes] = (back_hidden * swish).astype(BF)
        normed[:, lanes] = (back_hidden * up_pre * sig * (1.0 + gate_pre * (1.0 - sig))).astype(BF)

    def gradient(side, i):
        result = jnp.dot(turned[...], side[:, 512 * i : 512 * (i + 1)], preferred_element_type=F32)
        return result.astype(BF).reshape(16, 2, 64, 512)

    def return_part(i):
        rows = pl.ds(512 * i, 512)
        value = rows_by_rows(normed[...], weight_g[rows]) + rows_by_rows(grad_out[...], weight_d[rows])
        part[:, :, rows] = value.astype(BF).reshape(4, 96, 512)

    slots = []

    def leave(i):
        slot = (weight_o, weights.at[2])[i % 2]
        if i >= 2:
            slots[i - 2].wait()
        slot[...] = gradient(grad_out, i)
        slots.append(move.start(slot, o_grads.at[:, :, :, pl.ds(512 * i, 512)]))

    tile(0)
    weight_o[...] = gradient(normed, 0)
    sums[0].start()
    tile(1)
    weights[2] = gradient(normed, 1)
    sums[1].start()
    sums[0].first_ring()
    tile(2)
    weights[0] = gradient(normed, 2)
    sums[2].start()
    sums[1].first_ring()
    tile(3)
    weights[1] = gradient(normed, 3)
    sums[3].start()
    stores = [move.start(hidden, o_hidden)]
    sums[0].one.middle()
    sums[2].first_ring()
    return_part(0)
    return_part(1)
    for z_back in z_backs:
        z_back.start_a()
    sums[1].one.middle()
    sums[3].first_ring()
    return_part(2)
    return_part(3)
    for z_back in z_backs:
        z_back.start_b()
    load_down = move.start(w_down, weight_g)
    sums[0].swap.wait_send()
    leave(0)
    sums[0].second_ring()
    sums[1].swap.wait_send()
    leave(1)
    z_backs[0].middle()
    z_backs[1].middle()
    sums[2].one.middle()
    sums[1].second_ring()
    leave(2)
    sums[0].two.middle()
    sums[3].one.middle()
    leave(3)
    sums[2].second_ring()
    sums[1].two.middle()
    load_down.wait()
    for half in (0, 1):
        rows = pl.ds(1024 * half, 1024)
        normed_two[:, :, rows] = rows_by_rows(hidden[...], weight_g[rows]).astype(BF).reshape(4, 96, 1024)
    stores.append(move.start(normed_two, o_forth))
    sums[3].second_ring()
    sums[0].finish(out_gate.at[:, pl.ds(0, 512)])
    sums[2].two.middle()
    sums[1].finish(out_gate.at[:, pl.ds(512, 512)])
    for i in (0, 1):

        def put(at, total, i=i):
            grad_two[parts[i], at] = total

        z_backs[i].finish(put)
    sums[3].two.middle()
    for i in (2, 3):
        sums[i].finish(out_gate.at[:, pl.ds(512 * i, 512)])
    for copy in (*stores, *slots[2:]):
        copy.wait()
    for s in sums:
        s.one.drain()
        s.two.drain()
    for s in sums[2:]:
        s.swap.wait_send()
    for ring in (*z_backs, y_ring, x_ring):
        ring.drain()
    swap.wait_send()
    give.wait_send()
    pltpu.make_async_copy(others, others, send.at[26]).wait()


def front(cid, *args):
    shape = jax.ShapeDtypeStruct
    low = lambda *dims: pltpu.VMEM(dims, BF)
    full = lambda *dims: pltpu.VMEM(dims, F32)
    return pl.pallas_call(
        front_kernel,
        out_shape=(
            shape((2048, 384), BF),
            shape((2048, 384), BF),
            shape((384, 512), BF),
            shape((384, 512), BF),
            shape((384, 512), BF),
            shape((4, 384, 384), BF),
            shape((384, 512), F32),
            shape((384, 512), F32),
            shape((384, 512), BF),
            shape((384, 2048), BF),
            shape((16, 2, 64, 2048), BF),
            shape((384, 512), F32),
            shape((384, 128), F32),
            shape((4, 96, 2048), BF),
            shape((96, 2048), BF),
            shape((8, 128), F32),
            shape((8, 128), F32),
            shape((4, 128, 128), F32),
            shape((4, 128, 128), F32),
            shape((4, 256, 256), BF),
            shape((4, 256, 256), BF),
            shape((2, 2, 128, 128), BF),
            shape((96, 2048), F32),
            shape((96, 2048), F32),
            shape((64, 2048), F32),
        ),
        in_specs=[VMEM] * 3 + [SMEM] + [ANYWHERE] * 9,
        out_specs=(ANYWHERE,) * 14 + (VMEM,) * 11,
        scratch_shapes=[
            full(384, 1),
            full(4, 128),
            low(3, 16, 2, 64, 512),
            low(16, 2, 64, 512),
            low(2048, 2048),
            low(2048, 2048),
            low(384, 2048),
            low(4, 96, 2048),
            low(384, 2048),
            low(2048, 384),
            low(384, 2048),
            low(4, 16, 64, 512),
            low(4, 4, 256, 512),
            low(4, 8, 256, 256),
            low(4, 4, 64, 512),
            low(4, 8, 64, 256),
            full(384, 128),
            full(384, 2048),
            low(384, 512),
            low(384, 512),
            low(384, 512),
            low(4, 384, 384),
            full(384, 512),
            full(384, 512),
            low(384, 512),
            full(8, 128),
            full(32, 8, 128),
            low(4, 128, 256),
            full(4, 128, 128),
            low(2, 128, 256),
            full(2, 128, 128),
            full(2, 128, 128),
            low(4, 96, 2048),
            low(2, 8, 48, 1024),
            pltpu.SemaphoreType.DMA((32,)),
            pltpu.SemaphoreType.DMA((103,)),
            pltpu.SemaphoreType.DMA((103,)),
        ],
        name="front",
        compiler_params=params(cid, 63),
    )(*args)


def neighbours():
    x, y, c = ring_places()
    z = lax.axis_index("tensor")
    near = [{"seq_2": 1 - c}]
    for axis, at in (("seq_0", x), ("seq_1", y), ("tensor", z)):
        near += [{axis: lax.rem(at + 1, 4)}, {axis: lax.rem(at + 3, 4)}]
    return near


def rest_kernel(
    grad_two,
    middle,
    gain_attn,
    gain_mlp,
    grad_out,
    offset,
    gate_logit,
    memory,
    ys,
    xs,
    pair_e,
    i_grad_out_t,
    i_hidden,
    i_query,
    i_key,
    i_value,
    i_probs,
    i_local_out,
    i_retrieved,
    i_mix,
    i_normed_t,
    i_recall,
    i_inverse,
    i_forth,
    w_query,
    w_key,
    w_value,
    w_output,
    tokens,
    o_layer_out,
    o_grad_tokens,
    o_later,
    o_out_down,
    o_out_query,
    o_out_key,
    o_out_value,
    o_out_output,
    o_gains,
    o_logits_out,
    layer_out,
    grad_tokens,
    later,
    out_down,
    out_query,
    out_key,
    out_value,
    out_output,
    gains,
    logits_out,
    gate,
    branch,
    grad_middle,
    grads,
    left,
    hidden,
    query,
    key,
    value,
    probs,
    local_out,
    retrieved,
    mix,
    weight_o,
    weight_in,
    products,
    got_rows,
    first_rows,
    first_bufs,
    second_rows,
    second_bufs,
    first_bufs_2,
    second_bufs_2,
    forth,
    z_bufs,
    own,
    inverse,
    recall,
    grad_mix,
    grad_query,
    grad_key,
    grad_value,
    source,
    got,
    s_y,
    s_x,
    pair_l,
    got_l,
    adjoint,
    line,
    lines,
    mine_gains,
    logits,
    by_z,
    total_line,
    by_seq,
    moves,
    send,
    recv,
):
    x, y, c = ring_places()
    z, me = lax.axis_index("tensor"), seq_index()
    move = Moves(moves)
    pairs = (
        (i_grad_out_t, left),
        (i_hidden, hidden),
        (i_forth, forth),
        (w_output, weight_o),
        (i_query, query),
        (i_inverse, inverse),
        (i_probs, probs),
        (i_key, key),
        (i_value, value),
        (i_mix, mix),
        (i_retrieved, retrieved),
        (i_local_out, local_out),
        (i_recall, recall),
        (w_query, weight_in.at[0]),
        (w_key, weight_in.at[1]),
        (w_value, weight_in.at[2]),
    )
    barrier = pltpu.get_barrier_semaphore()
    for device in neighbours():
        pl.semaphore_signal(barrier, inc=1, device_id=device, device_id_type=MESH_ID)
    loads = [move.start(src, dst) for src, dst in pairs]
    gate_rows(gate, gate_logit)
    partner = {"seq_2": 1 - c}
    mine, theirs = 2 * c, 2 * (1 - c)
    parts = [pl.ds(0, 48), pl.ds(48, 48)]
    z_branches = [RingGather(branch, send, recv, 6 * i, "tensor", parts[i]) for i in (0, 1)]
    z_forths = [RingSum(forth, z_bufs.at[i], send, recv, (12, 174)[i], "tensor", parts[i]) for i in (0, 1)]
    z_layer = RingGather(layer_out, send, recv, 18, "tensor")
    y_ring = RingGather(s_y, send, recv, 24, "seq_1")
    x_ring = RingGather(s_x, send, recv, 30, "seq_0")
    swap = remote(source.at[pl.ds(theirs, 2)], got, send.at[36], recv.at[36], partner)
    give = remote(pair_l, got_l, send.at[37], recv.at[37], partner)
    z_ends = [RingSum(forth, z_bufs.at[i], send, recv, 143 + 6 * i, "tensor", parts[i]) for i in (0, 1)]
    z_tokens = [RingGather(grad_tokens, send, recv, 155 + 6 * i, "tensor", parts[i]) for i in (0, 1)]
    total = TotalOfAll(mine_gains, logits, by_z, total_line, by_seq, gains, send, recv, 167)

    def seq_sums(base, first_bufs, second_bufs):
        return [
            SeqSum(
                products.at[i], got_rows.at[i], first_rows.at[i], first_bufs.at[i], second_rows.at[i],
                second_bufs.at[i], send, recv, base + 13 * i, i % 2 == 0,
            )
            for i in range(4)
        ]

    sums, ends = seq_sums(39, first_bufs, second_bufs), seq_sums(91, first_bufs_2, second_bufs_2)
    cols = [slice(128 * h, 128 * (h + 1)) for h in range(4)]
    of = [pl.ds(0, 128), pl.ds(128, 128)]
    feat_q = lambda h: feature_of(query[:, cols[h]].astype(F32))
    feat_k = lambda h: feature_of(key[:, cols[h]].astype(F32))
    scale = 128 ** (-0.5)

    def product(group, i, right):
        result = jnp.dot(left[...], right, preferred_element_type=F32).astype(BF)
        products[i] = result.reshape(16, 2, 64, 512)
        group[i].start()

    def down(i):
        product(sums, i, hidden[:, 512 * i : 512 * (i + 1)])

    def norm_back(stream, grad_normed, gain, first_row, i):
        inv = lax.rsqrt(jnp.mean(stream * stream, axis=1, keepdims=True) + epsilon)
        weighted = grad_normed * gain[...]
        inner = jnp.sum(weighted * stream, axis=1, keepdims=True)
        scaled = stream * inv
        line_of = jnp.sum(grad_normed * scaled, axis=0, keepdims=True)
        for r in range(16):
            at = (first_row + r // 8, slice(r % 8, r % 8 + 1))
            piece = line_of[:, 128 * r : 128 * (r + 1)]
            mine_gains[at] = piece if i == 0 else mine_gains[at] + piece
        return inv * weighted - scaled * (inv * inv * inner * (1.0 / stream.shape[1]))

    for i in (0, 1):
        rows = parts[i]
        result = grad_out[rows].astype(F32) + norm_back(middle[rows], grad_two[rows], gain_mlp, 2, i)
        grad_middle[rows] = result
        branch[z, rows] = result.astype(BF)
        if i == 0:
            pl.semaphore_wait(barrier, 7)
        z_branches[i].start()
    loads[0].wait()
    loads[1].wait()
    down(0)
    down(1)
    z_branches[0].middle()
    sums[0].first_ring()
    z_branches[1].middle()
    down(2)
    sums[1].first_ring()
    down(3)
    sums[2].add()
    sums[0].one.middle()
    sums[3].add()
    for load in loads[2:6]:
        load.wait()
    for z_branch in z_branches:
        z_branch.finish()
    for z_forth in z_forths:
        z_forth.start()
    grad_mix[...] = jnp.dot(branch[...].reshape(384, 2048), weight_o[...], preferred_element_type=F32)

    def point(h):
        return gate[h : h + 1] * grad_mix[:, cols[h]] * inverse[:, h : h + 1]

    for h in range(4):
        source[h] = mul_t(feat_q(h), point(h)).astype(BF)
    swap.start()

    def attend(h):
        at = cols[h]
        grad_local = ((1.0 - gate[h : h + 1]) * grad_mix[:, at]).astype(BF)
        low = probs[h]
        p = low.astype(F32)
        grad_probs = rows_by_rows(grad_local, value[:, at])
        grad_value[:, at] = mul_t(low, grad_local)
        grad_scores = (p * (grad_probs - jnp.sum(grad_probs * p, axis=1, keepdims=True))).astype(BF)
        grad_query[:, at] = mul(grad_scores, key[:, at]) * scale
        grad_key[:, at] = mul_t(grad_scores, query[:, at]) * scale

    for load in loads[6:9]:
        load.wait()
    attend(0)
    sums[1].one.middle()
    swap.wait_recv()
    seconds = []
    for h in (0, 1):
        here, there = source[mine + h].astype(F32), got[h].astype(F32)
        first, second = jnp.where(c == 0, here, there), jnp.where(c == 0, there, here)
        seconds.append(second)
        s_y[y, of[h]] = (first + second - mul_t(pair_e[0, h], second)).astype(BF)
    y_ring.start()
    attend(1)
    y_ring.middle()
    sums[0].second_ring()
    attend(2)
    for z_forth in z_forths:
        z_forth.middle()
    sums[1].second_ring()
    for s in sums:
        s.swap.wait_send()
    left[...] = branch[...].reshape(384, 2048).T
    for z_branch in z_branches:
        z_branch.drain()
    load_own = move.start(tokens.at[pl.ds(pl.multiple_of(96 * z, 96), 96)], branch.at[0])
    y_ring.finish()
    for h in (0, 1):
        so_far = s_y[3, of[h]].astype(F32)
        for k in (2, 1, 0):
            so_far = s_y[k, of[h]].astype(F32) + so_far - mul_t(ys[k, of[h]][:, :128], so_far)
        s_x[x, of[h]] = so_far.astype(BF)
    x_ring.start()
    for load in loads[9:13]:
        load.wait()
    product(ends, 0, mix[...])
    x_ring.middle()
    load_t = move.start(i_normed_t, left)
    attend(3)
    logit_rows = []
    for h in range(4):
        at, gate_h, g = cols[h], gate[h : h + 1], grad_mix[:, cols[h]]
        ret = retrieved[:, at]
        moved = jnp.sum(g * (ret - local_out[:, at]), axis=0, keepdims=True) * gate_h * (1.0 - gate_h)
        logit_rows.append(jnp.sum(moved, axis=1, keepdims=True))
        grad_den = -jnp.sum(gate_h * g * ret, axis=1, keepdims=True) * inverse[:, h : h + 1]
        q = query[:, at].astype(F32)
        grad_feat = rows_by_rows(point(h).astype(BF), memory[h].astype(BF)) + grad_den * offset[h : h + 1]
        grads[:, at] = (grad_query[:, at] + grad_feat * slope_of(q)).astype(BF)
        line[h : h + 1] = jnp.sum(grad_den * feature_of(q), axis=0, keepdims=True)
    lane = lax.broadcasted_iota(jnp.int32, (8, 128), 1)
    row = lax.broadcasted_iota(jnp.int32, (8, 128), 0)
    spot = jnp.zeros((8, 128), F32)
    for h in range(4):
        spot = jnp.where((lane == h) & (row == 0), logit_rows[h], spot)
    logits[...] = spot
    for i in (0, 1):

        def put_layer(at, result, i=i):
            lanes = slice(0, 1024) if at is z_forths[i].a else slice(1024, 2048)
            layer_out[z, parts[i], at] = (middle[parts[i], lanes] + result).astype(BF)

        z_forths[i].finish(put_layer)
    z_layer.start()
    sums[0].two.middle()
    sums[1].two.middle()
    x_ring.finish()
    sums[2].one.start()
    sums[3].one.start()
    for h in (0, 1):
        lam = jnp.where(x < 3, s_x[3, of[h]].astype(F32), 0.0)
        for k in (2, 1):
            lam = jnp.where(x < k, s_x[k, of[h]].astype(F32) + lam - mul_t(xs[k, of[h]][:, :128], lam), lam)
        for k in (3, 2, 1):
            lam = jnp.where(y < k, s_y[k, of[h]].astype(F32) + lam - mul_t(ys[k, of[h]][:, :128], lam), lam)
        first = lam + seconds[h] - mul_t(pair_e[1, h], lam)
        adjoint[mine + h] = jnp.where(c == 0, first, lam).astype(BF)
        pair_l[h] = jnp.where(c == 0, lam, first).astype(BF)
    give.start()
    for i in (0, 1):
        sums[i].finish(out_down.at[:, pl.ds(512 * i, 512)])
    give.wait_recv()
    for h in (0, 1):
        adjoint[theirs + h] = got_l[h]
    for h in range(4):
        at, fk = cols[h], feat_k(h)
        grad_update = mul(fk * inverse[:, 8:9], adjoint[h])
        grad_value[:, at] += grad_update
        grad_den = jnp.sum(grad_update * recall[:, at], axis=1, keepdims=True) * inverse[:, 4 + h : 5 + h]
        line[h : h + 1] += jnp.sum(grad_den * fk, axis=0, keepdims=True)
        grad_key[:, at] += slope_of(key[:, at].astype(F32)) * (
            grad_den * offset[h : h + 1]
            - rows_by_rows((grad_update * inverse[:, 4 + h : 5 + h]).astype(BF), memory[h].astype(BF))
        )
    line[4:8] = jnp.zeros((4, 128), F32)
    lines[me] = line[...]

    def push(k, carry):
        remote(line, lines.at[me], send.at[38], recv.at[38], seq_place(lax.rem(me + k, 32))).start()
        return carry

    lax.fori_loop(1, 32, push, 0)
    for h in range(4):
        at = cols[h]
        grads[:, 1024 + 128 * h : 1152 + 128 * h] = grad_value[:, at].astype(BF)
        update = value[:, at].astype(F32) - recall[:, at]
        grad_key[:, at] += (
            inverse[:, 8:9] * slope_of(key[:, at].astype(F32)) * rows_by_rows(update.astype(BF), adjoint[h])
        )
    sums[2].one.middle()
    load_t.wait()
    product(ends, 1, grads[:, 0:512])
    z_layer.middle()
    sums[3].one.middle()
    product(ends, 3, grads[:, 1024:1536])
    for s in sums[:2]:
        s.one.drain()
        s.two.drain()
    ends[0].first_ring()
    for z_forth in z_forths:
        z_forth.drain()
    for load in (*loads[13:], load_own):
        load.wait()
    others = lines.at[pl.ds(0, 31)]
    pltpu.make_async_copy(others, others, recv.at[38]).wait()
    passed = lax.broadcasted_iota(jnp.int32, (32, 8, 128), 0) > me
    after = jnp.sum(jnp.where(passed, lines[...], 0.0), axis=0)
    later[...] = after
    stores = [move.start(later, o_later)]
    for h in range(4):
        at = cols[h]
        late = inverse[:, 8:9] * after[h : h + 1] * slope_of(key[:, at].astype(F32))
        grads[:, 512 + 128 * h : 640 + 128 * h] = (grad_key[:, at] + late).astype(BF)
    z_layer.finish()
    stores.append(move.start(layer_out, o_layer_out))
    for half in (0, 1):
        rows = pl.ds(1024 * half, 1024)
        value = sum(rows_by_rows(grads[:, 512 * i : 512 * (i + 1)], weight_in[i, rows]) for i in range(3))
        forth[:, :, rows] = value.astype(BF).reshape(4, 96, 1024)
        for z_end in z_ends:
            (z_end.start_a, z_end.start_b)[half]()
    sums[2].second_ring()
    sums[3].second_ring()
    ends[1].first_ring()
    product(ends, 2, grads[:, 512:1024])
    z_ends[0].middle()
    z_ends[1].middle()
    ends[0].one.middle()
    for i in (2, 3):
        sums[i].two.middle()
        sums[i].one.drain()
    ends[3].first_ring()
    ends[1].one.middle()

    def put(at, result):
        own[:, at] = result

    for i in (0, 1):
        rows = parts[i]
        z_ends[i].finish(put)
        result = grad_middle[rows] + norm_back(branch[0, rows].astype(F32), own[...], gain_attn, 0, i)
        grad_tokens[z, rows] = result.astype(BF)
        z_tokens[i].start()
    total.start()
    ends[2].first_ring()
    for i in (2, 3):
        sums[i].finish(out_down.at[:, pl.ds(512 * i, 512)])
        sums[i].two.drain()
    stores.append(move.start(out_down, o_out_down))
    ends[0].second_ring()
    ends[3].one.middle()
    for z_token in z_tokens:
        z_token.middle()
    ends[1].second_ring()
    total.over_seq()
    ends[2].one.middle()
    ends[0].two.middle()
    ends[3].second_ring()
    ends[1].two.middle()
    total.over_tensor(logits_out)
    stores.append(move.start(logits_out, o_logits_out))
    ends[2].second_ring()
    ends[0].finish(out_output)
    stores.append(move.start(out_output, o_out_output))
    ends[3].two.middle()
    ends[1].finish(out_query)
    stores.append(move.start(out_query, o_out_query))
    ends[2].two.middle()
    ends[3].finish(out_value)
    stores.append(move.start(out_value, o_out_value))
    ends[2].finish(out_key)
    stores.append(move.start(out_key, o_out_key))
    total.finish()
    stores.append(move.start(gains, o_gains))
    for z_token in z_tokens:
        z_token.finish()
    stores.append(move.start(grad_tokens, o_grad_tokens))
    for part in (z_layer, y_ring, x_ring, *z_ends, *z_tokens, total, *ends):
        part.drain()
    swap.wait_send()
    give.wait_send()
    for store in stores:
        store.wait()
    pltpu.make_async_copy(others, others, send.at[38]).wait()


def rest(cid, *args):
    shape = jax.ShapeDtypeStruct
    low = lambda *dims: pltpu.VMEM(dims, BF)
    full = lambda *dims: pltpu.VMEM(dims, F32)
    weight_grad = shape((64, 512), F32)
    return pl.pallas_call(
        rest_kernel,
        out_shape=(
            shape((4, 96, 2048), BF),
            shape((4, 96, 2048), BF),
            shape((8, 128), F32),
            shape((64, 2048), F32),
            weight_grad,
            weight_grad,
            weight_grad,
            weight_grad,
            shape((4, 8, 128), F32),
            shape((8, 128), F32),
        ),
        in_specs=[VMEM] * 6 + [SMEM] + [VMEM] * 4 + [ANYWHERE] * 18,
        out_specs=(ANYWHERE,) * 10,
        scratch_shapes=[
            low(4, 96, 2048),
            low(4, 96, 2048),
            full(8, 128),
            full(64, 2048),
            full(64, 512),
            full(64, 512),
            full(64, 512),
            full(64, 512),
            full(4, 8, 128),
            full(8, 128),
            full(4, 128),
            low(4, 96, 2048),
            full(96, 2048),
            low(384, 1536),
            low(2048, 384),
            low(384, 2048),
            low(384, 512),
            low(384, 512),
            low(384, 512),
            low(4, 384, 384),
            full(384, 512),
            full(384, 512),
            low(384, 512),
            low(2048, 512),
            low(3, 2048, 512),
            low(4, 16, 2, 64, 512),
            low(4, 16, 64, 512),
            low(4, 4, 256, 512),
            low(4, 8, 256, 256),
            low(4, 4, 64, 512),
            low(4, 8, 64, 256),
            low(4, 8, 256, 256),
            low(4, 8, 64, 256),
            low(4, 96, 2048),
            low(2, 8, 48, 1024),
            full(48, 2048),
            full(384, 128),
            full(384, 512),
            full(384, 512),
            full(384, 512),
            full(384, 512),
            full(384, 512),
            low(4, 128, 128),
            low(2, 128, 128),
            low(4, 256, 128),
            low(4, 256, 128),
            low(2, 128, 128),
            low(2, 128, 128),
            low(4, 128, 128),
            full(8, 128),
            full(32, 8, 128),
            full(4, 8, 128),
            full(8, 128),
            full(4, 8, 128),
            full(16, 128),
            full(32, 16, 128),
            pltpu.SemaphoreType.DMA((28,)),
            pltpu.SemaphoreType.DMA((180,)),
            pltpu.SemaphoreType.DMA((180,)),
        ],
        name="rest",
        compiler_params=params(cid, 63),
    )(*args)


def last_kernel(*refs):
    ins, outs = refs[:14], refs[14:29]
    narrow, wide, rows, up, sems = refs[29:]
    move = Moves(sems)
    grad_tokens, mlp_grads, gains, *same = ins
    o_tokens, o_up, o_attn, o_mlp, *o_same = outs
    fetch_rows = move.start(mlp_grads, rows)
    fetch = [move.start(grad_tokens.at[q], narrow.at[q]) for q in range(4)]
    copies = [move.start(src, dst) for src, dst in zip(same, o_same)]
    copies.append(move.start(gains.at[pl.ds(0, 2)], o_attn))
    copies.append(move.start(gains.at[pl.ds(2, 2)], o_mlp))
    for q in range(4):
        fetch[q].wait()
        wide[q] = narrow[q].astype(F32)
        copies.append(move.start(wide.at[q], o_tokens.at[q]))
    fetch_rows.wait()
    up[...] = rows[...].astype(F32)
    copies.append(move.start(up, o_up))
    for copy in copies:
        copy.wait()


def last(grad_tokens, mlp_grads, gains, *same):
    shape = jax.ShapeDtypeStruct
    wide = shape(mlp_grads.shape, F32)
    gain = shape((2, 8, 128), F32)
    outs = (shape(grad_tokens.shape, F32), wide, gain, gain, *(shape(a.shape, a.dtype) for a in same))
    return pl.pallas_call(
        last_kernel,
        out_shape=outs,
        in_specs=[ANYWHERE] * 14,
        out_specs=(ANYWHERE,) * len(outs),
        scratch_shapes=[
            pltpu.VMEM(grad_tokens.shape, BF),
            pltpu.VMEM(grad_tokens.shape, F32),
            pltpu.VMEM(mlp_grads.shape, BF),
            pltpu.VMEM(wide.shape, F32),
            pltpu.SemaphoreType.DMA((23,)),
        ],
        name="last",
        compiler_params=pltpu.CompilerParams(vmem_limit_bytes=63 << 20),
    )(grad_tokens, mlp_grads, gains, *same)


def on_device(
    tokens,
    cotangent,
    w_query,
    w_key,
    w_value,
    w_output,
    w_gate,
    w_up,
    w_down,
    gain_attn,
    gain_mlp,
    gate_logit,
    valid_count,
):
    valid = valid_count[None]
    rows = (16, 2, 64, 512)
    (
        normed_t, grad_out_t, query, key, value, probs, local_out, retrieved, mix, hidden, mlp_grads,
        recall, inverse, forth, grad_out_own, offset, normal_next, memory_prev, memory_next, ys, xs, pair_e, middle,
        grad_two, grad_gate,
    ) = front(
        0, gain_attn[None], gain_mlp[None], valid, gate_logit, tokens, cotangent,
        *(w.reshape(rows) for w in (w_query, w_key, w_value, w_output)), w_down, w_gate, w_up,
    )
    mlp_grads = lax.psum_scatter(mlp_grads.reshape(2048, -1), SEQ, scatter_dimension=0, tiled=True)
    (
        layer_out, grad_tokens, later_offset, grad_down, grad_query, grad_key, grad_value, grad_output, gains, logit_grad,
    ) = rest(
        1, grad_two, middle, gain_attn[None], gain_mlp[None], grad_out_own, offset, gate_logit, memory_prev, ys, xs, pair_e,
        grad_out_t, hidden, query, key, value, probs, local_out, retrieved, mix, normed_t, recall, inverse,
        forth, w_query, w_key, w_value, w_output, tokens,
    )
    (
        grad_tokens, grad_up, gain_attn_grad, gain_mlp_grad, layer_out, grad_query, grad_key, grad_value, grad_output,
        grad_gate, grad_down, logit_grad, memory_next, normal_next, later_offset,
    ) = last(
        grad_tokens, mlp_grads, gains, layer_out, grad_query, grad_key, grad_value, grad_output, grad_gate, grad_down,
        logit_grad, memory_next, normal_next, later_offset,
    )
    return (
        layer_out.reshape(tokens.shape),
        grad_tokens.reshape(tokens.shape),
        grad_query,
        grad_key,
        grad_value,
        grad_output,
        grad_gate,
        grad_up,
        grad_down,
        gain_attn_grad.reshape(-1),
        gain_mlp_grad.reshape(-1),
        logit_grad[0, :4],
        memory_next[None],
        normal_next[None, :4],
        later_offset[None, :4],
    )


def solution(mesh):
    torus = Mesh(
        mesh.devices.reshape(4, 4, 2, mesh.shape["tensor"]), ("seq_0", "seq_1", "seq_2", "tensor")
    )
    weight = P(None, "tensor")
    grad = P(SEQ, "tensor")
    return jax.shard_map(
        on_device,
        mesh=torus,
        in_specs=(P(SEQ, None), P(SEQ, None)) + (weight,) * 7 + (P(), P(), P("tensor"), P()),
        out_specs=(P(SEQ, None), P(SEQ, None))
        + (grad,) * 7
        + (P(), P(), P("tensor"), P(SEQ, "tensor", None, None), P(SEQ, "tensor", None), P(SEQ, "tensor", None)),
        check_vma=False,
    )
```

```python
import functools

import jax
import jax.numpy as jnp
from jax import lax
from jax.experimental import pallas as pl
from jax.experimental.pallas import tpu as pltpu
from jax.sharding import Mesh
from jax.sharding import PartitionSpec as P

SEQ = ("seq_0", "seq_1", "seq_2")
MESH_ID = pl.DeviceIdType.MESH
VMEM = pl.BlockSpec(memory_space=pltpu.VMEM)
BF = jnp.bfloat16
F32 = jnp.float32

epsilon = 1e-06


def remote(src, dst, send, recv, device):
    return pltpu.make_async_remote_copy(
        src_ref=src, dst_ref=dst, send_sem=send, recv_sem=recv, device_id=device, device_id_type=MESH_ID
    )


def meet(devices):
    barrier = pltpu.get_barrier_semaphore()
    for device in devices:
        pl.semaphore_signal(barrier, inc=1, device_id=device, device_id_type=MESH_ID)
    pl.semaphore_wait(barrier, len(devices))


def params(collective_id, mib):
    return pltpu.CompilerParams(
        collective_id=collective_id, has_side_effects=True, vmem_limit_bytes=mib << 20
    )


def seq_place(index):
    return {"seq_0": index // 8, "seq_1": lax.rem(index // 2, 4), "seq_2": lax.rem(index, 2)}


def seq_index():
    return lax.axis_index("seq_0") * 8 + lax.axis_index("seq_1") * 2 + lax.axis_index("seq_2")


def mul(a, b):
    return jnp.dot(a.astype(BF), b.astype(BF), preferred_element_type=F32)


def mul_t(a, b):
    return lax.dot_general(a.astype(BF), b.astype(BF), (((0,), (0,)), ((), ())), preferred_element_type=F32)


def ring_places():
    x, y, c = (lax.axis_index(a) for a in SEQ)
    return x, y, c


def rows_by_rows(a, b):
    return lax.dot_general(a, b, (((1,), (1,)), ((), ())), preferred_element_type=F32)


class RingSum:
    def __init__(self, src, bufs, send, recv, base, axis, rows=None):
        self.src, self.bufs, self.me = src, bufs, lax.axis_index(axis)
        rows = pl.ds(0, src.shape[1]) if rows is None else rows
        self.rows = rows
        half = src.shape[2] // 2
        self.a, self.b = pl.ds(0, half), pl.ds(half, half)
        self.right, self.left = lax.rem(self.me + 1, 4), lax.rem(self.me + 3, 4)
        far = lax.rem(self.me + 2, 4)
        to_right, to_left = {axis: self.right}, {axis: self.left}

        def copy(piece, landing, slot, device):
            return remote(piece, bufs.at[landing], send.at[base + slot], recv.at[base + slot], device)

        self.c0 = copy(src.at[far, rows, self.a], 0, 0, to_right)
        self.c1 = copy(src.at[far, rows, self.b], 1, 1, to_left)
        self.c2 = copy(src.at[self.right, rows, self.b], 2, 2, to_right)
        self.c3 = copy(src.at[self.left, rows, self.a], 3, 3, to_left)
        self.c4 = copy(bufs.at[6], 4, 4, to_right)
        self.c5 = copy(bufs.at[7], 5, 5, to_left)

    def start_a(self):
        self.c0.start()
        self.c3.start()

    def start_b(self):
        self.c1.start()
        self.c2.start()

    def start(self):
        self.c0.start()
        self.c1.start()
        self.c3.start()
        self.c2.start()

    def middle(self):
        src, bufs = self.src, self.bufs
        self.c0.wait_recv()
        bufs[6] = (bufs[0].astype(F32) + src[self.right, self.rows, self.a].astype(F32)).astype(BF)
        self.c4.start()
        self.c1.wait_recv()
        bufs[7] = (bufs[1].astype(F32) + src[self.left, self.rows, self.b].astype(F32)).astype(BF)
        self.c5.start()

    def finish(self, put):
        src, bufs = self.src, self.bufs
        self.c3.wait_recv()
        self.c4.wait_recv()
        put(self.a, src[self.me, self.rows, self.a].astype(F32) + bufs[4].astype(F32) + bufs[3].astype(F32))
        self.c2.wait_recv()
        self.c5.wait_recv()
        put(self.b, src[self.me, self.rows, self.b].astype(F32) + bufs[5].astype(F32) + bufs[2].astype(F32))

    def drain(self):
        for copy in (self.c0, self.c1, self.c2, self.c3, self.c4, self.c5):
            copy.wait_send()


class RingGather:
    def __init__(self, buf, send, recv, base, axis, rows=None):
        self.me = lax.axis_index(axis)
        half = buf.shape[1 if rows is None else 2] // 2
        right, left = lax.rem(self.me + 1, 4), lax.rem(self.me + 3, 4)
        to_right, to_left = {axis: right}, {axis: left}

        def copy(q, h, slot, device):
            part = pl.ds(half * h, half)
            piece = buf.at[q, part] if rows is None else buf.at[q, rows, part]
            return remote(piece, piece, send.at[base + slot], recv.at[base + slot], device)

        self.r0, self.l1 = copy(self.me, 0, 0, to_right), copy(self.me, 1, 1, to_left)
        self.r1, self.l0 = copy(self.me, 1, 2, to_right), copy(self.me, 0, 3, to_left)
        self.f0, self.f1 = copy(left, 0, 4, to_right), copy(right, 1, 5, to_left)

    def start(self):
        for copy in (self.r0, self.l1, self.r1, self.l0):
            copy.start()

    def middle(self):
        self.r0.wait_recv()
        self.f0.start()
        self.l1.wait_recv()
        self.f1.start()

    def finish(self):
        for copy in (self.r1, self.l0, self.f0, self.f1):
            copy.wait_recv()

    def drain(self):
        for copy in (self.r0, self.l1, self.r1, self.l0, self.f0, self.f1):
            copy.wait_send()


class SeqSum:
    def __init__(self, product, got, first, first_bufs, second, second_bufs, send, recv, base, x_first):
        self.product, self.got, self.first, self.second, self.x_first = product, got, first, second, x_first
        self.core = lax.axis_index("seq_2")
        self.swap = remote(
            product.at[pl.ds(0, 16), 1 - self.core], got, send.at[base], recv.at[base], {"seq_2": 1 - self.core}
        )
        axes = ("seq_0", "seq_1") if x_first else ("seq_1", "seq_0")
        self.one = RingSum(first, first_bufs, send, recv, base + 1, axes[0])
        self.two = RingSum(second, second_bufs, send, recv, base + 7, axes[1])

    def start(self):
        self.swap.start()

    def first_ring(self):
        self.add()
        self.one.start()

    def add(self):
        self.swap.wait_recv()
        for x in range(4):
            for y in range(4):
                at = 4 * x + y
                q, r = (x, y) if self.x_first else (y, x)
                total = self.product[at, self.core].astype(F32) + self.got[at].astype(F32)
                self.first[q, pl.ds(64 * r, 64)] = total.astype(BF)

    def second_ring(self):
        def put(cols, value):
            for r in range(4):
                self.second[r, :, cols] = value[64 * r : 64 * (r + 1)].astype(BF)

        self.one.finish(put)
        self.two.start()

    def finish(self, out):
        def put(cols, value):
            out[:, cols] = value

        self.two.finish(put)

    def drain(self):
        self.swap.wait_send()
        self.one.drain()
        self.two.drain()


def greet_all():
    barrier = pltpu.get_barrier_semaphore()
    me, z = seq_index(), lax.axis_index("tensor")

    def greet_seq(k, carry):
        pl.semaphore_signal(barrier, inc=1, device_id=seq_place(lax.rem(me + k, 32)), device_id_type=MESH_ID)
        return carry

    lax.fori_loop(1, 32, greet_seq, 0)
    for k in (1, 2, 3):
        pl.semaphore_signal(barrier, inc=1, device_id={"tensor": lax.rem(z + k, 4)}, device_id_type=MESH_ID)


def all_greeted():
    pl.semaphore_wait(pltpu.get_barrier_semaphore(), 34)


class TotalOfAll:
    def __init__(self, mine, extra, by_z, line, by_seq, total, send, recv, base):
        self.mine, self.extra, self.by_z, self.line, self.by_seq, self.total = mine, extra, by_z, line, by_seq, total
        self.z, self.me = lax.axis_index("tensor"), seq_index()
        self.send, self.recv, self.base = send, recv, base
        peers = [lax.rem(self.z + k, 4) for k in (1, 2, 3)]
        self.split = [
            remote(mine.at[p], by_z.at[self.z], send.at[base + k], recv.at[base + k], {"tensor": p})
            for k, p in enumerate(peers)
        ]
        self.join = [
            remote(total.at[self.z], total.at[self.z], send.at[base + 3 + k], recv.at[base + 3 + k], {"tensor": p})
            for k, p in enumerate(peers)
        ]

    def start(self):
        for copy in self.split:
            copy.start()

    def over_seq(self):
        self.by_z[self.z] = self.mine[self.z]
        for copy in self.split:
            copy.wait_recv()
        self.line[0:8] = (self.by_z[0] + self.by_z[1]) + (self.by_z[2] + self.by_z[3])
        self.line[8:16] = self.extra[...]
        self.by_seq[self.me] = self.line[...]

        def push(k, carry):
            device = seq_place(lax.rem(self.me + k, 32))
            remote(self.line, self.by_seq.at[self.me], self.send.at[self.base + 6], self.recv.at[self.base + 6], device).start()
            return carry

        lax.fori_loop(1, 32, push, 0)

    def over_tensor(self, extra_out):
        others = self.by_seq.at[pl.ds(0, 31)]
        pltpu.make_async_copy(others, others, self.recv.at[self.base + 6]).wait()
        summed = jnp.sum(self.by_seq[...], axis=0)
        self.total[self.z] = summed[0:8]
        extra_out[...] = summed[8:16]
        for copy in self.join:
            copy.start()

    def finish(self):
        for copy in self.join:
            copy.wait_recv()

    def drain(self):
        for copy in (*self.split, *self.join):
            copy.wait_send()
        others = self.by_seq.at[pl.ds(0, 31)]
        pltpu.make_async_copy(others, others, self.send.at[self.base + 6]).wait()


def feature_of(v):
    return jnp.where(v > 0, v + 1.0, jnp.exp(jnp.minimum(v, 0.0)))


def slope_of(v):
    return jnp.where(v > 0, 1.0, jnp.exp(jnp.minimum(v, 0.0)))


ANYWHERE = pl.BlockSpec(memory_space=pl.ANY)


def keep_of(valid):
    length = jnp.where(seq_index() == 31, valid[...], 384)
    return (lax.broadcasted_iota(jnp.int32, (384, 1), 0) < length).astype(F32)


SMEM = pl.BlockSpec(memory_space=pltpu.SMEM)


def gate_rows(gate, logit):
    for h in range(4):
        gate[h : h + 1] = jax.nn.sigmoid(jnp.full((1, 128), logit[h], F32))


def flat(weight):
    return weight.reshape(-1, 512)


class Moves:
    def __init__(self, sems):
        self.sems, self.count = sems, 0

    def start(self, src, dst):
        copy = pltpu.make_async_copy(src, dst, self.sems.at[self.count])
        self.count += 1
        copy.start()
        return copy


def front_kernel(
    gain_attn,
    gain_mlp,
    valid,
    gate_logit,
    i_tokens,
    cotangent,
    w_query,
    w_key,
    w_value,
    w_output,
    w_down,
    w_gate,
    w_up,
    o_normed_t,
    o_grad_out_t,
    o_query,
    o_key,
    o_value,
    o_probs,
    o_local_out,
    o_retrieved,
    o_mix,
    o_hidden,
    o_grads,
    o_recall,
    o_inverse,
    o_forth,
    grad_out_own,
    offset,
    normal_next,
    memory_prev,
    memory_next,
    ys,
    xs,
    pair_e,
    middle,
    grad_two,
    keep,
    gate,
    weights,
    weight_o,
    weight_d,
    weight_g,
    hidden,
    normed_two,
    normed,
    turned,
    grad_out,
    got_rows,
    pair_rows,
    inverse,
    grad_hidden,
    query,
    key,
    value,
    probs,
    local_out,
    retrieved,
    mix,
    line,
    lines,
    eb,
    source,
    got,
    pair_m,
    got_m,
    part,
    part_bufs,
    moves,
    send,
    recv,
):
    move = Moves(moves)
    tokens = hidden
    load_tokens = move.start(i_tokens, tokens)
    loads = [move.start(w, weights.at[i]) for i, w in enumerate((w_key, w_query, w_value))]
    load_cotangent = move.start(cotangent, grad_out)
    load_o = move.start(w_output, weight_o)
    load_d = [move.start(w_down.at[pl.ds(512 * i, 512)], weight_d.at[pl.ds(512 * i, 512)]) for i in range(4)]
    greet_all()
    keep[...] = keep_of(valid)
    gate_rows(gate, gate_logit)
    x, y, c = ring_places()
    z, me = lax.axis_index("tensor"), seq_index()
    partner = {"seq_2": 1 - c}
    mine, theirs = 2 * c, 2 * (1 - c)
    slots = (weight_o, weights.at[2], weights.at[0], weights.at[1])
    swaps = [
        remote(slots[i % 4].at[pl.ds(0, 16), 1 - c], got_rows.at[i], send.at[27 + i], recv.at[27 + i], partner)
        for i in range(8)
    ]
    parts = [pl.ds(0, 48), pl.ds(48, 48)]
    z_sums = [RingSum(part, part_bufs.at[i], send, recv, 79 + 6 * i, "tensor", parts[i]) for i in (0, 1)]
    z_gathers = [RingGather(normed_two, send, recv, 91 + 6 * i, "tensor", parts[i]) for i in (0, 1)]
    z_backs = [RingSum(part, part_bufs.at[i], send, recv, 6 * i, "tensor", parts[i]) for i in (0, 1)]
    y_ring = RingGather(ys, send, recv, 12, "seq_1")
    x_ring = RingGather(xs, send, recv, 18, "seq_0")
    swap = remote(eb.at[pl.ds(theirs, 2)], got, send.at[24], recv.at[24], partner)
    give = remote(pair_m, got_m, send.at[25], recv.at[25], partner)
    cols = [slice(128 * h, 128 * (h + 1)) for h in range(4)]
    stores = []

    load_tokens.wait()
    for q in range(4):
        rows = pl.ds(96 * q, 96)
        stream = tokens[rows].astype(F32)
        inv = lax.rsqrt(jnp.mean(stream * stream, axis=1, keepdims=True) + epsilon)
        normed[rows] = (stream * inv * gain_attn[...]).astype(BF)
    loads[0].wait()
    key[...] = jnp.dot(normed[...], flat(weights[0]), preferred_element_type=F32).astype(BF)
    feat_q = lambda h: feature_of(query[:, cols[h]].astype(F32))
    feat_k = lambda h: feature_of(key[:, cols[h]].astype(F32))
    line[...] = jnp.zeros_like(line)
    for h in range(4):
        line[h : h + 1] = jnp.sum(feat_k(h) * keep[...], axis=0, keepdims=True)
    lines[me] = line[...]
    all_greeted()

    def push(k, carry):
        remote(line, lines.at[me], send.at[26], recv.at[26], seq_place(lax.rem(me + k, 32))).start()
        return carry

    lax.fori_loop(1, 32, push, 0)
    stores.append(move.start(key, o_key))
    loads[1].wait()
    query[...] = jnp.dot(normed[...], flat(weights[1]), preferred_element_type=F32).astype(BF)
    stores.append(move.start(query, o_query))
    loads[2].wait()
    value[...] = jnp.dot(normed[...], flat(weights[2]), preferred_element_type=F32).astype(BF)
    stores.append(move.start(value, o_value))
    load_g = move.start(w_gate, weight_g)
    at_row = lax.broadcasted_iota(jnp.int32, (384, 384), 0)
    at_col = lax.broadcasted_iota(jnp.int32, (384, 384), 1)
    valid = jnp.sum(keep[...], axis=0, keepdims=True)
    allowed = (at_row >= at_col) & (at_col.astype(F32) < valid)

    def attend(h):
        at = cols[h]
        scores = rows_by_rows(query[:, at], key[:, at]) * 128 ** (-0.5)
        masked = jnp.where(allowed, scores, -1e30)
        raised = jnp.exp(masked - jnp.max(masked, axis=1, keepdims=True))
        low = (raised * (1.0 / jnp.sum(raised, axis=1, keepdims=True))).astype(BF)
        probs[h] = low
        local_out[:, at] = jnp.dot(low, value[:, at], preferred_element_type=F32)
        total = mul_t(feat_k(h) * keep[...], value[:, at])
        source[h] = total
        eb[h, :, 128:256] = total.astype(BF)

    for h in range(4):
        attend(h)
    stores.append(move.start(probs, o_probs))
    stores.append(move.start(local_out, o_local_out))
    others = lines.at[pl.ds(0, 31)]
    pltpu.make_async_copy(others, others, recv.at[26]).wait()
    passed = lax.broadcasted_iota(jnp.int32, (32, 8, 128), 0) < me
    before = jnp.sum(jnp.where(passed, lines[...], 0.0), axis=0)
    normal_next[...] = before + line[...]
    offset[...] = before + 384.0
    for h in range(4):
        fk = feat_k(h)
        kept = fk * keep[...] * (1.0 / jnp.sum(fk * offset[h : h + 1], axis=1, keepdims=True))
        eb[h, :, 0:128] = mul_t(kept, fk).astype(BF)
    swap.start()
    load_cotangent.wait()
    grad_out[...] = grad_out[...] * keep[...].astype(BF)
    grad_out_own[...] = grad_out[pl.ds(pl.multiple_of(96 * z, 96), 96)]
    swap.wait_recv()
    of = [pl.ds(0, 128), pl.ds(128, 128)]
    firsts = []
    for h in (0, 1):
        here, there = eb[mine + h].astype(F32), got[h].astype(F32)
        first, second = jnp.where(c == 0, here, there), jnp.where(c == 0, there, here)
        firsts.append(first)
        pair_e[0, h] = first[:, :128].astype(BF)
        pair_e[1, h] = second[:, :128].astype(BF)
        ys[y, of[h]] = (first + second - mul(second[:, :128], first)).astype(BF)
    y_ring.start()

    def hidden_part(i):
        load_d[i].wait()
        rows = pl.ds(512 * i, 512)
        product = jnp.dot(grad_out[:, 512 * i : 512 * (i + 1)], weight_d[rows], preferred_element_type=F32)
        if i == 0:
            grad_hidden[...] = product
        else:
            grad_hidden[...] += product

    hidden_part(0)
    y_ring.middle()
    hidden_part(1)
    y_ring.finish()
    starts = []
    for h in (0, 1):
        so_far = ys[0, of[h]].astype(F32)
        start = jnp.where(y > 0, so_far, 0.0)
        for k in (1, 2, 3):
            step = ys[k, of[h]].astype(F32)
            so_far = so_far + step - mul(step[:, :128], so_far)
            if k < 3:
                start = jnp.where(y > k, so_far, start)
        xs[x, of[h]] = so_far.astype(BF)
        starts.append(start)
    x_ring.start()
    hidden_part(2)
    x_ring.middle()
    hidden_part(3)
    load_u = move.start(w_up, weight_d)
    load_o.wait()
    x_ring.finish()
    for h in (0, 1):
        m = jnp.where(x > 0, xs[0, of[h]][:, 128:].astype(F32), 0.0)
        for k in (1, 2):
            step = xs[k, of[h]].astype(F32)
            m = jnp.where(x > k, m + step[:, 128:] - mul(step[:, :128], m), m)
        m = m + starts[h][:, 128:] - mul(starts[h][:, :128], m)
        second = m + firsts[h][:, 128:] - mul(firsts[h][:, :128], m)
        memory_prev[mine + h] = jnp.where(c == 0, m, second)
        pair_m[h] = jnp.where(c == 0, second, m)
    give.start()
    give.wait_recv()
    inverse[...] = jnp.zeros_like(inverse)
    inverse[:, 8:9] = keep[...]
    for h in (0, 1):
        memory_prev[theirs + h] = got_m[h]
    for h in range(4):
        at, fq, sig = cols[h], feat_q(h), gate[h : h + 1]
        inv_q = 1.0 / jnp.sum(fq * offset[h : h + 1], axis=1, keepdims=True)
        inverse[:, h : h + 1] = inv_q
        found = mul(fq, memory_prev[h]) * inv_q
        retrieved[:, at] = found
        mix[:, at] = (sig * found + (1.0 - sig) * local_out[:, at]).astype(BF)
    for half in (0, 1):
        rows = pl.ds(1024 * half, 1024)
        part[:, :, rows] = rows_by_rows(mix[...], flat(weight_o[8 * half : 8 * half + 8])).astype(BF).reshape(4, 96, 1024)
        for z_sum in z_sums:
            (z_sum.start_a, z_sum.start_b)[half]()
    store_found = move.start(retrieved, o_retrieved)
    stores.append(move.start(mix, o_mix))
    for h in range(4):
        m = memory_prev[h]
        memory_next[h] = m + source[h] - mul(eb[h][:, :128], m)
    turned[...] = normed[...].T
    store_t = move.start(turned, o_normed_t)
    z_sums[0].middle()
    z_sums[1].middle()
    store_found.wait()
    recall = retrieved
    for h in range(4):
        fk, off = feat_k(h), offset[h : h + 1]
        inv_k = 1.0 / jnp.sum(fk * off, axis=1, keepdims=True)
        inverse[:, 4 + h : 5 + h] = inv_k
        recall[:, cols[h]] = mul(fk, memory_prev[h]) * inv_k
    stores.append(move.start(recall, o_recall))
    stores.append(move.start(inverse, o_inverse))

    def second_norm(i):
        own_tokens = tokens[pl.ds(pl.multiple_of(96 * z + 48 * i, 16), 48)].astype(F32)

        def put(at, total):
            lanes = slice(0, 1024) if at is z_sums[i].a else slice(1024, 2048)
            middle[parts[i], at] = own_tokens[:, lanes] + total

        z_sums[i].finish(put)
        stream = middle[parts[i]]
        inv = lax.rsqrt(jnp.mean(stream * stream, axis=1, keepdims=True) + epsilon)
        normed_two[z, parts[i]] = (stream * inv * gain_mlp[...]).astype(BF)
        z_gathers[i].start()

    second_norm(0)
    second_norm(1)
    z_gathers[0].middle()
    z_gathers[1].middle()
    store_t.wait()
    turned[...] = grad_out[...].T
    store_t = move.start(turned, o_grad_out_t)
    for store in stores:
        store.wait()
    store_t.wait()
    for z_sum in z_sums:
        z_sum.drain()
    load_g.wait()
    load_u.wait()
    for z_gather in z_gathers:
        z_gather.finish()
    for z_gather in z_gathers:
        z_gather.drain()
    turned[...] = normed_two[...].reshape(384, 2048).T

    def tile(i):
        for half in (2 * i, 2 * i + 1):
            narrow_tile(half)

    def narrow_tile(i):
        lanes = slice(256 * i, 256 * (i + 1))
        rows = normed_two[...].reshape(384, 2048)
        gate_pre = jnp.dot(rows, weight_g[:, lanes], preferred_element_type=F32)
        up_pre = jnp.dot(rows, weight_d[:, lanes], preferred_element_type=F32)
        back_hidden = grad_hidden[:, lanes]
        sig = jax.nn.sigmoid(gate_pre)
        swish = gate_pre * sig
        hidden[:, lanes] = (swish * up_pre).astype(BF)
        grad_out[:, lanes] = (back_hidden * swish).astype(BF)
        normed[:, lanes] = (back_hidden * up_pre * sig * (1.0 + gate_pre * (1.0 - sig))).astype(BF)

    def return_part(i):
        rows = pl.ds(512 * i, 512)
        value = rows_by_rows(normed[...], weight_g[rows]) + rows_by_rows(grad_out[...], weight_d[rows])
        part[:, :, rows] = value.astype(BF).reshape(4, 96, 512)

    leaving = []

    def gradient(i):
        if i >= 4:
            swaps[i - 4].wait_send()
        side = (normed, grad_out)[i // 4]
        lanes = slice(512 * (i % 4), 512 * (i % 4 + 1))
        result = jnp.dot(turned[...], side[:, lanes], preferred_element_type=F32)
        slots[i % 4][...] = result.astype(BF).reshape(16, 2, 64, 512)
        swaps[i].start()

    def pair_sum(i):
        if i >= 3:
            leaving[i - 3].wait()
        swaps[i].wait_recv()
        for at in range(16):
            pair_rows[i % 3, at] = (slots[i % 4][at, c].astype(F32) + got_rows[i, at].astype(F32)).astype(BF)
        leaving.append(move.start(pair_rows.at[i % 3], o_grads.at[:, :, pl.ds(512 * i, 512)]))

    tile(0)
    gradient(0)
    tile(1)
    gradient(1)
    tile(2)
    pair_sum(0)
    gradient(2)
    tile(3)
    pair_sum(1)
    gradient(3)
    stores = [move.start(hidden, o_hidden)]
    return_part(0)
    return_part(1)
    for z_back in z_backs:
        z_back.start_a()
    pair_sum(2)
    return_part(2)
    return_part(3)
    for z_back in z_backs:
        z_back.start_b()
    load_down = move.start(w_down, weight_g)
    pair_sum(3)
    gradient(4)
    gradient(5)
    z_backs[0].middle()
    z_backs[1].middle()
    pair_sum(4)
    gradient(6)
    pair_sum(5)
    gradient(7)
    pair_sum(6)
    load_down.wait()
    for half in (0, 1):
        rows = pl.ds(1024 * half, 1024)
        normed_two[:, :, rows] = rows_by_rows(hidden[...], weight_g[rows]).astype(BF).reshape(4, 96, 1024)
    stores.append(move.start(normed_two, o_forth))
    pair_sum(7)
    for i in (0, 1):

        def put(at, total, i=i):
            grad_two[parts[i], at] = total

        z_backs[i].finish(put)
    for copy in (*stores, *leaving[5:]):
        copy.wait()
    for swap_rows in swaps[4:]:
        swap_rows.wait_send()
    for ring in (*z_backs, y_ring, x_ring):
        ring.drain()
    swap.wait_send()
    give.wait_send()
    pltpu.make_async_copy(others, others, send.at[26]).wait()


def front(cid, *args):
    shape = jax.ShapeDtypeStruct
    low = lambda *dims: pltpu.VMEM(dims, BF)
    full = lambda *dims: pltpu.VMEM(dims, F32)
    return pl.pallas_call(
        front_kernel,
        out_shape=(
            shape((2048, 384), BF),
            shape((2048, 384), BF),
            shape((384, 512), BF),
            shape((384, 512), BF),
            shape((384, 512), BF),
            shape((4, 384, 384), BF),
            shape((384, 512), F32),
            shape((384, 512), F32),
            shape((384, 512), BF),
            shape((384, 2048), BF),
            shape((16, 64, 4096), BF),
            shape((384, 512), F32),
            shape((384, 128), F32),
            shape((4, 96, 2048), BF),
            shape((96, 2048), BF),
            shape((8, 128), F32),
            shape((8, 128), F32),
            shape((4, 128, 128), F32),
            shape((4, 128, 128), F32),
            shape((4, 256, 256), BF),
            shape((4, 256, 256), BF),
            shape((2, 2, 128, 128), BF),
            shape((96, 2048), F32),
            shape((96, 2048), F32),
        ),
        in_specs=[VMEM] * 3 + [SMEM] + [ANYWHERE] * 9,
        out_specs=(ANYWHERE,) * 14 + (VMEM,) * 10,
        scratch_shapes=[
            full(384, 1),
            full(4, 128),
            low(3, 16, 2, 64, 512),
            low(16, 2, 64, 512),
            low(2048, 2048),
            low(2048, 2048),
            low(384, 2048),
            low(4, 96, 2048),
            low(384, 2048),
            low(2048, 384),
            low(384, 2048),
            low(8, 16, 64, 512),
            low(3, 16, 64, 512),
            full(384, 128),
            full(384, 2048),
            low(384, 512),
            low(384, 512),
            low(384, 512),
            low(4, 384, 384),
            full(384, 512),
            full(384, 512),
            low(384, 512),
            full(8, 128),
            full(32, 8, 128),
            low(4, 128, 256),
            full(4, 128, 128),
            low(2, 128, 256),
            full(2, 128, 128),
            full(2, 128, 128),
            low(4, 96, 2048),
            low(2, 8, 48, 1024),
            pltpu.SemaphoreType.DMA((36,)),
            pltpu.SemaphoreType.DMA((103,)),
            pltpu.SemaphoreType.DMA((103,)),
        ],
        name="front",
        compiler_params=params(cid, 63),
    )(*args)


def neighbours():
    x, y, c = ring_places()
    z = lax.axis_index("tensor")
    near = [{"seq_2": 1 - c}]
    for axis, at in (("seq_0", x), ("seq_1", y), ("tensor", z)):
        near += [{axis: lax.rem(at + 1, 4)}, {axis: lax.rem(at + 3, 4)}]
    return near


def rest_kernel(
    grad_two,
    middle,
    gain_attn,
    gain_mlp,
    grad_out,
    offset,
    gate_logit,
    memory,
    ys,
    xs,
    pair_e,
    i_grad_out_t,
    i_hidden,
    i_query,
    i_key,
    i_value,
    i_probs,
    i_local_out,
    i_retrieved,
    i_mix,
    i_normed_t,
    i_recall,
    i_inverse,
    i_forth,
    w_query,
    w_key,
    w_value,
    w_output,
    tokens,
    o_layer_out,
    o_grad_tokens,
    o_later,
    o_out_down,
    o_out_query,
    o_out_key,
    o_out_value,
    o_out_output,
    o_gains,
    o_logits_out,
    layer_out,
    grad_tokens,
    later,
    out_down,
    out_query,
    out_key,
    out_value,
    out_output,
    gains,
    logits_out,
    gate,
    branch,
    grad_middle,
    grads,
    left,
    hidden,
    query,
    key,
    value,
    probs,
    local_out,
    retrieved,
    mix,
    weight_o,
    weight_in,
    products,
    got_rows,
    first_rows,
    first_bufs,
    second_rows,
    second_bufs,
    first_bufs_2,
    second_bufs_2,
    forth,
    z_bufs,
    own,
    inverse,
    recall,
    grad_mix,
    grad_query,
    grad_key,
    grad_value,
    source,
    got,
    s_y,
    s_x,
    pair_l,
    got_l,
    adjoint,
    line,
    lines,
    mine_gains,
    logits,
    by_z,
    total_line,
    by_seq,
    moves,
    send,
    recv,
):
    x, y, c = ring_places()
    z, me = lax.axis_index("tensor"), seq_index()
    move = Moves(moves)
    pairs = (
        (i_grad_out_t, left),
        (i_hidden, hidden),
        (i_forth, forth),
        (w_output, weight_o),
        (i_query, query),
        (i_inverse, inverse),
        (i_probs, probs),
        (i_key, key),
        (i_value, value),
        (i_mix, mix),
        (i_retrieved, retrieved),
        (i_local_out, local_out),
        (i_recall, recall),
        (w_query, weight_in.at[0]),
        (w_key, weight_in.at[1]),
        (w_value, weight_in.at[2]),
    )
    barrier = pltpu.get_barrier_semaphore()
    for device in neighbours():
        pl.semaphore_signal(barrier, inc=1, device_id=device, device_id_type=MESH_ID)
    loads = [move.start(src, dst) for src, dst in pairs]
    gate_rows(gate, gate_logit)
    partner = {"seq_2": 1 - c}
    mine, theirs = 2 * c, 2 * (1 - c)
    parts = [pl.ds(0, 48), pl.ds(48, 48)]
    z_branches = [RingGather(branch, send, recv, 6 * i, "tensor", parts[i]) for i in (0, 1)]
    z_forths = [RingSum(forth, z_bufs.at[i], send, recv, (12, 174)[i], "tensor", parts[i]) for i in (0, 1)]
    z_layer = RingGather(layer_out, send, recv, 18, "tensor")
    y_ring = RingGather(s_y, send, recv, 24, "seq_1")
    x_ring = RingGather(s_x, send, recv, 30, "seq_0")
    swap = remote(source.at[pl.ds(theirs, 2)], got, send.at[36], recv.at[36], partner)
    give = remote(pair_l, got_l, send.at[37], recv.at[37], partner)
    z_ends = [RingSum(forth, z_bufs.at[i], send, recv, 143 + 6 * i, "tensor", parts[i]) for i in (0, 1)]
    z_tokens = [RingGather(grad_tokens, send, recv, 155 + 6 * i, "tensor", parts[i]) for i in (0, 1)]
    total = TotalOfAll(mine_gains, logits, by_z, total_line, by_seq, gains, send, recv, 167)

    def seq_sums(base, first_bufs, second_bufs):
        return [
            SeqSum(
                products.at[i], got_rows.at[i], first_rows.at[i], first_bufs.at[i], second_rows.at[i],
                second_bufs.at[i], send, recv, base + 13 * i, i % 2 == 0,
            )
            for i in range(4)
        ]

    sums, ends = seq_sums(39, first_bufs, second_bufs), seq_sums(91, first_bufs_2, second_bufs_2)
    cols = [slice(128 * h, 128 * (h + 1)) for h in range(4)]
    of = [pl.ds(0, 128), pl.ds(128, 128)]
    feat_q = lambda h: feature_of(query[:, cols[h]].astype(F32))
    feat_k = lambda h: feature_of(key[:, cols[h]].astype(F32))
    scale = 128 ** (-0.5)

    def product(group, i, right):
        result = jnp.dot(left[...], right, preferred_element_type=F32).astype(BF)
        products[i] = result.reshape(16, 2, 64, 512)
        group[i].start()

    def down(i):
        product(sums, i, hidden[:, 512 * i : 512 * (i + 1)])

    def norm_back(stream, grad_normed, gain, first_row, i):
        inv = lax.rsqrt(jnp.mean(stream * stream, axis=1, keepdims=True) + epsilon)
        weighted = grad_normed * gain[...]
        inner = jnp.sum(weighted * stream, axis=1, keepdims=True)
        scaled = stream * inv
        line_of = jnp.sum(grad_normed * scaled, axis=0, keepdims=True)
        for r in range(16):
            at = (first_row + r // 8, slice(r % 8, r % 8 + 1))
            piece = line_of[:, 128 * r : 128 * (r + 1)]
            mine_gains[at] = piece if i == 0 else mine_gains[at] + piece
        return inv * weighted - scaled * (inv * inv * inner * (1.0 / stream.shape[1]))

    for i in (0, 1):
        rows = parts[i]
        result = grad_out[rows].astype(F32) + norm_back(middle[rows], grad_two[rows], gain_mlp, 2, i)
        grad_middle[rows] = result
        branch[z, rows] = result.astype(BF)
        if i == 0:
            pl.semaphore_wait(barrier, 7)
        z_branches[i].start()
    loads[0].wait()
    loads[1].wait()
    down(0)
    down(1)
    z_branches[0].middle()
    sums[0].first_ring()
    z_branches[1].middle()
    down(2)
    sums[1].first_ring()
    down(3)
    sums[2].add()
    sums[0].one.middle()
    sums[3].add()
    for load in loads[2:6]:
        load.wait()
    for z_branch in z_branches:
        z_branch.finish()
    for z_forth in z_forths:
        z_forth.start()
    grad_mix[...] = jnp.dot(branch[...].reshape(384, 2048), weight_o[...], preferred_element_type=F32)

    def point(h):
        return gate[h : h + 1] * grad_mix[:, cols[h]] * inverse[:, h : h + 1]

    for h in range(4):
        source[h] = mul_t(feat_q(h), point(h)).astype(BF)
    swap.start()

    def attend(h):
        at = cols[h]
        grad_local = ((1.0 - gate[h : h + 1]) * grad_mix[:, at]).astype(BF)
        low = probs[h]
        p = low.astype(F32)
        grad_probs = rows_by_rows(grad_local, value[:, at])
        grad_value[:, at] = mul_t(low, grad_local)
        grad_scores = (p * (grad_probs - jnp.sum(grad_probs * p, axis=1, keepdims=True))).astype(BF)
        grad_query[:, at] = mul(grad_scores, key[:, at]) * scale
        grad_key[:, at] = mul_t(grad_scores, query[:, at]) * scale

    for load in loads[6:9]:
        load.wait()
    attend(0)
    sums[1].one.middle()
    swap.wait_recv()
    seconds = []
    for h in (0, 1):
        here, there = source[mine + h].astype(F32), got[h].astype(F32)
        first, second = jnp.where(c == 0, here, there), jnp.where(c == 0, there, here)
        seconds.append(second)
        s_y[y, of[h]] = (first + second - mul_t(pair_e[0, h], second)).astype(BF)
    y_ring.start()
    attend(1)
    y_ring.middle()
    sums[0].second_ring()
    attend(2)
    for z_forth in z_forths:
        z_forth.middle()
    sums[1].second_ring()
    for s in sums:
        s.swap.wait_send()
    left[...] = branch[...].reshape(384, 2048).T
    for z_branch in z_branches:
        z_branch.drain()
    load_own = move.start(tokens.at[pl.ds(pl.multiple_of(96 * z, 96), 96)], branch.at[0])
    y_ring.finish()
    for h in (0, 1):
        so_far = s_y[3, of[h]].astype(F32)
        for k in (2, 1, 0):
            so_far = s_y[k, of[h]].astype(F32) + so_far - mul_t(ys[k, of[h]][:, :128], so_far)
        s_x[x, of[h]] = so_far.astype(BF)
    x_ring.start()
    for load in loads[9:13]:
        load.wait()
    product(ends, 0, mix[...])
    x_ring.middle()
    load_t = move.start(i_normed_t, left)
    attend(3)
    logit_rows = []
    for h in range(4):
        at, gate_h, g = cols[h], gate[h : h + 1], grad_mix[:, cols[h]]
        ret = retrieved[:, at]
        moved = jnp.sum(g * (ret - local_out[:, at]), axis=0, keepdims=True) * gate_h * (1.0 - gate_h)
        logit_rows.append(jnp.sum(moved, axis=1, keepdims=True))
        grad_den = -jnp.sum(gate_h * g * ret, axis=1, keepdims=True) * inverse[:, h : h + 1]
        q = query[:, at].astype(F32)
        grad_feat = rows_by_rows(point(h).astype(BF), memory[h].astype(BF)) + grad_den * offset[h : h + 1]
        grads[:, at] = (grad_query[:, at] + grad_feat * slope_of(q)).astype(BF)
        line[h : h + 1] = jnp.sum(grad_den * feature_of(q), axis=0, keepdims=True)
    lane = lax.broadcasted_iota(jnp.int32, (8, 128), 1)
    row = lax.broadcasted_iota(jnp.int32, (8, 128), 0)
    spot = jnp.zeros((8, 128), F32)
    for h in range(4):
        spot = jnp.where((lane == h) & (row == 0), logit_rows[h], spot)
    logits[...] = spot
    for i in (0, 1):

        def put_layer(at, result, i=i):
            lanes = slice(0, 1024) if at is z_forths[i].a else slice(1024, 2048)
            layer_out[z, parts[i], at] = (middle[parts[i], lanes] + result).astype(BF)

        z_forths[i].finish(put_layer)
    z_layer.start()
    sums[0].two.middle()
    sums[1].two.middle()
    x_ring.finish()
    sums[2].one.start()
    sums[3].one.start()
    for h in (0, 1):
        lam = jnp.where(x < 3, s_x[3, of[h]].astype(F32), 0.0)
        for k in (2, 1):
            lam = jnp.where(x < k, s_x[k, of[h]].astype(F32) + lam - mul_t(xs[k, of[h]][:, :128], lam), lam)
        for k in (3, 2, 1):
            lam = jnp.where(y < k, s_y[k, of[h]].astype(F32) + lam - mul_t(ys[k, of[h]][:, :128], lam), lam)
        first = lam + seconds[h] - mul_t(pair_e[1, h], lam)
        adjoint[mine + h] = jnp.where(c == 0, first, lam).astype(BF)
        pair_l[h] = jnp.where(c == 0, lam, first).astype(BF)
    give.start()
    for i in (0, 1):
        sums[i].finish(out_down.at[:, pl.ds(512 * i, 512)])
    give.wait_recv()
    for h in (0, 1):
        adjoint[theirs + h] = got_l[h]
    for h in range(4):
        at, fk = cols[h], feat_k(h)
        grad_update = mul(fk * inverse[:, 8:9], adjoint[h])
        grad_value[:, at] += grad_update
        grad_den = jnp.sum(grad_update * recall[:, at], axis=1, keepdims=True) * inverse[:, 4 + h : 5 + h]
        line[h : h + 1] += jnp.sum(grad_den * fk, axis=0, keepdims=True)
        grad_key[:, at] += slope_of(key[:, at].astype(F32)) * (
            grad_den * offset[h : h + 1]
            - rows_by_rows((grad_update * inverse[:, 4 + h : 5 + h]).astype(BF), memory[h].astype(BF))
        )
    line[4:8] = jnp.zeros((4, 128), F32)
    lines[me] = line[...]

    def push(k, carry):
        remote(line, lines.at[me], send.at[38], recv.at[38], seq_place(lax.rem(me + k, 32))).start()
        return carry

    lax.fori_loop(1, 32, push, 0)
    for h in range(4):
        at = cols[h]
        grads[:, 1024 + 128 * h : 1152 + 128 * h] = grad_value[:, at].astype(BF)
        update = value[:, at].astype(F32) - recall[:, at]
        grad_key[:, at] += (
            inverse[:, 8:9] * slope_of(key[:, at].astype(F32)) * rows_by_rows(update.astype(BF), adjoint[h])
        )
    sums[2].one.middle()
    load_t.wait()
    product(ends, 1, grads[:, 0:512])
    z_layer.middle()
    sums[3].one.middle()
    product(ends, 3, grads[:, 1024:1536])
    for s in sums[:2]:
        s.one.drain()
        s.two.drain()
    ends[0].first_ring()
    for z_forth in z_forths:
        z_forth.drain()
    for load in (*loads[13:], load_own):
        load.wait()
    others = lines.at[pl.ds(0, 31)]
    pltpu.make_async_copy(others, others, recv.at[38]).wait()
    passed = lax.broadcasted_iota(jnp.int32, (32, 8, 128), 0) > me
    after = jnp.sum(jnp.where(passed, lines[...], 0.0), axis=0)
    later[...] = after
    stores = [move.start(later, o_later)]
    for h in range(4):
        at = cols[h]
        late = inverse[:, 8:9] * after[h : h + 1] * slope_of(key[:, at].astype(F32))
        grads[:, 512 + 128 * h : 640 + 128 * h] = (grad_key[:, at] + late).astype(BF)
    z_layer.finish()
    stores.append(move.start(layer_out, o_layer_out))
    for half in (0, 1):
        rows = pl.ds(1024 * half, 1024)
        value = sum(rows_by_rows(grads[:, 512 * i : 512 * (i + 1)], weight_in[i, rows]) for i in range(3))
        forth[:, :, rows] = value.astype(BF).reshape(4, 96, 1024)
        for z_end in z_ends:
            (z_end.start_a, z_end.start_b)[half]()
    sums[2].second_ring()
    sums[3].second_ring()
    ends[1].first_ring()
    product(ends, 2, grads[:, 512:1024])
    z_ends[0].middle()
    z_ends[1].middle()
    ends[0].one.middle()
    for i in (2, 3):
        sums[i].two.middle()
        sums[i].one.drain()
    ends[3].first_ring()
    ends[1].one.middle()

    def put(at, result):
        own[:, at] = result

    for i in (0, 1):
        rows = parts[i]
        z_ends[i].finish(put)
        result = grad_middle[rows] + norm_back(branch[0, rows].astype(F32), own[...], gain_attn, 0, i)
        grad_tokens[z, rows] = result.astype(BF)
        z_tokens[i].start()
    total.start()
    ends[2].first_ring()
    for i in (2, 3):
        sums[i].finish(out_down.at[:, pl.ds(512 * i, 512)])
        sums[i].two.drain()
    stores.append(move.start(out_down, o_out_down))
    ends[0].second_ring()
    ends[3].one.middle()
    for z_token in z_tokens:
        z_token.middle()
    ends[1].second_ring()
    total.over_seq()
    ends[2].one.middle()
    ends[0].two.middle()
    ends[3].second_ring()
    ends[1].two.middle()
    total.over_tensor(logits_out)
    stores.append(move.start(logits_out, o_logits_out))
    ends[2].second_ring()
    ends[0].finish(out_output)
    stores.append(move.start(out_output, o_out_output))
    ends[3].two.middle()
    ends[1].finish(out_query)
    stores.append(move.start(out_query, o_out_query))
    ends[2].two.middle()
    ends[3].finish(out_value)
    stores.append(move.start(out_value, o_out_value))
    ends[2].finish(out_key)
    stores.append(move.start(out_key, o_out_key))
    total.finish()
    stores.append(move.start(gains, o_gains))
    for z_token in z_tokens:
        z_token.finish()
    stores.append(move.start(grad_tokens, o_grad_tokens))
    for part in (z_layer, y_ring, x_ring, *z_ends, *z_tokens, total, *ends):
        part.drain()
    swap.wait_send()
    give.wait_send()
    for store in stores:
        store.wait()
    pltpu.make_async_copy(others, others, send.at[38]).wait()


def rest(cid, *args):
    shape = jax.ShapeDtypeStruct
    low = lambda *dims: pltpu.VMEM(dims, BF)
    full = lambda *dims: pltpu.VMEM(dims, F32)
    weight_grad = shape((64, 512), F32)
    return pl.pallas_call(
        rest_kernel,
        out_shape=(
            shape((4, 96, 2048), BF),
            shape((4, 96, 2048), BF),
            shape((8, 128), F32),
            shape((64, 2048), F32),
            weight_grad,
            weight_grad,
            weight_grad,
            weight_grad,
            shape((4, 8, 128), F32),
            shape((8, 128), F32),
        ),
        in_specs=[VMEM] * 6 + [SMEM] + [VMEM] * 4 + [ANYWHERE] * 18,
        out_specs=(ANYWHERE,) * 10,
        scratch_shapes=[
            low(4, 96, 2048),
            low(4, 96, 2048),
            full(8, 128),
            full(64, 2048),
            full(64, 512),
            full(64, 512),
            full(64, 512),
            full(64, 512),
            full(4, 8, 128),
            full(8, 128),
            full(4, 128),
            low(4, 96, 2048),
            full(96, 2048),
            low(384, 1536),
            low(2048, 384),
            low(384, 2048),
            low(384, 512),
            low(384, 512),
            low(384, 512),
            low(4, 384, 384),
            full(384, 512),
            full(384, 512),
            low(384, 512),
            low(2048, 512),
            low(3, 2048, 512),
            low(4, 16, 2, 64, 512),
            low(4, 16, 64, 512),
            low(4, 4, 256, 512),
            low(4, 8, 256, 256),
            low(4, 4, 64, 512),
            low(4, 8, 64, 256),
            low(4, 8, 256, 256),
            low(4, 8, 64, 256),
            low(4, 96, 2048),
            low(2, 8, 48, 1024),
            full(48, 2048),
            full(384, 128),
            full(384, 512),
            full(384, 512),
            full(384, 512),
            full(384, 512),
            full(384, 512),
            low(4, 128, 128),
            low(2, 128, 128),
            low(4, 256, 128),
            low(4, 256, 128),
            low(2, 128, 128),
            low(2, 128, 128),
            low(4, 128, 128),
            full(8, 128),
            full(32, 8, 128),
            full(4, 8, 128),
            full(8, 128),
            full(4, 8, 128),
            full(16, 128),
            full(32, 16, 128),
            pltpu.SemaphoreType.DMA((28,)),
            pltpu.SemaphoreType.DMA((180,)),
            pltpu.SemaphoreType.DMA((180,)),
        ],
        name="rest",
        compiler_params=params(cid, 63),
    )(*args)


def last_kernel(*refs):
    ins, outs = refs[:13], refs[13:28]
    narrow, wide, rows, gate, up, sems, *held = refs[28:]
    move = Moves(sems)
    grad_tokens, mlp_grads, gains, *same = ins
    o_tokens, o_gate, o_up, o_attn, o_mlp, *o_same = outs
    fetch = [move.start(grad_tokens.at[q], narrow.at[q]) for q in range(4)]
    fetch_same = [move.start(src, dst) for src, dst in zip((gains, *same), held)]
    fetch_rows = move.start(mlp_grads, rows)
    copies = []
    for q in range(4):
        fetch[q].wait()
        wide[q] = narrow[q].astype(F32)
        copies.append(move.start(wide.at[q], o_tokens.at[q]))
    for copy in fetch_same:
        copy.wait()
    copies.append(move.start(held[0].at[pl.ds(0, 2)], o_attn))
    copies.append(move.start(held[0].at[pl.ds(2, 2)], o_mlp))
    copies += [move.start(src, dst) for src, dst in zip(held[1:], o_same)]
    fetch_rows.wait()
    units = gate.shape[1]
    gate[...] = rows[:, :units].astype(F32)
    copies.append(move.start(gate, o_gate))
    up[...] = rows[:, units:].astype(F32)
    copies.append(move.start(up, o_up))
    for copy in copies:
        copy.wait()


def last(grad_tokens, mlp_grads, gains, *same):
    shape = jax.ShapeDtypeStruct
    wide = shape((64, mlp_grads.shape[1] // 2), F32)
    gain = shape((2, 8, 128), F32)
    outs = (shape(grad_tokens.shape, F32), wide, wide, gain, gain, *(shape(a.shape, a.dtype) for a in same))
    return pl.pallas_call(
        last_kernel,
        out_shape=outs,
        in_specs=[ANYWHERE] * 13,
        out_specs=(ANYWHERE,) * len(outs),
        scratch_shapes=[
            pltpu.VMEM(grad_tokens.shape, BF),
            pltpu.VMEM(grad_tokens.shape, F32),
            pltpu.VMEM(mlp_grads.shape, BF),
            pltpu.VMEM(wide.shape, F32),
            pltpu.VMEM(wide.shape, F32),
            pltpu.SemaphoreType.DMA((34,)),
            *(pltpu.VMEM(a.shape, a.dtype) for a in (gains, *same)),
        ],
        name="last",
        compiler_params=pltpu.CompilerParams(vmem_limit_bytes=63 << 20),
    )(grad_tokens, mlp_grads, gains, *same)


def on_device(
    tokens,
    cotangent,
    w_query,
    w_key,
    w_value,
    w_output,
    w_gate,
    w_up,
    w_down,
    gain_attn,
    gain_mlp,
    gate_logit,
    valid_count,
):
    valid = valid_count[None]
    rows = (16, 2, 64, 512)
    (
        normed_t, grad_out_t, query, key, value, probs, local_out, retrieved, mix, hidden, mlp_grads,
        recall, inverse, forth, grad_out_own, offset, normal_next, memory_prev, memory_next, ys, xs, pair_e, middle,
        grad_two,
    ) = front(
        0, gain_attn[None], gain_mlp[None], valid, gate_logit, tokens, cotangent,
        *(w.reshape(rows) for w in (w_query, w_key, w_value, w_output)), w_down, w_gate, w_up,
    )
    mlp_grads = lax.psum_scatter(mlp_grads.reshape(1024, -1), SEQ[:2], scatter_dimension=0, tiled=True)
    (
        layer_out, grad_tokens, later_offset, grad_down, grad_query, grad_key, grad_value, grad_output, gains, logit_grad,
    ) = rest(
        1, grad_two, middle, gain_attn[None], gain_mlp[None], grad_out_own, offset, gate_logit, memory_prev, ys, xs, pair_e,
        grad_out_t, hidden, query, key, value, probs, local_out, retrieved, mix, normed_t, recall, inverse,
        forth, w_query, w_key, w_value, w_output, tokens,
    )
    (
        grad_tokens, grad_gate, grad_up, gain_attn_grad, gain_mlp_grad, layer_out, grad_query, grad_key, grad_value,
        grad_output, grad_down, logit_grad, memory_next, normal_next, later_offset,
    ) = last(
        grad_tokens, mlp_grads, gains, layer_out, grad_query, grad_key, grad_value, grad_output, grad_down, logit_grad,
        memory_next, normal_next, later_offset,
    )
    return (
        layer_out.reshape(tokens.shape),
        grad_tokens.reshape(tokens.shape),
        grad_query,
        grad_key,
        grad_value,
        grad_output,
        grad_gate,
        grad_up,
        grad_down,
        gain_attn_grad.reshape(-1),
        gain_mlp_grad.reshape(-1),
        logit_grad[0, :4],
        memory_next[None],
        normal_next[None, :4],
        later_offset[None, :4],
    )


def solution(mesh):
    torus = Mesh(
        mesh.devices.reshape(4, 4, 2, mesh.shape["tensor"]), ("seq_0", "seq_1", "seq_2", "tensor")
    )
    weight = P(None, "tensor")
    grad = P(SEQ, "tensor")
    return jax.shard_map(
        on_device,
        mesh=torus,
        in_specs=(P(SEQ, None), P(SEQ, None)) + (weight,) * 7 + (P(), P(), P("tensor"), P()),
        out_specs=(P(SEQ, None), P(SEQ, None))
        + (grad,) * 7
        + (P(), P(), P("tensor"), P(SEQ, "tensor", None, None), P(SEQ, "tensor", None), P(SEQ, "tensor", None)),
        check_vma=False,
    )
```

```python
import functools

import jax
import jax.numpy as jnp
from jax import lax
from jax.experimental import pallas as pl
from jax.experimental.pallas import tpu as pltpu
from jax.sharding import Mesh
from jax.sharding import PartitionSpec as P

SEQ = ("seq_0", "seq_1", "seq_2")
MESH_ID = pl.DeviceIdType.MESH
VMEM = pl.BlockSpec(memory_space=pltpu.VMEM)
BF = jnp.bfloat16
F32 = jnp.float32

epsilon = 1e-06


def remote(src, dst, send, recv, device):
    return pltpu.make_async_remote_copy(
        src_ref=src, dst_ref=dst, send_sem=send, recv_sem=recv, device_id=device, device_id_type=MESH_ID
    )


def meet(devices):
    barrier = pltpu.get_barrier_semaphore()
    for device in devices:
        pl.semaphore_signal(barrier, inc=1, device_id=device, device_id_type=MESH_ID)
    pl.semaphore_wait(barrier, len(devices))


def params(collective_id, mib):
    return pltpu.CompilerParams(
        collective_id=collective_id, has_side_effects=True, vmem_limit_bytes=mib << 20
    )


def seq_place(index):
    return {"seq_0": index // 8, "seq_1": lax.rem(index // 2, 4), "seq_2": lax.rem(index, 2)}


def seq_index():
    return lax.axis_index("seq_0") * 8 + lax.axis_index("seq_1") * 2 + lax.axis_index("seq_2")


def mul(a, b):
    return jnp.dot(a.astype(BF), b.astype(BF), preferred_element_type=F32)


def mul_t(a, b):
    return lax.dot_general(a.astype(BF), b.astype(BF), (((0,), (0,)), ((), ())), preferred_element_type=F32)


def ring_places():
    x, y, c = (lax.axis_index(a) for a in SEQ)
    return x, y, c


def rows_by_rows(a, b):
    return lax.dot_general(a, b, (((1,), (1,)), ((), ())), preferred_element_type=F32)


class RingSum:
    def __init__(self, src, bufs, send, recv, base, axis, rows=None):
        self.src, self.bufs, self.me = src, bufs, lax.axis_index(axis)
        rows = pl.ds(0, src.shape[1]) if rows is None else rows
        self.rows = rows
        half = src.shape[2] // 2
        self.a, self.b = pl.ds(0, half), pl.ds(half, half)
        self.right, self.left = lax.rem(self.me + 1, 4), lax.rem(self.me + 3, 4)
        far = lax.rem(self.me + 2, 4)
        to_right, to_left = {axis: self.right}, {axis: self.left}

        def copy(piece, landing, slot, device):
            return remote(piece, bufs.at[landing], send.at[base + slot], recv.at[base + slot], device)

        self.c0 = copy(src.at[far, rows, self.a], 0, 0, to_right)
        self.c1 = copy(src.at[far, rows, self.b], 1, 1, to_left)
        self.c2 = copy(src.at[self.right, rows, self.b], 2, 2, to_right)
        self.c3 = copy(src.at[self.left, rows, self.a], 3, 3, to_left)
        self.c4 = copy(bufs.at[0], 4, 4, to_right)
        self.c5 = copy(bufs.at[1], 5, 5, to_left)

    def start_a(self):
        self.c0.start()
        self.c3.start()

    def start_b(self):
        self.c1.start()
        self.c2.start()

    def start(self):
        self.c0.start()
        self.c1.start()
        self.c3.start()
        self.c2.start()

    def middle(self):
        src, bufs = self.src, self.bufs
        self.c0.wait_recv()
        bufs[0] = (bufs[0].astype(F32) + src[self.right, self.rows, self.a].astype(F32)).astype(BF)
        self.c4.start()
        self.c1.wait_recv()
        bufs[1] = (bufs[1].astype(F32) + src[self.left, self.rows, self.b].astype(F32)).astype(BF)
        self.c5.start()

    def finish(self, put):
        src, bufs = self.src, self.bufs
        self.c3.wait_recv()
        self.c4.wait_recv()
        put(self.a, src[self.me, self.rows, self.a].astype(F32) + bufs[4].astype(F32) + bufs[3].astype(F32))
        self.c2.wait_recv()
        self.c5.wait_recv()
        put(self.b, src[self.me, self.rows, self.b].astype(F32) + bufs[5].astype(F32) + bufs[2].astype(F32))

    def drain(self):
        for copy in (self.c0, self.c1, self.c2, self.c3, self.c4, self.c5):
            copy.wait_send()


class RingGather:
    def __init__(self, buf, send, recv, base, axis, rows=None):
        self.me = lax.axis_index(axis)
        half = buf.shape[1 if rows is None else 2] // 2
        right, left = lax.rem(self.me + 1, 4), lax.rem(self.me + 3, 4)
        to_right, to_left = {axis: right}, {axis: left}

        def copy(q, h, slot, device):
            part = pl.ds(half * h, half)
            piece = buf.at[q, part] if rows is None else buf.at[q, rows, part]
            return remote(piece, piece, send.at[base + slot], recv.at[base + slot], device)

        self.r0, self.l1 = copy(self.me, 0, 0, to_right), copy(self.me, 1, 1, to_left)
        self.r1, self.l0 = copy(self.me, 1, 2, to_right), copy(self.me, 0, 3, to_left)
        self.f0, self.f1 = copy(left, 0, 4, to_right), copy(right, 1, 5, to_left)

    def start(self):
        for copy in (self.r0, self.l1, self.r1, self.l0):
            copy.start()

    def middle(self):
        self.r0.wait_recv()
        self.f0.start()
        self.l1.wait_recv()
        self.f1.start()

    def finish(self):
        for copy in (self.r1, self.l0, self.f0, self.f1):
            copy.wait_recv()

    def drain(self):
        for copy in (self.r0, self.l1, self.r1, self.l0, self.f0, self.f1):
            copy.wait_send()


class SeqSum:
    def __init__(self, product, got, first, first_bufs, second, second_bufs, send, recv, base, x_first):
        self.got, self.first, self.second, self.x_first = got, first, second, x_first
        core = lax.axis_index("seq_2")
        self.swap = remote(product, got, send.at[base], recv.at[base], {"seq_2": 1 - core})
        axes = ("seq_0", "seq_1") if x_first else ("seq_1", "seq_0")
        self.one = RingSum(first, first_bufs, send, recv, base + 1, axes[0])
        self.two = RingSum(second, second_bufs, send, recv, base + 7, axes[1])

    def start(self):
        self.swap.start()

    def store(self, own):
        for x in range(4):
            for y in range(4):
                at = 4 * x + y
                q, r = (x, y) if self.x_first else (y, x)
                self.first[q, pl.ds(64 * r, 64)] = own[64 * at : 64 * (at + 1)].astype(BF)

    def add(self, own):
        self.swap.wait_recv()
        self.store(own + flat(self.got[...]).astype(F32))

    def add_stored(self):
        self.swap.wait_recv()
        for x in range(4):
            for y in range(4):
                q, r = (x, y) if self.x_first else (y, x)
                rows = pl.ds(64 * r, 64)
                self.first[q, rows] = (self.first[q, rows].astype(F32) + self.got[4 * x + y].astype(F32)).astype(BF)

    def second_ring(self):
        def put(cols, value):
            for r in range(4):
                self.second[r, :, cols] = value[64 * r : 64 * (r + 1)].astype(BF)

        self.one.finish(put)
        self.two.start()

    def finish(self, out):
        def put(cols, value):
            out[:, cols] = value

        self.two.finish(put)

    def drain(self):
        self.swap.wait_send()
        self.one.drain()
        self.two.drain()


def greet_all():
    barrier = pltpu.get_barrier_semaphore()
    me, z = seq_index(), lax.axis_index("tensor")

    def greet_seq(k, carry):
        pl.semaphore_signal(barrier, inc=1, device_id=seq_place(lax.rem(me + k, 32)), device_id_type=MESH_ID)
        return carry

    lax.fori_loop(1, 32, greet_seq, 0)
    for k in (1, 2, 3):
        pl.semaphore_signal(barrier, inc=1, device_id={"tensor": lax.rem(z + k, 4)}, device_id_type=MESH_ID)


def all_greeted():
    pl.semaphore_wait(pltpu.get_barrier_semaphore(), 34)


class TotalOfAll:
    def __init__(self, mine, extra, by_z, line, by_seq, total, send, recv, base):
        self.mine, self.extra, self.by_z, self.line, self.by_seq, self.total = mine, extra, by_z, line, by_seq, total
        self.z, self.me = lax.axis_index("tensor"), seq_index()
        self.send, self.recv, self.base = send, recv, base
        peers = [lax.rem(self.z + k, 4) for k in (1, 2, 3)]
        self.split = [
            remote(mine.at[p], by_z.at[self.z], send.at[base + k], recv.at[base + k], {"tensor": p})
            for k, p in enumerate(peers)
        ]
        self.join = [
            remote(total.at[self.z], total.at[self.z], send.at[base + 3 + k], recv.at[base + 3 + k], {"tensor": p})
            for k, p in enumerate(peers)
        ]

    def start(self):
        for copy in self.split:
            copy.start()

    def over_seq(self):
        self.by_z[self.z] = self.mine[self.z]
        for copy in self.split:
            copy.wait_recv()
        self.line[0:8] = (self.by_z[0] + self.by_z[1]) + (self.by_z[2] + self.by_z[3])
        self.line[8:16] = self.extra[...]
        self.by_seq[self.me] = self.line[...]

        def push(k, carry):
            device = seq_place(lax.rem(self.me + k, 32))
            remote(self.line, self.by_seq.at[self.me], self.send.at[self.base + 6], self.recv.at[self.base + 6], device).start()
            return carry

        lax.fori_loop(1, 32, push, 0)

    def over_tensor(self, extra_out):
        others = self.by_seq.at[pl.ds(0, 31)]
        pltpu.make_async_copy(others, others, self.recv.at[self.base + 6]).wait()
        summed = jnp.sum(self.by_seq[...], axis=0)
        self.total[self.z] = summed[0:8]
        extra_out[...] = summed[8:16]
        for copy in self.join:
            copy.start()

    def finish(self):
        for copy in self.join:
            copy.wait_recv()

    def drain(self):
        for copy in (*self.split, *self.join):
            copy.wait_send()
        others = self.by_seq.at[pl.ds(0, 31)]
        pltpu.make_async_copy(others, others, self.send.at[self.base + 6]).wait()


def feature_of(v):
    return jnp.where(v > 0, v + 1.0, jnp.exp(jnp.minimum(v, 0.0)))


def slope_of(v):
    return jnp.where(v > 0, 1.0, jnp.exp(jnp.minimum(v, 0.0)))


ANYWHERE = pl.BlockSpec(memory_space=pl.ANY)


def keep_of(valid):
    length = jnp.where(seq_index() == 31, valid[...], 384)
    return (lax.broadcasted_iota(jnp.int32, (384, 1), 0) < length).astype(F32)


SMEM = pl.BlockSpec(memory_space=pltpu.SMEM)


def gate_rows(gate, logit):
    for h in range(4):
        gate[h : h + 1] = jax.nn.sigmoid(jnp.full((1, 128), logit[h], F32))


def flat(weight):
    return weight.reshape(-1, 512)


def core_rows(turned, core):
    return turned[pl.ds(0, 16), core].reshape(1024, 384)


class Moves:
    def __init__(self, sems):
        self.sems, self.count = sems, 0

    def start(self, src, dst):
        copy = pltpu.make_async_copy(src, dst, self.sems.at[self.count])
        self.count += 1
        copy.start()
        return copy


def front_kernel(
    gain_attn,
    gain_mlp,
    valid,
    gate_logit,
    i_tokens,
    cotangent,
    w_query,
    w_key,
    w_value,
    w_output,
    w_down,
    w_gate,
    w_up,
    o_normed_t,
    o_grad_out_t,
    o_query,
    o_key,
    o_value,
    o_probs,
    o_local_out,
    o_retrieved,
    o_mix,
    o_hidden,
    o_grads,
    o_recall,
    o_inverse,
    o_forth,
    grad_out_own,
    offset,
    normal_next,
    memory_prev,
    memory_next,
    ys,
    xs,
    pair_e,
    middle,
    grad_two,
    out_gate,
    keep,
    gate,
    weights,
    weight_o,
    weight_d,
    weight_g,
    hidden,
    normed_two,
    normed,
    turned,
    grad_out,
    got_rows,
    first_rows,
    first_bufs,
    second_rows,
    second_bufs,
    pair_rows,
    inverse,
    grad_hidden,
    query,
    key,
    value,
    probs,
    local_out,
    retrieved,
    mix,
    line,
    lines,
    eb,
    source,
    got,
    pair_m,
    got_m,
    part,
    part_bufs,
    moves,
    send,
    recv,
):
    move = Moves(moves)
    tokens = hidden
    load_tokens = move.start(i_tokens, tokens)
    loads = [move.start(w, weights.at[i]) for i, w in enumerate((w_key, w_query, w_value))]
    load_cotangent = move.start(cotangent, grad_out)
    load_o = move.start(w_output, weight_o)
    load_d = [move.start(w_down.at[pl.ds(512 * i, 512)], weight_d.at[pl.ds(512 * i, 512)]) for i in range(4)]
    greet_all()
    keep[...] = keep_of(valid)
    gate_rows(gate, gate_logit)
    x, y, c = ring_places()
    z, me = lax.axis_index("tensor"), seq_index()
    partner = {"seq_2": 1 - c}
    mine, theirs = 2 * c, 2 * (1 - c)
    slots = [
        held.at[pl.ds(0, 16), j] for held in (weight_o, weights.at[0], weights.at[1], weights.at[2]) for j in (0, 1)
    ]
    sums = [
        SeqSum(
            slots[i], got_rows.at[i], first_rows.at[i], first_bufs.at[i], second_rows.at[i], second_bufs.at[i],
            send, recv, 27 + 13 * i, i % 2 == 0,
        )
        for i in range(2)
    ]
    swaps = [remote(slots[2 + i], got_rows.at[2 + i], send.at[53 + i], recv.at[53 + i], partner) for i in range(6)]
    parts = [pl.ds(0, 48), pl.ds(48, 48)]
    z_sums = [RingSum(part, part_bufs.at[i], send, recv, 79 + 6 * i, "tensor", parts[i]) for i in (0, 1)]
    z_gathers = [RingGather(normed_two, send, recv, 91 + 6 * i, "tensor", parts[i]) for i in (0, 1)]
    z_backs = [RingSum(part, part_bufs.at[i], send, recv, 6 * i, "tensor", parts[i]) for i in (0, 1)]
    y_ring = RingGather(ys, send, recv, 12, "seq_1")
    x_ring = RingGather(xs, send, recv, 18, "seq_0")
    swap = remote(eb.at[pl.ds(theirs, 2)], got, send.at[24], recv.at[24], partner)
    give = remote(pair_m, got_m, send.at[25], recv.at[25], partner)
    cols = [slice(128 * h, 128 * (h + 1)) for h in range(4)]
    stores = []

    load_tokens.wait()
    for q in range(4):
        rows = pl.ds(96 * q, 96)
        stream = tokens[rows].astype(F32)
        inv = lax.rsqrt(jnp.mean(stream * stream, axis=1, keepdims=True) + epsilon)
        normed[rows] = (stream * inv * gain_attn[...]).astype(BF)
    loads[0].wait()
    key[...] = jnp.dot(normed[...], flat(weights[0]), preferred_element_type=F32).astype(BF)
    feat_q = lambda h: feature_of(query[:, cols[h]].astype(F32))
    feat_k = lambda h: feature_of(key[:, cols[h]].astype(F32))
    line[...] = jnp.zeros_like(line)
    for h in range(4):
        line[h : h + 1] = jnp.sum(feat_k(h) * keep[...], axis=0, keepdims=True)
    lines[me] = line[...]
    all_greeted()

    def push(k, carry):
        remote(line, lines.at[me], send.at[26], recv.at[26], seq_place(lax.rem(me + k, 32))).start()
        return carry

    lax.fori_loop(1, 32, push, 0)
    stores.append(move.start(key, o_key))
    loads[1].wait()
    query[...] = jnp.dot(normed[...], flat(weights[1]), preferred_element_type=F32).astype(BF)
    stores.append(move.start(query, o_query))
    loads[2].wait()
    value[...] = jnp.dot(normed[...], flat(weights[2]), preferred_element_type=F32).astype(BF)
    stores.append(move.start(value, o_value))
    load_g = move.start(w_gate, weight_g)
    at_row = lax.broadcasted_iota(jnp.int32, (384, 384), 0)
    at_col = lax.broadcasted_iota(jnp.int32, (384, 384), 1)
    valid = jnp.sum(keep[...], axis=0, keepdims=True)
    allowed = (at_row >= at_col) & (at_col.astype(F32) < valid)

    def attend(h):
        at = cols[h]
        scores = rows_by_rows(query[:, at], key[:, at]) * 128 ** (-0.5)
        masked = jnp.where(allowed, scores, -1e30)
        raised = jnp.exp(masked - jnp.max(masked, axis=1, keepdims=True))
        low = (raised * (1.0 / jnp.sum(raised, axis=1, keepdims=True))).astype(BF)
        probs[h] = low
        local_out[:, at] = jnp.dot(low, value[:, at], preferred_element_type=F32)
        total = mul_t(feat_k(h) * keep[...], value[:, at])
        source[h] = total
        eb[h, :, 128:256] = total.astype(BF)

    for h in range(4):
        attend(h)
    stores.append(move.start(probs, o_probs))
    stores.append(move.start(local_out, o_local_out))
    others = lines.at[pl.ds(0, 31)]
    pltpu.make_async_copy(others, others, recv.at[26]).wait()
    passed = lax.broadcasted_iota(jnp.int32, (32, 8, 128), 0) < me
    before = jnp.sum(jnp.where(passed, lines[...], 0.0), axis=0)
    normal_next[...] = (before + line[...])[0:4]
    offset[...] = before + 384.0
    for h in range(4):
        fk = feat_k(h)
        kept = fk * keep[...] * (1.0 / jnp.sum(fk * offset[h : h + 1], axis=1, keepdims=True))
        eb[h, :, 0:128] = mul_t(kept, fk).astype(BF)
    swap.start()
    load_cotangent.wait()
    grad_out[...] = grad_out[...] * keep[...].astype(BF)
    grad_out_own[...] = grad_out[pl.ds(pl.multiple_of(96 * z, 96), 96)]
    swap.wait_recv()
    of = [pl.ds(0, 128), pl.ds(128, 128)]
    firsts = []
    for h in (0, 1):
        here, there = eb[mine + h].astype(F32), got[h].astype(F32)
        first, second = jnp.where(c == 0, here, there), jnp.where(c == 0, there, here)
        firsts.append(first)
        pair_e[0, h] = first[:, :128].astype(BF)
        pair_e[1, h] = second[:, :128].astype(BF)
        ys[y, of[h]] = (first + second - mul(second[:, :128], first)).astype(BF)
    y_ring.start()

    def hidden_part(i):
        load_d[i].wait()
        rows = pl.ds(512 * i, 512)
        product = jnp.dot(grad_out[:, 512 * i : 512 * (i + 1)], weight_d[rows], preferred_element_type=F32)
        if i == 0:
            grad_hidden[...] = product
        else:
            grad_hidden[...] += product

    hidden_part(0)
    y_ring.middle()
    hidden_part(1)
    y_ring.finish()
    starts = []
    for h in (0, 1):
        so_far = ys[0, of[h]].astype(F32)
        start = jnp.where(y > 0, so_far, 0.0)
        for k in (1, 2, 3):
            step = ys[k, of[h]].astype(F32)
            so_far = so_far + step - mul(step[:, :128], so_far)
            if k < 3:
                start = jnp.where(y > k, so_far, start)
        xs[x, of[h]] = so_far.astype(BF)
        starts.append(start)
    x_ring.start()
    hidden_part(2)
    x_ring.middle()
    hidden_part(3)
    load_u = move.start(w_up, weight_d)
    load_o.wait()
    x_ring.finish()
    for h in (0, 1):
        m = jnp.where(x > 0, xs[0, of[h]][:, 128:].astype(F32), 0.0)
        for k in (1, 2):
            step = xs[k, of[h]].astype(F32)
            m = jnp.where(x > k, m + step[:, 128:] - mul(step[:, :128], m), m)
        m = m + starts[h][:, 128:] - mul(starts[h][:, :128], m)
        second = m + firsts[h][:, 128:] - mul(firsts[h][:, :128], m)
        memory_prev[mine + h] = jnp.where(c == 0, m, second)
        pair_m[h] = jnp.where(c == 0, second, m)
    give.start()
    give.wait_recv()
    inverse[...] = jnp.zeros_like(inverse)
    inverse[:, 8:9] = keep[...]
    for h in (0, 1):
        memory_prev[theirs + h] = got_m[h]
    for h in range(4):
        at, fq, sig = cols[h], feat_q(h), gate[h : h + 1]
        inv_q = 1.0 / jnp.sum(fq * offset[h : h + 1], axis=1, keepdims=True)
        inverse[:, h : h + 1] = inv_q
        found = mul(fq, memory_prev[h]) * inv_q
        retrieved[:, at] = found
        mix[:, at] = (sig * found + (1.0 - sig) * local_out[:, at]).astype(BF)
    for half in (0, 1):
        rows = pl.ds(1024 * half, 1024)
        part[:, :, rows] = rows_by_rows(mix[...], flat(weight_o[8 * half : 8 * half + 8])).astype(BF).reshape(4, 96, 1024)
        for z_sum in z_sums:
            (z_sum.start_a, z_sum.start_b)[half]()
    store_found = move.start(retrieved, o_retrieved)
    stores.append(move.start(mix, o_mix))
    for h in range(4):
        m = memory_prev[h]
        memory_next[h] = m + source[h] - mul(eb[h][:, :128], m)
    turned[...] = normed[...].T.reshape(16, 2, 64, 384)
    store_t = move.start(turned, o_normed_t)
    z_sums[0].middle()
    z_sums[1].middle()
    store_found.wait()
    recall = retrieved
    for h in range(4):
        fk, off = feat_k(h), offset[h : h + 1]
        inv_k = 1.0 / jnp.sum(fk * off, axis=1, keepdims=True)
        inverse[:, 4 + h : 5 + h] = inv_k
        recall[:, cols[h]] = mul(fk, memory_prev[h]) * inv_k
    stores.append(move.start(recall, o_recall))
    stores.append(move.start(inverse, o_inverse))

    def second_norm(i):
        own_tokens = tokens[pl.ds(pl.multiple_of(96 * z + 48 * i, 16), 48)].astype(F32)

        def put(at, total):
            lanes = slice(0, 1024) if at is z_sums[i].a else slice(1024, 2048)
            middle[parts[i], at] = own_tokens[:, lanes] + total

        z_sums[i].finish(put)
        z_sums[i].drain()
        stream = middle[parts[i]]
        inv = lax.rsqrt(jnp.mean(stream * stream, axis=1, keepdims=True) + epsilon)
        normed_two[z, parts[i]] = (stream * inv * gain_mlp[...]).astype(BF)
        z_gathers[i].start()

    second_norm(0)
    second_norm(1)
    z_gathers[0].middle()
    z_gathers[1].middle()
    store_t.wait()
    turned[...] = grad_out[...].T.reshape(16, 2, 64, 384)
    store_t = move.start(turned, o_grad_out_t)
    for store in stores:
        store.wait()
    store_t.wait()
    load_g.wait()
    load_u.wait()
    for z_gather in z_gathers:
        z_gather.finish()
    for z_gather in z_gathers:
        z_gather.drain()
    turned[...] = normed_two[...].reshape(384, 2048).T.reshape(16, 2, 64, 384)

    def tile(i):
        for half in (2 * i, 2 * i + 1):
            narrow_tile(half)

    def narrow_tile(i):
        lanes = slice(256 * i, 256 * (i + 1))
        rows = normed_two[...].reshape(384, 2048)
        gate_pre = jnp.dot(rows, weight_g[:, lanes], preferred_element_type=F32)
        up_pre = jnp.dot(rows, weight_d[:, lanes], preferred_element_type=F32)
        back_hidden = grad_hidden[:, lanes]
        sig = jax.nn.sigmoid(gate_pre)
        swish = gate_pre * sig
        hidden[:, lanes] = (swish * up_pre).astype(BF)
        grad_out[:, lanes] = (back_hidden * swish).astype(BF)
        normed[:, lanes] = (back_hidden * up_pre * sig * (1.0 + gate_pre * (1.0 - sig))).astype(BF)

    def return_part(i):
        rows = pl.ds(512 * i, 512)
        value = rows_by_rows(normed[...], weight_g[rows]) + rows_by_rows(grad_out[...], weight_d[rows])
        part[:, :, rows] = value.astype(BF).reshape(4, 96, 512)

    leaving = []

    def gradient(i, core):
        side = (normed, grad_out)[i // 4]
        lanes = slice(512 * (i % 4), 512 * (i % 4 + 1))
        return jnp.dot(core_rows(turned, core), side[:, lanes], preferred_element_type=F32)

    def give_half(i):
        slots[i][...] = gradient(i, 1 - c).astype(BF).reshape(16, 64, 512)
        if i < 2:
            sums[i].start()
        else:
            swaps[i - 2].start()

    def gate_ring(i):
        sums[i].add(gradient(i, c))
        sums[i].one.start()

    def pair_sum(i):
        own_rows = gradient(2 + i, c)
        swaps[i].wait_recv()
        if i >= 1:
            leaving[i - 1].wait()
        pair_rows[...] = (own_rows + flat(got_rows[2 + i]).astype(F32)).astype(BF).reshape(16, 64, 512)
        leaving.append(move.start(pair_rows, o_grads.at[:, :, pl.ds(512 * i, 512)]))

    tile(0)
    give_half(0)
    tile(1)
    give_half(1)
    tile(2)
    gate_ring(0)
    tile(3)
    gate_ring(1)
    stores = [move.start(hidden, o_hidden)]
    return_part(0)
    return_part(1)
    for z_back in z_backs:
        z_back.start_a()
    return_part(2)
    return_part(3)
    for z_back in z_backs:
        z_back.start_b()
    load_down = move.start(w_down, weight_g)
    give_half(2)
    sums[0].one.middle()
    give_half(3)
    sums[1].one.middle()
    give_half(4)
    pair_sum(0)
    give_half(5)
    pair_sum(1)
    z_backs[0].middle()
    z_backs[1].middle()
    sums[0].second_ring()
    give_half(6)
    pair_sum(2)
    sums[1].second_ring()
    give_half(7)
    pair_sum(3)
    load_down.wait()
    sums[0].two.middle()
    for half in (0, 1):
        rows = pl.ds(1024 * half, 1024)
        normed_two[:, :, rows] = rows_by_rows(hidden[...], weight_g[rows]).astype(BF).reshape(4, 96, 1024)
        pair_sum(4 + half)
    stores.append(move.start(normed_two, o_forth))
    sums[1].two.middle()
    for i in (0, 1):

        def put(at, total, i=i):
            grad_two[parts[i], at] = total

        z_backs[i].finish(put)
    for i in (0, 1):
        sums[i].finish(out_gate.at[:, pl.ds(512 * i, 512)])
    for copy in (*stores, leaving[5]):
        copy.wait()
    for swap_rows in swaps:
        swap_rows.wait_send()
    for part_sum in sums:
        part_sum.drain()
    for ring in (*z_backs, y_ring, x_ring):
        ring.drain()
    swap.wait_send()
    give.wait_send()
    pltpu.make_async_copy(others, others, send.at[26]).wait()


def front(cid, *args):
    shape = jax.ShapeDtypeStruct
    low = lambda *dims: pltpu.VMEM(dims, BF)
    full = lambda *dims: pltpu.VMEM(dims, F32)
    return pl.pallas_call(
        front_kernel,
        out_shape=(
            shape((16, 2, 64, 384), BF),
            shape((16, 2, 64, 384), BF),
            shape((384, 512), BF),
            shape((384, 512), BF),
            shape((384, 512), BF),
            shape((4, 384, 384), BF),
            shape((384, 512), F32),
            shape((384, 512), F32),
            shape((384, 512), BF),
            shape((384, 2048), BF),
            shape((16, 64, 3072), BF),
            shape((384, 512), F32),
            shape((384, 128), F32),
            shape((4, 96, 2048), BF),
            shape((96, 2048), BF),
            shape((8, 128), F32),
            shape((4, 128), F32),
            shape((4, 128, 128), F32),
            shape((4, 128, 128), F32),
            shape((4, 256, 256), BF),
            shape((4, 256, 256), BF),
            shape((2, 2, 128, 128), BF),
            shape((96, 2048), F32),
            shape((96, 2048), F32),
            shape((64, 1024), F32),
        ),
        in_specs=[VMEM] * 3 + [SMEM] + [ANYWHERE] * 9,
        out_specs=(ANYWHERE,) * 14 + (VMEM,) * 11,
        scratch_shapes=[
            full(384, 1),
            full(4, 128),
            low(3, 16, 2, 64, 512),
            low(16, 2, 64, 512),
            low(2048, 2048),
            low(2048, 2048),
            low(384, 2048),
            low(4, 96, 2048),
            low(384, 2048),
            low(16, 2, 64, 384),
            low(384, 2048),
            low(8, 16, 64, 512),
            low(2, 4, 256, 512),
            low(2, 6, 256, 256),
            low(2, 4, 64, 512),
            low(2, 6, 64, 256),
            low(16, 64, 512),
            full(384, 128),
            full(384, 2048),
            low(384, 512),
            low(384, 512),
            low(384, 512),
            low(4, 384, 384),
            full(384, 512),
            full(384, 512),
            low(384, 512),
            full(8, 128),
            full(32, 8, 128),
            low(4, 128, 256),
            full(4, 128, 128),
            low(2, 128, 256),
            full(2, 128, 128),
            full(2, 128, 128),
            low(4, 96, 2048),
            low(2, 6, 48, 1024),
            pltpu.SemaphoreType.DMA((34,)),
            pltpu.SemaphoreType.DMA((107,)),
            pltpu.SemaphoreType.DMA((107,)),
        ],
        name="front",
        compiler_params=params(cid, 63),
    )(*args)


def neighbours():
    x, y, c = ring_places()
    z = lax.axis_index("tensor")
    near = [{"seq_2": 1 - c}]
    for axis, at in (("seq_0", x), ("seq_1", y), ("tensor", z)):
        near += [{axis: lax.rem(at + 1, 4)}, {axis: lax.rem(at + 3, 4)}]
    return near


def rest_kernel(
    grad_two,
    middle,
    gain_attn,
    gain_mlp,
    grad_out,
    offset,
    gate_logit,
    memory,
    ys,
    xs,
    pair_e,
    i_grad_out_t,
    i_hidden,
    i_query,
    i_key,
    i_value,
    i_probs,
    i_local_out,
    i_retrieved,
    i_mix,
    i_normed_t,
    i_recall,
    i_inverse,
    i_forth,
    w_query,
    w_key,
    w_value,
    w_output,
    tokens,
    o_layer_out,
    o_grad_tokens,
    o_later,
    o_out_down,
    o_out_query,
    o_out_key,
    o_out_value,
    o_out_output,
    o_gains,
    o_logits_out,
    layer_out,
    grad_tokens,
    later,
    out_down,
    out_query,
    out_key,
    out_value,
    out_output,
    gains,
    logits_out,
    gate,
    branch,
    grad_middle,
    grads,
    left,
    hidden,
    query,
    key,
    value,
    probs,
    local_out,
    retrieved,
    mix,
    weight_o,
    weight_in,
    products,
    got_rows,
    first_rows,
    first_bufs,
    second_rows,
    second_bufs,
    first_bufs_2,
    second_bufs_2,
    forth,
    z_bufs,
    own,
    inverse,
    recall,
    grad_mix,
    grad_query,
    grad_key,
    grad_value,
    source,
    got,
    s_y,
    s_x,
    pair_l,
    got_l,
    adjoint,
    line,
    lines,
    mine_gains,
    logits,
    by_z,
    total_line,
    by_seq,
    moves,
    send,
    recv,
):
    x, y, c = ring_places()
    z, me = lax.axis_index("tensor"), seq_index()
    move = Moves(moves)
    pairs = (
        (i_grad_out_t, left),
        (i_hidden, hidden),
        (i_forth, forth),
        (w_output, weight_o),
        (i_query, query),
        (i_inverse, inverse),
        (i_probs, probs),
        (i_key, key),
        (i_value, value),
        (i_mix, mix),
        (i_retrieved, retrieved),
        (i_local_out, local_out),
        (i_recall, recall),
        (w_query, weight_in.at[0]),
        (w_key, weight_in.at[1]),
        (w_value, weight_in.at[2]),
    )
    barrier = pltpu.get_barrier_semaphore()
    for device in neighbours():
        pl.semaphore_signal(barrier, inc=1, device_id=device, device_id_type=MESH_ID)
    loads = [move.start(src, dst) for src, dst in pairs]
    gate_rows(gate, gate_logit)
    partner = {"seq_2": 1 - c}
    mine, theirs = 2 * c, 2 * (1 - c)
    parts = [pl.ds(0, 48), pl.ds(48, 48)]
    z_branches = [RingGather(branch, send, recv, 6 * i, "tensor", parts[i]) for i in (0, 1)]
    z_forths = [RingSum(forth, z_bufs.at[i], send, recv, (12, 174)[i], "tensor", parts[i]) for i in (0, 1)]
    z_layer = RingGather(layer_out, send, recv, 18, "tensor")
    y_ring = RingGather(s_y, send, recv, 24, "seq_1")
    x_ring = RingGather(s_x, send, recv, 30, "seq_0")
    swap = remote(source.at[pl.ds(theirs, 2)], got, send.at[36], recv.at[36], partner)
    give = remote(pair_l, got_l, send.at[37], recv.at[37], partner)
    z_ends = [RingSum(forth, z_bufs.at[i], send, recv, 143 + 6 * i, "tensor", parts[i]) for i in (0, 1)]
    z_tokens = [RingGather(grad_tokens, send, recv, 155 + 6 * i, "tensor", parts[i]) for i in (0, 1)]
    total = TotalOfAll(mine_gains, logits, by_z, total_line, by_seq, gains, send, recv, 167)

    def seq_sums(base, first_bufs, second_bufs, order):
        return [
            SeqSum(
                products.at[i], got_rows.at[i], first_rows.at[order[i]], first_bufs.at[i], second_rows.at[i],
                second_bufs.at[i], send, recv, base + 13 * i, i % 2 == 0,
            )
            for i in range(4)
        ]

    sums, ends = seq_sums(39, first_bufs, second_bufs, (0, 1, 2, 3)), seq_sums(91, first_bufs_2, second_bufs_2, (4, 1, 2, 3))
    cols = [slice(128 * h, 128 * (h + 1)) for h in range(4)]
    of = [pl.ds(0, 128), pl.ds(128, 128)]
    feat_q = lambda h: feature_of(query[:, cols[h]].astype(F32))
    feat_k = lambda h: feature_of(key[:, cols[h]].astype(F32))
    scale = 128 ** (-0.5)

    def half_product(right, core):
        return jnp.dot(core_rows(left, core), right, preferred_element_type=F32)

    def product(group, i, right):
        products[i] = half_product(right, 1 - c).astype(BF).reshape(16, 64, 512)
        group[i].start()

    def down(i):
        product(sums, i, hidden[:, 512 * i : 512 * (i + 1)])

    def down_add(i):
        sums[i].add(half_product(hidden[:, 512 * i : 512 * (i + 1)], c))

    def grads_ring(i):
        ends[i].add(half_product(grads[:, 512 * (i - 1) : 512 * i], c))
        ends[i].one.start()

    def norm_back(stream, grad_normed, gain, first_row, i):
        inv = lax.rsqrt(jnp.mean(stream * stream, axis=1, keepdims=True) + epsilon)
        weighted = grad_normed * gain[...]
        inner = jnp.sum(weighted * stream, axis=1, keepdims=True)
        scaled = stream * inv
        line_of = jnp.sum(grad_normed * scaled, axis=0, keepdims=True)
        for r in range(16):
            at = (first_row + r // 8, slice(r % 8, r % 8 + 1))
            piece = line_of[:, 128 * r : 128 * (r + 1)]
            mine_gains[at] = piece if i == 0 else mine_gains[at] + piece
        return inv * weighted - scaled * (inv * inv * inner * (1.0 / stream.shape[1]))

    for i in (0, 1):
        rows = parts[i]
        result = grad_out[rows].astype(F32) + norm_back(middle[rows], grad_two[rows], gain_mlp, 2, i)
        grad_middle[rows] = result
        branch[z, rows] = result.astype(BF)
        if i == 0:
            pl.semaphore_wait(barrier, 7)
        z_branches[i].start()
    loads[0].wait()
    loads[1].wait()
    down(0)
    down(1)
    z_branches[0].middle()
    down_add(0)
    sums[0].one.start()
    z_branches[1].middle()
    down(2)
    down_add(1)
    sums[1].one.start()
    down(3)
    down_add(2)
    sums[0].one.middle()
    down_add(3)
    for load in loads[2:6]:
        load.wait()
    for z_branch in z_branches:
        z_branch.finish()
    for z_forth in z_forths:
        z_forth.start()
    grad_mix[...] = jnp.dot(branch[...].reshape(384, 2048), weight_o[...], preferred_element_type=F32)

    def point(h):
        return gate[h : h + 1] * grad_mix[:, cols[h]] * inverse[:, h : h + 1]

    for h in range(4):
        source[h] = mul_t(feat_q(h), point(h)).astype(BF)
    swap.start()

    def attend(h):
        at = cols[h]
        grad_local = ((1.0 - gate[h : h + 1]) * grad_mix[:, at]).astype(BF)
        low = probs[h]
        p = low.astype(F32)
        grad_probs = rows_by_rows(grad_local, value[:, at])
        grad_value[:, at] = mul_t(low, grad_local)
        grad_scores = (p * (grad_probs - jnp.sum(grad_probs * p, axis=1, keepdims=True))).astype(BF)
        grad_query[:, at] = mul(grad_scores, key[:, at]) * scale
        grad_key[:, at] = mul_t(grad_scores, query[:, at]) * scale

    for load in loads[6:9]:
        load.wait()
    attend(0)
    sums[1].one.middle()
    swap.wait_recv()
    seconds = []
    for h in (0, 1):
        here, there = source[mine + h].astype(F32), got[h].astype(F32)
        first, second = jnp.where(c == 0, here, there), jnp.where(c == 0, there, here)
        seconds.append(second)
        s_y[y, of[h]] = (first + second - mul_t(pair_e[0, h], second)).astype(BF)
    y_ring.start()
    attend(1)
    y_ring.middle()
    sums[0].second_ring()
    attend(2)
    for z_forth in z_forths:
        z_forth.middle()
    sums[1].second_ring()
    for s in sums:
        s.swap.wait_send()
    left[...] = branch[...].reshape(384, 2048).T.reshape(16, 2, 64, 384)
    for z_branch in z_branches:
        z_branch.drain()
    load_own = move.start(tokens.at[pl.ds(pl.multiple_of(96 * z, 96), 96)], branch.at[0])
    y_ring.finish()
    for h in (0, 1):
        so_far = s_y[3, of[h]].astype(F32)
        for k in (2, 1, 0):
            so_far = s_y[k, of[h]].astype(F32) + so_far - mul_t(ys[k, of[h]][:, :128], so_far)
        s_x[x, of[h]] = so_far.astype(BF)
    x_ring.start()
    for load in loads[9:13]:
        load.wait()
    product(ends, 0, mix[...])
    ends[0].store(half_product(mix[...], c))
    x_ring.middle()
    load_t = move.start(i_normed_t, left)
    attend(3)
    logit_rows = []
    for h in range(4):
        at, gate_h, g = cols[h], gate[h : h + 1], grad_mix[:, cols[h]]
        ret = retrieved[:, at]
        moved = jnp.sum(g * (ret - local_out[:, at]), axis=0, keepdims=True) * gate_h * (1.0 - gate_h)
        logit_rows.append(jnp.sum(moved, axis=1, keepdims=True))
        grad_den = -jnp.sum(gate_h * g * ret, axis=1, keepdims=True) * inverse[:, h : h + 1]
        q = query[:, at].astype(F32)
        grad_feat = rows_by_rows(point(h).astype(BF), memory[h].astype(BF)) + grad_den * offset[h : h + 1]
        grads[:, at] = (grad_query[:, at] + grad_feat * slope_of(q)).astype(BF)
        line[h : h + 1] = jnp.sum(grad_den * feature_of(q), axis=0, keepdims=True)
    lane = lax.broadcasted_iota(jnp.int32, (8, 128), 1)
    row = lax.broadcasted_iota(jnp.int32, (8, 128), 0)
    spot = jnp.zeros((8, 128), F32)
    for h in range(4):
        spot = jnp.where((lane == h) & (row == 0), logit_rows[h], spot)
    logits[...] = spot
    for i in (0, 1):

        def put_layer(at, result, i=i):
            lanes = slice(0, 1024) if at is z_forths[i].a else slice(1024, 2048)
            layer_out[z, parts[i], at] = (middle[parts[i], lanes] + result).astype(BF)

        z_forths[i].finish(put_layer)
        z_forths[i].drain()
    z_layer.start()
    sums[0].two.middle()
    sums[1].two.middle()
    x_ring.finish()
    sums[2].one.start()
    sums[3].one.start()
    for h in (0, 1):
        lam = jnp.where(x < 3, s_x[3, of[h]].astype(F32), 0.0)
        for k in (2, 1):
            lam = jnp.where(x < k, s_x[k, of[h]].astype(F32) + lam - mul_t(xs[k, of[h]][:, :128], lam), lam)
        for k in (3, 2, 1):
            lam = jnp.where(y < k, s_y[k, of[h]].astype(F32) + lam - mul_t(ys[k, of[h]][:, :128], lam), lam)
        first = lam + seconds[h] - mul_t(pair_e[1, h], lam)
        adjoint[mine + h] = jnp.where(c == 0, first, lam).astype(BF)
        pair_l[h] = jnp.where(c == 0, lam, first).astype(BF)
    give.start()
    for i in (0, 1):
        sums[i].finish(out_down.at[:, pl.ds(512 * i, 512)])
    give.wait_recv()
    for h in (0, 1):
        adjoint[theirs + h] = got_l[h]
    for h in range(4):
        at, fk = cols[h], feat_k(h)
        grad_update = mul(fk * inverse[:, 8:9], adjoint[h])
        grad_value[:, at] += grad_update
        grad_den = jnp.sum(grad_update * recall[:, at], axis=1, keepdims=True) * inverse[:, 4 + h : 5 + h]
        line[h : h + 1] += jnp.sum(grad_den * fk, axis=0, keepdims=True)
        grad_key[:, at] += slope_of(key[:, at].astype(F32)) * (
            grad_den * offset[h : h + 1]
            - rows_by_rows((grad_update * inverse[:, 4 + h : 5 + h]).astype(BF), memory[h].astype(BF))
        )
    line[4:8] = jnp.zeros((4, 128), F32)
    lines[me] = line[...]

    def push(k, carry):
        remote(line, lines.at[me], send.at[38], recv.at[38], seq_place(lax.rem(me + k, 32))).start()
        return carry

    lax.fori_loop(1, 32, push, 0)
    for h in range(4):
        at = cols[h]
        grads[:, 1024 + 128 * h : 1152 + 128 * h] = grad_value[:, at].astype(BF)
        update = value[:, at].astype(F32) - recall[:, at]
        grad_key[:, at] += (
            inverse[:, 8:9] * slope_of(key[:, at].astype(F32)) * rows_by_rows(update.astype(BF), adjoint[h])
        )
    sums[2].one.middle()
    load_t.wait()
    product(ends, 1, grads[:, 0:512])
    z_layer.middle()
    sums[3].one.middle()
    product(ends, 3, grads[:, 1024:1536])
    for s in sums[:2]:
        s.one.drain()
        s.two.drain()
    ends[0].add_stored()
    ends[0].one.start()
    for load in (*loads[13:], load_own):
        load.wait()
    others = lines.at[pl.ds(0, 31)]
    pltpu.make_async_copy(others, others, recv.at[38]).wait()
    passed = lax.broadcasted_iota(jnp.int32, (32, 8, 128), 0) > me
    after = jnp.sum(jnp.where(passed, lines[...], 0.0), axis=0)
    later[...] = after[0:4]
    stores = [move.start(later, o_later)]
    for h in range(4):
        at = cols[h]
        late = inverse[:, 8:9] * after[h : h + 1] * slope_of(key[:, at].astype(F32))
        grads[:, 512 + 128 * h : 640 + 128 * h] = (grad_key[:, at] + late).astype(BF)
    z_layer.finish()
    stores.append(move.start(layer_out, o_layer_out))
    for half in (0, 1):
        rows = pl.ds(1024 * half, 1024)
        value = sum(rows_by_rows(grads[:, 512 * i : 512 * (i + 1)], weight_in[i, rows]) for i in range(3))
        forth[:, :, rows] = value.astype(BF).reshape(4, 96, 1024)
        for z_end in z_ends:
            (z_end.start_a, z_end.start_b)[half]()
    sums[2].second_ring()
    sums[3].second_ring()
    grads_ring(1)
    product(ends, 2, grads[:, 512:1024])
    z_ends[0].middle()
    z_ends[1].middle()
    ends[0].one.middle()
    for i in (2, 3):
        sums[i].two.middle()
        sums[i].one.drain()
    grads_ring(3)
    ends[1].one.middle()

    def put(at, result):
        own[:, at] = result

    for i in (0, 1):
        rows = parts[i]
        z_ends[i].finish(put)
        result = grad_middle[rows] + norm_back(branch[0, rows].astype(F32), own[...], gain_attn, 0, i)
        grad_tokens[z, rows] = result.astype(BF)
        z_tokens[i].start()
    total.start()
    grads_ring(2)
    for i in (2, 3):
        sums[i].finish(out_down.at[:, pl.ds(512 * i, 512)])
        sums[i].two.drain()
    stores.append(move.start(out_down, o_out_down))
    ends[0].second_ring()
    ends[3].one.middle()
    for z_token in z_tokens:
        z_token.middle()
    ends[1].second_ring()
    total.over_seq()
    ends[2].one.middle()
    ends[0].two.middle()
    ends[3].second_ring()
    ends[1].two.middle()
    total.over_tensor(logits_out)
    stores.append(move.start(logits_out, o_logits_out))
    ends[2].second_ring()
    ends[0].finish(out_output)
    stores.append(move.start(out_output, o_out_output))
    ends[3].two.middle()
    ends[1].finish(out_query)
    stores.append(move.start(out_query, o_out_query))
    ends[2].two.middle()
    ends[3].finish(out_value)
    stores.append(move.start(out_value, o_out_value))
    ends[2].finish(out_key)
    stores.append(move.start(out_key, o_out_key))
    total.finish()
    stores.append(move.start(gains, o_gains))
    for z_token in z_tokens:
        z_token.finish()
    stores.append(move.start(grad_tokens, o_grad_tokens))
    for part in (z_layer, y_ring, x_ring, *z_ends, *z_tokens, total, *ends):
        part.drain()
    swap.wait_send()
    give.wait_send()
    for store in stores:
        store.wait()
    pltpu.make_async_copy(others, others, send.at[38]).wait()


def rest(cid, *args):
    shape = jax.ShapeDtypeStruct
    low = lambda *dims: pltpu.VMEM(dims, BF)
    full = lambda *dims: pltpu.VMEM(dims, F32)
    weight_grad = shape((64, 512), F32)
    return pl.pallas_call(
        rest_kernel,
        out_shape=(
            shape((4, 96, 2048), BF),
            shape((4, 96, 2048), BF),
            shape((4, 128), F32),
            shape((64, 2048), F32),
            weight_grad,
            weight_grad,
            weight_grad,
            weight_grad,
            shape((4, 8, 128), F32),
            shape((8, 128), F32),
        ),
        in_specs=[VMEM] * 6 + [SMEM] + [VMEM] * 4 + [ANYWHERE] * 18,
        out_specs=(ANYWHERE,) * 10,
        scratch_shapes=[
            low(4, 96, 2048),
            low(4, 96, 2048),
            full(4, 128),
            full(64, 2048),
            full(64, 512),
            full(64, 512),
            full(64, 512),
            full(64, 512),
            full(4, 8, 128),
            full(8, 128),
            full(4, 128),
            low(4, 96, 2048),
            full(96, 2048),
            low(384, 1536),
            low(16, 2, 64, 384),
            low(384, 2048),
            low(384, 512),
            low(384, 512),
            low(384, 512),
            low(4, 384, 384),
            full(384, 512),
            full(384, 512),
            low(384, 512),
            low(2048, 512),
            low(3, 2048, 512),
            low(4, 16, 64, 512),
            low(4, 16, 64, 512),
            low(5, 4, 256, 512),
            low(4, 6, 256, 256),
            low(4, 4, 64, 512),
            low(4, 6, 64, 256),
            low(4, 6, 256, 256),
            low(4, 6, 64, 256),
            low(4, 96, 2048),
            low(2, 6, 48, 1024),
            full(48, 2048),
            full(384, 128),
            full(384, 512),
            full(384, 512),
            full(384, 512),
            full(384, 512),
            full(384, 512),
            low(4, 128, 128),
            low(2, 128, 128),
            low(4, 256, 128),
            low(4, 256, 128),
            low(2, 128, 128),
            low(2, 128, 128),
            low(4, 128, 128),
            full(8, 128),
            full(32, 8, 128),
            full(4, 8, 128),
            full(8, 128),
            full(4, 8, 128),
            full(16, 128),
            full(32, 16, 128),
            pltpu.SemaphoreType.DMA((28,)),
            pltpu.SemaphoreType.DMA((180,)),
            pltpu.SemaphoreType.DMA((180,)),
        ],
        name="rest",
        compiler_params=params(cid, 63),
    )(*args)


def last_kernel(*refs):
    ins, outs = refs[:14], refs[14:29]
    narrow, wide, rows, gate, up, sems, *held = refs[29:]
    move = Moves(sems)
    grad_tokens, mlp_grads, grad_gate, gains, *same = ins
    o_tokens, o_gate, o_up, o_attn, o_mlp, *o_same = outs
    fetch = [move.start(grad_tokens.at[q], narrow.at[q]) for q in range(4)]
    known = grad_gate.shape[1]
    fetch_gate = move.start(grad_gate, gate.at[:, pl.ds(0, known)])
    fetch_same = [move.start(src, dst) for src, dst in zip((gains, *same), held)]
    fetch_rows = move.start(mlp_grads, rows)
    copies = []
    for q in range(4):
        fetch[q].wait()
        wide[q] = narrow[q].astype(F32)
        copies.append(move.start(wide.at[q], o_tokens.at[q]))
    fetch_gate.wait()
    for copy in fetch_same:
        copy.wait()
    copies.append(move.start(held[0].at[pl.ds(0, 2)], o_attn))
    copies.append(move.start(held[0].at[pl.ds(2, 2)], o_mlp))
    copies += [move.start(src, dst) for src, dst in zip(held[1:], o_same)]
    fetch_rows.wait()
    split = gate.shape[1] - known
    gate[:, known:] = rows[:, :split].astype(F32)
    copies.append(move.start(gate, o_gate))
    up[...] = rows[:, split:].astype(F32)
    copies.append(move.start(up, o_up))
    for copy in copies:
        copy.wait()


def last(grad_tokens, mlp_grads, grad_gate, gains, *same):
    shape = jax.ShapeDtypeStruct
    wide = shape((64, (mlp_grads.shape[1] + grad_gate.shape[1]) // 2), F32)
    gain = shape((2, 8, 128), F32)
    outs = (shape(grad_tokens.shape, F32), wide, wide, gain, gain, *(shape(a.shape, a.dtype) for a in same))
    return pl.pallas_call(
        last_kernel,
        out_shape=outs,
        in_specs=[ANYWHERE] * 14,
        out_specs=(ANYWHERE,) * len(outs),
        scratch_shapes=[
            pltpu.VMEM(grad_tokens.shape, BF),
            pltpu.VMEM(grad_tokens.shape, F32),
            pltpu.VMEM(mlp_grads.shape, BF),
            pltpu.VMEM(wide.shape, F32),
            pltpu.VMEM(wide.shape, F32),
            pltpu.SemaphoreType.DMA((36,)),
            *(pltpu.VMEM(a.shape, a.dtype) for a in (gains, *same)),
        ],
        name="last",
        compiler_params=pltpu.CompilerParams(vmem_limit_bytes=63 << 20),
    )(grad_tokens, mlp_grads, grad_gate, gains, *same)


def on_device(
    tokens,
    cotangent,
    w_query,
    w_key,
    w_value,
    w_output,
    w_gate,
    w_up,
    w_down,
    gain_attn,
    gain_mlp,
    gate_logit,
    valid_count,
):
    valid = valid_count[None]
    rows = (16, 2, 64, 512)
    (
        normed_t, grad_out_t, query, key, value, probs, local_out, retrieved, mix, hidden, mlp_grads,
        recall, inverse, forth, grad_out_own, offset, normal_next, memory_prev, memory_next, ys, xs, pair_e, middle,
        grad_two, grad_gate,
    ) = front(
        0, gain_attn[None], gain_mlp[None], valid, gate_logit, tokens, cotangent,
        *(w.reshape(rows) for w in (w_query, w_key, w_value, w_output)), w_down, w_gate, w_up,
    )
    mlp_grads = lax.psum_scatter(mlp_grads.reshape(1024, -1), SEQ[:2], scatter_dimension=0, tiled=True)
    (
        layer_out, grad_tokens, later_offset, grad_down, grad_query, grad_key, grad_value, grad_output, gains, logit_grad,
    ) = rest(
        1, grad_two, middle, gain_attn[None], gain_mlp[None], grad_out_own, offset, gate_logit, memory_prev, ys, xs, pair_e,
        grad_out_t, hidden, query, key, value, probs, local_out, retrieved, mix, normed_t, recall, inverse,
        forth, w_query, w_key, w_value, w_output, tokens,
    )
    (
        grad_tokens, grad_gate, grad_up, gain_attn_grad, gain_mlp_grad, layer_out, grad_query, grad_key, grad_value,
        grad_output, grad_down, logit_grad, memory_next, normal_next, later_offset,
    ) = last(
        grad_tokens, mlp_grads, grad_gate, gains, layer_out, grad_query, grad_key, grad_value, grad_output, grad_down,
        logit_grad, memory_next, normal_next, later_offset,
    )
    return (
        layer_out.reshape(tokens.shape),
        grad_tokens.reshape(tokens.shape),
        grad_query,
        grad_key,
        grad_value,
        grad_output,
        grad_gate,
        grad_up,
        grad_down,
        gain_attn_grad.reshape(-1),
        gain_mlp_grad.reshape(-1),
        logit_grad[0, :4],
        memory_next[None],
        normal_next[None],
        later_offset[None],
    )


def solution(mesh):
    torus = Mesh(
        mesh.devices.reshape(4, 4, 2, mesh.shape["tensor"]), ("seq_0", "seq_1", "seq_2", "tensor")
    )
    weight = P(None, "tensor")
    grad = P(SEQ, "tensor")
    return jax.shard_map(
        on_device,
        mesh=torus,
        in_specs=(P(SEQ, None), P(SEQ, None)) + (weight,) * 7 + (P(), P(), P("tensor"), P()),
        out_specs=(P(SEQ, None), P(SEQ, None))
        + (grad,) * 7
        + (P(), P(), P("tensor"), P(SEQ, "tensor", None, None), P(SEQ, "tensor", None), P(SEQ, "tensor", None)),
        check_vma=False,
    )
```

```python
import functools

import jax
import jax.numpy as jnp
from jax import lax
from jax.experimental import pallas as pl
from jax.experimental.pallas import tpu as pltpu
from jax.sharding import Mesh
from jax.sharding import PartitionSpec as P

SEQ = ("seq_0", "seq_1", "seq_2")
MESH_ID = pl.DeviceIdType.MESH
VMEM = pl.BlockSpec(memory_space=pltpu.VMEM)
BF = jnp.bfloat16
F32 = jnp.float32

epsilon = 1e-06


def remote(src, dst, send, recv, device):
    return pltpu.make_async_remote_copy(
        src_ref=src, dst_ref=dst, send_sem=send, recv_sem=recv, device_id=device, device_id_type=MESH_ID
    )


def meet(devices):
    barrier = pltpu.get_barrier_semaphore()
    for device in devices:
        pl.semaphore_signal(barrier, inc=1, device_id=device, device_id_type=MESH_ID)
    pl.semaphore_wait(barrier, len(devices))


def params(collective_id, mib):
    return pltpu.CompilerParams(
        collective_id=collective_id, has_side_effects=True, vmem_limit_bytes=mib << 20
    )


def seq_place(index):
    return {"seq_0": index // 8, "seq_1": lax.rem(index // 2, 4), "seq_2": lax.rem(index, 2)}


def seq_index():
    return lax.axis_index("seq_0") * 8 + lax.axis_index("seq_1") * 2 + lax.axis_index("seq_2")


def mul(a, b):
    return jnp.dot(a.astype(BF), b.astype(BF), preferred_element_type=F32)


def mul_t(a, b):
    return lax.dot_general(a.astype(BF), b.astype(BF), (((0,), (0,)), ((), ())), preferred_element_type=F32)


def ring_places():
    x, y, c = (lax.axis_index(a) for a in SEQ)
    return x, y, c


def rows_by_rows(a, b):
    return lax.dot_general(a, b, (((1,), (1,)), ((), ())), preferred_element_type=F32)


class RingSum:
    def __init__(self, src, bufs, send, recv, base, axis, rows=None):
        self.src, self.bufs, self.me = src, bufs, lax.axis_index(axis)
        rows = pl.ds(0, src.shape[1]) if rows is None else rows
        self.rows = rows
        half = src.shape[2] // 2
        self.a, self.b = pl.ds(0, half), pl.ds(half, half)
        self.right, self.left = lax.rem(self.me + 1, 4), lax.rem(self.me + 3, 4)
        far = lax.rem(self.me + 2, 4)
        to_right, to_left = {axis: self.right}, {axis: self.left}

        def copy(piece, landing, slot, device):
            return remote(piece, bufs.at[landing], send.at[base + slot], recv.at[base + slot], device)

        self.c0 = copy(src.at[far, rows, self.a], 0, 0, to_right)
        self.c1 = copy(src.at[far, rows, self.b], 1, 1, to_left)
        self.c2 = copy(src.at[self.right, rows, self.b], 2, 2, to_right)
        self.c3 = copy(src.at[self.left, rows, self.a], 3, 3, to_left)
        self.c4 = copy(bufs.at[0], 4, 4, to_right)
        self.c5 = copy(bufs.at[1], 5, 5, to_left)

    def start_a(self):
        self.c0.start()
        self.c3.start()

    def start_b(self):
        self.c1.start()
        self.c2.start()

    def start(self):
        self.c0.start()
        self.c1.start()
        self.c3.start()
        self.c2.start()

    def middle(self):
        src, bufs = self.src, self.bufs
        self.c0.wait_recv()
        bufs[0] = (bufs[0].astype(F32) + src[self.right, self.rows, self.a].astype(F32)).astype(BF)
        self.c4.start()
        self.c1.wait_recv()
        bufs[1] = (bufs[1].astype(F32) + src[self.left, self.rows, self.b].astype(F32)).astype(BF)
        self.c5.start()

    def finish(self, put):
        src, bufs = self.src, self.bufs
        self.c3.wait_recv()
        self.c4.wait_recv()
        put(self.a, src[self.me, self.rows, self.a].astype(F32) + bufs[4].astype(F32) + bufs[3].astype(F32))
        self.c2.wait_recv()
        self.c5.wait_recv()
        put(self.b, src[self.me, self.rows, self.b].astype(F32) + bufs[5].astype(F32) + bufs[2].astype(F32))

    def drain(self):
        for copy in (self.c0, self.c1, self.c2, self.c3, self.c4, self.c5):
            copy.wait_send()


class RingGather:
    def __init__(self, buf, send, recv, base, axis, rows=None):
        self.me = lax.axis_index(axis)
        half = buf.shape[1 if rows is None else 2] // 2
        right, left = lax.rem(self.me + 1, 4), lax.rem(self.me + 3, 4)
        to_right, to_left = {axis: right}, {axis: left}

        def copy(q, h, slot, device):
            part = pl.ds(half * h, half)
            piece = buf.at[q, part] if rows is None else buf.at[q, rows, part]
            return remote(piece, piece, send.at[base + slot], recv.at[base + slot], device)

        self.r0, self.l1 = copy(self.me, 0, 0, to_right), copy(self.me, 1, 1, to_left)
        self.r1, self.l0 = copy(self.me, 1, 2, to_right), copy(self.me, 0, 3, to_left)
        self.f0, self.f1 = copy(left, 0, 4, to_right), copy(right, 1, 5, to_left)

    def start(self):
        for copy in (self.r0, self.l1, self.r1, self.l0):
            copy.start()

    def middle(self):
        self.r0.wait_recv()
        self.f0.start()
        self.l1.wait_recv()
        self.f1.start()

    def finish(self):
        for copy in (self.r1, self.l0, self.f0, self.f1):
            copy.wait_recv()

    def drain(self):
        for copy in (self.r0, self.l1, self.r1, self.l0, self.f0, self.f1):
            copy.wait_send()


class SeqSum:
    def __init__(self, product, got, first, first_bufs, second, second_bufs, send, recv, base, x_first):
        self.got, self.first, self.second, self.x_first = got, first, second, x_first
        core = lax.axis_index("seq_2")
        self.swap = remote(product, got, send.at[base], recv.at[base], {"seq_2": 1 - core})
        axes = ("seq_0", "seq_1") if x_first else ("seq_1", "seq_0")
        self.one = RingSum(first, first_bufs, send, recv, base + 1, axes[0])
        self.two = RingSum(second, second_bufs, send, recv, base + 7, axes[1])

    def start(self):
        self.swap.start()

    def store(self, own):
        for x in range(4):
            for y in range(4):
                at = 4 * x + y
                q, r = (x, y) if self.x_first else (y, x)
                self.first[q, pl.ds(64 * r, 64)] = own[64 * at : 64 * (at + 1)].astype(BF)

    def add(self, own):
        self.swap.wait_recv()
        self.store(own + flat(self.got[...]).astype(F32))

    def add_stored(self):
        self.swap.wait_recv()
        for x in range(4):
            for y in range(4):
                q, r = (x, y) if self.x_first else (y, x)
                rows = pl.ds(64 * r, 64)
                self.first[q, rows] = (self.first[q, rows].astype(F32) + self.got[4 * x + y].astype(F32)).astype(BF)

    def second_ring(self):
        def put(cols, value):
            for r in range(4):
                self.second[r, :, cols] = value[64 * r : 64 * (r + 1)].astype(BF)

        self.one.finish(put)
        self.two.start()

    def finish(self, out):
        def put(cols, value):
            out[:, cols] = value

        self.two.finish(put)

    def drain(self):
        self.swap.wait_send()
        self.one.drain()
        self.two.drain()


def greet_all():
    barrier = pltpu.get_barrier_semaphore()
    me, z = seq_index(), lax.axis_index("tensor")

    def greet_seq(k, carry):
        pl.semaphore_signal(barrier, inc=1, device_id=seq_place(lax.rem(me + k, 32)), device_id_type=MESH_ID)
        return carry

    lax.fori_loop(1, 32, greet_seq, 0)
    for k in (1, 2, 3):
        pl.semaphore_signal(barrier, inc=1, device_id={"tensor": lax.rem(z + k, 4)}, device_id_type=MESH_ID)


def all_greeted():
    pl.semaphore_wait(pltpu.get_barrier_semaphore(), 34)


class TotalOfAll:
    def __init__(self, mine, extra, by_z, line, by_seq, total, send, recv, base):
        self.mine, self.extra, self.by_z, self.line, self.by_seq, self.total = mine, extra, by_z, line, by_seq, total
        self.z, self.me = lax.axis_index("tensor"), seq_index()
        self.send, self.recv, self.base = send, recv, base
        peers = [lax.rem(self.z + k, 4) for k in (1, 2, 3)]
        self.split = [
            remote(mine.at[p], by_z.at[self.z], send.at[base + k], recv.at[base + k], {"tensor": p})
            for k, p in enumerate(peers)
        ]
        self.join = [
            remote(total.at[self.z], total.at[self.z], send.at[base + 3 + k], recv.at[base + 3 + k], {"tensor": p})
            for k, p in enumerate(peers)
        ]

    def start(self):
        for copy in self.split:
            copy.start()

    def over_seq(self):
        self.by_z[self.z] = self.mine[self.z]
        for copy in self.split:
            copy.wait_recv()
        self.line[0:8] = (self.by_z[0] + self.by_z[1]) + (self.by_z[2] + self.by_z[3])
        self.line[8:16] = self.extra[...]
        self.by_seq[self.me] = self.line[...]

        def push(k, carry):
            device = seq_place(lax.rem(self.me + k, 32))
            remote(self.line, self.by_seq.at[self.me], self.send.at[self.base + 6], self.recv.at[self.base + 6], device).start()
            return carry

        lax.fori_loop(1, 32, push, 0)

    def over_tensor(self, extra_out):
        others = self.by_seq.at[pl.ds(0, 31)]
        pltpu.make_async_copy(others, others, self.recv.at[self.base + 6]).wait()
        summed = jnp.sum(self.by_seq[...], axis=0)
        self.total[self.z] = summed[0:8]
        extra_out[...] = summed[8:16]
        for copy in self.join:
            copy.start()

    def finish(self):
        for copy in self.join:
            copy.wait_recv()

    def drain(self):
        for copy in (*self.split, *self.join):
            copy.wait_send()
        others = self.by_seq.at[pl.ds(0, 31)]
        pltpu.make_async_copy(others, others, self.send.at[self.base + 6]).wait()


def feature_of(v):
    return jnp.where(v > 0, v + 1.0, jnp.exp(jnp.minimum(v, 0.0)))


def slope_of(v):
    return jnp.where(v > 0, 1.0, jnp.exp(jnp.minimum(v, 0.0)))


ANYWHERE = pl.BlockSpec(memory_space=pl.ANY)


def keep_of(valid):
    length = jnp.where(seq_index() == 31, valid[...], 384)
    return (lax.broadcasted_iota(jnp.int32, (384, 1), 0) < length).astype(F32)


SMEM = pl.BlockSpec(memory_space=pltpu.SMEM)


def gate_rows(gate, logit):
    for h in range(4):
        gate[h : h + 1] = jax.nn.sigmoid(jnp.full((1, 128), logit[h], F32))


def flat(weight):
    return weight.reshape(-1, 512)


def core_rows(turned, core):
    return turned[pl.ds(0, 16), core].reshape(1024, 384)


class Moves:
    def __init__(self, sems):
        self.sems, self.count = sems, 0

    def start(self, src, dst):
        copy = pltpu.make_async_copy(src, dst, self.sems.at[self.count])
        self.count += 1
        copy.start()
        return copy


def front_kernel(
    gain_attn,
    gain_mlp,
    valid,
    gate_logit,
    i_tokens,
    cotangent,
    w_query,
    w_key,
    w_value,
    w_output,
    w_down,
    w_gate,
    w_up,
    o_normed_t,
    o_grad_out_t,
    o_query,
    o_key,
    o_value,
    o_probs,
    o_local_out,
    o_retrieved,
    o_mix,
    o_hidden,
    o_grads,
    o_recall,
    o_inverse,
    o_forth,
    grad_out_own,
    offset,
    normal_next,
    memory_prev,
    memory_next,
    ys,
    xs,
    pair_e,
    middle,
    grad_two,
    out_gate,
    keep,
    gate,
    weights,
    weight_o,
    weight_d,
    weight_g,
    hidden,
    normed_two,
    normed,
    turned,
    grad_out,
    got_rows,
    first_rows,
    first_bufs,
    second_rows,
    second_bufs,
    pair_rows,
    inverse,
    grad_hidden,
    query,
    key,
    value,
    probs,
    local_out,
    retrieved,
    mix,
    line,
    lines,
    eb,
    source,
    got,
    pair_m,
    got_m,
    part,
    part_bufs,
    free,
    moves,
    send,
    recv,
):
    move = Moves(moves)
    tokens = hidden
    load_tokens = move.start(i_tokens, tokens)
    loads = [move.start(w, weights.at[i]) for i, w in enumerate((w_key, w_query, w_value))]
    load_cotangent = move.start(cotangent, grad_out)
    load_o = move.start(w_output, weight_o)
    load_d = [move.start(w_down.at[pl.ds(512 * i, 512)], weight_d.at[pl.ds(512 * i, 512)]) for i in range(4)]
    greet_all()
    keep[...] = keep_of(valid)
    gate_rows(gate, gate_logit)
    x, y, c = ring_places()
    z, me = lax.axis_index("tensor"), seq_index()
    partner = {"seq_2": 1 - c}
    mine, theirs = 2 * c, 2 * (1 - c)
    slots = [
        held.at[pl.ds(0, 16), j] for held in (weight_o, weights.at[0], weights.at[1], weights.at[2]) for j in (0, 1)
    ]
    sums = [
        SeqSum(
            slots[i], got_rows.at[i], first_rows.at[i], first_bufs.at[i], second_rows.at[i], second_bufs.at[i],
            send, recv, 27 + 13 * i, i % 2 == 0,
        )
        for i in range(4)
    ]
    swaps = [remote(slots[4 + i], got_rows.at[i], send.at[103 + i], recv.at[103 + i], partner) for i in range(4)]
    parts = [pl.ds(0, 48), pl.ds(48, 48)]
    z_sums = [RingSum(part, part_bufs.at[i], send, recv, 79 + 6 * i, "tensor", parts[i]) for i in (0, 1)]
    z_gathers = [RingGather(normed_two, send, recv, 91 + 6 * i, "tensor", parts[i]) for i in (0, 1)]
    z_backs = [RingSum(part, part_bufs.at[i], send, recv, 6 * i, "tensor", parts[i]) for i in (0, 1)]
    y_ring = RingGather(ys, send, recv, 12, "seq_1")
    x_ring = RingGather(xs, send, recv, 18, "seq_0")
    swap = remote(eb.at[pl.ds(theirs, 2)], got, send.at[24], recv.at[24], partner)
    give = remote(pair_m, got_m, send.at[25], recv.at[25], partner)
    cols = [slice(128 * h, 128 * (h + 1)) for h in range(4)]
    stores = []

    load_tokens.wait()
    for q in range(4):
        rows = pl.ds(96 * q, 96)
        stream = tokens[rows].astype(F32)
        inv = lax.rsqrt(jnp.mean(stream * stream, axis=1, keepdims=True) + epsilon)
        normed[rows] = (stream * inv * gain_attn[...]).astype(BF)
    loads[0].wait()
    key[...] = jnp.dot(normed[...], flat(weights[0]), preferred_element_type=F32).astype(BF)
    feat_q = lambda h: feature_of(query[:, cols[h]].astype(F32))
    feat_k = lambda h: feature_of(key[:, cols[h]].astype(F32))
    line[...] = jnp.zeros_like(line)
    for h in range(4):
        line[h : h + 1] = jnp.sum(feat_k(h) * keep[...], axis=0, keepdims=True)
    lines[me] = line[...]
    all_greeted()

    def push(k, carry):
        remote(line, lines.at[me], send.at[26], recv.at[26], seq_place(lax.rem(me + k, 32))).start()
        return carry

    lax.fori_loop(1, 32, push, 0)
    stores.append(move.start(key, o_key))
    loads[1].wait()
    query[...] = jnp.dot(normed[...], flat(weights[1]), preferred_element_type=F32).astype(BF)
    stores.append(move.start(query, o_query))
    loads[2].wait()
    value[...] = jnp.dot(normed[...], flat(weights[2]), preferred_element_type=F32).astype(BF)
    stores.append(move.start(value, o_value))
    load_g = move.start(w_gate, weight_g)
    at_row = lax.broadcasted_iota(jnp.int32, (384, 384), 0)
    at_col = lax.broadcasted_iota(jnp.int32, (384, 384), 1)
    valid = jnp.sum(keep[...], axis=0, keepdims=True)
    allowed = (at_row >= at_col) & (at_col.astype(F32) < valid)

    def attend(h):
        at = cols[h]
        scores = rows_by_rows(query[:, at], key[:, at]) * 128 ** (-0.5)
        masked = jnp.where(allowed, scores, -1e30)
        raised = jnp.exp(masked - jnp.max(masked, axis=1, keepdims=True))
        low = (raised * (1.0 / jnp.sum(raised, axis=1, keepdims=True))).astype(BF)
        probs[h] = low
        local_out[:, at] = jnp.dot(low, value[:, at], preferred_element_type=F32)
        total = mul_t(feat_k(h) * keep[...], value[:, at])
        source[h] = total
        eb[h, :, 128:256] = total.astype(BF)

    for h in range(4):
        attend(h)
    stores.append(move.start(probs, o_probs))
    stores.append(move.start(local_out, o_local_out))
    others = lines.at[pl.ds(0, 31)]
    pltpu.make_async_copy(others, others, recv.at[26]).wait()
    passed = lax.broadcasted_iota(jnp.int32, (32, 8, 128), 0) < me
    before = jnp.sum(jnp.where(passed, lines[...], 0.0), axis=0)
    normal_next[...] = (before + line[...])[0:4]
    offset[...] = before + 384.0
    for h in range(4):
        fk = feat_k(h)
        kept = fk * keep[...] * (1.0 / jnp.sum(fk * offset[h : h + 1], axis=1, keepdims=True))
        eb[h, :, 0:128] = mul_t(kept, fk).astype(BF)
    swap.start()
    load_cotangent.wait()
    grad_out[...] = grad_out[...] * keep[...].astype(BF)
    grad_out_own[...] = grad_out[pl.ds(pl.multiple_of(96 * z, 96), 96)]
    swap.wait_recv()
    of = [pl.ds(0, 128), pl.ds(128, 128)]
    firsts = []
    for h in (0, 1):
        here, there = eb[mine + h].astype(F32), got[h].astype(F32)
        first, second = jnp.where(c == 0, here, there), jnp.where(c == 0, there, here)
        firsts.append(first)
        pair_e[0, h] = first[:, :128].astype(BF)
        pair_e[1, h] = second[:, :128].astype(BF)
        ys[y, of[h]] = (first + second - mul(second[:, :128], first)).astype(BF)
    y_ring.start()

    def hidden_part(i):
        load_d[i].wait()
        rows = pl.ds(512 * i, 512)
        product = jnp.dot(grad_out[:, 512 * i : 512 * (i + 1)], weight_d[rows], preferred_element_type=F32)
        if i == 0:
            grad_hidden[...] = product
        else:
            grad_hidden[...] += product

    hidden_part(0)
    y_ring.middle()
    hidden_part(1)
    y_ring.finish()
    starts = []
    for h in (0, 1):
        so_far = ys[0, of[h]].astype(F32)
        start = jnp.where(y > 0, so_far, 0.0)
        for k in (1, 2, 3):
            step = ys[k, of[h]].astype(F32)
            so_far = so_far + step - mul(step[:, :128], so_far)
            if k < 3:
                start = jnp.where(y > k, so_far, start)
        xs[x, of[h]] = so_far.astype(BF)
        starts.append(start)
    x_ring.start()
    hidden_part(2)
    x_ring.middle()
    hidden_part(3)
    load_u = move.start(w_up, weight_d)
    load_o.wait()
    x_ring.finish()
    for h in (0, 1):
        m = jnp.where(x > 0, xs[0, of[h]][:, 128:].astype(F32), 0.0)
        for k in (1, 2):
            step = xs[k, of[h]].astype(F32)
            m = jnp.where(x > k, m + step[:, 128:] - mul(step[:, :128], m), m)
        m = m + starts[h][:, 128:] - mul(starts[h][:, :128], m)
        second = m + firsts[h][:, 128:] - mul(firsts[h][:, :128], m)
        memory_prev[mine + h] = jnp.where(c == 0, m, second)
        pair_m[h] = jnp.where(c == 0, second, m)
    give.start()
    give.wait_recv()
    inverse[...] = jnp.zeros_like(inverse)
    inverse[:, 8:9] = keep[...]
    for h in (0, 1):
        memory_prev[theirs + h] = got_m[h]
    for h in range(4):
        at, fq, sig = cols[h], feat_q(h), gate[h : h + 1]
        inv_q = 1.0 / jnp.sum(fq * offset[h : h + 1], axis=1, keepdims=True)
        inverse[:, h : h + 1] = inv_q
        found = mul(fq, memory_prev[h]) * inv_q
        retrieved[:, at] = found
        mix[:, at] = (sig * found + (1.0 - sig) * local_out[:, at]).astype(BF)
    for half in (0, 1):
        rows = pl.ds(1024 * half, 1024)
        part[:, :, rows] = rows_by_rows(mix[...], flat(weight_o[8 * half : 8 * half + 8])).astype(BF).reshape(4, 96, 1024)
        for z_sum in z_sums:
            (z_sum.start_a, z_sum.start_b)[half]()
    store_found = move.start(retrieved, o_retrieved)
    stores.append(move.start(mix, o_mix))
    for h in range(4):
        m = memory_prev[h]
        memory_next[h] = m + source[h] - mul(eb[h][:, :128], m)
    turned[...] = normed[...].T.reshape(16, 2, 64, 384)
    store_t = move.start(turned, o_normed_t)
    z_sums[0].middle()
    z_sums[1].middle()
    store_found.wait()
    recall = retrieved
    for h in range(4):
        fk, off = feat_k(h), offset[h : h + 1]
        inv_k = 1.0 / jnp.sum(fk * off, axis=1, keepdims=True)
        inverse[:, 4 + h : 5 + h] = inv_k
        recall[:, cols[h]] = mul(fk, memory_prev[h]) * inv_k
    stores.append(move.start(recall, o_recall))
    stores.append(move.start(inverse, o_inverse))

    def second_norm(i):
        own_tokens = tokens[pl.ds(pl.multiple_of(96 * z + 48 * i, 16), 48)].astype(F32)

        def put(at, total):
            lanes = slice(0, 1024) if at is z_sums[i].a else slice(1024, 2048)
            middle[parts[i], at] = own_tokens[:, lanes] + total

        z_sums[i].finish(put)
        z_sums[i].drain()
        stream = middle[parts[i]]
        inv = lax.rsqrt(jnp.mean(stream * stream, axis=1, keepdims=True) + epsilon)
        normed_two[z, parts[i]] = (stream * inv * gain_mlp[...]).astype(BF)
        z_gathers[i].start()

    second_norm(0)
    second_norm(1)
    z_gathers[0].middle()
    z_gathers[1].middle()
    store_t.wait()
    turned[...] = grad_out[...].T.reshape(16, 2, 64, 384)
    store_t = move.start(turned, o_grad_out_t)
    for store in stores:
        store.wait()
    store_t.wait()
    load_g.wait()
    load_u.wait()
    for z_gather in z_gathers:
        z_gather.finish()
    for z_gather in z_gathers:
        z_gather.drain()
    turned[...] = normed_two[...].reshape(384, 2048).T.reshape(16, 2, 64, 384)

    def tile(i):
        for half in (2 * i, 2 * i + 1):
            narrow_tile(half)

    def narrow_tile(i):
        lanes = slice(256 * i, 256 * (i + 1))
        rows = normed_two[...].reshape(384, 2048)
        gate_pre = jnp.dot(rows, weight_g[:, lanes], preferred_element_type=F32)
        up_pre = jnp.dot(rows, weight_d[:, lanes], preferred_element_type=F32)
        back_hidden = grad_hidden[:, lanes]
        sig = jax.nn.sigmoid(gate_pre)
        swish = gate_pre * sig
        hidden[:, lanes] = (swish * up_pre).astype(BF)
        grad_out[:, lanes] = (back_hidden * swish).astype(BF)
        normed[:, lanes] = (back_hidden * up_pre * sig * (1.0 + gate_pre * (1.0 - sig))).astype(BF)

    def return_part(i):
        rows = pl.ds(512 * i, 512)
        value = rows_by_rows(normed[...], weight_g[rows]) + rows_by_rows(grad_out[...], weight_d[rows])
        part[:, :, rows] = value.astype(BF).reshape(4, 96, 512)

    leaving = []

    def gradient(i, core):
        side = (normed, grad_out)[i // 4]
        lanes = slice(512 * (i % 4), 512 * (i % 4 + 1))
        return jnp.dot(core_rows(turned, core), side[:, lanes], preferred_element_type=F32)

    def give_half(i):
        slots[i][...] = gradient(i, 1 - c).astype(BF).reshape(16, 64, 512)
        if i < 4:
            sums[i].start()
        else:
            pl.semaphore_wait(free.at[i - 4], 1)
            swaps[i - 4].start()

    def gate_ring(i):
        sums[i].add(gradient(i, c))
        sums[i].one.start()
        pl.semaphore_signal(free.at[i], inc=1, device_id=partner, device_id_type=MESH_ID)

    def pair_sum(i):
        own_rows = gradient(4 + i, c)
        swaps[i].wait_recv()
        if i >= 1:
            leaving[i - 1].wait()
        pair_rows[...] = (own_rows + flat(got_rows[i]).astype(F32)).astype(BF).reshape(16, 64, 512)
        leaving.append(move.start(pair_rows, o_grads.at[:, :, pl.ds(512 * i, 512)]))

    tile(0)
    give_half(0)
    tile(1)
    give_half(1)
    gate_ring(0)
    tile(2)
    give_half(2)
    gate_ring(1)
    tile(3)
    give_half(3)
    gate_ring(2)
    stores = [move.start(hidden, o_hidden)]
    return_part(0)
    return_part(1)
    for z_back in z_backs:
        z_back.start_a()
    gate_ring(3)
    sums[0].one.middle()
    return_part(2)
    return_part(3)
    for z_back in z_backs:
        z_back.start_b()
    load_down = move.start(w_down, weight_g)
    sums[1].one.middle()
    give_half(4)
    give_half(5)
    sums[2].one.middle()
    sums[0].second_ring()
    pair_sum(0)
    z_backs[0].middle()
    z_backs[1].middle()
    give_half(6)
    pair_sum(1)
    sums[1].second_ring()
    sums[3].one.middle()
    give_half(7)
    pair_sum(2)
    sums[0].two.middle()
    sums[2].second_ring()
    pair_sum(3)
    load_down.wait()
    for half in (0, 1):
        rows = pl.ds(1024 * half, 1024)
        normed_two[:, :, rows] = rows_by_rows(hidden[...], weight_g[rows]).astype(BF).reshape(4, 96, 1024)
        if half == 0:
            sums[1].two.middle()
    stores.append(move.start(normed_two, o_forth))
    sums[3].second_ring()
    sums[2].two.middle()
    for i in (0, 1):
        sums[i].finish(out_gate.at[:, pl.ds(512 * i, 512)])
    for i in (0, 1):

        def put(at, total, i=i):
            grad_two[parts[i], at] = total

        z_backs[i].finish(put)
    sums[3].two.middle()
    for i in (2, 3):
        sums[i].finish(out_gate.at[:, pl.ds(512 * i, 512)])
    for copy in (*stores, leaving[3]):
        copy.wait()
    for swap_rows in swaps:
        swap_rows.wait_send()
    for part_sum in sums:
        part_sum.drain()
    for ring in (*z_backs, y_ring, x_ring):
        ring.drain()
    swap.wait_send()
    give.wait_send()
    pltpu.make_async_copy(others, others, send.at[26]).wait()


def front(cid, *args):
    shape = jax.ShapeDtypeStruct
    low = lambda *dims: pltpu.VMEM(dims, BF)
    full = lambda *dims: pltpu.VMEM(dims, F32)
    return pl.pallas_call(
        front_kernel,
        out_shape=(
            shape((16, 2, 64, 384), BF),
            shape((16, 2, 64, 384), BF),
            shape((384, 512), BF),
            shape((384, 512), BF),
            shape((384, 512), BF),
            shape((4, 384, 384), BF),
            shape((384, 512), F32),
            shape((384, 512), F32),
            shape((384, 512), BF),
            shape((384, 2048), BF),
            shape((16, 64, 2048), BF),
            shape((384, 512), F32),
            shape((384, 128), F32),
            shape((4, 96, 2048), BF),
            shape((96, 2048), BF),
            shape((8, 128), F32),
            shape((4, 128), F32),
            shape((4, 128, 128), F32),
            shape((4, 128, 128), F32),
            shape((4, 256, 256), BF),
            shape((4, 256, 256), BF),
            shape((2, 2, 128, 128), BF),
            shape((96, 2048), F32),
            shape((96, 2048), F32),
            shape((64, 2048), F32),
        ),
        in_specs=[VMEM] * 3 + [SMEM] + [ANYWHERE] * 9,
        out_specs=(ANYWHERE,) * 14 + (VMEM,) * 11,
        scratch_shapes=[
            full(384, 1),
            full(4, 128),
            low(3, 16, 2, 64, 512),
            low(16, 2, 64, 512),
            low(2048, 2048),
            low(2048, 2048),
            low(384, 2048),
            low(4, 96, 2048),
            low(384, 2048),
            low(16, 2, 64, 384),
            low(384, 2048),
            low(4, 16, 64, 512),
            low(4, 4, 256, 512),
            low(4, 6, 256, 256),
            low(4, 4, 64, 512),
            low(4, 6, 64, 256),
            low(16, 64, 512),
            full(384, 128),
            full(384, 2048),
            low(384, 512),
            low(384, 512),
            low(384, 512),
            low(4, 384, 384),
            full(384, 512),
            full(384, 512),
            low(384, 512),
            full(8, 128),
            full(32, 8, 128),
            low(4, 128, 256),
            full(4, 128, 128),
            low(2, 128, 256),
            full(2, 128, 128),
            full(2, 128, 128),
            low(4, 96, 2048),
            low(2, 6, 48, 1024),
            pltpu.SemaphoreType.REGULAR((4,)),
            pltpu.SemaphoreType.DMA((32,)),
            pltpu.SemaphoreType.DMA((107,)),
            pltpu.SemaphoreType.DMA((107,)),
        ],
        name="front",
        compiler_params=params(cid, 63),
    )(*args)


def neighbours():
    x, y, c = ring_places()
    z = lax.axis_index("tensor")
    near = [{"seq_2": 1 - c}]
    for axis, at in (("seq_0", x), ("seq_1", y), ("tensor", z)):
        near += [{axis: lax.rem(at + 1, 4)}, {axis: lax.rem(at + 3, 4)}]
    return near


def rest_kernel(
    grad_two,
    middle,
    gain_attn,
    gain_mlp,
    grad_out,
    offset,
    gate_logit,
    memory,
    ys,
    xs,
    pair_e,
    i_grad_out_t,
    i_hidden,
    i_query,
    i_key,
    i_value,
    i_probs,
    i_local_out,
    i_retrieved,
    i_mix,
    i_normed_t,
    i_recall,
    i_inverse,
    i_forth,
    w_query,
    w_key,
    w_value,
    w_output,
    tokens,
    o_layer_out,
    o_grad_tokens,
    o_later,
    o_out_down,
    o_out_query,
    o_out_key,
    o_out_value,
    o_out_output,
    o_gains,
    o_logits_out,
    layer_out,
    grad_tokens,
    later,
    out_down,
    out_query,
    out_key,
    out_value,
    out_output,
    gains,
    logits_out,
    gate,
    branch,
    grad_middle,
    grads,
    left,
    hidden,
    query,
    key,
    value,
    probs,
    local_out,
    retrieved,
    mix,
    weight_o,
    weight_in,
    products,
    got_rows,
    first_rows,
    first_bufs,
    second_rows,
    second_bufs,
    first_bufs_2,
    second_bufs_2,
    forth,
    z_bufs,
    own,
    inverse,
    recall,
    grad_mix,
    grad_query,
    grad_key,
    grad_value,
    source,
    got,
    s_y,
    s_x,
    pair_l,
    got_l,
    adjoint,
    line,
    lines,
    mine_gains,
    logits,
    by_z,
    total_line,
    by_seq,
    moves,
    send,
    recv,
):
    x, y, c = ring_places()
    z, me = lax.axis_index("tensor"), seq_index()
    move = Moves(moves)
    pairs = (
        (i_grad_out_t, left),
        (i_hidden, hidden),
        (i_forth, forth),
        (w_output, weight_o),
        (i_query, query),
        (i_inverse, inverse),
        (i_probs, probs),
        (i_key, key),
        (i_value, value),
        (i_mix, mix),
        (i_retrieved, retrieved),
        (i_local_out, local_out),
        (i_recall, recall),
        (w_query, weight_in.at[0]),
        (w_key, weight_in.at[1]),
        (w_value, weight_in.at[2]),
    )
    barrier = pltpu.get_barrier_semaphore()
    for device in neighbours():
        pl.semaphore_signal(barrier, inc=1, device_id=device, device_id_type=MESH_ID)
    loads = [move.start(src, dst) for src, dst in pairs]
    gate_rows(gate, gate_logit)
    partner = {"seq_2": 1 - c}
    mine, theirs = 2 * c, 2 * (1 - c)
    parts = [pl.ds(0, 48), pl.ds(48, 48)]
    z_branches = [RingGather(branch, send, recv, 6 * i, "tensor", parts[i]) for i in (0, 1)]
    z_forths = [RingSum(forth, z_bufs.at[i], send, recv, (12, 174)[i], "tensor", parts[i]) for i in (0, 1)]
    z_layer = RingGather(layer_out, send, recv, 18, "tensor")
    y_ring = RingGather(s_y, send, recv, 24, "seq_1")
    x_ring = RingGather(s_x, send, recv, 30, "seq_0")
    swap = remote(source.at[pl.ds(theirs, 2)], got, send.at[36], recv.at[36], partner)
    give = remote(pair_l, got_l, send.at[37], recv.at[37], partner)
    z_ends = [RingSum(forth, z_bufs.at[i], send, recv, 143 + 6 * i, "tensor", parts[i]) for i in (0, 1)]
    z_tokens = [RingGather(grad_tokens, send, recv, 155 + 6 * i, "tensor", parts[i]) for i in (0, 1)]
    total = TotalOfAll(mine_gains, logits, by_z, total_line, by_seq, gains, send, recv, 167)

    def seq_sums(base, first_bufs, second_bufs, order):
        return [
            SeqSum(
                products.at[i], got_rows.at[i], first_rows.at[order[i]], first_bufs.at[i], second_rows.at[i],
                second_bufs.at[i], send, recv, base + 13 * i, i % 2 == 0,
            )
            for i in range(4)
        ]

    sums, ends = seq_sums(39, first_bufs, second_bufs, (0, 1, 2, 3)), seq_sums(91, first_bufs_2, second_bufs_2, (4, 1, 2, 3))
    cols = [slice(128 * h, 128 * (h + 1)) for h in range(4)]
    of = [pl.ds(0, 128), pl.ds(128, 128)]
    feat_q = lambda h: feature_of(query[:, cols[h]].astype(F32))
    feat_k = lambda h: feature_of(key[:, cols[h]].astype(F32))
    scale = 128 ** (-0.5)

    def half_product(right, core):
        return jnp.dot(core_rows(left, core), right, preferred_element_type=F32)

    def product(group, i, right):
        products[i] = half_product(right, 1 - c).astype(BF).reshape(16, 64, 512)
        group[i].start()

    def down(i):
        product(sums, i, hidden[:, 512 * i : 512 * (i + 1)])

    def down_add(i):
        sums[i].add(half_product(hidden[:, 512 * i : 512 * (i + 1)], c))

    def grads_ring(i):
        ends[i].add(half_product(grads[:, 512 * (i - 1) : 512 * i], c))
        ends[i].one.start()

    def norm_back(stream, grad_normed, gain, first_row, i):
        inv = lax.rsqrt(jnp.mean(stream * stream, axis=1, keepdims=True) + epsilon)
        weighted = grad_normed * gain[...]
        inner = jnp.sum(weighted * stream, axis=1, keepdims=True)
        scaled = stream * inv
        line_of = jnp.sum(grad_normed * scaled, axis=0, keepdims=True)
        for r in range(16):
            at = (first_row + r // 8, slice(r % 8, r % 8 + 1))
            piece = line_of[:, 128 * r : 128 * (r + 1)]
            mine_gains[at] = piece if i == 0 else mine_gains[at] + piece
        return inv * weighted - scaled * (inv * inv * inner * (1.0 / stream.shape[1]))

    for i in (0, 1):
        rows = parts[i]
        result = grad_out[rows].astype(F32) + norm_back(middle[rows], grad_two[rows], gain_mlp, 2, i)
        grad_middle[rows] = result
        branch[z, rows] = result.astype(BF)
        if i == 0:
            pl.semaphore_wait(barrier, 7)
        z_branches[i].start()
    loads[0].wait()
    loads[1].wait()
    down(0)
    down(1)
    z_branches[0].middle()
    down_add(0)
    sums[0].one.start()
    z_branches[1].middle()
    down(2)
    down_add(1)
    sums[1].one.start()
    down(3)
    down_add(2)
    sums[0].one.middle()
    down_add(3)
    for load in loads[2:6]:
        load.wait()
    for z_branch in z_branches:
        z_branch.finish()
    for z_forth in z_forths:
        z_forth.start()
    grad_mix[...] = jnp.dot(branch[...].reshape(384, 2048), weight_o[...], preferred_element_type=F32)

    def point(h):
        return gate[h : h + 1] * grad_mix[:, cols[h]] * inverse[:, h : h + 1]

    for h in range(4):
        source[h] = mul_t(feat_q(h), point(h)).astype(BF)
    swap.start()

    def attend(h):
        at = cols[h]
        grad_local = ((1.0 - gate[h : h + 1]) * grad_mix[:, at]).astype(BF)
        low = probs[h]
        p = low.astype(F32)
        grad_probs = rows_by_rows(grad_local, value[:, at])
        grad_value[:, at] = mul_t(low, grad_local)
        grad_scores = (p * (grad_probs - jnp.sum(grad_probs * p, axis=1, keepdims=True))).astype(BF)
        grad_query[:, at] = mul(grad_scores, key[:, at]) * scale
        grad_key[:, at] = mul_t(grad_scores, query[:, at]) * scale

    for load in loads[6:9]:
        load.wait()
    attend(0)
    sums[1].one.middle()
    swap.wait_recv()
    seconds = []
    for h in (0, 1):
        here, there = source[mine + h].astype(F32), got[h].astype(F32)
        first, second = jnp.where(c == 0, here, there), jnp.where(c == 0, there, here)
        seconds.append(second)
        s_y[y, of[h]] = (first + second - mul_t(pair_e[0, h], second)).astype(BF)
    y_ring.start()
    attend(1)
    y_ring.middle()
    sums[0].second_ring()
    attend(2)
    for z_forth in z_forths:
        z_forth.middle()
    sums[1].second_ring()
    for s in sums:
        s.swap.wait_send()
    left[...] = branch[...].reshape(384, 2048).T.reshape(16, 2, 64, 384)
    for z_branch in z_branches:
        z_branch.drain()
    load_own = move.start(tokens.at[pl.ds(pl.multiple_of(96 * z, 96), 96)], branch.at[0])
    y_ring.finish()
    for h in (0, 1):
        so_far = s_y[3, of[h]].astype(F32)
        for k in (2, 1, 0):
            so_far = s_y[k, of[h]].astype(F32) + so_far - mul_t(ys[k, of[h]][:, :128], so_far)
        s_x[x, of[h]] = so_far.astype(BF)
    x_ring.start()
    for load in loads[9:13]:
        load.wait()
    product(ends, 0, mix[...])
    ends[0].store(half_product(mix[...], c))
    x_ring.middle()
    load_t = move.start(i_normed_t, left)
    attend(3)
    logit_rows = []
    for h in range(4):
        at, gate_h, g = cols[h], gate[h : h + 1], grad_mix[:, cols[h]]
        ret = retrieved[:, at]
        moved = jnp.sum(g * (ret - local_out[:, at]), axis=0, keepdims=True) * gate_h * (1.0 - gate_h)
        logit_rows.append(jnp.sum(moved, axis=1, keepdims=True))
        grad_den = -jnp.sum(gate_h * g * ret, axis=1, keepdims=True) * inverse[:, h : h + 1]
        q = query[:, at].astype(F32)
        grad_feat = rows_by_rows(point(h).astype(BF), memory[h].astype(BF)) + grad_den * offset[h : h + 1]
        grads[:, at] = (grad_query[:, at] + grad_feat * slope_of(q)).astype(BF)
        line[h : h + 1] = jnp.sum(grad_den * feature_of(q), axis=0, keepdims=True)
    lane = lax.broadcasted_iota(jnp.int32, (8, 128), 1)
    row = lax.broadcasted_iota(jnp.int32, (8, 128), 0)
    spot = jnp.zeros((8, 128), F32)
    for h in range(4):
        spot = jnp.where((lane == h) & (row == 0), logit_rows[h], spot)
    logits[...] = spot
    for i in (0, 1):

        def put_layer(at, result, i=i):
            lanes = slice(0, 1024) if at is z_forths[i].a else slice(1024, 2048)
            layer_out[z, parts[i], at] = (middle[parts[i], lanes] + result).astype(BF)

        z_forths[i].finish(put_layer)
        z_forths[i].drain()
    z_layer.start()
    sums[0].two.middle()
    sums[1].two.middle()
    x_ring.finish()
    sums[2].one.start()
    sums[3].one.start()
    for h in (0, 1):
        lam = jnp.where(x < 3, s_x[3, of[h]].astype(F32), 0.0)
        for k in (2, 1):
            lam = jnp.where(x < k, s_x[k, of[h]].astype(F32) + lam - mul_t(xs[k, of[h]][:, :128], lam), lam)
        for k in (3, 2, 1):
            lam = jnp.where(y < k, s_y[k, of[h]].astype(F32) + lam - mul_t(ys[k, of[h]][:, :128], lam), lam)
        first = lam + seconds[h] - mul_t(pair_e[1, h], lam)
        adjoint[mine + h] = jnp.where(c == 0, first, lam).astype(BF)
        pair_l[h] = jnp.where(c == 0, lam, first).astype(BF)
    give.start()
    for i in (0, 1):
        sums[i].finish(out_down.at[:, pl.ds(512 * i, 512)])
    give.wait_recv()
    for h in (0, 1):
        adjoint[theirs + h] = got_l[h]
    for h in range(4):
        at, fk = cols[h], feat_k(h)
        grad_update = mul(fk * inverse[:, 8:9], adjoint[h])
        grad_value[:, at] += grad_update
        grad_den = jnp.sum(grad_update * recall[:, at], axis=1, keepdims=True) * inverse[:, 4 + h : 5 + h]
        line[h : h + 1] += jnp.sum(grad_den * fk, axis=0, keepdims=True)
        grad_key[:, at] += slope_of(key[:, at].astype(F32)) * (
            grad_den * offset[h : h + 1]
            - rows_by_rows((grad_update * inverse[:, 4 + h : 5 + h]).astype(BF), memory[h].astype(BF))
        )
    line[4:8] = jnp.zeros((4, 128), F32)
    lines[me] = line[...]

    def push(k, carry):
        remote(line, lines.at[me], send.at[38], recv.at[38], seq_place(lax.rem(me + k, 32))).start()
        return carry

    lax.fori_loop(1, 32, push, 0)
    for h in range(4):
        at = cols[h]
        grads[:, 1024 + 128 * h : 1152 + 128 * h] = grad_value[:, at].astype(BF)
        update = value[:, at].astype(F32) - recall[:, at]
        grad_key[:, at] += (
            inverse[:, 8:9] * slope_of(key[:, at].astype(F32)) * rows_by_rows(update.astype(BF), adjoint[h])
        )
    sums[2].one.middle()
    load_t.wait()
    product(ends, 1, grads[:, 0:512])
    z_layer.middle()
    sums[3].one.middle()
    product(ends, 3, grads[:, 1024:1536])
    for s in sums[:2]:
        s.one.drain()
        s.two.drain()
    ends[0].add_stored()
    ends[0].one.start()
    for load in (*loads[13:], load_own):
        load.wait()
    others = lines.at[pl.ds(0, 31)]
    pltpu.make_async_copy(others, others, recv.at[38]).wait()
    passed = lax.broadcasted_iota(jnp.int32, (32, 8, 128), 0) > me
    after = jnp.sum(jnp.where(passed, lines[...], 0.0), axis=0)
    later[...] = after[0:4]
    stores = [move.start(later, o_later)]
    for h in range(4):
        at = cols[h]
        late = inverse[:, 8:9] * after[h : h + 1] * slope_of(key[:, at].astype(F32))
        grads[:, 512 + 128 * h : 640 + 128 * h] = (grad_key[:, at] + late).astype(BF)
    z_layer.finish()
    stores.append(move.start(layer_out, o_layer_out))
    for half in (0, 1):
        rows = pl.ds(1024 * half, 1024)
        value = sum(rows_by_rows(grads[:, 512 * i : 512 * (i + 1)], weight_in[i, rows]) for i in range(3))
        forth[:, :, rows] = value.astype(BF).reshape(4, 96, 1024)
        for z_end in z_ends:
            (z_end.start_a, z_end.start_b)[half]()
    sums[2].second_ring()
    sums[3].second_ring()
    grads_ring(1)
    product(ends, 2, grads[:, 512:1024])
    z_ends[0].middle()
    z_ends[1].middle()
    ends[0].one.middle()
    for i in (2, 3):
        sums[i].two.middle()
        sums[i].one.drain()
    grads_ring(3)
    ends[1].one.middle()

    def put(at, result):
        own[:, at] = result

    for i in (0, 1):
        rows = parts[i]
        z_ends[i].finish(put)
        result = grad_middle[rows] + norm_back(branch[0, rows].astype(F32), own[...], gain_attn, 0, i)
        grad_tokens[z, rows] = result.astype(BF)
        z_tokens[i].start()
    total.start()
    grads_ring(2)
    for i in (2, 3):
        sums[i].finish(out_down.at[:, pl.ds(512 * i, 512)])
        sums[i].two.drain()
    stores.append(move.start(out_down, o_out_down))
    ends[0].second_ring()
    ends[3].one.middle()
    for z_token in z_tokens:
        z_token.middle()
    ends[1].second_ring()
    total.over_seq()
    ends[2].one.middle()
    ends[0].two.middle()
    ends[3].second_ring()
    ends[1].two.middle()
    total.over_tensor(logits_out)
    stores.append(move.start(logits_out, o_logits_out))
    ends[2].second_ring()
    ends[0].finish(out_output)
    stores.append(move.start(out_output, o_out_output))
    ends[3].two.middle()
    ends[1].finish(out_query)
    stores.append(move.start(out_query, o_out_query))
    ends[2].two.middle()
    ends[3].finish(out_value)
    stores.append(move.start(out_value, o_out_value))
    ends[2].finish(out_key)
    stores.append(move.start(out_key, o_out_key))
    total.finish()
    stores.append(move.start(gains, o_gains))
    for z_token in z_tokens:
        z_token.finish()
    stores.append(move.start(grad_tokens, o_grad_tokens))
    for part in (z_layer, y_ring, x_ring, *z_ends, *z_tokens, total, *ends):
        part.drain()
    swap.wait_send()
    give.wait_send()
    for store in stores:
        store.wait()
    pltpu.make_async_copy(others, others, send.at[38]).wait()


def rest(cid, *args):
    shape = jax.ShapeDtypeStruct
    low = lambda *dims: pltpu.VMEM(dims, BF)
    full = lambda *dims: pltpu.VMEM(dims, F32)
    weight_grad = shape((64, 512), F32)
    return pl.pallas_call(
        rest_kernel,
        out_shape=(
            shape((4, 96, 2048), BF),
            shape((4, 96, 2048), BF),
            shape((4, 128), F32),
            shape((64, 2048), F32),
            weight_grad,
            weight_grad,
            weight_grad,
            weight_grad,
            shape((4, 8, 128), F32),
            shape((8, 128), F32),
        ),
        in_specs=[VMEM] * 6 + [SMEM] + [VMEM] * 4 + [ANYWHERE] * 18,
        out_specs=(ANYWHERE,) * 10,
        scratch_shapes=[
            low(4, 96, 2048),
            low(4, 96, 2048),
            full(4, 128),
            full(64, 2048),
            full(64, 512),
            full(64, 512),
            full(64, 512),
            full(64, 512),
            full(4, 8, 128),
            full(8, 128),
            full(4, 128),
            low(4, 96, 2048),
            full(96, 2048),
            low(384, 1536),
            low(16, 2, 64, 384),
            low(384, 2048),
            low(384, 512),
            low(384, 512),
            low(384, 512),
            low(4, 384, 384),
            full(384, 512),
            full(384, 512),
            low(384, 512),
            low(2048, 512),
            low(3, 2048, 512),
            low(4, 16, 64, 512),
            low(4, 16, 64, 512),
            low(5, 4, 256, 512),
            low(4, 6, 256, 256),
            low(4, 4, 64, 512),
            low(4, 6, 64, 256),
            low(4, 6, 256, 256),
            low(4, 6, 64, 256),
            low(4, 96, 2048),
            low(2, 6, 48, 1024),
            full(48, 2048),
            full(384, 128),
            full(384, 512),
            full(384, 512),
            full(384, 512),
            full(384, 512),
            full(384, 512),
            low(4, 128, 128),
            low(2, 128, 128),
            low(4, 256, 128),
            low(4, 256, 128),
            low(2, 128, 128),
            low(2, 128, 128),
            low(4, 128, 128),
            full(8, 128),
            full(32, 8, 128),
            full(4, 8, 128),
            full(8, 128),
            full(4, 8, 128),
            full(16, 128),
            full(32, 16, 128),
            pltpu.SemaphoreType.DMA((28,)),
            pltpu.SemaphoreType.DMA((180,)),
            pltpu.SemaphoreType.DMA((180,)),
        ],
        name="rest",
        compiler_params=params(cid, 63),
    )(*args)


def last_kernel(*refs):
    ins, outs = refs[:14], refs[14:29]
    narrow, wide, rows, gate, up, sems, *held = refs[29:]
    move = Moves(sems)
    grad_tokens, mlp_grads, grad_gate, gains, *same = ins
    o_tokens, o_gate, o_up, o_attn, o_mlp, *o_same = outs
    fetch = [move.start(grad_tokens.at[q], narrow.at[q]) for q in range(4)]
    fetch_gate = move.start(grad_gate, gate)
    fetch_same = [move.start(src, dst) for src, dst in zip((gains, *same), held)]
    fetch_rows = move.start(mlp_grads, rows)
    copies = []
    for q in range(4):
        fetch[q].wait()
        wide[q] = narrow[q].astype(F32)
        copies.append(move.start(wide.at[q], o_tokens.at[q]))
    fetch_gate.wait()
    for copy in fetch_same:
        copy.wait()
    copies.append(move.start(held[0].at[pl.ds(0, 2)], o_attn))
    copies.append(move.start(held[0].at[pl.ds(2, 2)], o_mlp))
    copies += [move.start(src, dst) for src, dst in zip(held[1:], o_same)]
    copies.append(move.start(gate, o_gate))
    fetch_rows.wait()
    up[...] = rows[...].astype(F32)
    copies.append(move.start(up, o_up))
    for copy in copies:
        copy.wait()


def last(grad_tokens, mlp_grads, grad_gate, gains, *same):
    shape = jax.ShapeDtypeStruct
    wide = shape(mlp_grads.shape, F32)
    gain = shape((2, 8, 128), F32)
    outs = (shape(grad_tokens.shape, F32), wide, wide, gain, gain, *(shape(a.shape, a.dtype) for a in same))
    return pl.pallas_call(
        last_kernel,
        out_shape=outs,
        in_specs=[ANYWHERE] * 14,
        out_specs=(ANYWHERE,) * len(outs),
        scratch_shapes=[
            pltpu.VMEM(grad_tokens.shape, BF),
            pltpu.VMEM(grad_tokens.shape, F32),
            pltpu.VMEM(mlp_grads.shape, BF),
            pltpu.VMEM(wide.shape, F32),
            pltpu.VMEM(wide.shape, F32),
            pltpu.SemaphoreType.DMA((36,)),
            *(pltpu.VMEM(a.shape, a.dtype) for a in (gains, *same)),
        ],
        name="last",
        compiler_params=pltpu.CompilerParams(vmem_limit_bytes=63 << 20),
    )(grad_tokens, mlp_grads, grad_gate, gains, *same)


def on_device(
    tokens,
    cotangent,
    w_query,
    w_key,
    w_value,
    w_output,
    w_gate,
    w_up,
    w_down,
    gain_attn,
    gain_mlp,
    gate_logit,
    valid_count,
):
    valid = valid_count[None]
    rows = (16, 2, 64, 512)
    (
        normed_t, grad_out_t, query, key, value, probs, local_out, retrieved, mix, hidden, mlp_grads,
        recall, inverse, forth, grad_out_own, offset, normal_next, memory_prev, memory_next, ys, xs, pair_e, middle,
        grad_two, grad_gate,
    ) = front(
        0, gain_attn[None], gain_mlp[None], valid, gate_logit, tokens, cotangent,
        *(w.reshape(rows) for w in (w_query, w_key, w_value, w_output)), w_down, w_gate, w_up,
    )
    mlp_grads = lax.psum_scatter(mlp_grads.reshape(1024, -1), SEQ[:2], scatter_dimension=0, tiled=True)
    (
        layer_out, grad_tokens, later_offset, grad_down, grad_query, grad_key, grad_value, grad_output, gains, logit_grad,
    ) = rest(
        1, grad_two, middle, gain_attn[None], gain_mlp[None], grad_out_own, offset, gate_logit, memory_prev, ys, xs, pair_e,
        grad_out_t, hidden, query, key, value, probs, local_out, retrieved, mix, normed_t, recall, inverse,
        forth, w_query, w_key, w_value, w_output, tokens,
    )
    (
        grad_tokens, grad_gate, grad_up, gain_attn_grad, gain_mlp_grad, layer_out, grad_query, grad_key, grad_value,
        grad_output, grad_down, logit_grad, memory_next, normal_next, later_offset,
    ) = last(
        grad_tokens, mlp_grads, grad_gate, gains, layer_out, grad_query, grad_key, grad_value, grad_output, grad_down,
        logit_grad, memory_next, normal_next, later_offset,
    )
    return (
        layer_out.reshape(tokens.shape),
        grad_tokens.reshape(tokens.shape),
        grad_query,
        grad_key,
        grad_value,
        grad_output,
        grad_gate,
        grad_up,
        grad_down,
        gain_attn_grad.reshape(-1),
        gain_mlp_grad.reshape(-1),
        logit_grad[0, :4],
        memory_next[None],
        normal_next[None],
        later_offset[None],
    )


def solution(mesh):
    torus = Mesh(
        mesh.devices.reshape(4, 4, 2, mesh.shape["tensor"]), ("seq_0", "seq_1", "seq_2", "tensor")
    )
    weight = P(None, "tensor")
    grad = P(SEQ, "tensor")
    return jax.shard_map(
        on_device,
        mesh=torus,
        in_specs=(P(SEQ, None), P(SEQ, None)) + (weight,) * 7 + (P(), P(), P("tensor"), P()),
        out_specs=(P(SEQ, None), P(SEQ, None))
        + (grad,) * 7
        + (P(), P(), P("tensor"), P(SEQ, "tensor", None, None), P(SEQ, "tensor", None), P(SEQ, "tensor", None)),
        check_vma=False,
    )
```

```python
import functools

import jax
import jax.numpy as jnp
from jax import lax
from jax.experimental import pallas as pl
from jax.experimental.pallas import tpu as pltpu
from jax.sharding import Mesh
from jax.sharding import PartitionSpec as P

SEQ = ("seq_0", "seq_1", "seq_2")
MESH_ID = pl.DeviceIdType.MESH
VMEM = pl.BlockSpec(memory_space=pltpu.VMEM)
BF = jnp.bfloat16
F32 = jnp.float32

epsilon = 1e-06


def remote(src, dst, send, recv, device):
    return pltpu.make_async_remote_copy(
        src_ref=src, dst_ref=dst, send_sem=send, recv_sem=recv, device_id=device, device_id_type=MESH_ID
    )


def meet(devices):
    barrier = pltpu.get_barrier_semaphore()
    for device in devices:
        pl.semaphore_signal(barrier, inc=1, device_id=device, device_id_type=MESH_ID)
    pl.semaphore_wait(barrier, len(devices))


def params(collective_id, mib):
    return pltpu.CompilerParams(
        collective_id=collective_id, has_side_effects=True, vmem_limit_bytes=mib << 20
    )


def seq_place(index):
    return {"seq_0": index // 8, "seq_1": lax.rem(index // 2, 4), "seq_2": lax.rem(index, 2)}


def seq_index():
    return lax.axis_index("seq_0") * 8 + lax.axis_index("seq_1") * 2 + lax.axis_index("seq_2")


def mul(a, b):
    return jnp.dot(a.astype(BF), b.astype(BF), preferred_element_type=F32)


def mul_t(a, b):
    return lax.dot_general(a.astype(BF), b.astype(BF), (((0,), (0,)), ((), ())), preferred_element_type=F32)


def ring_places():
    x, y, c = (lax.axis_index(a) for a in SEQ)
    return x, y, c


def rows_by_rows(a, b):
    return lax.dot_general(a, b, (((1,), (1,)), ((), ())), preferred_element_type=F32)


class RingSum:
    def __init__(self, src, bufs, send, recv, base, axis, rows=None):
        self.src, self.bufs, self.me = src, bufs, lax.axis_index(axis)
        rows = pl.ds(0, src.shape[1]) if rows is None else rows
        self.rows = rows
        half = src.shape[2] // 2
        self.a, self.b = pl.ds(0, half), pl.ds(half, half)
        self.right, self.left = lax.rem(self.me + 1, 4), lax.rem(self.me + 3, 4)
        far = lax.rem(self.me + 2, 4)
        to_right, to_left = {axis: self.right}, {axis: self.left}

        def copy(piece, landing, slot, device):
            return remote(piece, bufs.at[landing], send.at[base + slot], recv.at[base + slot], device)

        self.c0 = copy(src.at[far, rows, self.a], 0, 0, to_right)
        self.c1 = copy(src.at[far, rows, self.b], 1, 1, to_left)
        self.c2 = copy(src.at[self.right, rows, self.b], 2, 2, to_right)
        self.c3 = copy(src.at[self.left, rows, self.a], 3, 3, to_left)
        self.c4 = copy(bufs.at[0], 4, 4, to_right)
        self.c5 = copy(bufs.at[1], 5, 5, to_left)

    def start_a(self):
        self.c0.start()
        self.c3.start()

    def start_b(self):
        self.c1.start()
        self.c2.start()

    def start(self):
        self.c0.start()
        self.c1.start()
        self.c3.start()
        self.c2.start()

    def middle(self):
        src, bufs = self.src, self.bufs
        self.c0.wait_recv()
        bufs[0] = (bufs[0].astype(F32) + src[self.right, self.rows, self.a].astype(F32)).astype(BF)
        self.c4.start()
        self.c1.wait_recv()
        bufs[1] = (bufs[1].astype(F32) + src[self.left, self.rows, self.b].astype(F32)).astype(BF)
        self.c5.start()

    def finish(self, put):
        src, bufs = self.src, self.bufs
        self.c3.wait_recv()
        self.c4.wait_recv()
        put(self.a, src[self.me, self.rows, self.a].astype(F32) + bufs[4].astype(F32) + bufs[3].astype(F32))
        self.c2.wait_recv()
        self.c5.wait_recv()
        put(self.b, src[self.me, self.rows, self.b].astype(F32) + bufs[5].astype(F32) + bufs[2].astype(F32))

    def drain(self):
        for copy in (self.c0, self.c1, self.c2, self.c3, self.c4, self.c5):
            copy.wait_send()


class RingGather:
    def __init__(self, buf, send, recv, base, axis, rows=None):
        self.me = lax.axis_index(axis)
        half = buf.shape[1 if rows is None else 2] // 2
        right, left = lax.rem(self.me + 1, 4), lax.rem(self.me + 3, 4)
        to_right, to_left = {axis: right}, {axis: left}

        def copy(q, h, slot, device):
            part = pl.ds(half * h, half)
            piece = buf.at[q, part] if rows is None else buf.at[q, rows, part]
            return remote(piece, piece, send.at[base + slot], recv.at[base + slot], device)

        self.r0, self.l1 = copy(self.me, 0, 0, to_right), copy(self.me, 1, 1, to_left)
        self.r1, self.l0 = copy(self.me, 1, 2, to_right), copy(self.me, 0, 3, to_left)
        self.f0, self.f1 = copy(left, 0, 4, to_right), copy(right, 1, 5, to_left)

    def start(self):
        for copy in (self.r0, self.l1, self.r1, self.l0):
            copy.start()

    def middle(self):
        self.r0.wait_recv()
        self.f0.start()
        self.l1.wait_recv()
        self.f1.start()

    def finish(self):
        for copy in (self.r1, self.l0, self.f0, self.f1):
            copy.wait_recv()

    def drain(self):
        for copy in (self.r0, self.l1, self.r1, self.l0, self.f0, self.f1):
            copy.wait_send()


class SeqSum:
    def __init__(self, product, got, first, first_bufs, second, second_bufs, send, recv, base, x_first):
        self.got, self.first, self.second, self.x_first = got, first, second, x_first
        core = lax.axis_index("seq_2")
        self.swap = remote(product, got, send.at[base], recv.at[base], {"seq_2": 1 - core})
        axes = ("seq_0", "seq_1") if x_first else ("seq_1", "seq_0")
        self.one = RingSum(first, first_bufs, send, recv, base + 1, axes[0])
        self.two = RingSum(second, second_bufs, send, recv, base + 7, axes[1])

    def start(self):
        self.swap.start()

    def store(self, own):
        for x in range(4):
            for y in range(4):
                at = 4 * x + y
                q, r = (x, y) if self.x_first else (y, x)
                self.first[q, pl.ds(64 * r, 64)] = own[64 * at : 64 * (at + 1)].astype(BF)

    def add(self, own):
        self.swap.wait_recv()
        self.store(own + flat(self.got[...]).astype(F32))

    def add_stored(self):
        self.swap.wait_recv()
        for x in range(4):
            for y in range(4):
                q, r = (x, y) if self.x_first else (y, x)
                rows = pl.ds(64 * r, 64)
                self.first[q, rows] = (self.first[q, rows].astype(F32) + self.got[4 * x + y].astype(F32)).astype(BF)

    def second_ring(self):
        def put(cols, value):
            for r in range(4):
                self.second[r, :, cols] = value[64 * r : 64 * (r + 1)].astype(BF)

        self.one.finish(put)
        self.two.start()

    def finish(self, out):
        def put(cols, value):
            out[:, cols] = value

        self.two.finish(put)

    def drain(self):
        self.swap.wait_send()
        self.one.drain()
        self.two.drain()


def greet_all():
    barrier = pltpu.get_barrier_semaphore()
    me, z = seq_index(), lax.axis_index("tensor")

    def greet_seq(k, carry):
        pl.semaphore_signal(barrier, inc=1, device_id=seq_place(lax.rem(me + k, 32)), device_id_type=MESH_ID)
        return carry

    lax.fori_loop(1, 32, greet_seq, 0)
    for k in (1, 2, 3):
        pl.semaphore_signal(barrier, inc=1, device_id={"tensor": lax.rem(z + k, 4)}, device_id_type=MESH_ID)


def all_greeted():
    pl.semaphore_wait(pltpu.get_barrier_semaphore(), 34)


class TotalOfAll:
    def __init__(self, mine, extra, by_z, line, by_seq, total, send, recv, base):
        self.mine, self.extra, self.by_z, self.line, self.by_seq, self.total = mine, extra, by_z, line, by_seq, total
        self.z, self.me = lax.axis_index("tensor"), seq_index()
        self.send, self.recv, self.base = send, recv, base
        peers = [lax.rem(self.z + k, 4) for k in (1, 2, 3)]
        self.split = [
            remote(mine.at[p], by_z.at[self.z], send.at[base + k], recv.at[base + k], {"tensor": p})
            for k, p in enumerate(peers)
        ]
        self.join = [
            remote(total.at[self.z], total.at[self.z], send.at[base + 3 + k], recv.at[base + 3 + k], {"tensor": p})
            for k, p in enumerate(peers)
        ]

    def start(self):
        for copy in self.split:
            copy.start()

    def over_seq(self):
        self.by_z[self.z] = self.mine[self.z]
        for copy in self.split:
            copy.wait_recv()
        self.line[0:8] = (self.by_z[0] + self.by_z[1]) + (self.by_z[2] + self.by_z[3])
        self.line[8:16] = self.extra[...]
        self.by_seq[self.me] = self.line[...]

        def push(k, carry):
            device = seq_place(lax.rem(self.me + k, 32))
            remote(self.line, self.by_seq.at[self.me], self.send.at[self.base + 6], self.recv.at[self.base + 6], device).start()
            return carry

        lax.fori_loop(1, 32, push, 0)

    def over_tensor(self, extra_out):
        others = self.by_seq.at[pl.ds(0, 31)]
        pltpu.make_async_copy(others, others, self.recv.at[self.base + 6]).wait()
        summed = jnp.sum(self.by_seq[...], axis=0)
        self.total[self.z] = summed[0:8]
        extra_out[...] = summed[8:16]
        for copy in self.join:
            copy.start()

    def finish(self):
        for copy in self.join:
            copy.wait_recv()

    def drain(self):
        for copy in (*self.split, *self.join):
            copy.wait_send()
        others = self.by_seq.at[pl.ds(0, 31)]
        pltpu.make_async_copy(others, others, self.send.at[self.base + 6]).wait()


def feature_of(v):
    return jnp.where(v > 0, v + 1.0, jnp.exp(jnp.minimum(v, 0.0)))


def slope_of(v):
    return jnp.where(v > 0, 1.0, jnp.exp(jnp.minimum(v, 0.0)))


ANYWHERE = pl.BlockSpec(memory_space=pl.ANY)


def keep_of(valid):
    length = jnp.where(seq_index() == 31, valid[...], 384)
    return (lax.broadcasted_iota(jnp.int32, (384, 1), 0) < length).astype(F32)


SMEM = pl.BlockSpec(memory_space=pltpu.SMEM)


def gate_rows(gate, logit):
    for h in range(4):
        gate[h : h + 1] = jax.nn.sigmoid(jnp.full((1, 128), logit[h], F32))


def flat(weight):
    return weight.reshape(-1, 512)


def core_rows(turned, core):
    return turned[pl.ds(0, 16), core].reshape(1024, 384)


class Moves:
    def __init__(self, sems):
        self.sems, self.count = sems, 0

    def start(self, src, dst):
        copy = pltpu.make_async_copy(src, dst, self.sems.at[self.count])
        self.count += 1
        copy.start()
        return copy


def front_kernel(
    gain_attn,
    gain_mlp,
    valid,
    gate_logit,
    i_tokens,
    cotangent,
    w_query,
    w_key,
    w_value,
    w_output,
    w_down,
    w_gate,
    w_up,
    o_normed_t,
    o_grad_out_t,
    o_query,
    o_key,
    o_value,
    o_probs,
    o_local_out,
    o_retrieved,
    o_mix,
    o_hidden,
    o_grads,
    o_recall,
    o_inverse,
    grad_out_own,
    offset,
    normal_next,
    memory_prev,
    memory_next,
    ys,
    xs,
    pair_e,
    middle,
    grad_two,
    out_gate,
    keep,
    gate,
    weights,
    weight_o,
    weight_d,
    weight_g,
    hidden,
    normed_two,
    normed,
    turned,
    grad_out,
    got_rows,
    first_rows,
    first_bufs,
    second_rows,
    second_bufs,
    pair_rows,
    inverse,
    grad_hidden,
    query,
    key,
    value,
    probs,
    local_out,
    retrieved,
    mix,
    line,
    lines,
    eb,
    source,
    got,
    pair_m,
    got_m,
    part,
    part_bufs,
    moves,
    send,
    recv,
):
    move = Moves(moves)
    tokens = hidden
    load_tokens = move.start(i_tokens, tokens)
    loads = [move.start(w, weights.at[i]) for i, w in enumerate((w_key, w_query, w_value))]
    load_cotangent = move.start(cotangent, grad_out)
    load_o = move.start(w_output, weight_o)
    load_d = [move.start(w_down.at[pl.ds(512 * i, 512)], weight_d.at[pl.ds(512 * i, 512)]) for i in range(4)]
    greet_all()
    keep[...] = keep_of(valid)
    gate_rows(gate, gate_logit)
    x, y, c = ring_places()
    z, me = lax.axis_index("tensor"), seq_index()
    partner = {"seq_2": 1 - c}
    mine, theirs = 2 * c, 2 * (1 - c)
    slots = [
        held.at[pl.ds(0, 16), j] for held in (weight_o, weights.at[0], weights.at[1], weights.at[2]) for j in (0, 1)
    ]
    sums = [
        SeqSum(
            slots[i], got_rows.at[i], first_rows.at[i], first_bufs.at[i], second_rows.at[i], second_bufs.at[i],
            send, recv, 27 + 13 * i, i % 2 == 0,
        )
        for i in range(2)
    ]
    swaps = [remote(slots[2 + i], got_rows.at[2 + i], send.at[53 + i], recv.at[53 + i], partner) for i in range(6)]
    parts = [pl.ds(0, 48), pl.ds(48, 48)]
    z_sums = [RingSum(part, part_bufs.at[i], send, recv, 79 + 6 * i, "tensor", parts[i]) for i in (0, 1)]
    z_gathers = [RingGather(normed_two, send, recv, 91 + 6 * i, "tensor", parts[i]) for i in (0, 1)]
    z_backs = [RingSum(part, part_bufs.at[i], send, recv, 6 * i, "tensor", parts[i]) for i in (0, 1)]
    y_ring = RingGather(ys, send, recv, 12, "seq_1")
    x_ring = RingGather(xs, send, recv, 18, "seq_0")
    swap = remote(eb.at[pl.ds(theirs, 2)], got, send.at[24], recv.at[24], partner)
    give = remote(pair_m, got_m, send.at[25], recv.at[25], partner)
    cols = [slice(128 * h, 128 * (h + 1)) for h in range(4)]
    stores = []

    load_tokens.wait()
    for q in range(4):
        rows = pl.ds(96 * q, 96)
        stream = tokens[rows].astype(F32)
        inv = lax.rsqrt(jnp.mean(stream * stream, axis=1, keepdims=True) + epsilon)
        normed[rows] = (stream * inv * gain_attn[...]).astype(BF)
    loads[0].wait()
    key[...] = jnp.dot(normed[...], flat(weights[0]), preferred_element_type=F32).astype(BF)
    feat_q = lambda h: feature_of(query[:, cols[h]].astype(F32))
    feat_k = lambda h: feature_of(key[:, cols[h]].astype(F32))
    line[...] = jnp.zeros_like(line)
    for h in range(4):
        line[h : h + 1] = jnp.sum(feat_k(h) * keep[...], axis=0, keepdims=True)
    lines[me] = line[...]
    all_greeted()

    def push(k, carry):
        remote(line, lines.at[me], send.at[26], recv.at[26], seq_place(lax.rem(me + k, 32))).start()
        return carry

    lax.fori_loop(1, 32, push, 0)
    stores.append(move.start(key, o_key))
    loads[1].wait()
    query[...] = jnp.dot(normed[...], flat(weights[1]), preferred_element_type=F32).astype(BF)
    stores.append(move.start(query, o_query))
    loads[2].wait()
    value[...] = jnp.dot(normed[...], flat(weights[2]), preferred_element_type=F32).astype(BF)
    stores.append(move.start(value, o_value))
    load_g = move.start(w_gate, weight_g)
    at_row = lax.broadcasted_iota(jnp.int32, (384, 384), 0)
    at_col = lax.broadcasted_iota(jnp.int32, (384, 384), 1)
    valid = jnp.sum(keep[...], axis=0, keepdims=True)
    allowed = (at_row >= at_col) & (at_col.astype(F32) < valid)

    def attend(h):
        at = cols[h]
        scores = rows_by_rows(query[:, at], key[:, at]) * 128 ** (-0.5)
        masked = jnp.where(allowed, scores, -1e30)
        raised = jnp.exp(masked - jnp.max(masked, axis=1, keepdims=True))
        low = (raised * (1.0 / jnp.sum(raised, axis=1, keepdims=True))).astype(BF)
        probs[h] = low
        local_out[:, at] = jnp.dot(low, value[:, at], preferred_element_type=F32)
        total = mul_t(feat_k(h) * keep[...], value[:, at])
        source[h] = total
        eb[h, :, 128:256] = total.astype(BF)

    for h in range(4):
        attend(h)
    stores.append(move.start(probs, o_probs))
    stores.append(move.start(local_out, o_local_out))
    others = lines.at[pl.ds(0, 31)]
    pltpu.make_async_copy(others, others, recv.at[26]).wait()
    passed = lax.broadcasted_iota(jnp.int32, (32, 8, 128), 0) < me
    before = jnp.sum(jnp.where(passed, lines[...], 0.0), axis=0)
    normal_next[...] = (before + line[...])[0:4]
    offset[...] = before + 384.0
    for h in range(4):
        fk = feat_k(h)
        kept = fk * keep[...] * (1.0 / jnp.sum(fk * offset[h : h + 1], axis=1, keepdims=True))
        eb[h, :, 0:128] = mul_t(kept, fk).astype(BF)
    swap.start()
    load_cotangent.wait()
    grad_out[...] = grad_out[...] * keep[...].astype(BF)
    grad_out_own[...] = grad_out[pl.ds(pl.multiple_of(96 * z, 96), 96)]
    swap.wait_recv()
    of = [pl.ds(0, 128), pl.ds(128, 128)]
    firsts = []
    for h in (0, 1):
        here, there = eb[mine + h].astype(F32), got[h].astype(F32)
        first, second = jnp.where(c == 0, here, there), jnp.where(c == 0, there, here)
        firsts.append(first)
        pair_e[0, h] = first[:, :128].astype(BF)
        pair_e[1, h] = second[:, :128].astype(BF)
        ys[y, of[h]] = (first + second - mul(second[:, :128], first)).astype(BF)
    y_ring.start()

    def hidden_part(i):
        load_d[i].wait()
        rows = pl.ds(512 * i, 512)
        product = jnp.dot(grad_out[:, 512 * i : 512 * (i + 1)], weight_d[rows], preferred_element_type=F32)
        if i == 0:
            grad_hidden[...] = product
        else:
            grad_hidden[...] += product

    hidden_part(0)
    y_ring.middle()
    hidden_part(1)
    y_ring.finish()
    starts = []
    for h in (0, 1):
        so_far = ys[0, of[h]].astype(F32)
        start = jnp.where(y > 0, so_far, 0.0)
        for k in (1, 2, 3):
            step = ys[k, of[h]].astype(F32)
            so_far = so_far + step - mul(step[:, :128], so_far)
            if k < 3:
                start = jnp.where(y > k, so_far, start)
        xs[x, of[h]] = so_far.astype(BF)
        starts.append(start)
    x_ring.start()
    hidden_part(2)
    x_ring.middle()
    hidden_part(3)
    load_u = move.start(w_up, weight_d)
    load_o.wait()
    x_ring.finish()
    for h in (0, 1):
        m = jnp.where(x > 0, xs[0, of[h]][:, 128:].astype(F32), 0.0)
        for k in (1, 2):
            step = xs[k, of[h]].astype(F32)
            m = jnp.where(x > k, m + step[:, 128:] - mul(step[:, :128], m), m)
        m = m + starts[h][:, 128:] - mul(starts[h][:, :128], m)
        second = m + firsts[h][:, 128:] - mul(firsts[h][:, :128], m)
        memory_prev[mine + h] = jnp.where(c == 0, m, second)
        pair_m[h] = jnp.where(c == 0, second, m)
    give.start()
    give.wait_recv()
    inverse[...] = jnp.zeros_like(inverse)
    inverse[:, 8:9] = keep[...]
    for h in (0, 1):
        memory_prev[theirs + h] = got_m[h]
    for h in range(4):
        at, fq, sig = cols[h], feat_q(h), gate[h : h + 1]
        inv_q = 1.0 / jnp.sum(fq * offset[h : h + 1], axis=1, keepdims=True)
        inverse[:, h : h + 1] = inv_q
        found = mul(fq, memory_prev[h]) * inv_q
        retrieved[:, at] = found
        mix[:, at] = (sig * found + (1.0 - sig) * local_out[:, at]).astype(BF)
    for half in (0, 1):
        rows = pl.ds(1024 * half, 1024)
        part[:, :, rows] = rows_by_rows(mix[...], flat(weight_o[8 * half : 8 * half + 8])).astype(BF).reshape(4, 96, 1024)
        for z_sum in z_sums:
            (z_sum.start_a, z_sum.start_b)[half]()
    store_found = move.start(retrieved, o_retrieved)
    stores.append(move.start(mix, o_mix))
    for h in range(4):
        m = memory_prev[h]
        memory_next[h] = m + source[h] - mul(eb[h][:, :128], m)
    turned[...] = normed[...].T.reshape(16, 2, 64, 384)
    store_t = move.start(turned, o_normed_t)
    z_sums[0].middle()
    z_sums[1].middle()
    store_found.wait()
    recall = retrieved
    for h in range(4):
        fk, off = feat_k(h), offset[h : h + 1]
        inv_k = 1.0 / jnp.sum(fk * off, axis=1, keepdims=True)
        inverse[:, 4 + h : 5 + h] = inv_k
        recall[:, cols[h]] = mul(fk, memory_prev[h]) * inv_k
    stores.append(move.start(recall, o_recall))
    stores.append(move.start(inverse, o_inverse))

    def second_norm(i):
        own_tokens = tokens[pl.ds(pl.multiple_of(96 * z + 48 * i, 16), 48)].astype(F32)

        def put(at, total):
            lanes = slice(0, 1024) if at is z_sums[i].a else slice(1024, 2048)
            middle[parts[i], at] = own_tokens[:, lanes] + total

        z_sums[i].finish(put)
        z_sums[i].drain()
        stream = middle[parts[i]]
        inv = lax.rsqrt(jnp.mean(stream * stream, axis=1, keepdims=True) + epsilon)
        normed_two[z, parts[i]] = (stream * inv * gain_mlp[...]).astype(BF)
        z_gathers[i].start()

    second_norm(0)
    second_norm(1)
    z_gathers[0].middle()
    z_gathers[1].middle()
    store_t.wait()
    turned[...] = grad_out[...].T.reshape(16, 2, 64, 384)
    store_t = move.start(turned, o_grad_out_t)
    for store in stores:
        store.wait()
    store_t.wait()
    load_g.wait()
    load_u.wait()
    for z_gather in z_gathers:
        z_gather.finish()
    for z_gather in z_gathers:
        z_gather.drain()
    turned[...] = normed_two[...].reshape(384, 2048).T.reshape(16, 2, 64, 384)

    def tile(i):
        for half in (2 * i, 2 * i + 1):
            narrow_tile(half)

    def narrow_tile(i):
        lanes = slice(256 * i, 256 * (i + 1))
        rows = normed_two[...].reshape(384, 2048)
        gate_pre = jnp.dot(rows, weight_g[:, lanes], preferred_element_type=F32)
        up_pre = jnp.dot(rows, weight_d[:, lanes], preferred_element_type=F32)
        back_hidden = grad_hidden[:, lanes]
        sig = jax.nn.sigmoid(gate_pre)
        swish = gate_pre * sig
        hidden[:, lanes] = (swish * up_pre).astype(BF)
        grad_out[:, lanes] = (back_hidden * swish).astype(BF)
        normed[:, lanes] = (back_hidden * up_pre * sig * (1.0 + gate_pre * (1.0 - sig))).astype(BF)

    def return_part(i):
        rows = pl.ds(512 * i, 512)
        value = rows_by_rows(normed[...], weight_g[rows]) + rows_by_rows(grad_out[...], weight_d[rows])
        part[:, :, rows] = value.astype(BF).reshape(4, 96, 512)

    leaving = []

    def gradient(i, core):
        side = (normed, grad_out)[i // 4]
        lanes = slice(512 * (i % 4), 512 * (i % 4 + 1))
        return jnp.dot(core_rows(turned, core), side[:, lanes], preferred_element_type=F32)

    def give_half(i):
        slots[i][...] = gradient(i, 1 - c).astype(BF).reshape(16, 64, 512)
        if i < 2:
            sums[i].start()
        else:
            swaps[i - 2].start()

    def gate_ring(i):
        sums[i].add(gradient(i, c))
        sums[i].one.start()

    def pair_sum(i):
        own_rows = gradient(2 + i, c)
        swaps[i].wait_recv()
        if i >= 1:
            leaving[i - 1].wait()
        pair_rows[...] = (own_rows + flat(got_rows[2 + i]).astype(F32)).astype(BF).reshape(16, 64, 512)
        leaving.append(move.start(pair_rows, o_grads.at[:, :, pl.ds(512 * i, 512)]))

    tile(0)
    give_half(0)
    tile(1)
    give_half(1)
    tile(2)
    gate_ring(0)
    tile(3)
    gate_ring(1)
    stores = [move.start(hidden, o_hidden)]
    return_part(0)
    return_part(1)
    for z_back in z_backs:
        z_back.start_a()
    return_part(2)
    return_part(3)
    for z_back in z_backs:
        z_back.start_b()
    give_half(2)
    sums[0].one.middle()
    give_half(3)
    sums[1].one.middle()
    give_half(4)
    pair_sum(0)
    give_half(5)
    pair_sum(1)
    z_backs[0].middle()
    z_backs[1].middle()
    sums[0].second_ring()
    give_half(6)
    pair_sum(2)
    sums[1].second_ring()
    give_half(7)
    pair_sum(3)
    sums[0].two.middle()
    pair_sum(4)
    sums[1].two.middle()
    pair_sum(5)
    for i in (0, 1):

        def put(at, total, i=i):
            grad_two[parts[i], at] = total

        z_backs[i].finish(put)
    for i in (0, 1):
        sums[i].finish(out_gate.at[:, pl.ds(512 * i, 512)])
    for copy in (*stores, leaving[5]):
        copy.wait()
    for swap_rows in swaps:
        swap_rows.wait_send()
    for part_sum in sums:
        part_sum.drain()
    for ring in (*z_backs, y_ring, x_ring):
        ring.drain()
    swap.wait_send()
    give.wait_send()
    pltpu.make_async_copy(others, others, send.at[26]).wait()


def front(cid, *args):
    shape = jax.ShapeDtypeStruct
    low = lambda *dims: pltpu.VMEM(dims, BF)
    full = lambda *dims: pltpu.VMEM(dims, F32)
    return pl.pallas_call(
        front_kernel,
        out_shape=(
            shape((16, 2, 64, 384), BF),
            shape((16, 2, 64, 384), BF),
            shape((384, 512), BF),
            shape((384, 512), BF),
            shape((384, 512), BF),
            shape((4, 384, 384), BF),
            shape((384, 512), F32),
            shape((384, 512), F32),
            shape((384, 512), BF),
            shape((384, 2048), BF),
            shape((16, 64, 3072), BF),
            shape((384, 512), F32),
            shape((384, 128), F32),
            shape((96, 2048), BF),
            shape((8, 128), F32),
            shape((4, 128), F32),
            shape((4, 128, 128), F32),
            shape((4, 128, 128), F32),
            shape((4, 256, 256), BF),
            shape((4, 256, 256), BF),
            shape((2, 2, 128, 128), BF),
            shape((96, 2048), F32),
            shape((96, 2048), F32),
            shape((64, 1024), F32),
        ),
        in_specs=[VMEM] * 3 + [SMEM] + [ANYWHERE] * 9,
        out_specs=(ANYWHERE,) * 13 + (VMEM,) * 11,
        scratch_shapes=[
            full(384, 1),
            full(4, 128),
            low(3, 16, 2, 64, 512),
            low(16, 2, 64, 512),
            low(2048, 2048),
            low(2048, 2048),
            low(384, 2048),
            low(4, 96, 2048),
            low(384, 2048),
            low(16, 2, 64, 384),
            low(384, 2048),
            low(8, 16, 64, 512),
            low(2, 4, 256, 512),
            low(2, 6, 256, 256),
            low(2, 4, 64, 512),
            low(2, 6, 64, 256),
            low(16, 64, 512),
            full(384, 128),
            full(384, 2048),
            low(384, 512),
            low(384, 512),
            low(384, 512),
            low(4, 384, 384),
            full(384, 512),
            full(384, 512),
            low(384, 512),
            full(8, 128),
            full(32, 8, 128),
            low(4, 128, 256),
            full(4, 128, 128),
            low(2, 128, 256),
            full(2, 128, 128),
            full(2, 128, 128),
            low(4, 96, 2048),
            low(2, 6, 48, 1024),
            pltpu.SemaphoreType.DMA((34,)),
            pltpu.SemaphoreType.DMA((107,)),
            pltpu.SemaphoreType.DMA((107,)),
        ],
        name="front",
        compiler_params=params(cid, 63),
    )(*args)


def neighbours():
    x, y, c = ring_places()
    z = lax.axis_index("tensor")
    near = [{"seq_2": 1 - c}]
    for axis, at in (("seq_0", x), ("seq_1", y), ("tensor", z)):
        near += [{axis: lax.rem(at + 1, 4)}, {axis: lax.rem(at + 3, 4)}]
    return near


def rest_kernel(
    grad_two,
    middle,
    gain_attn,
    gain_mlp,
    grad_out,
    offset,
    gate_logit,
    i_memory,
    i_ys,
    i_xs,
    i_pair_e,
    i_grad_out_t,
    i_hidden,
    i_query,
    i_key,
    i_value,
    i_probs,
    i_local_out,
    i_retrieved,
    i_mix,
    i_normed_t,
    i_recall,
    i_inverse,
    w_query,
    w_key,
    w_value,
    w_output,
    w_down,
    tokens,
    o_layer_out,
    o_grad_tokens,
    o_later,
    o_out_down,
    o_out_query,
    o_out_key,
    o_out_value,
    o_out_output,
    o_gains,
    o_logits_out,
    layer_out,
    grad_tokens,
    later,
    out_down,
    out_query,
    out_key,
    out_value,
    out_output,
    gains,
    logits_out,
    memory,
    ys,
    xs,
    pair_e,
    gate,
    branch,
    grad_middle,
    grads,
    left,
    hidden,
    query,
    key,
    value,
    probs,
    local_out,
    retrieved,
    mix,
    weight_o,
    weight_in,
    products,
    got_rows,
    first_rows,
    first_bufs,
    second_rows,
    second_bufs,
    first_bufs_2,
    second_bufs_2,
    forth,
    z_bufs,
    own,
    inverse,
    recall,
    grad_mix,
    grad_query,
    grad_key,
    grad_value,
    source,
    got,
    s_y,
    s_x,
    pair_l,
    got_l,
    adjoint,
    line,
    lines,
    mine_gains,
    logits,
    by_z,
    total_line,
    by_seq,
    moves,
    send,
    recv,
):
    x, y, c = ring_places()
    z, me = lax.axis_index("tensor"), seq_index()
    move = Moves(moves)
    pairs = (
        (i_grad_out_t, left),
        (i_hidden, hidden),
        (w_output, weight_o),
        (i_query, query),
        (i_inverse, inverse),
        (i_probs, probs),
        (i_key, key),
        (i_value, value),
        (i_mix, mix),
        (i_retrieved, retrieved),
        (i_local_out, local_out),
        (i_recall, recall),
        (i_pair_e, pair_e),
        (i_ys, ys),
        (i_xs, xs),
        (i_memory, memory),
    )
    barrier = pltpu.get_barrier_semaphore()
    for device in neighbours():
        pl.semaphore_signal(barrier, inc=1, device_id=device, device_id_type=MESH_ID)
    blocks = [weight_in.at[k, pl.ds(1024 * j, 1024)] for k in range(3) for j in (0, 1)]

    def load_down(half, q, block):
        return move.start(w_down.at[pl.ds(1024 * half, 1024), pl.ds(512 * q, 512)], blocks[block])

    loads = [move.start(src, dst) for src, dst in pairs[:2]]
    downs = [load_down(0, q, q) for q in range(4)] + [load_down(1, q, 4 + q) for q in (0, 1)]
    loads += [move.start(src, dst) for src, dst in pairs[2:]]
    gate_rows(gate, gate_logit)
    partner = {"seq_2": 1 - c}
    mine, theirs = 2 * c, 2 * (1 - c)
    parts = [pl.ds(0, 48), pl.ds(48, 48)]
    z_branches = [RingGather(branch, send, recv, 6 * i, "tensor", parts[i]) for i in (0, 1)]
    z_forths = [RingSum(forth, z_bufs.at[i], send, recv, (12, 174)[i], "tensor", parts[i]) for i in (0, 1)]
    z_layer = RingGather(layer_out, send, recv, 18, "tensor")
    y_ring = RingGather(s_y, send, recv, 24, "seq_1")
    x_ring = RingGather(s_x, send, recv, 30, "seq_0")
    swap = remote(source.at[pl.ds(theirs, 2)], got, send.at[36], recv.at[36], partner)
    give = remote(pair_l, got_l, send.at[37], recv.at[37], partner)
    z_ends = [RingSum(forth, z_bufs.at[i], send, recv, 143 + 6 * i, "tensor", parts[i]) for i in (0, 1)]
    z_tokens = [RingGather(grad_tokens, send, recv, 155 + 6 * i, "tensor", parts[i]) for i in (0, 1)]
    total = TotalOfAll(mine_gains, logits, by_z, total_line, by_seq, gains, send, recv, 167)

    def seq_sums(base, first_bufs, second_bufs, order):
        return [
            SeqSum(
                products.at[i], got_rows.at[i], first_rows.at[order[i]], first_bufs.at[i], second_rows.at[i],
                second_bufs.at[i], send, recv, base + 13 * i, i % 2 == 0,
            )
            for i in range(4)
        ]

    sums, ends = seq_sums(39, first_bufs, second_bufs, (0, 1, 2, 3)), seq_sums(91, first_bufs_2, second_bufs_2, (4, 1, 2, 3))
    cols = [slice(128 * h, 128 * (h + 1)) for h in range(4)]
    of = [pl.ds(0, 128), pl.ds(128, 128)]
    feat_q = lambda h: feature_of(query[:, cols[h]].astype(F32))
    feat_k = lambda h: feature_of(key[:, cols[h]].astype(F32))
    scale = 128 ** (-0.5)

    def half_product(right, core):
        return jnp.dot(core_rows(left, core), right, preferred_element_type=F32)

    def product(group, i, right):
        products[i] = half_product(right, 1 - c).astype(BF).reshape(16, 64, 512)
        group[i].start()

    def down(i):
        product(sums, i, hidden[:, 512 * i : 512 * (i + 1)])

    def down_add(i):
        sums[i].add(half_product(hidden[:, 512 * i : 512 * (i + 1)], c))

    def grads_ring(i):
        ends[i].add(half_product(grads[:, 512 * (i - 1) : 512 * i], c))
        ends[i].one.start()

    def norm_back(stream, grad_normed, gain, first_row, i):
        inv = lax.rsqrt(jnp.mean(stream * stream, axis=1, keepdims=True) + epsilon)
        weighted = grad_normed * gain[...]
        inner = jnp.sum(weighted * stream, axis=1, keepdims=True)
        scaled = stream * inv
        line_of = jnp.sum(grad_normed * scaled, axis=0, keepdims=True)
        for r in range(16):
            at = (first_row + r // 8, slice(r % 8, r % 8 + 1))
            piece = line_of[:, 128 * r : 128 * (r + 1)]
            mine_gains[at] = piece if i == 0 else mine_gains[at] + piece
        return inv * weighted - scaled * (inv * inv * inner * (1.0 / stream.shape[1]))

    def forward_part(half, order):
        value = sum(rows_by_rows(hidden[:, 512 * q : 512 * (q + 1)], blocks[order[q]][...]) for q in range(4))
        forth[:, :, pl.ds(1024 * half, 1024)] = value.astype(BF).reshape(4, 96, 1024)

    for i in (0, 1):
        rows = parts[i]
        result = grad_out[rows].astype(F32) + norm_back(middle[rows], grad_two[rows], gain_mlp, 2, i)
        grad_middle[rows] = result
        branch[z, rows] = result.astype(BF)
        if i == 0:
            pl.semaphore_wait(barrier, 7)
        z_branches[i].start()
    loads[0].wait()
    loads[1].wait()
    down(0)
    down(1)
    z_branches[0].middle()
    down_add(0)
    sums[0].one.start()
    z_branches[1].middle()
    down(2)
    down_add(1)
    sums[1].one.start()
    for load in downs[:4]:
        load.wait()
    forward_part(0, (0, 1, 2, 3))
    downs += [load_down(1, q, q - 2) for q in (2, 3)]
    down(3)
    down_add(2)
    sums[0].one.middle()
    down_add(3)
    for load in downs[4:]:
        load.wait()
    forward_part(1, (4, 5, 0, 1))
    late = [move.start(w, weight_in.at[i]) for i, w in enumerate((w_query, w_key, w_value))]
    for load in loads[2:5]:
        load.wait()
    for z_branch in z_branches:
        z_branch.finish()
    for z_forth in z_forths:
        z_forth.start()
    grad_mix[...] = jnp.dot(branch[...].reshape(384, 2048), weight_o[...], preferred_element_type=F32)

    def point(h):
        return gate[h : h + 1] * grad_mix[:, cols[h]] * inverse[:, h : h + 1]

    for h in range(4):
        source[h] = mul_t(feat_q(h), point(h)).astype(BF)
    swap.start()

    def attend(h):
        at = cols[h]
        grad_local = ((1.0 - gate[h : h + 1]) * grad_mix[:, at]).astype(BF)
        low = probs[h]
        p = low.astype(F32)
        grad_probs = rows_by_rows(grad_local, value[:, at])
        grad_value[:, at] = mul_t(low, grad_local)
        grad_scores = (p * (grad_probs - jnp.sum(grad_probs * p, axis=1, keepdims=True))).astype(BF)
        grad_query[:, at] = mul(grad_scores, key[:, at]) * scale
        grad_key[:, at] = mul_t(grad_scores, query[:, at]) * scale

    for load in loads[5:8]:
        load.wait()
    attend(0)
    sums[1].one.middle()
    swap.wait_recv()
    for load in loads[12:16]:
        load.wait()
    seconds = []
    for h in (0, 1):
        here, there = source[mine + h].astype(F32), got[h].astype(F32)
        first, second = jnp.where(c == 0, here, there), jnp.where(c == 0, there, here)
        seconds.append(second)
        s_y[y, of[h]] = (first + second - mul_t(pair_e[0, h], second)).astype(BF)
    y_ring.start()
    attend(1)
    y_ring.middle()
    sums[0].second_ring()
    attend(2)
    for z_forth in z_forths:
        z_forth.middle()
    sums[1].second_ring()
    for s in sums:
        s.swap.wait_send()
    left[...] = branch[...].reshape(384, 2048).T.reshape(16, 2, 64, 384)
    for z_branch in z_branches:
        z_branch.drain()
    load_own = move.start(tokens.at[pl.ds(pl.multiple_of(96 * z, 96), 96)], branch.at[0])
    y_ring.finish()
    for h in (0, 1):
        so_far = s_y[3, of[h]].astype(F32)
        for k in (2, 1, 0):
            so_far = s_y[k, of[h]].astype(F32) + so_far - mul_t(ys[k, of[h]][:, :128], so_far)
        s_x[x, of[h]] = so_far.astype(BF)
    x_ring.start()
    for load in loads[8:12]:
        load.wait()
    product(ends, 0, mix[...])
    ends[0].store(half_product(mix[...], c))
    x_ring.middle()
    load_t = move.start(i_normed_t, left)
    attend(3)
    logit_rows = []
    for h in range(4):
        at, gate_h, g = cols[h], gate[h : h + 1], grad_mix[:, cols[h]]
        ret = retrieved[:, at]
        moved = jnp.sum(g * (ret - local_out[:, at]), axis=0, keepdims=True) * gate_h * (1.0 - gate_h)
        logit_rows.append(jnp.sum(moved, axis=1, keepdims=True))
        grad_den = -jnp.sum(gate_h * g * ret, axis=1, keepdims=True) * inverse[:, h : h + 1]
        q = query[:, at].astype(F32)
        grad_feat = rows_by_rows(point(h).astype(BF), memory[h].astype(BF)) + grad_den * offset[h : h + 1]
        grads[:, at] = (grad_query[:, at] + grad_feat * slope_of(q)).astype(BF)
        line[h : h + 1] = jnp.sum(grad_den * feature_of(q), axis=0, keepdims=True)
    lane = lax.broadcasted_iota(jnp.int32, (8, 128), 1)
    row = lax.broadcasted_iota(jnp.int32, (8, 128), 0)
    spot = jnp.zeros((8, 128), F32)
    for h in range(4):
        spot = jnp.where((lane == h) & (row == 0), logit_rows[h], spot)
    logits[...] = spot
    for i in (0, 1):

        def put_layer(at, result, i=i):
            lanes = slice(0, 1024) if at is z_forths[i].a else slice(1024, 2048)
            layer_out[z, parts[i], at] = (middle[parts[i], lanes] + result).astype(BF)

        z_forths[i].finish(put_layer)
        z_forths[i].drain()
    z_layer.start()
    sums[0].two.middle()
    sums[1].two.middle()
    x_ring.finish()
    sums[2].one.start()
    sums[3].one.start()
    for h in (0, 1):
        lam = jnp.where(x < 3, s_x[3, of[h]].astype(F32), 0.0)
        for k in (2, 1):
            lam = jnp.where(x < k, s_x[k, of[h]].astype(F32) + lam - mul_t(xs[k, of[h]][:, :128], lam), lam)
        for k in (3, 2, 1):
            lam = jnp.where(y < k, s_y[k, of[h]].astype(F32) + lam - mul_t(ys[k, of[h]][:, :128], lam), lam)
        first = lam + seconds[h] - mul_t(pair_e[1, h], lam)
        adjoint[mine + h] = jnp.where(c == 0, first, lam).astype(BF)
        pair_l[h] = jnp.where(c == 0, lam, first).astype(BF)
    give.start()
    for i in (0, 1):
        sums[i].finish(out_down.at[:, pl.ds(512 * i, 512)])
    give.wait_recv()
    for h in (0, 1):
        adjoint[theirs + h] = got_l[h]
    for h in range(4):
        at, fk = cols[h], feat_k(h)
        grad_update = mul(fk * inverse[:, 8:9], adjoint[h])
        grad_value[:, at] += grad_update
        grad_den = jnp.sum(grad_update * recall[:, at], axis=1, keepdims=True) * inverse[:, 4 + h : 5 + h]
        line[h : h + 1] += jnp.sum(grad_den * fk, axis=0, keepdims=True)
        grad_key[:, at] += slope_of(key[:, at].astype(F32)) * (
            grad_den * offset[h : h + 1]
            - rows_by_rows((grad_update * inverse[:, 4 + h : 5 + h]).astype(BF), memory[h].astype(BF))
        )
    line[4:8] = jnp.zeros((4, 128), F32)
    lines[me] = line[...]

    def push(k, carry):
        remote(line, lines.at[me], send.at[38], recv.at[38], seq_place(lax.rem(me + k, 32))).start()
        return carry

    lax.fori_loop(1, 32, push, 0)
    for h in range(4):
        at = cols[h]
        grads[:, 1024 + 128 * h : 1152 + 128 * h] = grad_value[:, at].astype(BF)
        update = value[:, at].astype(F32) - recall[:, at]
        grad_key[:, at] += (
            inverse[:, 8:9] * slope_of(key[:, at].astype(F32)) * rows_by_rows(update.astype(BF), adjoint[h])
        )
    sums[2].one.middle()
    load_t.wait()
    product(ends, 1, grads[:, 0:512])
    z_layer.middle()
    sums[3].one.middle()
    product(ends, 3, grads[:, 1024:1536])
    for s in sums[:2]:
        s.one.drain()
        s.two.drain()
    ends[0].add_stored()
    ends[0].one.start()
    for load in (*late, load_own):
        load.wait()
    others = lines.at[pl.ds(0, 31)]
    pltpu.make_async_copy(others, others, recv.at[38]).wait()
    passed = lax.broadcasted_iota(jnp.int32, (32, 8, 128), 0) > me
    after = jnp.sum(jnp.where(passed, lines[...], 0.0), axis=0)
    later[...] = after[0:4]
    stores = [move.start(later, o_later)]
    for h in range(4):
        at = cols[h]
        late = inverse[:, 8:9] * after[h : h + 1] * slope_of(key[:, at].astype(F32))
        grads[:, 512 + 128 * h : 640 + 128 * h] = (grad_key[:, at] + late).astype(BF)
    z_layer.finish()
    stores.append(move.start(layer_out, o_layer_out))
    for half in (0, 1):
        rows = pl.ds(1024 * half, 1024)
        value = sum(rows_by_rows(grads[:, 512 * i : 512 * (i + 1)], weight_in[i, rows]) for i in range(3))
        forth[:, :, rows] = value.astype(BF).reshape(4, 96, 1024)
        for z_end in z_ends:
            (z_end.start_a, z_end.start_b)[half]()
    sums[2].second_ring()
    sums[3].second_ring()
    grads_ring(1)
    product(ends, 2, grads[:, 512:1024])
    z_ends[0].middle()
    z_ends[1].middle()
    ends[0].one.middle()
    for i in (2, 3):
        sums[i].two.middle()
        sums[i].one.drain()
    grads_ring(3)
    ends[1].one.middle()

    def put(at, result):
        own[:, at] = result

    for i in (0, 1):
        rows = parts[i]
        z_ends[i].finish(put)
        result = grad_middle[rows] + norm_back(branch[0, rows].astype(F32), own[...], gain_attn, 0, i)
        grad_tokens[z, rows] = result.astype(BF)
        z_tokens[i].start()
    total.start()
    grads_ring(2)
    for i in (2, 3):
        sums[i].finish(out_down.at[:, pl.ds(512 * i, 512)])
        sums[i].two.drain()
    stores.append(move.start(out_down, o_out_down))
    ends[0].second_ring()
    ends[3].one.middle()
    for z_token in z_tokens:
        z_token.middle()
    ends[1].second_ring()
    total.over_seq()
    ends[2].one.middle()
    ends[0].two.middle()
    ends[3].second_ring()
    ends[1].two.middle()
    total.over_tensor(logits_out)
    stores.append(move.start(logits_out, o_logits_out))
    ends[2].second_ring()
    ends[0].finish(out_output)
    stores.append(move.start(out_output, o_out_output))
    ends[3].two.middle()
    ends[1].finish(out_query)
    stores.append(move.start(out_query, o_out_query))
    ends[2].two.middle()
    ends[3].finish(out_value)
    stores.append(move.start(out_value, o_out_value))
    ends[2].finish(out_key)
    stores.append(move.start(out_key, o_out_key))
    total.finish()
    stores.append(move.start(gains, o_gains))
    for z_token in z_tokens:
        z_token.finish()
    stores.append(move.start(grad_tokens, o_grad_tokens))
    for part in (z_layer, y_ring, x_ring, *z_ends, *z_tokens, total, *ends):
        part.drain()
    swap.wait_send()
    give.wait_send()
    for store in stores:
        store.wait()
    pltpu.make_async_copy(others, others, send.at[38]).wait()


def rest(cid, *args):
    shape = jax.ShapeDtypeStruct
    low = lambda *dims: pltpu.VMEM(dims, BF)
    full = lambda *dims: pltpu.VMEM(dims, F32)
    weight_grad = shape((64, 512), F32)
    return pl.pallas_call(
        rest_kernel,
        out_shape=(
            shape((4, 96, 2048), BF),
            shape((4, 96, 2048), BF),
            shape((4, 128), F32),
            shape((64, 2048), F32),
            weight_grad,
            weight_grad,
            weight_grad,
            weight_grad,
            shape((4, 8, 128), F32),
            shape((8, 128), F32),
        ),
        in_specs=[VMEM] * 6 + [SMEM] + [ANYWHERE] * 22,
        out_specs=(ANYWHERE,) * 10,
        scratch_shapes=[
            low(4, 96, 2048),
            low(4, 96, 2048),
            full(4, 128),
            full(64, 2048),
            full(64, 512),
            full(64, 512),
            full(64, 512),
            full(64, 512),
            full(4, 8, 128),
            full(8, 128),
            full(4, 128, 128),
            low(4, 256, 256),
            low(4, 256, 256),
            low(2, 2, 128, 128),
            full(4, 128),
            low(4, 96, 2048),
            full(96, 2048),
            low(384, 1536),
            low(16, 2, 64, 384),
            low(384, 2048),
            low(384, 512),
            low(384, 512),
            low(384, 512),
            low(4, 384, 384),
            full(384, 512),
            full(384, 512),
            low(384, 512),
            low(2048, 512),
            low(3, 2048, 512),
            low(4, 16, 64, 512),
            low(4, 16, 64, 512),
            low(5, 4, 256, 512),
            low(4, 6, 256, 256),
            low(4, 4, 64, 512),
            low(4, 6, 64, 256),
            low(4, 6, 256, 256),
            low(4, 6, 64, 256),
            low(4, 96, 2048),
            low(2, 6, 48, 1024),
            full(48, 2048),
            full(384, 128),
            full(384, 512),
            full(384, 512),
            full(384, 512),
            full(384, 512),
            full(384, 512),
            low(4, 128, 128),
            low(2, 128, 128),
            low(4, 256, 128),
            low(4, 256, 128),
            low(2, 128, 128),
            low(2, 128, 128),
            low(4, 128, 128),
            full(8, 128),
            full(32, 8, 128),
            full(4, 8, 128),
            full(8, 128),
            full(4, 8, 128),
            full(16, 128),
            full(32, 16, 128),
            pltpu.SemaphoreType.DMA((42,)),
            pltpu.SemaphoreType.DMA((180,)),
            pltpu.SemaphoreType.DMA((180,)),
        ],
        name="rest",
        compiler_params=params(cid, 63),
    )(*args)


def last_kernel(*refs):
    ins, outs = refs[:14], refs[14:29]
    narrow, wide, rows, gate, up, sems, *held = refs[29:]
    move = Moves(sems)
    grad_tokens, mlp_grads, grad_gate, gains, *same = ins
    o_tokens, o_gate, o_up, o_attn, o_mlp, *o_same = outs
    fetch = [move.start(grad_tokens.at[q], narrow.at[q]) for q in range(4)]
    known = grad_gate.shape[1]
    fetch_gate = move.start(grad_gate, gate.at[:, pl.ds(0, known)])
    fetch_same = [move.start(src, dst) for src, dst in zip((gains, *same), held)]
    fetch_rows = move.start(mlp_grads, rows)
    copies = []
    for q in range(4):
        fetch[q].wait()
        wide[q] = narrow[q].astype(F32)
        copies.append(move.start(wide.at[q], o_tokens.at[q]))
    fetch_gate.wait()
    for copy in fetch_same:
        copy.wait()
    copies.append(move.start(held[0].at[pl.ds(0, 2)], o_attn))
    copies.append(move.start(held[0].at[pl.ds(2, 2)], o_mlp))
    copies += [move.start(src, dst) for src, dst in zip(held[1:], o_same)]
    fetch_rows.wait()
    split = gate.shape[1] - known
    gate[:, known:] = rows[:, :split].astype(F32)
    copies.append(move.start(gate, o_gate))
    up[...] = rows[:, split:].astype(F32)
    copies.append(move.start(up, o_up))
    for copy in copies:
        copy.wait()


def last(grad_tokens, mlp_grads, grad_gate, gains, *same):
    shape = jax.ShapeDtypeStruct
    wide = shape((64, (mlp_grads.shape[1] + grad_gate.shape[1]) // 2), F32)
    gain = shape((2, 8, 128), F32)
    outs = (shape(grad_tokens.shape, F32), wide, wide, gain, gain, *(shape(a.shape, a.dtype) for a in same))
    return pl.pallas_call(
        last_kernel,
        out_shape=outs,
        in_specs=[ANYWHERE] * 14,
        out_specs=(ANYWHERE,) * len(outs),
        scratch_shapes=[
            pltpu.VMEM(grad_tokens.shape, BF),
            pltpu.VMEM(grad_tokens.shape, F32),
            pltpu.VMEM(mlp_grads.shape, BF),
            pltpu.VMEM(wide.shape, F32),
            pltpu.VMEM(wide.shape, F32),
            pltpu.SemaphoreType.DMA((36,)),
            *(pltpu.VMEM(a.shape, a.dtype) for a in (gains, *same)),
        ],
        name="last",
        compiler_params=pltpu.CompilerParams(vmem_limit_bytes=63 << 20),
    )(grad_tokens, mlp_grads, grad_gate, gains, *same)


def on_device(
    tokens,
    cotangent,
    w_query,
    w_key,
    w_value,
    w_output,
    w_gate,
    w_up,
    w_down,
    gain_attn,
    gain_mlp,
    gate_logit,
    valid_count,
):
    valid = valid_count[None]
    rows = (16, 2, 64, 512)
    (
        normed_t, grad_out_t, query, key, value, probs, local_out, retrieved, mix, hidden, mlp_grads,
        recall, inverse, grad_out_own, offset, normal_next, memory_prev, memory_next, ys, xs, pair_e, middle,
        grad_two, grad_gate,
    ) = front(
        0, gain_attn[None], gain_mlp[None], valid, gate_logit, tokens, cotangent,
        *(w.reshape(rows) for w in (w_query, w_key, w_value, w_output)), w_down, w_gate, w_up,
    )
    mlp_grads = lax.psum_scatter(mlp_grads.reshape(1024, -1), SEQ[:2], scatter_dimension=0, tiled=True)
    (
        layer_out, grad_tokens, later_offset, grad_down, grad_query, grad_key, grad_value, grad_output, gains, logit_grad,
    ) = rest(
        1, grad_two, middle, gain_attn[None], gain_mlp[None], grad_out_own, offset, gate_logit, memory_prev, ys, xs, pair_e,
        grad_out_t, hidden, query, key, value, probs, local_out, retrieved, mix, normed_t, recall, inverse,
        w_query, w_key, w_value, w_output, w_down, tokens,
    )
    (
        grad_tokens, grad_gate, grad_up, gain_attn_grad, gain_mlp_grad, layer_out, grad_query, grad_key, grad_value,
        grad_output, grad_down, logit_grad, memory_next, normal_next, later_offset,
    ) = last(
        grad_tokens, mlp_grads, grad_gate, gains, layer_out, grad_query, grad_key, grad_value, grad_output, grad_down,
        logit_grad, memory_next, normal_next, later_offset,
    )
    return (
        layer_out.reshape(tokens.shape),
        grad_tokens.reshape(tokens.shape),
        grad_query,
        grad_key,
        grad_value,
        grad_output,
        grad_gate,
        grad_up,
        grad_down,
        gain_attn_grad.reshape(-1),
        gain_mlp_grad.reshape(-1),
        logit_grad[0, :4],
        memory_next[None],
        normal_next[None],
        later_offset[None],
    )


def solution(mesh):
    torus = Mesh(
        mesh.devices.reshape(4, 4, 2, mesh.shape["tensor"]), ("seq_0", "seq_1", "seq_2", "tensor")
    )
    weight = P(None, "tensor")
    grad = P(SEQ, "tensor")
    return jax.shard_map(
        on_device,
        mesh=torus,
        in_specs=(P(SEQ, None), P(SEQ, None)) + (weight,) * 7 + (P(), P(), P("tensor"), P()),
        out_specs=(P(SEQ, None), P(SEQ, None))
        + (grad,) * 7
        + (P(), P(), P("tensor"), P(SEQ, "tensor", None, None), P(SEQ, "tensor", None), P(SEQ, "tensor", None)),
        check_vma=False,
    )
```

```python
import functools

import jax
import jax.numpy as jnp
from jax import lax
from jax.experimental import pallas as pl
from jax.experimental.pallas import tpu as pltpu
from jax.sharding import Mesh
from jax.sharding import PartitionSpec as P

SEQ = ("seq_0", "seq_1", "seq_2")
MESH_ID = pl.DeviceIdType.MESH
VMEM = pl.BlockSpec(memory_space=pltpu.VMEM)
BF = jnp.bfloat16
F32 = jnp.float32

epsilon = 1e-06


def remote(src, dst, send, recv, device):
    return pltpu.make_async_remote_copy(
        src_ref=src, dst_ref=dst, send_sem=send, recv_sem=recv, device_id=device, device_id_type=MESH_ID
    )


def meet(devices):
    barrier = pltpu.get_barrier_semaphore()
    for device in devices:
        pl.semaphore_signal(barrier, inc=1, device_id=device, device_id_type=MESH_ID)
    pl.semaphore_wait(barrier, len(devices))


def params(collective_id, mib):
    return pltpu.CompilerParams(
        collective_id=collective_id, has_side_effects=True, vmem_limit_bytes=mib << 20
    )


def seq_place(index):
    return {"seq_0": index // 8, "seq_1": lax.rem(index // 2, 4), "seq_2": lax.rem(index, 2)}


def seq_index():
    return lax.axis_index("seq_0") * 8 + lax.axis_index("seq_1") * 2 + lax.axis_index("seq_2")


def mul(a, b):
    return jnp.dot(a.astype(BF), b.astype(BF), preferred_element_type=F32)


def mul_t(a, b):
    return lax.dot_general(a.astype(BF), b.astype(BF), (((0,), (0,)), ((), ())), preferred_element_type=F32)


def ring_places():
    x, y, c = (lax.axis_index(a) for a in SEQ)
    return x, y, c


def rows_by_rows(a, b):
    return lax.dot_general(a, b, (((1,), (1,)), ((), ())), preferred_element_type=F32)


class RingSum:
    def __init__(self, src, bufs, send, recv, base, axis, rows=None):
        self.src, self.bufs, self.me = src, bufs, lax.axis_index(axis)
        rows = pl.ds(0, src.shape[1]) if rows is None else rows
        self.rows = rows
        half = src.shape[2] // 2
        self.a, self.b = pl.ds(0, half), pl.ds(half, half)
        self.right, self.left = lax.rem(self.me + 1, 4), lax.rem(self.me + 3, 4)
        far = lax.rem(self.me + 2, 4)
        to_right, to_left = {axis: self.right}, {axis: self.left}

        def copy(piece, landing, slot, device):
            return remote(piece, bufs.at[landing], send.at[base + slot], recv.at[base + slot], device)

        self.c0 = copy(src.at[far, rows, self.a], 0, 0, to_right)
        self.c1 = copy(src.at[far, rows, self.b], 1, 1, to_left)
        self.c2 = copy(src.at[self.right, rows, self.b], 2, 2, to_right)
        self.c3 = copy(src.at[self.left, rows, self.a], 3, 3, to_left)
        self.c4 = copy(bufs.at[0], 4, 4, to_right)
        self.c5 = copy(bufs.at[1], 5, 5, to_left)

    def start_a(self):
        self.c0.start()
        self.c3.start()

    def start_b(self):
        self.c1.start()
        self.c2.start()

    def start(self):
        self.c0.start()
        self.c1.start()
        self.c3.start()
        self.c2.start()

    def middle(self):
        src, bufs = self.src, self.bufs
        self.c0.wait_recv()
        bufs[0] = (bufs[0].astype(F32) + src[self.right, self.rows, self.a].astype(F32)).astype(BF)
        self.c4.start()
        self.c1.wait_recv()
        bufs[1] = (bufs[1].astype(F32) + src[self.left, self.rows, self.b].astype(F32)).astype(BF)
        self.c5.start()

    def finish(self, put):
        src, bufs = self.src, self.bufs
        self.c3.wait_recv()
        self.c4.wait_recv()
        put(self.a, src[self.me, self.rows, self.a].astype(F32) + bufs[4].astype(F32) + bufs[3].astype(F32))
        self.c2.wait_recv()
        self.c5.wait_recv()
        put(self.b, src[self.me, self.rows, self.b].astype(F32) + bufs[5].astype(F32) + bufs[2].astype(F32))

    def drain(self):
        for copy in (self.c0, self.c1, self.c2, self.c3, self.c4, self.c5):
            copy.wait_send()


class RingGather:
    def __init__(self, buf, send, recv, base, axis, rows=None):
        self.me = lax.axis_index(axis)
        half = buf.shape[1 if rows is None else 2] // 2
        right, left = lax.rem(self.me + 1, 4), lax.rem(self.me + 3, 4)
        to_right, to_left = {axis: right}, {axis: left}

        def copy(q, h, slot, device):
            part = pl.ds(half * h, half)
            piece = buf.at[q, part] if rows is None else buf.at[q, rows, part]
            return remote(piece, piece, send.at[base + slot], recv.at[base + slot], device)

        self.r0, self.l1 = copy(self.me, 0, 0, to_right), copy(self.me, 1, 1, to_left)
        self.r1, self.l0 = copy(self.me, 1, 2, to_right), copy(self.me, 0, 3, to_left)
        self.f0, self.f1 = copy(left, 0, 4, to_right), copy(right, 1, 5, to_left)

    def start(self):
        for copy in (self.r0, self.l1, self.r1, self.l0):
            copy.start()

    def middle(self):
        self.r0.wait_recv()
        self.f0.start()
        self.l1.wait_recv()
        self.f1.start()

    def finish(self):
        for copy in (self.r1, self.l0, self.f0, self.f1):
            copy.wait_recv()

    def drain(self):
        for copy in (self.r0, self.l1, self.r1, self.l0, self.f0, self.f1):
            copy.wait_send()


class SeqSum:
    def __init__(self, product, got, first, first_bufs, second, second_bufs, send, recv, base, x_first):
        self.got, self.first, self.second, self.x_first = got, first, second, x_first
        core = lax.axis_index("seq_2")
        self.swap = remote(product, got, send.at[base], recv.at[base], {"seq_2": 1 - core})
        axes = ("seq_0", "seq_1") if x_first else ("seq_1", "seq_0")
        self.one = RingSum(first, first_bufs, send, recv, base + 1, axes[0])
        self.two = RingSum(second, second_bufs, send, recv, base + 7, axes[1])

    def start(self):
        self.swap.start()

    def store(self, own):
        for x in range(4):
            for y in range(4):
                at = 4 * x + y
                q, r = (x, y) if self.x_first else (y, x)
                self.first[q, pl.ds(64 * r, 64)] = own[64 * at : 64 * (at + 1)].astype(BF)

    def add(self, own):
        self.swap.wait_recv()
        self.store(own + flat(self.got[...]).astype(F32))

    def add_stored(self):
        self.swap.wait_recv()
        for x in range(4):
            for y in range(4):
                q, r = (x, y) if self.x_first else (y, x)
                rows = pl.ds(64 * r, 64)
                self.first[q, rows] = (self.first[q, rows].astype(F32) + self.got[4 * x + y].astype(F32)).astype(BF)

    def second_ring(self):
        def put(cols, value):
            for r in range(4):
                self.second[r, :, cols] = value[64 * r : 64 * (r + 1)].astype(BF)

        self.one.finish(put)
        self.two.start()

    def finish(self, out):
        def put(cols, value):
            out[:, cols] = value

        self.two.finish(put)

    def drain(self):
        self.swap.wait_send()
        self.one.drain()
        self.two.drain()


def greet_all():
    barrier = pltpu.get_barrier_semaphore()
    me, z = seq_index(), lax.axis_index("tensor")

    def greet_seq(k, carry):
        pl.semaphore_signal(barrier, inc=1, device_id=seq_place(lax.rem(me + k, 32)), device_id_type=MESH_ID)
        return carry

    lax.fori_loop(1, 32, greet_seq, 0)
    for k in (1, 2, 3):
        pl.semaphore_signal(barrier, inc=1, device_id={"tensor": lax.rem(z + k, 4)}, device_id_type=MESH_ID)


def all_greeted():
    pl.semaphore_wait(pltpu.get_barrier_semaphore(), 34)


class TotalOfAll:
    def __init__(self, mine, extra, by_z, line, by_seq, total, send, recv, base):
        self.mine, self.extra, self.by_z, self.line, self.by_seq, self.total = mine, extra, by_z, line, by_seq, total
        self.z, self.me = lax.axis_index("tensor"), seq_index()
        self.send, self.recv, self.base = send, recv, base
        peers = [lax.rem(self.z + k, 4) for k in (1, 2, 3)]
        self.split = [
            remote(mine.at[p], by_z.at[self.z], send.at[base + k], recv.at[base + k], {"tensor": p})
            for k, p in enumerate(peers)
        ]
        self.join = [
            remote(total.at[self.z], total.at[self.z], send.at[base + 3 + k], recv.at[base + 3 + k], {"tensor": p})
            for k, p in enumerate(peers)
        ]

    def start(self):
        for copy in self.split:
            copy.start()

    def over_seq(self):
        self.by_z[self.z] = self.mine[self.z]
        for copy in self.split:
            copy.wait_recv()
        self.line[0:8] = (self.by_z[0] + self.by_z[1]) + (self.by_z[2] + self.by_z[3])
        self.line[8:16] = self.extra[...]
        self.by_seq[self.me] = self.line[...]

        def push(k, carry):
            device = seq_place(lax.rem(self.me + k, 32))
            remote(self.line, self.by_seq.at[self.me], self.send.at[self.base + 6], self.recv.at[self.base + 6], device).start()
            return carry

        lax.fori_loop(1, 32, push, 0)

    def over_tensor(self, extra_out):
        others = self.by_seq.at[pl.ds(0, 31)]
        pltpu.make_async_copy(others, others, self.recv.at[self.base + 6]).wait()
        summed = jnp.sum(self.by_seq[...], axis=0)
        self.total[self.z] = summed[0:8]
        extra_out[...] = summed[8:16]
        for copy in self.join:
            copy.start()

    def finish(self):
        for copy in self.join:
            copy.wait_recv()

    def drain(self):
        for copy in (*self.split, *self.join):
            copy.wait_send()
        others = self.by_seq.at[pl.ds(0, 31)]
        pltpu.make_async_copy(others, others, self.send.at[self.base + 6]).wait()


def feature_of(v):
    return jnp.where(v > 0, v + 1.0, jnp.exp(jnp.minimum(v, 0.0)))


def slope_of(v):
    return jnp.where(v > 0, 1.0, jnp.exp(jnp.minimum(v, 0.0)))


ANYWHERE = pl.BlockSpec(memory_space=pl.ANY)


def keep_of(valid):
    length = jnp.where(seq_index() == 31, valid[...], 384)
    return (lax.broadcasted_iota(jnp.int32, (384, 1), 0) < length).astype(F32)


SMEM = pl.BlockSpec(memory_space=pltpu.SMEM)


def gate_rows(gate, logit):
    for h in range(4):
        gate[h : h + 1] = jax.nn.sigmoid(jnp.full((1, 128), logit[h], F32))


def flat(weight):
    return weight.reshape(-1, 512)


def core_rows(turned, core):
    return turned[pl.ds(0, 16), core].reshape(1024, 384)


class Moves:
    def __init__(self, sems):
        self.sems, self.count = sems, 0

    def start(self, src, dst):
        copy = pltpu.make_async_copy(src, dst, self.sems.at[self.count])
        self.count += 1
        copy.start()
        return copy


def front_kernel(
    gain_attn,
    gain_mlp,
    valid,
    gate_logit,
    i_tokens,
    cotangent,
    w_query,
    w_key,
    w_value,
    w_output,
    w_down,
    w_gate,
    w_up,
    o_normed_t,
    o_grad_out_t,
    o_query,
    o_key,
    o_value,
    o_probs,
    o_local_out,
    o_retrieved,
    o_mix,
    o_hidden,
    o_grads,
    o_recall,
    o_inverse,
    grad_out_own,
    offset,
    normal_next,
    memory_prev,
    memory_next,
    ys,
    xs,
    pair_e,
    middle,
    grad_two,
    out_gate,
    keep,
    gate,
    weights,
    weight_o,
    weight_d,
    weight_g,
    hidden,
    normed_two,
    normed,
    turned,
    grad_out,
    got_rows,
    first_rows,
    first_bufs,
    second_rows,
    second_bufs,
    pair_rows,
    inverse,
    grad_hidden,
    query,
    key,
    value,
    probs,
    local_out,
    retrieved,
    mix,
    line,
    lines,
    eb,
    source,
    got,
    pair_m,
    got_m,
    part,
    part_bufs,
    moves,
    send,
    recv,
):
    move = Moves(moves)
    tokens = hidden
    load_tokens = move.start(i_tokens, tokens)
    loads = [move.start(w, weights.at[i]) for i, w in enumerate((w_key, w_query, w_value))]
    load_cotangent = move.start(cotangent, grad_out)
    load_o = move.start(w_output, weight_o)
    load_d = [move.start(w_down.at[pl.ds(512 * i, 512)], weight_d.at[pl.ds(512 * i, 512)]) for i in range(4)]
    greet_all()
    keep[...] = keep_of(valid)
    gate_rows(gate, gate_logit)
    x, y, c = ring_places()
    z, me = lax.axis_index("tensor"), seq_index()
    partner = {"seq_2": 1 - c}
    mine, theirs = 2 * c, 2 * (1 - c)
    slots = [
        held.at[pl.ds(0, 16), j] for held in (weight_o, weights.at[0], weights.at[1], weights.at[2]) for j in (0, 1)
    ]
    sums = [
        SeqSum(
            slots[i], got_rows.at[i], first_rows.at[i], first_bufs.at[i], second_rows.at[i], second_bufs.at[i],
            send, recv, 27 + 13 * i, i % 2 == 0,
        )
        for i in range(2)
    ]
    swaps = [remote(slots[2 + i], got_rows.at[2 + i], send.at[53 + i], recv.at[53 + i], partner) for i in range(6)]
    parts = [pl.ds(0, 48), pl.ds(48, 48)]
    z_sums = [RingSum(part, part_bufs.at[i], send, recv, 79 + 6 * i, "tensor", parts[i]) for i in (0, 1)]
    z_gathers = [RingGather(normed_two, send, recv, 91 + 6 * i, "tensor", parts[i]) for i in (0, 1)]
    z_backs = [RingSum(part, part_bufs.at[i], send, recv, 6 * i, "tensor", parts[i]) for i in (0, 1)]
    y_ring = RingGather(ys, send, recv, 12, "seq_1")
    x_ring = RingGather(xs, send, recv, 18, "seq_0")
    swap = remote(eb.at[pl.ds(theirs, 2)], got, send.at[24], recv.at[24], partner)
    give = remote(pair_m, got_m, send.at[25], recv.at[25], partner)
    cols = [slice(128 * h, 128 * (h + 1)) for h in range(4)]
    stores = []

    load_tokens.wait()
    for q in range(4):
        rows = pl.ds(96 * q, 96)
        stream = tokens[rows].astype(F32)
        inv = lax.rsqrt(jnp.mean(stream * stream, axis=1, keepdims=True) + epsilon)
        normed[rows] = (stream * inv * gain_attn[...]).astype(BF)
    loads[0].wait()
    key[...] = jnp.dot(normed[...], flat(weights[0]), preferred_element_type=F32).astype(BF)
    feat_q = lambda h: feature_of(query[:, cols[h]].astype(F32))
    feat_k = lambda h: feature_of(key[:, cols[h]].astype(F32))
    line[...] = jnp.zeros_like(line)
    for h in range(4):
        line[h : h + 1] = jnp.sum(feat_k(h) * keep[...], axis=0, keepdims=True)
    lines[me] = line[...]
    all_greeted()

    def push(k, carry):
        remote(line, lines.at[me], send.at[26], recv.at[26], seq_place(lax.rem(me + k, 32))).start()
        return carry

    lax.fori_loop(1, 32, push, 0)
    stores.append(move.start(key, o_key))
    loads[1].wait()
    query[...] = jnp.dot(normed[...], flat(weights[1]), preferred_element_type=F32).astype(BF)
    stores.append(move.start(query, o_query))
    loads[2].wait()
    value[...] = jnp.dot(normed[...], flat(weights[2]), preferred_element_type=F32).astype(BF)
    stores.append(move.start(value, o_value))
    load_g = move.start(w_gate, weight_g)
    at_row = lax.broadcasted_iota(jnp.int32, (384, 384), 0)
    at_col = lax.broadcasted_iota(jnp.int32, (384, 384), 1)
    valid = jnp.sum(keep[...], axis=0, keepdims=True)
    allowed = (at_row >= at_col) & (at_col.astype(F32) < valid)

    def attend(h):
        at = cols[h]
        scores = rows_by_rows(query[:, at], key[:, at]) * 128 ** (-0.5)
        masked = jnp.where(allowed, scores, -1e30)
        raised = jnp.exp(masked - jnp.max(masked, axis=1, keepdims=True))
        low = (raised * (1.0 / jnp.sum(raised, axis=1, keepdims=True))).astype(BF)
        probs[h] = low
        local_out[:, at] = jnp.dot(low, value[:, at], preferred_element_type=F32)
        total = mul_t(feat_k(h) * keep[...], value[:, at])
        source[h] = total
        eb[h, :, 128:256] = total.astype(BF)

    for h in range(4):
        attend(h)
    stores.append(move.start(probs, o_probs))
    stores.append(move.start(local_out, o_local_out))
    others = lines.at[pl.ds(0, 31)]
    pltpu.make_async_copy(others, others, recv.at[26]).wait()
    passed = lax.broadcasted_iota(jnp.int32, (32, 8, 128), 0) < me
    before = jnp.sum(jnp.where(passed, lines[...], 0.0), axis=0)
    normal_next[...] = (before + line[...])[0:4]
    offset[...] = before + 384.0
    for h in range(4):
        fk = feat_k(h)
        kept = fk * keep[...] * (1.0 / jnp.sum(fk * offset[h : h + 1], axis=1, keepdims=True))
        eb[h, :, 0:128] = mul_t(kept, fk).astype(BF)
    swap.start()
    load_cotangent.wait()
    grad_out[...] = grad_out[...] * keep[...].astype(BF)
    grad_out_own[...] = grad_out[pl.ds(pl.multiple_of(96 * z, 96), 96)]
    swap.wait_recv()
    of = [pl.ds(0, 128), pl.ds(128, 128)]
    firsts = []
    for h in (0, 1):
        here, there = eb[mine + h].astype(F32), got[h].astype(F32)
        first, second = jnp.where(c == 0, here, there), jnp.where(c == 0, there, here)
        firsts.append(first)
        pair_e[0, h] = first[:, :128].astype(BF)
        pair_e[1, h] = second[:, :128].astype(BF)
        ys[y, of[h]] = (first + second - mul(second[:, :128], first)).astype(BF)
    y_ring.start()

    def hidden_part(i):
        load_d[i].wait()
        rows = pl.ds(512 * i, 512)
        product = jnp.dot(grad_out[:, 512 * i : 512 * (i + 1)], weight_d[rows], preferred_element_type=F32)
        if i == 0:
            grad_hidden[...] = product
        else:
            grad_hidden[...] += product

    hidden_part(0)
    y_ring.middle()
    hidden_part(1)
    y_ring.finish()
    starts = []
    for h in (0, 1):
        so_far = ys[0, of[h]].astype(F32)
        start = jnp.where(y > 0, so_far, 0.0)
        for k in (1, 2, 3):
            step = ys[k, of[h]].astype(F32)
            so_far = so_far + step - mul(step[:, :128], so_far)
            if k < 3:
                start = jnp.where(y > k, so_far, start)
        xs[x, of[h]] = so_far.astype(BF)
        starts.append(start)
    x_ring.start()
    hidden_part(2)
    x_ring.middle()
    hidden_part(3)
    load_u = move.start(w_up, weight_d)
    load_o.wait()
    x_ring.finish()
    for h in (0, 1):
        m = jnp.where(x > 0, xs[0, of[h]][:, 128:].astype(F32), 0.0)
        for k in (1, 2):
            step = xs[k, of[h]].astype(F32)
            m = jnp.where(x > k, m + step[:, 128:] - mul(step[:, :128], m), m)
        m = m + starts[h][:, 128:] - mul(starts[h][:, :128], m)
        second = m + firsts[h][:, 128:] - mul(firsts[h][:, :128], m)
        memory_prev[mine + h] = jnp.where(c == 0, m, second)
        pair_m[h] = jnp.where(c == 0, second, m)
    give.start()
    give.wait_recv()
    inverse[...] = jnp.zeros_like(inverse)
    inverse[:, 8:9] = keep[...]
    for h in (0, 1):
        memory_prev[theirs + h] = got_m[h]
    for h in range(4):
        at, fq, sig = cols[h], feat_q(h), gate[h : h + 1]
        inv_q = 1.0 / jnp.sum(fq * offset[h : h + 1], axis=1, keepdims=True)
        inverse[:, h : h + 1] = inv_q
        found = mul(fq, memory_prev[h]) * inv_q
        retrieved[:, at] = found
        mix[:, at] = (sig * found + (1.0 - sig) * local_out[:, at]).astype(BF)
    for half in (0, 1):
        rows = pl.ds(1024 * half, 1024)
        part[:, :, rows] = rows_by_rows(mix[...], flat(weight_o[8 * half : 8 * half + 8])).astype(BF).reshape(4, 96, 1024)
        for z_sum in z_sums:
            (z_sum.start_a, z_sum.start_b)[half]()
    store_found = move.start(retrieved, o_retrieved)
    stores.append(move.start(mix, o_mix))
    for h in range(4):
        m = memory_prev[h]
        memory_next[h] = m + source[h] - mul(eb[h][:, :128], m)
    turned[...] = normed[...].T.reshape(16, 2, 64, 384)
    store_t = move.start(turned, o_normed_t)
    z_sums[0].middle()
    z_sums[1].middle()
    store_found.wait()
    recall = retrieved
    for h in range(4):
        fk, off = feat_k(h), offset[h : h + 1]
        inv_k = 1.0 / jnp.sum(fk * off, axis=1, keepdims=True)
        inverse[:, 4 + h : 5 + h] = inv_k
        recall[:, cols[h]] = mul(fk, memory_prev[h]) * inv_k
    stores.append(move.start(recall, o_recall))
    stores.append(move.start(inverse, o_inverse))

    def second_norm(i):
        own_tokens = tokens[pl.ds(pl.multiple_of(96 * z + 48 * i, 16), 48)].astype(F32)

        def put(at, total):
            lanes = slice(0, 1024) if at is z_sums[i].a else slice(1024, 2048)
            middle[parts[i], at] = own_tokens[:, lanes] + total

        z_sums[i].finish(put)
        z_sums[i].drain()
        stream = middle[parts[i]]
        inv = lax.rsqrt(jnp.mean(stream * stream, axis=1, keepdims=True) + epsilon)
        normed_two[z, parts[i]] = (stream * inv * gain_mlp[...]).astype(BF)
        z_gathers[i].start()

    second_norm(0)
    second_norm(1)
    z_gathers[0].middle()
    z_gathers[1].middle()
    store_t.wait()
    turned[...] = grad_out[...].T.reshape(16, 2, 64, 384)
    store_t = move.start(turned, o_grad_out_t)
    for store in stores:
        store.wait()
    store_t.wait()
    load_g.wait()
    load_u.wait()
    for z_gather in z_gathers:
        z_gather.finish()
    for z_gather in z_gathers:
        z_gather.drain()
    turned[...] = normed_two[...].reshape(384, 2048).T.reshape(16, 2, 64, 384)

    def tile(i):
        for half in (2 * i, 2 * i + 1):
            narrow_tile(half)

    def narrow_tile(i):
        lanes = slice(256 * i, 256 * (i + 1))
        rows = normed_two[...].reshape(384, 2048)
        gate_pre = jnp.dot(rows, weight_g[:, lanes], preferred_element_type=F32)
        up_pre = jnp.dot(rows, weight_d[:, lanes], preferred_element_type=F32)
        back_hidden = grad_hidden[:, lanes]
        sig = jax.nn.sigmoid(gate_pre)
        swish = gate_pre * sig
        hidden[:, lanes] = (swish * up_pre).astype(BF)
        grad_out[:, lanes] = (back_hidden * swish).astype(BF)
        normed[:, lanes] = (back_hidden * up_pre * sig * (1.0 + gate_pre * (1.0 - sig))).astype(BF)

    def return_part(i):
        rows = pl.ds(512 * i, 512)
        value = rows_by_rows(normed[...], weight_g[rows]) + rows_by_rows(grad_out[...], weight_d[rows])
        part[:, :, rows] = value.astype(BF).reshape(4, 96, 512)

    leaving = []

    def gradient(i, core):
        side = (normed, grad_out)[i // 4]
        lanes = slice(512 * (i % 4), 512 * (i % 4 + 1))
        return jnp.dot(core_rows(turned, core), side[:, lanes], preferred_element_type=F32)

    def give_half(i):
        slots[i][...] = gradient(i, 1 - c).astype(BF).reshape(16, 64, 512)
        if i < 2:
            sums[i].start()
        else:
            swaps[i - 2].start()

    def gate_ring(i):
        sums[i].add(gradient(i, c))
        sums[i].one.start()

    def pair_sum(i):
        own_rows = gradient(2 + i, c)
        swaps[i].wait_recv()
        if i >= 1:
            leaving[i - 1].wait()
        pair_rows[...] = (own_rows + flat(got_rows[2 + i]).astype(F32)).astype(BF).reshape(16, 64, 512)
        leaving.append(move.start(pair_rows, o_grads.at[:, :, pl.ds(512 * i, 512)]))

    tile(0)
    give_half(0)
    tile(1)
    give_half(1)
    tile(2)
    gate_ring(0)
    tile(3)
    gate_ring(1)
    stores = [move.start(hidden, o_hidden)]
    return_part(0)
    return_part(1)
    for z_back in z_backs:
        z_back.start_a()
    return_part(2)
    return_part(3)
    for z_back in z_backs:
        z_back.start_b()
    give_half(2)
    sums[0].one.middle()
    give_half(3)
    sums[1].one.middle()
    give_half(4)
    pair_sum(0)
    give_half(5)
    pair_sum(1)
    z_backs[0].middle()
    z_backs[1].middle()
    sums[0].second_ring()
    give_half(6)
    pair_sum(2)
    sums[1].second_ring()
    give_half(7)
    pair_sum(3)
    sums[0].two.middle()
    pair_sum(4)
    sums[1].two.middle()
    pair_sum(5)
    for i in (0, 1):

        def put(at, total, i=i):
            grad_two[parts[i], at] = total

        z_backs[i].finish(put)
    for i in (0, 1):
        sums[i].finish(out_gate.at[:, pl.ds(512 * i, 512)])
    for copy in (*stores, leaving[5]):
        copy.wait()
    for swap_rows in swaps:
        swap_rows.wait_send()
    for part_sum in sums:
        part_sum.drain()
    for ring in (*z_backs, y_ring, x_ring):
        ring.drain()
    swap.wait_send()
    give.wait_send()
    pltpu.make_async_copy(others, others, send.at[26]).wait()


def front(cid, *args):
    shape = jax.ShapeDtypeStruct
    low = lambda *dims: pltpu.VMEM(dims, BF)
    full = lambda *dims: pltpu.VMEM(dims, F32)
    return pl.pallas_call(
        front_kernel,
        out_shape=(
            shape((16, 2, 64, 384), BF),
            shape((16, 2, 64, 384), BF),
            shape((384, 512), BF),
            shape((384, 512), BF),
            shape((384, 512), BF),
            shape((4, 384, 384), BF),
            shape((384, 512), F32),
            shape((384, 512), F32),
            shape((384, 512), BF),
            shape((384, 2048), BF),
            shape((16, 64, 3072), BF),
            shape((384, 512), F32),
            shape((384, 128), F32),
            shape((96, 2048), BF),
            shape((8, 128), F32),
            shape((4, 128), F32),
            shape((4, 128, 128), F32),
            shape((4, 128, 128), F32),
            shape((4, 256, 256), BF),
            shape((4, 256, 256), BF),
            shape((2, 2, 128, 128), BF),
            shape((96, 2048), F32),
            shape((96, 2048), F32),
            shape((64, 1024), F32),
        ),
        in_specs=[VMEM] * 3 + [SMEM] + [ANYWHERE] * 9,
        out_specs=(ANYWHERE,) * 13 + (VMEM,) * 11,
        scratch_shapes=[
            full(384, 1),
            full(4, 128),
            low(3, 16, 2, 64, 512),
            low(16, 2, 64, 512),
            low(2048, 2048),
            low(2048, 2048),
            low(384, 2048),
            low(4, 96, 2048),
            low(384, 2048),
            low(16, 2, 64, 384),
            low(384, 2048),
            low(8, 16, 64, 512),
            low(2, 4, 256, 512),
            low(2, 6, 256, 256),
            low(2, 4, 64, 512),
            low(2, 6, 64, 256),
            low(16, 64, 512),
            full(384, 128),
            full(384, 2048),
            low(384, 512),
            low(384, 512),
            low(384, 512),
            low(4, 384, 384),
            full(384, 512),
            full(384, 512),
            low(384, 512),
            full(8, 128),
            full(32, 8, 128),
            low(4, 128, 256),
            full(4, 128, 128),
            low(2, 128, 256),
            full(2, 128, 128),
            full(2, 128, 128),
            low(4, 96, 2048),
            low(2, 6, 48, 1024),
            pltpu.SemaphoreType.DMA((34,)),
            pltpu.SemaphoreType.DMA((107,)),
            pltpu.SemaphoreType.DMA((107,)),
        ],
        name="front",
        compiler_params=params(cid, 63),
    )(*args)


def neighbours():
    x, y, c = ring_places()
    z = lax.axis_index("tensor")
    near = [{"seq_2": 1 - c}]
    for axis, at in (("seq_0", x), ("seq_1", y), ("tensor", z)):
        near += [{axis: lax.rem(at + 1, 4)}, {axis: lax.rem(at + 3, 4)}]
    return near


def rest_kernel(
    grad_two,
    middle,
    gain_attn,
    gain_mlp,
    grad_out,
    offset,
    gate_logit,
    i_memory,
    i_ys,
    i_xs,
    i_pair_e,
    i_grad_out_t,
    i_hidden,
    i_query,
    i_key,
    i_value,
    i_probs,
    i_local_out,
    i_retrieved,
    i_mix,
    i_normed_t,
    i_recall,
    i_inverse,
    w_query,
    w_key,
    w_value,
    w_output,
    w_down,
    tokens,
    o_layer_out,
    o_grad_tokens,
    o_later,
    o_out_down,
    o_out_query,
    o_out_key,
    o_out_value,
    o_out_output,
    o_gains,
    o_logits_out,
    layer_out,
    grad_tokens,
    later,
    out_down,
    out_query,
    out_key,
    out_value,
    out_output,
    gains,
    logits_out,
    memory,
    ys,
    xs,
    pair_e,
    gate,
    branch,
    grad_middle,
    grads,
    left,
    hidden,
    query,
    key,
    value,
    probs,
    local_out,
    retrieved,
    mix,
    weight_o,
    weight_in,
    products,
    got_rows,
    first_rows,
    first_bufs,
    second_rows,
    second_bufs,
    first_bufs_2,
    second_bufs_2,
    forth,
    z_bufs,
    own,
    inverse,
    recall,
    grad_mix,
    grad_query,
    grad_key,
    grad_value,
    source,
    got,
    s_y,
    s_x,
    pair_l,
    got_l,
    adjoint,
    line,
    lines,
    mine_gains,
    logits,
    by_z,
    total_line,
    by_seq,
    moves,
    send,
    recv,
):
    x, y, c = ring_places()
    z, me = lax.axis_index("tensor"), seq_index()
    move = Moves(moves)
    pairs = (
        (i_grad_out_t, left),
        (i_hidden, hidden),
        (w_output, weight_o),
        (i_query, query),
        (i_inverse, inverse),
        (i_probs, probs),
        (i_key, key),
        (i_value, value),
        (i_mix, mix),
        (i_retrieved, retrieved),
        (i_local_out, local_out),
        (i_recall, recall),
        (i_pair_e, pair_e),
        (i_ys, ys),
        (i_xs, xs),
        (i_memory, memory),
    )
    barrier = pltpu.get_barrier_semaphore()
    for device in neighbours():
        pl.semaphore_signal(barrier, inc=1, device_id=device, device_id_type=MESH_ID)
    blocks = [weight_in.at[k, pl.ds(1024 * j, 1024)] for k in range(3) for j in (0, 1)]

    def load_down(half, q, block):
        return move.start(w_down.at[pl.ds(1024 * half, 1024), pl.ds(512 * q, 512)], blocks[block])

    loads = [move.start(src, dst) for src, dst in pairs[:2]]
    downs = [load_down(0, q, q) for q in range(4)] + [load_down(1, q, 4 + q) for q in (0, 1)]
    loads += [move.start(src, dst) for src, dst in pairs[2:]]
    gate_rows(gate, gate_logit)
    partner = {"seq_2": 1 - c}
    mine, theirs = 2 * c, 2 * (1 - c)
    parts = [pl.ds(0, 48), pl.ds(48, 48)]
    z_branches = [RingGather(branch, send, recv, 6 * i, "tensor", parts[i]) for i in (0, 1)]
    z_forths = [RingSum(forth, z_bufs.at[i], send, recv, (12, 174)[i], "tensor", parts[i]) for i in (0, 1)]
    z_layer = RingGather(layer_out, send, recv, 18, "tensor")
    y_ring = RingGather(s_y, send, recv, 24, "seq_1")
    x_ring = RingGather(s_x, send, recv, 30, "seq_0")
    swap = remote(source.at[pl.ds(theirs, 2)], got, send.at[36], recv.at[36], partner)
    give = remote(pair_l, got_l, send.at[37], recv.at[37], partner)
    z_ends = [RingSum(forth, z_bufs.at[i], send, recv, 143 + 6 * i, "tensor", parts[i]) for i in (0, 1)]
    z_tokens = [RingGather(grad_tokens, send, recv, 155 + 6 * i, "tensor", parts[i]) for i in (0, 1)]
    total = TotalOfAll(mine_gains, logits, by_z, total_line, by_seq, gains, send, recv, 167)

    def seq_sums(base, first_bufs, second_bufs, order):
        return [
            SeqSum(
                products.at[i], got_rows.at[i], first_rows.at[order[i]], first_bufs.at[i], second_rows.at[i],
                second_bufs.at[i], send, recv, base + 13 * i, i % 2 == 0,
            )
            for i in range(4)
        ]

    sums, ends = seq_sums(39, first_bufs, second_bufs, (0, 1, 2, 3)), seq_sums(91, first_bufs_2, second_bufs_2, (4, 1, 2, 3))
    cols = [slice(128 * h, 128 * (h + 1)) for h in range(4)]
    of = [pl.ds(0, 128), pl.ds(128, 128)]
    feat_q = lambda h: feature_of(query[:, cols[h]].astype(F32))
    feat_k = lambda h: feature_of(key[:, cols[h]].astype(F32))
    scale = 128 ** (-0.5)

    def half_product(right, core):
        return jnp.dot(core_rows(left, core), right, preferred_element_type=F32)

    def product(group, i, right):
        products[i] = half_product(right, 1 - c).astype(BF).reshape(16, 64, 512)
        group[i].start()

    def down(i):
        product(sums, i, hidden[:, 512 * i : 512 * (i + 1)])

    def down_add(i):
        sums[i].add(half_product(hidden[:, 512 * i : 512 * (i + 1)], c))

    def grads_ring(i):
        ends[i].add(half_product(grads[:, 512 * (i - 1) : 512 * i], c))
        ends[i].one.start()

    def norm_back(stream, grad_normed, gain, first_row, i):
        inv = lax.rsqrt(jnp.mean(stream * stream, axis=1, keepdims=True) + epsilon)
        weighted = grad_normed * gain[...]
        inner = jnp.sum(weighted * stream, axis=1, keepdims=True)
        scaled = stream * inv
        line_of = jnp.sum(grad_normed * scaled, axis=0, keepdims=True)
        for r in range(16):
            at = (first_row + r // 8, slice(r % 8, r % 8 + 1))
            piece = line_of[:, 128 * r : 128 * (r + 1)]
            mine_gains[at] = piece if i == 0 else mine_gains[at] + piece
        return inv * weighted - scaled * (inv * inv * inner * (1.0 / stream.shape[1]))

    def forward_part(half, order):
        value = sum(rows_by_rows(hidden[:, 512 * q : 512 * (q + 1)], blocks[order[q]][...]) for q in range(4))
        forth[:, :, pl.ds(1024 * half, 1024)] = value.astype(BF).reshape(4, 96, 1024)

    for i in (0, 1):
        rows = parts[i]
        result = grad_out[rows].astype(F32) + norm_back(middle[rows], grad_two[rows], gain_mlp, 2, i)
        grad_middle[rows] = result
        branch[z, rows] = result.astype(BF)
        if i == 0:
            pl.semaphore_wait(barrier, 7)
        z_branches[i].start()
    loads[0].wait()
    loads[1].wait()
    down(0)
    down(1)
    z_branches[0].middle()
    down_add(0)
    sums[0].one.start()
    z_branches[1].middle()
    down(2)
    down_add(1)
    sums[1].one.start()
    for load in downs[:4]:
        load.wait()
    forward_part(0, (0, 1, 2, 3))
    downs += [load_down(1, q, q - 2) for q in (2, 3)]
    down(3)
    down_add(2)
    sums[0].one.middle()
    down_add(3)
    for load in downs[4:]:
        load.wait()
    forward_part(1, (4, 5, 0, 1))
    late = [move.start(w, weight_in.at[i]) for i, w in enumerate((w_query, w_key, w_value))]
    for load in loads[2:5]:
        load.wait()
    for z_branch in z_branches:
        z_branch.finish()
    for z_forth in z_forths:
        z_forth.start()
    grad_mix[...] = jnp.dot(branch[...].reshape(384, 2048), weight_o[...], preferred_element_type=F32)

    def point(h):
        return gate[h : h + 1] * grad_mix[:, cols[h]] * inverse[:, h : h + 1]

    for h in range(4):
        source[h] = mul_t(feat_q(h), point(h)).astype(BF)
    swap.start()

    def attend(h):
        at = cols[h]
        grad_local = ((1.0 - gate[h : h + 1]) * grad_mix[:, at]).astype(BF)
        low = probs[h]
        p = low.astype(F32)
        grad_probs = rows_by_rows(grad_local, value[:, at])
        grad_value[:, at] = mul_t(low, grad_local)
        grad_scores = (p * (grad_probs - jnp.sum(grad_probs * p, axis=1, keepdims=True))).astype(BF)
        grad_query[:, at] = mul(grad_scores, key[:, at]) * scale
        grad_key[:, at] = mul_t(grad_scores, query[:, at]) * scale

    for load in loads[5:8]:
        load.wait()
    attend(0)
    sums[1].one.middle()
    swap.wait_recv()
    for load in loads[12:16]:
        load.wait()
    seconds = []
    for h in (0, 1):
        here, there = source[mine + h].astype(F32), got[h].astype(F32)
        first, second = jnp.where(c == 0, here, there), jnp.where(c == 0, there, here)
        seconds.append(second)
        s_y[y, of[h]] = (first + second - mul_t(pair_e[0, h], second)).astype(BF)
    y_ring.start()
    attend(1)
    y_ring.middle()
    sums[0].second_ring()
    attend(2)
    for z_forth in z_forths:
        z_forth.middle()
    sums[1].second_ring()
    for s in sums:
        s.swap.wait_send()
    left[...] = branch[...].reshape(384, 2048).T.reshape(16, 2, 64, 384)
    for z_branch in z_branches:
        z_branch.drain()
    load_own = move.start(tokens.at[pl.ds(pl.multiple_of(96 * z, 96), 96)], branch.at[0])
    y_ring.finish()
    for h in (0, 1):
        so_far = s_y[3, of[h]].astype(F32)
        for k in (2, 1, 0):
            so_far = s_y[k, of[h]].astype(F32) + so_far - mul_t(ys[k, of[h]][:, :128], so_far)
        s_x[x, of[h]] = so_far.astype(BF)
    x_ring.start()
    for load in loads[8:12]:
        load.wait()
    product(ends, 0, mix[...])
    ends[0].store(half_product(mix[...], c))
    x_ring.middle()
    load_t = move.start(i_normed_t, left)
    attend(3)
    logit_rows = []
    for h in range(4):
        at, gate_h, g = cols[h], gate[h : h + 1], grad_mix[:, cols[h]]
        ret = retrieved[:, at]
        moved = jnp.sum(g * (ret - local_out[:, at]), axis=0, keepdims=True) * gate_h * (1.0 - gate_h)
        logit_rows.append(jnp.sum(moved, axis=1, keepdims=True))
        grad_den = -jnp.sum(gate_h * g * ret, axis=1, keepdims=True) * inverse[:, h : h + 1]
        q = query[:, at].astype(F32)
        grad_feat = rows_by_rows(point(h).astype(BF), memory[h].astype(BF)) + grad_den * offset[h : h + 1]
        grads[:, at] = (grad_query[:, at] + grad_feat * slope_of(q)).astype(BF)
        line[h : h + 1] = jnp.sum(grad_den * feature_of(q), axis=0, keepdims=True)
    lane = lax.broadcasted_iota(jnp.int32, (8, 128), 1)
    row = lax.broadcasted_iota(jnp.int32, (8, 128), 0)
    spot = jnp.zeros((8, 128), F32)
    for h in range(4):
        spot = jnp.where((lane == h) & (row == 0), logit_rows[h], spot)
    logits[...] = spot
    for i in (0, 1):

        def put_layer(at, result, i=i):
            lanes = slice(0, 1024) if at is z_forths[i].a else slice(1024, 2048)
            layer_out[z, parts[i], at] = (middle[parts[i], lanes] + result).astype(BF)

        z_forths[i].finish(put_layer)
        z_forths[i].drain()
    z_layer.start()
    sums[0].two.middle()
    sums[1].two.middle()
    x_ring.finish()
    sums[2].one.start()
    sums[3].one.start()
    for h in (0, 1):
        lam = jnp.where(x < 3, s_x[3, of[h]].astype(F32), 0.0)
        for k in (2, 1):
            lam = jnp.where(x < k, s_x[k, of[h]].astype(F32) + lam - mul_t(xs[k, of[h]][:, :128], lam), lam)
        for k in (3, 2, 1):
            lam = jnp.where(y < k, s_y[k, of[h]].astype(F32) + lam - mul_t(ys[k, of[h]][:, :128], lam), lam)
        first = lam + seconds[h] - mul_t(pair_e[1, h], lam)
        adjoint[mine + h] = jnp.where(c == 0, first, lam).astype(BF)
        pair_l[h] = jnp.where(c == 0, lam, first).astype(BF)
    give.start()
    ends[0].add_stored()
    ends[0].one.start()
    for i in (0, 1):
        sums[i].finish(out_down.at[:, pl.ds(512 * i, 512)])
    give.wait_recv()
    for h in (0, 1):
        adjoint[theirs + h] = got_l[h]
    for h in range(4):
        at, fk = cols[h], feat_k(h)
        grad_update = mul(fk * inverse[:, 8:9], adjoint[h])
        grad_value[:, at] += grad_update
        grad_den = jnp.sum(grad_update * recall[:, at], axis=1, keepdims=True) * inverse[:, 4 + h : 5 + h]
        line[h : h + 1] += jnp.sum(grad_den * fk, axis=0, keepdims=True)
        grad_key[:, at] += slope_of(key[:, at].astype(F32)) * (
            grad_den * offset[h : h + 1]
            - rows_by_rows((grad_update * inverse[:, 4 + h : 5 + h]).astype(BF), memory[h].astype(BF))
        )
    line[4:8] = jnp.zeros((4, 128), F32)
    lines[me] = line[...]

    def push(k, carry):
        remote(line, lines.at[me], send.at[38], recv.at[38], seq_place(lax.rem(me + k, 32))).start()
        return carry

    lax.fori_loop(1, 32, push, 0)
    for h in range(4):
        at = cols[h]
        grads[:, 1024 + 128 * h : 1152 + 128 * h] = grad_value[:, at].astype(BF)
        update = value[:, at].astype(F32) - recall[:, at]
        grad_key[:, at] += (
            inverse[:, 8:9] * slope_of(key[:, at].astype(F32)) * rows_by_rows(update.astype(BF), adjoint[h])
        )
    sums[2].one.middle()
    load_t.wait()
    product(ends, 1, grads[:, 0:512])
    z_layer.middle()
    sums[3].one.middle()
    product(ends, 3, grads[:, 1024:1536])
    for s in sums[:2]:
        s.one.drain()
        s.two.drain()
    for load in (*late, load_own):
        load.wait()
    others = lines.at[pl.ds(0, 31)]
    pltpu.make_async_copy(others, others, recv.at[38]).wait()
    passed = lax.broadcasted_iota(jnp.int32, (32, 8, 128), 0) > me
    after = jnp.sum(jnp.where(passed, lines[...], 0.0), axis=0)
    later[...] = after[0:4]
    stores = [move.start(later, o_later)]
    for h in range(4):
        at = cols[h]
        late = inverse[:, 8:9] * after[h : h + 1] * slope_of(key[:, at].astype(F32))
        grads[:, 512 + 128 * h : 640 + 128 * h] = (grad_key[:, at] + late).astype(BF)
    z_layer.finish()
    stores.append(move.start(layer_out, o_layer_out))
    for half in (0, 1):
        rows = pl.ds(1024 * half, 1024)
        value = sum(rows_by_rows(grads[:, 512 * i : 512 * (i + 1)], weight_in[i, rows]) for i in range(3))
        forth[:, :, rows] = value.astype(BF).reshape(4, 96, 1024)
        for z_end in z_ends:
            (z_end.start_a, z_end.start_b)[half]()
    sums[2].second_ring()
    sums[3].second_ring()
    grads_ring(1)
    product(ends, 2, grads[:, 512:1024])
    z_ends[0].middle()
    z_ends[1].middle()
    ends[0].one.middle()
    for i in (2, 3):
        sums[i].two.middle()
        sums[i].one.drain()
    grads_ring(3)
    ends[1].one.middle()

    def put(at, result):
        own[:, at] = result

    for i in (0, 1):
        rows = parts[i]
        z_ends[i].finish(put)
        result = grad_middle[rows] + norm_back(branch[0, rows].astype(F32), own[...], gain_attn, 0, i)
        grad_tokens[z, rows] = result.astype(BF)
        z_tokens[i].start()
    total.start()
    grads_ring(2)
    for i in (2, 3):
        sums[i].finish(out_down.at[:, pl.ds(512 * i, 512)])
        sums[i].two.drain()
    stores.append(move.start(out_down, o_out_down))
    ends[0].second_ring()
    ends[3].one.middle()
    for z_token in z_tokens:
        z_token.middle()
    ends[1].second_ring()
    total.over_seq()
    ends[2].one.middle()
    ends[0].two.middle()
    ends[3].second_ring()
    ends[1].two.middle()
    total.over_tensor(logits_out)
    stores.append(move.start(logits_out, o_logits_out))
    ends[2].second_ring()
    ends[0].finish(out_output)
    stores.append(move.start(out_output, o_out_output))
    ends[3].two.middle()
    ends[1].finish(out_query)
    stores.append(move.start(out_query, o_out_query))
    ends[2].two.middle()
    ends[3].finish(out_value)
    stores.append(move.start(out_value, o_out_value))
    ends[2].finish(out_key)
    stores.append(move.start(out_key, o_out_key))
    total.finish()
    stores.append(move.start(gains, o_gains))
    for z_token in z_tokens:
        z_token.finish()
    stores.append(move.start(grad_tokens, o_grad_tokens))
    for part in (z_layer, y_ring, x_ring, *z_ends, *z_tokens, total, *ends):
        part.drain()
    swap.wait_send()
    give.wait_send()
    for store in stores:
        store.wait()
    pltpu.make_async_copy(others, others, send.at[38]).wait()


def rest(cid, *args):
    shape = jax.ShapeDtypeStruct
    low = lambda *dims: pltpu.VMEM(dims, BF)
    full = lambda *dims: pltpu.VMEM(dims, F32)
    weight_grad = shape((64, 512), F32)
    return pl.pallas_call(
        rest_kernel,
        out_shape=(
            shape((4, 96, 2048), BF),
            shape((4, 96, 2048), BF),
            shape((4, 128), F32),
            shape((64, 2048), F32),
            weight_grad,
            weight_grad,
            weight_grad,
            weight_grad,
            shape((4, 8, 128), F32),
            shape((8, 128), F32),
        ),
        in_specs=[VMEM] * 6 + [SMEM] + [ANYWHERE] * 22,
        out_specs=(ANYWHERE,) * 10,
        scratch_shapes=[
            low(4, 96, 2048),
            low(4, 96, 2048),
            full(4, 128),
            full(64, 2048),
            full(64, 512),
            full(64, 512),
            full(64, 512),
            full(64, 512),
            full(4, 8, 128),
            full(8, 128),
            full(4, 128, 128),
            low(4, 256, 256),
            low(4, 256, 256),
            low(2, 2, 128, 128),
            full(4, 128),
            low(4, 96, 2048),
            full(96, 2048),
            low(384, 1536),
            low(16, 2, 64, 384),
            low(384, 2048),
            low(384, 512),
            low(384, 512),
            low(384, 512),
            low(4, 384, 384),
            full(384, 512),
            full(384, 512),
            low(384, 512),
            low(2048, 512),
            low(3, 2048, 512),
            low(4, 16, 64, 512),
            low(4, 16, 64, 512),
            low(5, 4, 256, 512),
            low(4, 6, 256, 256),
            low(4, 4, 64, 512),
            low(4, 6, 64, 256),
            low(4, 6, 256, 256),
            low(4, 6, 64, 256),
            low(4, 96, 2048),
            low(2, 6, 48, 1024),
            full(48, 2048),
            full(384, 128),
            full(384, 512),
            full(384, 512),
            full(384, 512),
            full(384, 512),
            full(384, 512),
            low(4, 128, 128),
            low(2, 128, 128),
            low(4, 256, 128),
            low(4, 256, 128),
            low(2, 128, 128),
            low(2, 128, 128),
            low(4, 128, 128),
            full(8, 128),
            full(32, 8, 128),
            full(4, 8, 128),
            full(8, 128),
            full(4, 8, 128),
            full(16, 128),
            full(32, 16, 128),
            pltpu.SemaphoreType.DMA((42,)),
            pltpu.SemaphoreType.DMA((180,)),
            pltpu.SemaphoreType.DMA((180,)),
        ],
        name="rest",
        compiler_params=params(cid, 63),
    )(*args)


def last_kernel(*refs):
    ins, outs = refs[:14], refs[14:29]
    narrow, wide, rows, gate, up, sems, *held = refs[29:]
    move = Moves(sems)
    grad_tokens, mlp_grads, grad_gate, gains, *same = ins
    o_tokens, o_gate, o_up, o_attn, o_mlp, *o_same = outs
    fetch = [move.start(grad_tokens.at[q], narrow.at[q]) for q in range(4)]
    known = grad_gate.shape[1]
    fetch_gate = move.start(grad_gate, gate.at[:, pl.ds(0, known)])
    fetch_same = [move.start(src, dst) for src, dst in zip((gains, *same), held)]
    fetch_rows = move.start(mlp_grads, rows)
    copies = []
    for q in range(4):
        fetch[q].wait()
        wide[q] = narrow[q].astype(F32)
        copies.append(move.start(wide.at[q], o_tokens.at[q]))
    fetch_gate.wait()
    for copy in fetch_same:
        copy.wait()
    copies.append(move.start(held[0].at[pl.ds(0, 2)], o_attn))
    copies.append(move.start(held[0].at[pl.ds(2, 2)], o_mlp))
    copies += [move.start(src, dst) for src, dst in zip(held[1:], o_same)]
    fetch_rows.wait()
    split = gate.shape[1] - known
    gate[:, known:] = rows[:, :split].astype(F32)
    copies.append(move.start(gate, o_gate))
    up[...] = rows[:, split:].astype(F32)
    copies.append(move.start(up, o_up))
    for copy in copies:
        copy.wait()


def last(grad_tokens, mlp_grads, grad_gate, gains, *same):
    shape = jax.ShapeDtypeStruct
    wide = shape((64, (mlp_grads.shape[1] + grad_gate.shape[1]) // 2), F32)
    gain = shape((2, 8, 128), F32)
    outs = (shape(grad_tokens.shape, F32), wide, wide, gain, gain, *(shape(a.shape, a.dtype) for a in same))
    return pl.pallas_call(
        last_kernel,
        out_shape=outs,
        in_specs=[ANYWHERE] * 14,
        out_specs=(ANYWHERE,) * len(outs),
        scratch_shapes=[
            pltpu.VMEM(grad_tokens.shape, BF),
            pltpu.VMEM(grad_tokens.shape, F32),
            pltpu.VMEM(mlp_grads.shape, BF),
            pltpu.VMEM(wide.shape, F32),
            pltpu.VMEM(wide.shape, F32),
            pltpu.SemaphoreType.DMA((36,)),
            *(pltpu.VMEM(a.shape, a.dtype) for a in (gains, *same)),
        ],
        name="last",
        compiler_params=pltpu.CompilerParams(vmem_limit_bytes=63 << 20),
    )(grad_tokens, mlp_grads, grad_gate, gains, *same)


def on_device(
    tokens,
    cotangent,
    w_query,
    w_key,
    w_value,
    w_output,
    w_gate,
    w_up,
    w_down,
    gain_attn,
    gain_mlp,
    gate_logit,
    valid_count,
):
    valid = valid_count[None]
    rows = (16, 2, 64, 512)
    (
        normed_t, grad_out_t, query, key, value, probs, local_out, retrieved, mix, hidden, mlp_grads,
        recall, inverse, grad_out_own, offset, normal_next, memory_prev, memory_next, ys, xs, pair_e, middle,
        grad_two, grad_gate,
    ) = front(
        0, gain_attn[None], gain_mlp[None], valid, gate_logit, tokens, cotangent,
        *(w.reshape(rows) for w in (w_query, w_key, w_value, w_output)), w_down, w_gate, w_up,
    )
    mlp_grads = lax.psum_scatter(mlp_grads.reshape(1024, -1), SEQ[:2], scatter_dimension=0, tiled=True)
    (
        layer_out, grad_tokens, later_offset, grad_down, grad_query, grad_key, grad_value, grad_output, gains, logit_grad,
    ) = rest(
        1, grad_two, middle, gain_attn[None], gain_mlp[None], grad_out_own, offset, gate_logit, memory_prev, ys, xs, pair_e,
        grad_out_t, hidden, query, key, value, probs, local_out, retrieved, mix, normed_t, recall, inverse,
        w_query, w_key, w_value, w_output, w_down, tokens,
    )
    (
        grad_tokens, grad_gate, grad_up, gain_attn_grad, gain_mlp_grad, layer_out, grad_query, grad_key, grad_value,
        grad_output, grad_down, logit_grad, memory_next, normal_next, later_offset,
    ) = last(
        grad_tokens, mlp_grads, grad_gate, gains, layer_out, grad_query, grad_key, grad_value, grad_output, grad_down,
        logit_grad, memory_next, normal_next, later_offset,
    )
    return (
        layer_out.reshape(tokens.shape),
        grad_tokens.reshape(tokens.shape),
        grad_query,
        grad_key,
        grad_value,
        grad_output,
        grad_gate,
        grad_up,
        grad_down,
        gain_attn_grad.reshape(-1),
        gain_mlp_grad.reshape(-1),
        logit_grad[0, :4],
        memory_next[None],
        normal_next[None],
        later_offset[None],
    )


def solution(mesh):
    torus = Mesh(
        mesh.devices.reshape(4, 4, 2, mesh.shape["tensor"]), ("seq_0", "seq_1", "seq_2", "tensor")
    )
    weight = P(None, "tensor")
    grad = P(SEQ, "tensor")
    return jax.shard_map(
        on_device,
        mesh=torus,
        in_specs=(P(SEQ, None), P(SEQ, None)) + (weight,) * 7 + (P(), P(), P("tensor"), P()),
        out_specs=(P(SEQ, None), P(SEQ, None))
        + (grad,) * 7
        + (P(), P(), P("tensor"), P(SEQ, "tensor", None, None), P(SEQ, "tensor", None), P(SEQ, "tensor", None)),
        check_vma=False,
    )
```
